32 devices in a mesh: row: 8 (over y, x, core), col: 4 (over z).
Axes of the slice: x: 2, y: 2, z: 4, core: 2. Of those that a mesh axis runs over, the one named last changes fastest.
Arguments:
- p_cols: int32 [128, 16], P('row', 'col'), may hold values from -1 to 31, as said below
- p_data: float32 [8192, 1024], P('row', 'col'), may hold values from -1.5 to 1.5
Outputs:
- product: float32 [8192, 8192], P('row', 'col')
The draws below stay inside these ranges and needn't reach their ends.
Inputs may be any that keep to these rules, and one draw needn't show every extreme that they name: `p_cols`: in each column tile, each block row has 1 to 4 used slots, the used ones first, with distinct columns; the first block row of each device's rows has all 4 used.
All inputs are finite; a program needn't handle non-finite values.
Results may differ from the reference program's by a relative error of at most 0.0003.
Values sent between devices are 32-bit elements; how exact they have to be, the bound alone decides.
No kernel may reach another device: no remote copies, remote signals or barrier semaphores. Data moves between devices by JAX's collectives and lax.ppermute only.
A program may use at most 192 MiB of HBM per device.

```python
import jax
import jax.numpy as jnp
from jax import lax

BS = 64
W = 4
RB = 16
STEPS = 4
RATIO = 2
CB = 32
NB = 128
N_ROW = 8
N_COL = 4


def draw_p_cols(key, part):
    score_key = jax.random.fold_in(key, 11)
    count_key = jax.random.fold_in(key, 23)
    scores = jax.random.randint(score_key, (NB, N_COL, CB), 0, 1 << 20, dtype=jnp.int32)
    scores = scores * CB + jnp.arange(CB, dtype=jnp.int32)
    chosen = lax.top_k(scores, W)[1].astype(jnp.int32)
    counts = jax.random.randint(count_key, (NB, N_COL), 1, W + 1, dtype=jnp.int32)
    first_rows = jnp.arange(NB, dtype=jnp.int32) % RB == 0
    counts = jnp.where(first_rows[:, None], W, counts)
    used = jnp.arange(W, dtype=jnp.int32)[None, None, :] < counts[:, :, None]
    filled = jnp.where(used, chosen, -1)
    return filled.reshape(NB, N_COL * W).astype(jnp.int32)


def steps_of(key, dims, cuts, least, largest):
    level, own = 1.0, jax.random.fold_in(key, 6)
    for dim, blocks in cuts:
        heights = jnp.exp(jax.random.uniform(jax.random.fold_in(own, dim), (blocks,), jnp.float32, least / len(cuts), largest / len(cuts)))
        level = level * jnp.repeat(heights, dims[dim] // blocks).reshape([-1 if axis == dim else 1 for axis in range(len(dims))])
    return level


def noise(rng, dims, width, limit, pieces=(), kind=jnp.bfloat16):
    values = width * jax.random.normal(rng, dims, jnp.float32)
    if pieces:
        values = values * steps_of(rng, dims, pieces, -0.22, 0.18)
    return jnp.clip(values, -limit, limit).astype(kind)


def setup_inputs(seed: int = 0) -> dict:
    splits = jax.random.split(jax.random.key(seed), 3)
    p_cols = draw_p_cols(jax.random.fold_in(splits[2], 71), 0)
    p_data = noise(splits[1], (NB * BS, N_COL * W * BS), 0.25, 1.5, ((0, 8), (1, 4)), jnp.float32)
    return {"p_cols": p_cols, "p_data": p_data}


def tile_product(left_cols, left_data, right_cols, right_data, piece_index, block_rows, tile_cols):
    slot_count = left_cols.shape[1]
    inner_local = left_cols - piece_index * block_rows
    usable = (left_cols >= 0) & (inner_local >= 0) & (inner_local < block_rows)
    inner_row = jnp.clip(inner_local, 0, block_rows - 1).astype(jnp.int32)
    left_blocks = left_data.reshape(block_rows, BS, slot_count, BS).transpose(0, 2, 1, 3)
    left_blocks = jnp.where(usable[:, :, None, None], left_blocks, jnp.zeros_like(left_blocks))
    right_rows = right_data.reshape(block_rows, BS, slot_count * BS)[inner_row]
    targets = right_cols[inner_row]
    partial_prod = jnp.einsum("rwij,rwjk->rwik", left_blocks, right_rows, precision=lax.Precision.HIGHEST)
    partial_prod = partial_prod.reshape(block_rows, slot_count, BS, slot_count, BS)
    placing = (targets[..., None] == jnp.arange(tile_cols, dtype=jnp.int32)).astype(left_data.dtype)
    result = jnp.einsum("rwvc,rwivk->rick", placing, partial_prod, precision=lax.Precision.HIGHEST)
    return result.reshape(block_rows * BS, tile_cols * BS)


def reference(p_cols, p_data):
    def one_tile(tile_index):
        row_tile = tile_index // N_COL
        col_tile = tile_index % N_COL
        accum = jnp.zeros((RB * BS, CB * BS), p_data.dtype)
        for step_index in range(STEPS):
            inner_tile = (row_tile + RATIO * col_tile + step_index) % N_ROW
            left_tile_col = inner_tile // RATIO
            piece_index = inner_tile % RATIO
            left_cols = lax.dynamic_slice(p_cols, ((row_tile * RB).astype(jnp.int32), (left_tile_col * W).astype(jnp.int32)), (RB, W))
            left_data = lax.dynamic_slice(p_data, ((row_tile * RB * BS).astype(jnp.int32), (left_tile_col * W * BS).astype(jnp.int32)), (RB * BS, W * BS))
            right_cols = lax.dynamic_slice(p_cols, ((inner_tile * RB).astype(jnp.int32), (col_tile * W).astype(jnp.int32)), (RB, W))
            right_data = lax.dynamic_slice(p_data, ((inner_tile * RB * BS).astype(jnp.int32), (col_tile * W * BS).astype(jnp.int32)), (RB * BS, W * BS))
            accum = accum + tile_product(left_cols, left_data, right_cols, right_data, piece_index, RB, CB)
        return accum

    stacked = lax.map(one_tile, jnp.arange(N_ROW * N_COL, dtype=jnp.int32))
    stacked = stacked.reshape(N_ROW, N_COL, RB * BS, CB * BS).transpose(0, 2, 1, 3)
    return stacked.reshape(NB * BS, N_COL * CB * BS)
```

```python
import functools

import jax
import jax.numpy as jnp
import numpy as np
from jax import lax
from jax.experimental import pallas as pl
from jax.experimental.pallas import tpu as pltpu
from jax.sharding import PartitionSpec as P

BS = 64
STEPS = 4
UNROLL = 4
PARTS = 4


def left_offsets(row, ratio, n_col):
    seen = []
    for step in range(STEPS):
        offset = (row + step) // ratio % n_col
        if offset not in seen:
            seen.append(offset)
    return seen


def left_plan(n_row, n_col, ratio):
    offsets = [left_offsets(row, ratio, n_col) for row in range(n_row)]
    if (n_row, n_col, ratio) != (8, 4, 2):
        perms = []
        for slot in range(max(len(o) for o in offsets)):
            pairs = [
                ((row, (col + offsets[row][slot]) % n_col), (row, col))
                for row in range(n_row)
                for col in range(n_col)
                if slot < len(offsets[row]) and offsets[row][slot] != 0
            ]
            perms.append((0, pairs))
        return perms
    down, up, two, fwd_down, fwd_up, fwd_two = [], [], [], [], [], []
    for row in range(n_row):
        need = set(offsets[row])
        both = 1 in need and 3 in need
        if 1 in need:
            down += [((row, c), (row, c - 1)) for c in (1, 2, 3)]
        if 3 in need:
            up += [((row, c), (row, c + 1)) for c in (0, 1, 2)]
        if 1 in need and (both or need in ({0, 1}, {0, 1, 2})):
            down.append(((row, 0), (row, 3)))
        if 3 in need and (both or need in ({0, 3}, {0, 2, 3})):
            up.append(((row, 3), (row, 0)))
        if need == {0, 1, 2} or need == {0, 2, 3}:
            two += [((row, c), (row, (c + 2) % 4)) for c in range(4)]
        elif need == {1, 2}:
            two += [((row, 0), (row, 2)), ((row, 1), (row, 3))]
            fwd_down += [((row, 1), (row, 0)), ((row, 2), (row, 1))]
            fwd_two.append(((row, 2), (row, 3)))
        elif need == {2, 3}:
            two += [((row, 2), (row, 0)), ((row, 3), (row, 1))]
            fwd_up += [((row, 1), (row, 2)), ((row, 2), (row, 3))]
            fwd_two.append(((row, 1), (row, 0)))
        elif need == {1, 2, 3}:
            fwd_down += [((row, 1), (row, 0)), ((row, 2), (row, 1))]
            fwd_up += [((row, 1), (row, 2)), ((row, 2), (row, 3))]
    return [(0, down), (0, up), (0, two), (1, fwd_down), (2, fwd_up), (3, fwd_two)]


def left_sources(perms, n_row, n_col, ratio):
    held = [{(r, c): c for r in range(n_row) for c in range(n_col)}]
    for source, pairs in perms:
        held.append({dst: held[source][src] for src, dst in pairs})
    slots = (ratio - 1 + STEPS - 1) // ratio + 1
    table = np.full((n_row, n_col, slots), -1, np.int32)
    for r in range(n_row):
        for c in range(n_col):
            for slot, offset in enumerate(left_offsets(r, ratio, n_col)):
                tile = (c + offset) % n_col
                table[r, c, slot] = [i for i, h in enumerate(held) if h.get((r, c)) == tile][0]
    return table


def kernel(n_buf, slots, rb, src_ref, tiles_ref, count_ref, code_ref, rcol_ref, *refs):
    bufs, gathered, out_ref = refs[:n_buf], refs[n_buf], refs[n_buf + 1]
    left, raw, split, acc, lsem, rsem, osem = refs[n_buf + 2 :]
    rows, width = left.shape[1], left.shape[2]

    def right_copy(step):
        return pltpu.make_async_copy(gathered.at[tiles_ref[step]], raw.at[step], rsem.at[step])

    for step in range(STEPS):
        right_copy(step).start()
    for slot in range(slots):
        for index in range(n_buf):
            @pl.when(src_ref[slot] == index)
            def _():
                pltpu.make_async_copy(bufs[index], left.at[slot], lsem.at[slot]).start()

    @pl.loop(0, rows // BS)
    def _(r):
        acc[pl.ds(pl.multiple_of(r * BS, BS), BS), :] = jnp.zeros((BS, acc.shape[1]), jnp.float32)

    for step in range(STEPS):
        right_copy(step).wait()

        @pl.loop(0, rb)
        def _(i):
            x = raw[step, pl.ds(pl.multiple_of(i * BS, BS), BS), :]
            hi = x.astype(jnp.bfloat16)
            split[step * rb + i, 0:BS, :] = hi
            split[step * rb + i, BS : 2 * BS, :] = (x - hi.astype(jnp.float32)).astype(jnp.bfloat16)

    for slot in range(slots):
        @pl.when(src_ref[slot] >= 0)
        def _():
            pltpu.make_async_copy(bufs[0], left.at[slot], lsem.at[slot]).wait()

    low = lax.broadcasted_iota(jnp.int32, (BS, 2 * BS), 1) < BS
    half = lax.broadcasted_iota(jnp.int32, (BS, 2 * BS), 1) // BS

    def product(code):
        block = code & 255
        slot = (code >> 8) & 15
        tile = (code >> 12) & 15
        row = (code >> 16) * BS
        x = left[tile, pl.ds(pl.multiple_of(row, BS), BS), pl.ds(pl.multiple_of((slot >> 1) * 2 * BS, 2 * BS), 2 * BS)]
        turned = pltpu.roll(x, BS, 1)
        odd = (slot & 1) == 1
        first = jnp.where(odd, turned, x)
        second = jnp.where(odd, x, turned)
        first_hi = first.astype(jnp.bfloat16)
        second_lo = second - second.astype(jnp.bfloat16).astype(jnp.float32)
        mixed = jnp.where(low, first_hi.astype(jnp.float32), second_lo).astype(jnp.bfloat16)
        lhs = jnp.concatenate([mixed, first_hi[:, :BS]], axis=1)
        hi = split[block, 0:BS, :]
        rhs = jnp.concatenate([hi, hi, split[block, BS : 2 * BS, :]], axis=0)
        return block, row, jnp.dot(lhs, rhs, preferred_element_type=jnp.float32)

    def add(block, row, value):
        for pair in range(width // (2 * BS)):
            x = value[:, pair * 2 * BS : (pair + 1) * 2 * BS]
            turned = pltpu.roll(x, BS, 1)
            for side in range(2):
                col = rcol_ref[block * (width // BS) + 2 * pair + side]
                parity = jnp.where(col < 0, 2, col & 1)
                base = (jnp.maximum(col, 0) >> 1) * 2 * BS
                picked = jnp.where((col & 1) == side, x, turned)
                picked = jnp.where(half == parity, picked, 0.0)
                at = (pl.ds(pl.multiple_of(row, BS), BS), pl.ds(pl.multiple_of(base, 2 * BS), 2 * BS))
                acc[at] += picked

    part_rows = rows // PARTS
    per_part = code_ref.shape[0] // PARTS

    def out_copy(part):
        at = pl.ds(part * part_rows, part_rows)
        return pltpu.make_async_copy(acc.at[at], out_ref.at[at], osem.at[part])

    for part in range(PARTS):
        @pl.loop(0, count_ref[part])
        def _(group):
            done = [product(code_ref[part * per_part + group * UNROLL + u]) for u in range(UNROLL)]
            for item in done:
                add(*item)

        out_copy(part).start()
    for part in range(PARTS):
        out_copy(part).wait()


def entry_lists(left_cols, row_id, col_id, n_row, n_col, ratio, rb, slots):
    w = left_cols.shape[1] // n_col
    slot_col = jnp.arange(left_cols.shape[1], dtype=jnp.int32)
    tile_col = slot_col // w
    inner_tile = tile_col[None, :] * ratio + left_cols // rb
    step = (inner_tile - row_id - ratio * col_id) % n_row
    valid = (left_cols >= 0) & (step < STEPS)
    tile_slot = (tile_col - row_id // ratio - col_id) % n_col
    row = jnp.arange(left_cols.shape[0], dtype=jnp.int32)[:, None]
    block = step * rb + left_cols % rb
    code = block | (slot_col % w)[None, :] << 8 | tile_slot[None, :] << 12 | row << 16
    valid = valid.reshape(PARTS, -1)
    code = code.reshape(PARTS, -1)
    place = jnp.cumsum(valid.astype(jnp.int32), axis=1) - 1
    count = place[:, -1] + 1
    size = code.shape[1]
    spots = jnp.arange(size + UNROLL, dtype=jnp.int32)
    hit = (place[:, None, :] == spots[None, :, None]) & valid[:, None, :]
    packed = jnp.sum(jnp.where(hit, code[:, None, :], 0), axis=2)
    packed = jnp.where(spots[None, :] < count[:, None], packed, STEPS * rb)
    return (count + UNROLL - 1) // UNROLL, packed.reshape(-1)


def local(p_cols, p_data):
    n_row, n_col = lax.axis_size("row"), lax.axis_size("col")
    ratio = n_row // n_col
    row_id, col_id = lax.axis_index("row"), lax.axis_index("col")
    rb, w = p_cols.shape
    perms = left_plan(n_row, n_col, ratio)
    sources = left_sources(perms, n_row, n_col, ratio)
    slots = sources.shape[2]
    flat = lambda place: place[0] * n_col + place[1]
    bufs = [p_data]
    for source, pairs in perms:
        bufs.append(lax.ppermute(bufs[source], ("row", "col"), [(flat(s), flat(d)) for s, d in pairs]))
    gathered = lax.all_gather(p_data, "row")
    left_cols = lax.all_gather(p_cols, "col", axis=1, tiled=True)
    all_right = lax.all_gather(p_cols, "row")

    tiles = (row_id + ratio * col_id + jnp.arange(STEPS, dtype=jnp.int32)) % n_row
    right_cols = jnp.take(all_right, tiles, axis=0).reshape(-1)
    right_cols = jnp.concatenate([right_cols, jnp.full((w,), -1, jnp.int32)])
    counts, codes = entry_lists(left_cols, row_id, col_id, n_row, n_col, ratio, rb, slots)
    src = jnp.asarray(sources)[row_id, col_id]

    rows, width = p_data.shape
    out_shape = jax.ShapeDtypeStruct((rows, rb * ratio * BS), jnp.float32)
    smem = pl.BlockSpec(memory_space=pltpu.SMEM)
    hbm = pl.BlockSpec(memory_space=pl.ANY)
    return pl.pallas_call(
        functools.partial(kernel, len(bufs), slots, rb),
        out_shape=out_shape,
        in_specs=[smem] * 5 + [hbm] * (len(bufs) + 1),
        out_specs=hbm,
        scratch_shapes=[
            pltpu.VMEM((slots, rows, width), jnp.float32),
            pltpu.VMEM((STEPS, rows, width), jnp.float32),
            pltpu.VMEM((STEPS * rb + 1, 2 * BS, width), jnp.bfloat16),
            pltpu.VMEM(out_shape.shape, jnp.float32),
            pltpu.SemaphoreType.DMA((slots,)),
            pltpu.SemaphoreType.DMA((STEPS,)),
            pltpu.SemaphoreType.DMA((PARTS,)),
        ],
        compiler_params=pltpu.CompilerParams(vmem_limit_bytes=40 << 20),
        cost_estimate=pl.CostEstimate(flops=10**9, bytes_accessed=20 << 20, transcendentals=0),
    )(src, tiles, counts, codes, right_cols, *bufs, gathered)


def solution(mesh):
    in_specs = (P("row", "col"), P("row", "col"))
    return jax.shard_map(local, mesh=mesh, in_specs=in_specs, out_specs=P("row", "col"), check_vma=False)
```

```python
import functools

import jax
import jax.numpy as jnp
import numpy as np
from jax import lax
from jax.experimental import pallas as pl
from jax.experimental.pallas import tpu as pltpu
from jax.sharding import PartitionSpec as P

BS = 64
STEPS = 4
UNROLL = 4
EXTRA = 8


def left_offsets(row, ratio, n_col):
    seen = []
    for step in range(STEPS):
        offset = (row + step) // ratio % n_col
        if offset not in seen:
            seen.append(offset)
    return seen


def left_plan(n_row, n_col, ratio):
    offsets = [left_offsets(row, ratio, n_col) for row in range(n_row)]
    if (n_row, n_col, ratio) != (8, 4, 2):
        perms = []
        for slot in range(max(len(o) for o in offsets)):
            pairs = [
                ((row, (col + offsets[row][slot]) % n_col), (row, col))
                for row in range(n_row)
                for col in range(n_col)
                if slot < len(offsets[row]) and offsets[row][slot] != 0
            ]
            perms.append((0, pairs))
        return perms
    down, up, two, fwd_down, fwd_up, fwd_two = [], [], [], [], [], []
    for row in range(n_row):
        need = set(offsets[row])
        both = 1 in need and 3 in need
        if 1 in need:
            down += [((row, c), (row, c - 1)) for c in (1, 2, 3)]
        if 3 in need:
            up += [((row, c), (row, c + 1)) for c in (0, 1, 2)]
        if 1 in need and (both or need in ({0, 1}, {0, 1, 2})):
            down.append(((row, 0), (row, 3)))
        if 3 in need and (both or need in ({0, 3}, {0, 2, 3})):
            up.append(((row, 3), (row, 0)))
        if need == {0, 1, 2} or need == {0, 2, 3}:
            two += [((row, c), (row, (c + 2) % 4)) for c in range(4)]
        elif need == {1, 2}:
            two += [((row, 0), (row, 2)), ((row, 1), (row, 3))]
            fwd_down += [((row, 1), (row, 0)), ((row, 2), (row, 1))]
            fwd_two.append(((row, 2), (row, 3)))
        elif need == {2, 3}:
            two += [((row, 2), (row, 0)), ((row, 3), (row, 1))]
            fwd_up += [((row, 1), (row, 2)), ((row, 2), (row, 3))]
            fwd_two.append(((row, 1), (row, 0)))
        elif need == {1, 2, 3}:
            fwd_down += [((row, 1), (row, 0)), ((row, 2), (row, 1))]
            fwd_up += [((row, 1), (row, 2)), ((row, 2), (row, 3))]
    return [(0, down), (0, up), (0, two), (1, fwd_down), (2, fwd_up), (3, fwd_two)]


def right_plan(n_row, n_col, ratio):
    everyone = [(row, col) for row in range(n_row) for col in range(n_col)]
    if (n_row, n_col, ratio) != (8, 4, 2):
        return [
            (0, [(((r + ratio * c + step) % n_row, c), (r, c)) for r, c in everyone if (ratio * c + step) % n_row])
            for step in range(STEPS)
        ]
    first = [(((r + 2 * c) % 8, c), (r, c)) for r, c in everyone if c != 0]
    second = [(((r + 2 * c + 2) % 8, c), (r, c)) for r, c in everyone if c != 3]
    last = [(((r - 1 + 2 * c + 4) % 8, c), (r, c)) for r, c in everyone if r % 2 == 1]
    own_swap = [((r + 1, 0), (r, 0)) for r in range(0, 8, 2)] + [((r ^ 1, 3), (r, 3)) for r in range(8)]
    first_swap = [((r + 1, c), (r, c)) for r, c in everyone if r % 2 == 0 and c != 0]
    second_swap = [((r ^ 1, c), (r, c)) for r, c in everyone if c != 3]
    return [(0, first), (0, second), (0, last), (0, own_swap), (1, first_swap), (2, second_swap)]


def carry_out(perms, n_row, n_col):
    held = [{(r, c): (r, c) for r in range(n_row) for c in range(n_col)}]
    for source, pairs in perms:
        held.append({dst: held[source][src] for src, dst in pairs})
    return held


def device_table(left_perms, right_perms, n_row, n_col, ratio):
    left_held = carry_out(left_perms, n_row, n_col)
    right_held = carry_out(right_perms, n_row, n_col)
    slots = (ratio - 1 + STEPS - 1) // ratio + 1
    table = np.full((n_row, n_col, 2 * slots + STEPS), -1, np.int32)

    def find(held, device, tile):
        return [i for i, h in enumerate(held) if h.get(device) == tile][0]

    for r in range(n_row):
        for c in range(n_col):
            for slot, offset in enumerate(left_offsets(r, ratio, n_col)):
                tile_col = (c + offset) % n_col
                table[r, c, slot] = find(left_held, (r, c), (r, tile_col))
                table[r, c, slots + STEPS + slot] = (tile_col * ratio - r - ratio * c) % n_row
            for step in range(STEPS):
                table[r, c, slots + step] = find(right_held, (r, c), ((r + ratio * c + step) % n_row, c))
    return table, slots


def kernel(n_left, n_right, slots, n_row, rb, info_ref, *refs):
    left_bufs, right_bufs = refs[:n_left], refs[n_left : n_left + n_right]
    out_ref = refs[n_left + n_right]
    left, raw, split, acc, left_cols, right_cols, codes, lsem, rsem, lcsem, rcsem, osem = refs[n_left + n_right + 1 :]
    rows, width = raw.shape[1], raw.shape[2]
    w = width // BS

    def fetch(choice, bufs, index, data, cols, sem, col_sem):
        for number, buf in enumerate(bufs):
            @pl.when(choice == number)
            def _():
                pltpu.make_async_copy(buf.at[pl.ds(rows, EXTRA)], cols.at[index], col_sem.at[index]).start()
                pltpu.make_async_copy(buf.at[pl.ds(0, rows)], data.at[index], sem.at[index]).start()

    for slot in range(slots):
        fetch(info_ref[slot], left_bufs, slot, left, left_cols, lsem, lcsem)
    for step in range(STEPS):
        fetch(info_ref[slots + step], right_bufs, step, raw, right_cols, rsem, rcsem)

    @pl.loop(0, rb)
    def _(r):
        acc[pl.ds(pl.multiple_of(r * BS, BS), BS), :] = jnp.zeros((BS, acc.shape[1]), jnp.float32)

    for slot in range(slots):
        @pl.when(info_ref[slot] >= 0)
        def _():
            pltpu.make_async_copy(left_bufs[0].at[pl.ds(rows, EXTRA)], left_cols.at[slot], lcsem.at[slot]).wait()

    first_steps = [info_ref[slots + STEPS + slot] for slot in range(slots)]
    used = [info_ref[slot] >= 0 for slot in range(slots)]
    part_rows = rb // STEPS
    bounds = [0]
    for part in range(STEPS):
        pltpu.make_async_copy(right_bufs[0].at[pl.ds(0, rows)], raw.at[part], rsem.at[part]).wait()
        pltpu.make_async_copy(right_bufs[0].at[pl.ds(rows, EXTRA)], right_cols.at[part], rcsem.at[part]).wait()

        def prepare(i, place):
            row = part * part_rows + i
            for j in range(STEPS):
                block = i * STEPS + j
                x = raw[part, pl.ds(pl.multiple_of(block * BS, BS), BS), :]
                hi = x.astype(jnp.bfloat16)
                split[part * rb + block, 0:BS, :] = hi
                split[part * rb + block, BS : 2 * BS, :] = (x - hi.astype(jnp.float32)).astype(jnp.bfloat16)
            for slot in range(slots):
                for k in range(w):
                    col = left_cols[slot, 0, row * w + k].astype(jnp.int32)
                    step = first_steps[slot] + lax.div(col, rb)
                    step = jnp.where(step >= n_row, step - n_row, step)
                    valid = used[slot] & (col >= 0) & (step < STEPS)
                    codes[place] = (step * rb + lax.rem(col, rb)) | k << 8 | slot << 12 | row << 16
                    place = place + valid.astype(jnp.int32)
            return place

        place = lax.fori_loop(0, part_rows, prepare, bounds[-1])
        for u in range(UNROLL - 1):
            codes[place + u] = STEPS * rb
        bounds.append((place + UNROLL - 1) // UNROLL * UNROLL)
    for k in range(w):
        right_cols[STEPS, 0, k] = -1.0

    for slot in range(slots):
        @pl.when(info_ref[slot] >= 0)
        def _():
            pltpu.make_async_copy(left_bufs[0].at[pl.ds(0, rows)], left.at[slot], lsem.at[slot]).wait()

    low = lax.broadcasted_iota(jnp.int32, (BS, 2 * BS), 1) < BS
    half = lax.broadcasted_iota(jnp.int32, (BS, 2 * BS), 1) // BS

    def product(code):
        block = code & 255
        slot = (code >> 8) & 15
        tile = (code >> 12) & 15
        row = (code >> 16) * BS
        x = left[tile, pl.ds(pl.multiple_of(row, BS), BS), pl.ds(pl.multiple_of((slot >> 1) * 2 * BS, 2 * BS), 2 * BS)]
        turned = pltpu.roll(x, BS, 1)
        odd = (slot & 1) == 1
        first = jnp.where(odd, turned, x)
        second = jnp.where(odd, x, turned)
        first_hi = first.astype(jnp.bfloat16)
        second_lo = second - second.astype(jnp.bfloat16).astype(jnp.float32)
        mixed = jnp.where(low, first_hi.astype(jnp.float32), second_lo).astype(jnp.bfloat16)
        lhs = jnp.concatenate([mixed, first_hi[:, :BS]], axis=1)
        hi = split[block, 0:BS, :]
        rhs = jnp.concatenate([hi, hi, split[block, BS : 2 * BS, :]], axis=0)
        return block, row, jnp.dot(lhs, rhs, preferred_element_type=jnp.float32)

    def add(block, row, value):
        step = lax.div(block, rb)
        inner = lax.rem(block, rb) * w
        for pair in range(w // 2):
            x = value[:, pair * 2 * BS : (pair + 1) * 2 * BS]
            turned = pltpu.roll(x, BS, 1)
            for side in range(2):
                col = right_cols[step, 0, inner + 2 * pair + side].astype(jnp.int32)
                parity = jnp.where(col < 0, 2, col & 1)
                base = (jnp.maximum(col, 0) >> 1) * 2 * BS
                picked = jnp.where((col & 1) == side, x, turned)
                picked = jnp.where(half == parity, picked, 0.0)
                at = (pl.ds(pl.multiple_of(row, BS), BS), pl.ds(pl.multiple_of(base, 2 * BS), 2 * BS))
                acc[at] += picked

    def out_copy(part):
        at = pl.ds(part * part_rows * BS, part_rows * BS)
        return pltpu.make_async_copy(acc.at[at], out_ref.at[at], osem.at[part])

    for part in range(STEPS):
        @pl.loop(lax.div(bounds[part], UNROLL), lax.div(bounds[part + 1], UNROLL))
        def _(group):
            done = [product(codes[group * UNROLL + u]) for u in range(UNROLL)]
            for item in done:
                add(*item)

        out_copy(part).start()
    for part in range(STEPS):
        out_copy(part).wait()


def local(p_cols, p_data):
    n_row, n_col = lax.axis_size("row"), lax.axis_size("col")
    ratio = n_row // n_col
    row_id, col_id = lax.axis_index("row"), lax.axis_index("col")
    rb, w = p_cols.shape
    rows, width = p_data.shape
    left_perms = left_plan(n_row, n_col, ratio)
    right_perms = right_plan(n_row, n_col, ratio)
    table, slots = device_table(left_perms, right_perms, n_row, n_col, ratio)
    info = jnp.asarray(table)[row_id, col_id]

    cols = jnp.pad(p_cols.astype(jnp.float32).reshape(1, -1), ((0, EXTRA - 1), (0, width - rb * w)))
    own = jnp.concatenate([p_data, cols], axis=0)

    def carry(perms):
        bufs = [own]
        for source, pairs in perms:
            flat = [(s[0] * n_col + s[1], d[0] * n_col + d[1]) for s, d in pairs]
            bufs.append(lax.ppermute(bufs[source], ("row", "col"), flat))
        return bufs

    left_bufs = carry(left_perms)
    right_bufs = carry(right_perms)
    out_shape = jax.ShapeDtypeStruct((rows, rb * ratio * BS), jnp.float32)
    smem = pl.BlockSpec(memory_space=pltpu.SMEM)
    hbm = pl.BlockSpec(memory_space=pl.ANY)
    dma = pltpu.SemaphoreType.DMA
    return pl.pallas_call(
        functools.partial(kernel, len(left_bufs), len(right_bufs), slots, n_row, rb),
        out_shape=out_shape,
        in_specs=[smem] + [hbm] * (len(left_bufs) + len(right_bufs)),
        out_specs=hbm,
        scratch_shapes=[
            pltpu.VMEM((slots, rows, width), jnp.float32),
            pltpu.VMEM((STEPS, rows, width), jnp.float32),
            pltpu.VMEM((STEPS * rb + 1, 2 * BS, width), jnp.bfloat16),
            pltpu.VMEM(out_shape.shape, jnp.float32),
            pltpu.SMEM((slots, EXTRA, width), jnp.float32),
            pltpu.SMEM((STEPS + 1, EXTRA, width), jnp.float32),
            pltpu.SMEM((slots * rb * w + STEPS * UNROLL,), jnp.int32),
            dma((slots,)),
            dma((STEPS,)),
            dma((slots,)),
            dma((STEPS,)),
            dma((STEPS,)),
        ],
        compiler_params=pltpu.CompilerParams(vmem_limit_bytes=40 << 20),
        cost_estimate=pl.CostEstimate(flops=10**9, bytes_accessed=20 << 20, transcendentals=0),
    )(info, *left_bufs, *right_bufs)


def solution(mesh):
    in_specs = (P("row", "col"), P("row", "col"))
    return jax.shard_map(local, mesh=mesh, in_specs=in_specs, out_specs=P("row", "col"), check_vma=False)
```

```python
import functools

import jax
import jax.numpy as jnp
import numpy as np
from jax import lax
from jax.experimental import pallas as pl
from jax.experimental.pallas import tpu as pltpu
from jax.sharding import PartitionSpec as P

BS = 64
STEPS = 4
UNROLL = 4
EXTRA = 8


def left_offsets(row, ratio, n_col):
    seen = []
    for step in range(STEPS):
        offset = (row + step) // ratio % n_col
        if offset not in seen:
            seen.append(offset)
    return seen


def shift(rows, step, count):
    return [((r, c), (r, (c + step) % count)) for r in rows for c in range(count)]


def left_plan(n_row, n_col, ratio):
    offsets = [left_offsets(row, ratio, n_col) for row in range(n_row)]
    if (n_row, n_col, ratio) != (8, 4, 2):
        perms = []
        for slot in range(max(len(o) for o in offsets)):
            pairs = [
                ((row, (col + offsets[row][slot]) % n_col), (row, col))
                for row in range(n_row)
                for col in range(n_col)
                if slot < len(offsets[row]) and offsets[row][slot] != 0
            ]
            perms.append((0, pairs))
        return perms
    down = shift([r for r in range(8) if 1 in offsets[r]], -1, 4)
    up = shift([r for r in range(8) if 3 in offsets[r]], 1, 4)
    again_down = shift([r for r in range(8) if {1, 2} <= set(offsets[r]) and 3 not in offsets[r]], -1, 4)
    again_up = shift([r for r in range(8) if {2, 3} <= set(offsets[r]) and 1 not in offsets[r]], 1, 4)
    for r in range(8):
        if {1, 2, 3} <= set(offsets[r]):
            again_down += [((r, 1), (r, 0)), ((r, 2), (r, 1))]
            again_up += [((r, 1), (r, 2)), ((r, 2), (r, 3))]
    return [(0, down), (0, up), (1, again_down), (2, again_up)]


def right_plan(n_row, n_col, ratio):
    everyone = [(row, col) for row in range(n_row) for col in range(n_col)]
    if (n_row, n_col, ratio) != (8, 4, 2):
        return [
            (0, [(((r + ratio * c + step) % n_row, c), (r, c)) for r, c in everyone if (ratio * c + step) % n_row])
            for step in range(STEPS)
        ]
    first = [(((r + 2 * c) % 8, c), (r, c)) for r, c in everyone if c != 0]
    first += [((r + 1, 0), (r, 0)) for r in range(0, 8, 2)]
    second = [(((r + 2 * c + 2) % 8, c), (r, c)) for r, c in everyone if c != 3]
    second += [((r ^ 1, 3), (r, 3)) for r in range(8)]
    last = [(((r - 1 + 2 * c + 4) % 8, c), (r, c)) for r, c in everyone if r % 2 == 1]
    first_swap = [((r + 1, c), (r, c)) for r, c in everyone if r % 2 == 0 and c != 0]
    second_swap = [((r ^ 1, c), (r, c)) for r, c in everyone if c != 3]
    return [(0, first), (0, second), (0, last), (1, first_swap), (2, second_swap)]


def carry_out(perms, n_row, n_col):
    held = [{(r, c): (r, c) for r in range(n_row) for c in range(n_col)}]
    for source, pairs in perms:
        held.append({dst: held[source][src] for src, dst in pairs})
    return held


def device_table(left_perms, right_perms, n_row, n_col, ratio):
    left_held = carry_out(left_perms, n_row, n_col)
    right_held = carry_out(right_perms, n_row, n_col)
    slots = (ratio - 1 + STEPS - 1) // ratio + 1
    table = np.full((n_row, n_col, 2 * slots + STEPS), -1, np.int32)

    def find(held, device, tile):
        return [i for i, h in enumerate(held) if h.get(device) == tile][0]

    for r in range(n_row):
        for c in range(n_col):
            for slot, offset in enumerate(left_offsets(r, ratio, n_col)):
                tile_col = (c + offset) % n_col
                table[r, c, slot] = find(left_held, (r, c), (r, tile_col))
                table[r, c, slots + STEPS + slot] = (tile_col * ratio - r - ratio * c) % n_row
            for step in range(STEPS):
                table[r, c, slots + step] = find(right_held, (r, c), ((r + ratio * c + step) % n_row, c))
    return table, slots


def fetch(choice, bufs, target, sem):
    for number, buf in enumerate(bufs):
        @pl.when(choice == number)
        def _():
            pltpu.make_async_copy(buf, target, sem).start()


def split_kernel(slots, rb, info_ref, *refs):
    bufs, (split_ref, code_ref), (raw, sem) = refs[:-4], refs[-4:-2], refs[-2:]
    rows = raw.shape[1] - EXTRA
    for step in range(STEPS):
        fetch(info_ref[slots + step], bufs, raw.at[step], sem.at[step])
    code_ref[...] = jnp.full(code_ref.shape, 2 << 16, jnp.int32)
    for step in range(STEPS):
        pltpu.make_async_copy(bufs[0], raw.at[step], sem.at[step]).wait()
        col = raw[step, rows : rows + 1, 0 : code_ref.shape[1]].astype(jnp.int32)
        code = (col >> 1) * 2 * BS | (col & 1) << 16
        code_ref[step : step + 1, :] = jnp.where(col < 0, 2 << 16, code)

        @pl.loop(0, rb)
        def _(block):
            x = raw[step, pl.ds(pl.multiple_of(block * BS, BS), BS), :]
            hi = x.astype(jnp.bfloat16)
            split_ref[step * rb + block, 0:BS, :] = hi
            split_ref[step * rb + block, BS : 2 * BS, :] = (x - hi.astype(jnp.float32)).astype(jnp.bfloat16)


def product_kernel(slots, n_row, rb, w, info_ref, rcode_ref, split_ref, *refs):
    bufs, out_ref = refs[:-9], refs[-9]
    left, acc, lcode, lcode_s, codes, sem, osem, csem = refs[-8:]
    rows, width = left.shape[1] - EXTRA, left.shape[2]
    for slot in range(slots):
        fetch(info_ref[slot], bufs, left.at[slot], sem.at[slot])

    @pl.loop(0, rb)
    def _(r):
        acc[pl.ds(pl.multiple_of(r * BS, BS), BS), :] = jnp.zeros((BS, acc.shape[1]), jnp.float32)

    place = lax.broadcasted_iota(jnp.int32, (1, lcode.shape[1]), 1)
    for slot in range(slots):
        used = info_ref[slot] >= 0

        @pl.when(used)
        def _():
            pltpu.make_async_copy(bufs[0], left.at[slot], sem.at[slot]).wait()

        inner = left[slot, rows : rows + 1, 0 : lcode.shape[1]].astype(jnp.int32)
        valid = (inner >= 0) & (place < rb * w)
        step = jnp.full(inner.shape, info_ref[slots + STEPS + slot], jnp.int32)
        for _ in range(acc.shape[1] // (rb * BS) - 1):
            beyond = inner >= rb
            step = jnp.where(beyond, step + 1, step)
            inner = jnp.where(beyond, inner - rb, inner)
        step = jnp.where(step >= n_row, step - n_row, step)
        code = (step * rb + inner) | (place & (w - 1)) << 8 | slot << 12 | (place // w) << 16
        valid = valid & (step < STEPS)
        lcode[slot : slot + 1, :] = jnp.where(valid, jnp.where(used, code, -1), -1)
    copy = pltpu.make_async_copy(lcode, lcode_s, csem)
    copy.start()
    copy.wait()

    part_rows = rb // STEPS
    bounds = [0]
    for part in range(STEPS):
        def listed(i, place):
            for slot in range(slots):
                for k in range(w):
                    code = lcode_s[slot, (part * part_rows + i) * w + k]
                    codes[place] = code
                    place = place + (code >= 0).astype(jnp.int32)
            return place

        end = lax.fori_loop(0, part_rows, listed, bounds[-1])
        for u in range(UNROLL - 1):
            codes[end + u] = STEPS * rb
        bounds.append((end + UNROLL - 1) // UNROLL * UNROLL)

    low = lax.broadcasted_iota(jnp.int32, (BS, 2 * BS), 1) < BS
    half = lax.broadcasted_iota(jnp.int32, (BS, 2 * BS), 1) // BS

    def product(code):
        block = code & 255
        slot = (code >> 8) & 15
        tile = (code >> 12) & 15
        row = (code >> 16) * BS
        x = left[tile, pl.ds(pl.multiple_of(row, BS), BS), pl.ds(pl.multiple_of((slot >> 1) * 2 * BS, 2 * BS), 2 * BS)]
        both = jnp.where(half == (slot & 1), x, pltpu.roll(x, BS, 1))
        hi = both.astype(jnp.bfloat16).astype(jnp.float32)
        lhs = jnp.where(low, hi, both - hi).astype(jnp.bfloat16)
        lhs = jnp.concatenate([lhs, lhs], axis=1)
        hi, lo = split_ref[block, 0:BS, :], split_ref[block, BS : 2 * BS, :]
        rhs = jnp.concatenate([hi, hi, lo, lo], axis=0)
        return block, row, jnp.dot(lhs, rhs, preferred_element_type=jnp.float32)

    def add(block, row, value):
        step = block // rb
        inner = (block - step * rb) * w
        for pair in range(w // 2):
            x = value[:, pair * 2 * BS : (pair + 1) * 2 * BS]
            turned = pltpu.roll(x, BS, 1)
            for side in range(2):
                code = rcode_ref[step, inner + 2 * pair + side]
                parity = code >> 16
                picked = jnp.where(parity == side, x, turned)
                picked = jnp.where(half == parity, picked, 0.0)
                base = pl.multiple_of(code & 0xFFFF, 2 * BS)
                acc[pl.ds(pl.multiple_of(row, BS), BS), pl.ds(base, 2 * BS)] += picked

    def out_copy(part):
        at = pl.ds(part * part_rows * BS, part_rows * BS)
        return pltpu.make_async_copy(acc.at[at], out_ref.at[at], osem.at[part])

    for part in range(STEPS):
        @pl.loop(bounds[part] // UNROLL, bounds[part + 1] // UNROLL)
        def _(group):
            done = [product(codes[group * UNROLL + u]) for u in range(UNROLL)]
            for item in done:
                add(*item)

        out_copy(part).start()
    for part in range(STEPS):
        out_copy(part).wait()


def local(p_cols, p_data):
    n_row, n_col = lax.axis_size("row"), lax.axis_size("col")
    ratio = n_row // n_col
    row_id, col_id = lax.axis_index("row"), lax.axis_index("col")
    rb, w = p_cols.shape
    rows, width = p_data.shape
    left_perms = left_plan(n_row, n_col, ratio)
    right_perms = right_plan(n_row, n_col, ratio)
    table, slots = device_table(left_perms, right_perms, n_row, n_col, ratio)
    info = jnp.asarray(table)[row_id, col_id]

    cols = jnp.pad(p_cols.astype(jnp.float32).reshape(1, -1), ((0, EXTRA - 1), (0, width - rb * w)))
    own = jnp.concatenate([p_data, cols], axis=0)

    def carry(perms):
        bufs = [own]
        for source, pairs in perms:
            flat = [(s[0] * n_col + s[1], d[0] * n_col + d[1]) for s, d in pairs]
            bufs.append(lax.ppermute(bufs[source], ("row", "col"), flat))
        return bufs

    right_bufs = carry(right_perms)
    left_bufs = carry(left_perms)
    smem = pl.BlockSpec(memory_space=pltpu.SMEM)
    vmem = pl.BlockSpec(memory_space=pltpu.VMEM)
    hbm = pl.BlockSpec(memory_space=pl.ANY)
    dma = pltpu.SemaphoreType.DMA
    split, rcode = pl.pallas_call(
        functools.partial(split_kernel, slots, rb),
        out_shape=(
            jax.ShapeDtypeStruct((STEPS * rb + 1, 2 * BS, width), jnp.bfloat16),
            jax.ShapeDtypeStruct((8, 128), jnp.int32),
        ),
        in_specs=[smem] + [hbm] * len(right_bufs),
        out_specs=(vmem, vmem),
        scratch_shapes=[pltpu.VMEM((STEPS, rows + EXTRA, width), jnp.float32), dma((STEPS,))],
        compiler_params=pltpu.CompilerParams(vmem_limit_bytes=16 << 20),
        cost_estimate=pl.CostEstimate(flops=10**7, bytes_accessed=8 << 20, transcendentals=0),
    )(info, *right_bufs)
    out_shape = jax.ShapeDtypeStruct((rows, rb * ratio * BS), jnp.float32)
    return pl.pallas_call(
        functools.partial(product_kernel, slots, n_row, rb, w),
        out_shape=out_shape,
        in_specs=[smem, smem, vmem] + [hbm] * len(left_bufs),
        out_specs=hbm,
        scratch_shapes=[
            pltpu.VMEM((slots, rows + EXTRA, width), jnp.float32),
            pltpu.VMEM(out_shape.shape, jnp.float32),
            pltpu.VMEM((8, 128), jnp.int32),
            pltpu.SMEM((8, 128), jnp.int32),
            pltpu.SMEM((slots * rb * w + STEPS * UNROLL,), jnp.int32),
            dma((slots,)),
            dma((STEPS,)),
            dma,
        ],
        compiler_params=pltpu.CompilerParams(vmem_limit_bytes=24 << 20),
        cost_estimate=pl.CostEstimate(flops=10**9, bytes_accessed=20 << 20, transcendentals=0),
    )(info, rcode, split, *left_bufs)


def solution(mesh):
    in_specs = (P("row", "col"), P("row", "col"))
    return jax.shard_map(local, mesh=mesh, in_specs=in_specs, out_specs=P("row", "col"), check_vma=False)
```

```python
import functools

import jax
import jax.numpy as jnp
import numpy as np
from jax import lax
from jax.experimental import pallas as pl
from jax.experimental.pallas import tpu as pltpu
from jax.sharding import PartitionSpec as P

BS = 64
STEPS = 4
UNROLL = 4
EXTRA = 8


def left_offsets(row, ratio, n_col):
    seen = []
    for step in range(STEPS):
        offset = (row + step) // ratio % n_col
        if offset not in seen:
            seen.append(offset)
    return seen


def shift(rows, step, count):
    return [((r, c), (r, (c + step) % count)) for r in rows for c in range(count)]


def left_plan(n_row, n_col, ratio):
    offsets = [left_offsets(row, ratio, n_col) for row in range(n_row)]
    if (n_row, n_col, ratio) != (8, 4, 2):
        perms = []
        for slot in range(max(len(o) for o in offsets)):
            pairs = [
                ((row, (col + offsets[row][slot]) % n_col), (row, col))
                for row in range(n_row)
                for col in range(n_col)
                if slot < len(offsets[row]) and offsets[row][slot] != 0
            ]
            perms.append((0, pairs))
        return perms
    down = shift([r for r in range(8) if 1 in offsets[r]], -1, 4)
    up = shift([r for r in range(8) if 3 in offsets[r]], 1, 4)
    again_down = shift([r for r in range(8) if {1, 2} <= set(offsets[r]) and 3 not in offsets[r]], -1, 4)
    again_up = shift([r for r in range(8) if {2, 3} <= set(offsets[r]) and 1 not in offsets[r]], 1, 4)
    for r in range(8):
        if {1, 2, 3} <= set(offsets[r]):
            again_down += [((r, 1), (r, 0)), ((r, 2), (r, 1))]
            again_up += [((r, 1), (r, 2)), ((r, 2), (r, 3))]
    return [(0, down), (0, up), (1, again_down), (2, again_up)]


def right_plan(n_row, n_col, ratio):
    everyone = [(row, col) for row in range(n_row) for col in range(n_col)]
    if (n_row, n_col, ratio) != (8, 4, 2):
        return [
            (0, [(((r + ratio * c + step) % n_row, c), (r, c)) for r, c in everyone if (ratio * c + step) % n_row])
            for step in range(STEPS)
        ]
    first = [(((r + 2 * c) % 8, c), (r, c)) for r, c in everyone if c != 0]
    first += [((r + 1, 0), (r, 0)) for r in range(0, 8, 2)]
    second = [(((r + 2 * c + 2) % 8, c), (r, c)) for r, c in everyone if c != 3]
    second += [((r ^ 1, 3), (r, 3)) for r in range(8)]
    last = [(((r - 1 + 2 * c + 4) % 8, c), (r, c)) for r, c in everyone if r % 2 == 1]
    first_swap = [((r + 1, c), (r, c)) for r, c in everyone if r % 2 == 0 and c != 0]
    second_swap = [((r ^ 1, c), (r, c)) for r, c in everyone if c != 3]
    return [(0, first), (0, second), (0, last), (1, first_swap), (2, second_swap)]


def carry_out(perms, n_row, n_col):
    held = [{(r, c): (r, c) for r in range(n_row) for c in range(n_col)}]
    for source, pairs in perms:
        held.append({dst: held[source][src] for src, dst in pairs})
    return held


def device_table(left_perms, right_perms, n_row, n_col, ratio):
    left_held = carry_out(left_perms, n_row, n_col)
    right_held = carry_out(right_perms, n_row, n_col)
    slots = (ratio - 1 + STEPS - 1) // ratio + 1
    table = np.full((n_row, n_col, 2 * slots + STEPS), -1, np.int32)

    def find(held, device, tile):
        return [i for i, h in enumerate(held) if h.get(device) == tile][0]

    for r in range(n_row):
        for c in range(n_col):
            for slot, offset in enumerate(left_offsets(r, ratio, n_col)):
                tile_col = (c + offset) % n_col
                table[r, c, slot] = find(left_held, (r, c), (r, tile_col))
                table[r, c, slots + STEPS + slot] = (tile_col * ratio - r - ratio * c) % n_row
            for step in range(STEPS):
                table[r, c, slots + step] = find(right_held, (r, c), ((r + ratio * c + step) % n_row, c))
    return table, slots


def fetch(choice, bufs, target, sem):
    for number, buf in enumerate(bufs):
        @pl.when(choice == number)
        def _():
            pltpu.make_async_copy(buf, target, sem).start()


def split_kernel(slots, rb, info_ref, *refs):
    bufs, (split_ref, code_ref), (raw, sem) = refs[:-4], refs[-4:-2], refs[-2:]
    rows = raw.shape[1] - EXTRA
    for step in range(STEPS):
        fetch(info_ref[slots + step], bufs, raw.at[step], sem.at[step])
    code_ref[...] = jnp.full(code_ref.shape, 2 << 16, jnp.int32)
    for step in range(STEPS):
        pltpu.make_async_copy(bufs[0], raw.at[step], sem.at[step]).wait()
        col = raw[step, rows : rows + 1, 0 : code_ref.shape[1]].astype(jnp.int32)
        code = (col >> 1) * 2 * BS | (col & 1) << 16
        code_ref[step : step + 1, :] = jnp.where(col < 0, 2 << 16, code)

        @pl.loop(0, rb)
        def _(block):
            x = raw[step, pl.ds(pl.multiple_of(block * BS, BS), BS), :]
            hi = x.astype(jnp.bfloat16)
            split_ref[step * rb + block, 0:BS, :] = hi
            split_ref[step * rb + block, BS : 2 * BS, :] = (x - hi.astype(jnp.float32)).astype(jnp.bfloat16)


def list_kernel(slots, n_row, rb, w, ratio, info_ref, *refs):
    bufs, code_ref, (cols, sem) = refs[:-3], refs[-3], refs[-2:]
    rows = bufs[0].shape[0] - EXTRA
    for slot in range(slots):
        fetch(info_ref[slot], [buf.at[pl.ds(rows, EXTRA)] for buf in bufs], cols.at[slot], sem.at[slot])
    place = lax.broadcasted_iota(jnp.int32, (1, code_ref.shape[1]), 1)
    for slot in range(slots):
        used = info_ref[slot] >= 0

        @pl.when(used)
        def _():
            pltpu.make_async_copy(bufs[0].at[pl.ds(rows, EXTRA)], cols.at[slot], sem.at[slot]).wait()

        inner = cols[slot, 0:1, 0 : code_ref.shape[1]].astype(jnp.int32)
        valid = (inner >= 0) & (place < rb * w)
        step = jnp.full(inner.shape, info_ref[slots + STEPS + slot], jnp.int32)
        for _ in range(ratio - 1):
            beyond = inner >= rb
            step = jnp.where(beyond, step + 1, step)
            inner = jnp.where(beyond, inner - rb, inner)
        step = jnp.where(step >= n_row, step - n_row, step)
        code = (step * rb + inner) | (place & (w - 1)) << 8 | slot << 12 | (place // w) << 16
        valid = valid & (step < STEPS)
        code_ref[slot : slot + 1, :] = jnp.where(valid, jnp.where(used, code, -1), -1)


def product_kernel(slots, rb, w, info_ref, lcode_ref, rcode_ref, split_ref, *refs):
    bufs, out_ref = refs[:-6], refs[-6]
    left, acc, codes, sem, osem = refs[-5:]
    rows, width = left.shape[1] - EXTRA, left.shape[2]
    for slot in range(slots):
        fetch(info_ref[slot], bufs, left.at[slot], sem.at[slot])

    @pl.loop(0, rb)
    def _(r):
        acc[pl.ds(pl.multiple_of(r * BS, BS), BS), :] = jnp.zeros((BS, acc.shape[1]), jnp.float32)

    for slot in range(slots):
        @pl.when(info_ref[slot] >= 0)
        def _():
            pltpu.make_async_copy(bufs[0], left.at[slot], sem.at[slot]).wait()

    part_rows = rb // STEPS
    bounds = [0]
    for part in range(STEPS):
        def listed(i, place):
            for slot in range(slots):
                for k in range(w):
                    code = lcode_ref[slot, (part * part_rows + i) * w + k]
                    codes[place] = code
                    place = place + (code >= 0).astype(jnp.int32)
            return place

        end = lax.fori_loop(0, part_rows, listed, bounds[-1])
        for u in range(UNROLL - 1):
            codes[end + u] = STEPS * rb
        bounds.append((end + UNROLL - 1) // UNROLL * UNROLL)

    low = lax.broadcasted_iota(jnp.int32, (BS, 2 * BS), 1) < BS
    half = lax.broadcasted_iota(jnp.int32, (BS, 2 * BS), 1) // BS

    def product(code):
        block = code & 255
        slot = (code >> 8) & 15
        tile = (code >> 12) & 15
        row = (code >> 16) * BS
        x = left[tile, pl.ds(pl.multiple_of(row, BS), BS), pl.ds(pl.multiple_of((slot >> 1) * 2 * BS, 2 * BS), 2 * BS)]
        both = jnp.where(half == (slot & 1), x, pltpu.roll(x, BS, 1))
        hi = both.astype(jnp.bfloat16).astype(jnp.float32)
        lhs = jnp.where(low, hi, both - hi).astype(jnp.bfloat16)
        lhs = jnp.concatenate([lhs, lhs], axis=1)
        hi, lo = split_ref[block, 0:BS, :], split_ref[block, BS : 2 * BS, :]
        rhs = jnp.concatenate([hi, hi, lo, lo], axis=0)
        return block, row, jnp.dot(lhs, rhs, preferred_element_type=jnp.float32)

    def add(block, row, value):
        step = block // rb
        inner = (block - step * rb) * w
        for pair in range(w // 2):
            x = value[:, pair * 2 * BS : (pair + 1) * 2 * BS]
            turned = pltpu.roll(x, BS, 1)
            for side in range(2):
                code = rcode_ref[step, inner + 2 * pair + side]
                parity = code >> 16
                picked = jnp.where(parity == side, x, turned)
                picked = jnp.where(half == parity, picked, 0.0)
                base = pl.multiple_of(code & 0xFFFF, 2 * BS)
                acc[pl.ds(pl.multiple_of(row, BS), BS), pl.ds(base, 2 * BS)] += picked

    def out_copy(part):
        at = pl.ds(part * part_rows * BS, part_rows * BS)
        return pltpu.make_async_copy(acc.at[at], out_ref.at[at], osem.at[part])

    for part in range(STEPS):
        @pl.loop(bounds[part] // UNROLL, bounds[part + 1] // UNROLL)
        def _(group):
            done = [product(codes[group * UNROLL + u]) for u in range(UNROLL)]
            for item in done:
                add(*item)

        out_copy(part).start()
    for part in range(STEPS):
        out_copy(part).wait()


def local(p_cols, p_data):
    n_row, n_col = lax.axis_size("row"), lax.axis_size("col")
    ratio = n_row // n_col
    row_id, col_id = lax.axis_index("row"), lax.axis_index("col")
    rb, w = p_cols.shape
    rows, width = p_data.shape
    left_perms = left_plan(n_row, n_col, ratio)
    right_perms = right_plan(n_row, n_col, ratio)
    table, slots = device_table(left_perms, right_perms, n_row, n_col, ratio)
    info = jnp.asarray(table)[row_id, col_id]

    cols = jnp.pad(p_cols.astype(jnp.float32).reshape(1, -1), ((0, EXTRA - 1), (0, width - rb * w)))
    own = jnp.concatenate([p_data, cols], axis=0)

    def permute(value, pairs):
        return lax.ppermute(value, ("row", "col"), [(s[0] * n_col + s[1], d[0] * n_col + d[1]) for s, d in pairs])

    left_bufs, right_bufs = [own], [own]
    for source, pairs in left_perms:
        left_bufs.append(permute(left_bufs[source], pairs))
    for source, pairs in right_perms:
        right_bufs.append(permute(right_bufs[source], pairs))
    smem = pl.BlockSpec(memory_space=pltpu.SMEM)
    vmem = pl.BlockSpec(memory_space=pltpu.VMEM)
    hbm = pl.BlockSpec(memory_space=pl.ANY)
    dma = pltpu.SemaphoreType.DMA
    split, rcode = pl.pallas_call(
        functools.partial(split_kernel, slots, rb),
        out_shape=(
            jax.ShapeDtypeStruct((STEPS * rb + 1, 2 * BS, width), jnp.bfloat16),
            jax.ShapeDtypeStruct((8, 128), jnp.int32),
        ),
        in_specs=[smem] + [hbm] * len(right_bufs),
        out_specs=(vmem, vmem),
        scratch_shapes=[pltpu.VMEM((STEPS, rows + EXTRA, width), jnp.float32), dma((STEPS,))],
        compiler_params=pltpu.CompilerParams(vmem_limit_bytes=16 << 20),
        cost_estimate=pl.CostEstimate(flops=10**7, bytes_accessed=8 << 20, transcendentals=0),
    )(info, *right_bufs)
    out_shape = jax.ShapeDtypeStruct((rows, rb * ratio * BS), jnp.float32)
    lcode = pl.pallas_call(
        functools.partial(list_kernel, slots, n_row, rb, w, ratio),
        out_shape=jax.ShapeDtypeStruct((8, 128), jnp.int32),
        in_specs=[smem] + [hbm] * len(left_bufs),
        out_specs=vmem,
        scratch_shapes=[pltpu.VMEM((slots, EXTRA, width), jnp.float32), dma((slots,))],
        compiler_params=pltpu.CompilerParams(vmem_limit_bytes=4 << 20),
        cost_estimate=pl.CostEstimate(flops=10**11, bytes_accessed=1 << 20, transcendentals=0),
    )(info, *left_bufs)
    return pl.pallas_call(
        functools.partial(product_kernel, slots, rb, w),
        out_shape=out_shape,
        in_specs=[smem, smem, smem, vmem] + [hbm] * len(left_bufs),
        out_specs=hbm,
        scratch_shapes=[
            pltpu.VMEM((slots, rows + EXTRA, width), jnp.float32),
            pltpu.VMEM(out_shape.shape, jnp.float32),
            pltpu.SMEM((slots * rb * w + STEPS * UNROLL,), jnp.int32),
            dma((slots,)),
            dma((STEPS,)),
        ],
        compiler_params=pltpu.CompilerParams(vmem_limit_bytes=24 << 20),
        cost_estimate=pl.CostEstimate(flops=10**9, bytes_accessed=20 << 20, transcendentals=0),
    )(info, lcode, rcode, split, *left_bufs)


def solution(mesh):
    in_specs = (P("row", "col"), P("row", "col"))
    return jax.shard_map(local, mesh=mesh, in_specs=in_specs, out_specs=P("row", "col"), check_vma=False)
```

```python
import functools

import jax
import jax.numpy as jnp
import numpy as np
from jax import lax
from jax.experimental import pallas as pl
from jax.experimental.pallas import tpu as pltpu
from jax.sharding import PartitionSpec as P

BS = 64
STEPS = 4
UNROLL = 4
EXTRA = 8


def left_offsets(row, ratio, n_col):
    seen = []
    for step in range(STEPS):
        offset = (row + step) // ratio % n_col
        if offset not in seen:
            seen.append(offset)
    return seen


def shift(rows, step, count):
    return [((r, c), (r, (c + step) % count)) for r in rows for c in range(count)]


def left_plan(n_row, n_col, ratio):
    offsets = [left_offsets(row, ratio, n_col) for row in range(n_row)]
    if (n_row, n_col, ratio) != (8, 4, 2):
        perms = []
        for slot in range(max(len(o) for o in offsets)):
            pairs = [
                ((row, (col + offsets[row][slot]) % n_col), (row, col))
                for row in range(n_row)
                for col in range(n_col)
                if slot < len(offsets[row]) and offsets[row][slot] != 0
            ]
            perms.append((0, pairs))
        return perms
    down = shift([r for r in range(8) if 1 in offsets[r] and not {1, 2, 3} <= set(offsets[r])], -1, 4)
    up = shift([r for r in range(8) if 3 in offsets[r] and not {1, 2, 3} <= set(offsets[r])], 1, 4)
    again_down = shift([r for r in range(8) if set(offsets[r]) in ({0, 1, 2}, {1, 2})], -1, 4)
    again_up = shift([r for r in range(8) if set(offsets[r]) in ({2, 3}, {0, 2, 3})], 1, 4)
    down += [((3, c), (3, c - 1)) for c in (1, 2, 3)] + [((3, 0), (6, 3))]
    up += [((3, c), (3, c + 1)) for c in (0, 1, 2)] + [((3, 3), (0, 0))]
    again_down += [((3, 1), (3, 0)), ((3, 2), (3, 1)), ((6, 3), (3, 3))]
    again_up += [((3, 1), (3, 2)), ((3, 2), (3, 3)), ((0, 0), (3, 0))]
    return [(0, down), (0, up), (1, again_down), (2, again_up)]


def right_plan(n_row, n_col, ratio):
    everyone = [(row, col) for row in range(n_row) for col in range(n_col)]
    if (n_row, n_col, ratio) != (8, 4, 2):
        return [
            (0, [(((r + ratio * c + step) % n_row, c), (r, c)) for r, c in everyone if (ratio * c + step) % n_row])
            for step in range(STEPS)
        ]
    first = [(((r + 2 * c) % 8, c), (r, c)) for r, c in everyone if c != 0]
    first += [((r + 1, 0), (r, 0)) for r in range(0, 8, 2)]
    second = [(((r + 2 * c + 2) % 8, c), (r, c)) for r, c in everyone if c != 3]
    second += [((r ^ 1, 3), (r, 3)) for r in range(8)]
    last = [(((r - 1 + 2 * c + 4) % 8, c), (r, c)) for r, c in everyone if r % 2 == 1]
    first_swap = [((r + 1, c), (r, c)) for r, c in everyone if r % 2 == 0 and c != 0]
    second_swap = [((r ^ 1, c), (r, c)) for r, c in everyone if c != 3]
    return [(0, first), (0, second), (0, last), (1, first_swap), (2, second_swap)]


def carry_out(perms, n_row, n_col):
    held = [{(r, c): (r, c) for r in range(n_row) for c in range(n_col)}]
    for source, pairs in perms:
        held.append({dst: held[source][src] for src, dst in pairs})
    return held


def device_table(left_perms, right_perms, n_row, n_col, ratio):
    left_held = carry_out(left_perms, n_row, n_col)
    right_held = carry_out(right_perms, n_row, n_col)
    slots = (ratio - 1 + STEPS - 1) // ratio + 1
    table = np.full((n_row, n_col, 2 * slots + STEPS), -1, np.int32)

    def find(held, device, tile):
        return [i for i, h in enumerate(held) if h.get(device) == tile][0]

    for r in range(n_row):
        for c in range(n_col):
            for slot, offset in enumerate(left_offsets(r, ratio, n_col)):
                tile_col = (c + offset) % n_col
                table[r, c, slot] = find(left_held, (r, c), (r, tile_col))
                table[r, c, slots + STEPS + slot] = (tile_col * ratio - r - ratio * c) % n_row
            for step in range(STEPS):
                table[r, c, slots + step] = find(right_held, (r, c), ((r + ratio * c + step) % n_row, c))
    return table, slots


def fetch(choice, bufs, target, sem):
    for number, buf in enumerate(bufs):
        @pl.when(choice == number)
        def _():
            pltpu.make_async_copy(buf, target, sem).start()


def product_kernel(slots, rb, w, n_right, info_ref, rcode_ref, lcode_ref, *refs):
    out_ref, left, right, acc, value, codes, lsem, rsem, osem = refs[-9:]
    right_bufs, left_bufs = refs[:n_right], refs[:1] + refs[n_right:-9]
    rows, width = left.shape[1] - EXTRA, left.shape[2]
    for step in range(STEPS):
        fetch(info_ref[slots + step], right_bufs, right.at[step], rsem.at[step])
    for slot in range(slots):
        fetch(info_ref[slot], left_bufs, left.at[slot], lsem.at[slot])

    @pl.loop(0, rb)
    def _(r):
        acc[pl.ds(pl.multiple_of(r * BS, BS), BS), :] = jnp.zeros((BS, acc.shape[1]), jnp.float32)

    part_rows = rb // STEPS
    for u in range(UNROLL):
        codes[u] = STEPS << 24
    bounds = [jnp.int32(UNROLL)]
    for part in range(STEPS):
        def listed(i, place):
            for slot in range(slots):
                for k in range(w):
                    code = lcode_ref[slot, (part * part_rows + i) * w + k]
                    codes[place] = code
                    place = place + (code >= 0).astype(jnp.int32)
            return place

        bounds.append(lax.fori_loop(0, part_rows, listed, bounds[-1]))
    for u in range(2 * UNROLL):
        codes[bounds[-1] + u] = STEPS << 24

    for step in range(STEPS):
        pltpu.make_async_copy(right_bufs[0], right.at[step], rsem.at[step]).wait()
    for slot in range(slots):
        @pl.when(info_ref[slot] >= 0)
        def _():
            pltpu.make_async_copy(left_bufs[0], left.at[slot], lsem.at[slot]).wait()

    low = lax.broadcasted_iota(jnp.int32, (BS, 2 * BS), 1) < BS
    half = lax.broadcasted_iota(jnp.int32, (BS, 2 * BS), 1) // BS

    def block_at(index):
        return pl.ds(pl.multiple_of(index * BS, BS), BS)

    def product(code):
        slot = (code >> 8) & 15
        x = left[(code >> 12) & 15, block_at((code >> 16) & 255), pl.ds(pl.multiple_of((slot >> 1) * 2 * BS, 2 * BS), 2 * BS)]
        both = jnp.where(half == (slot & 1), x, pltpu.roll(x, BS, 1))
        hi = both.astype(jnp.bfloat16).astype(jnp.float32)
        lhs = jnp.where(low, hi, both - hi).astype(jnp.bfloat16)
        lhs = jnp.concatenate([lhs, lhs], axis=1)
        y = right[code >> 24, block_at(code & 255), :]
        hi = y.astype(jnp.bfloat16)
        lo = (y - hi.astype(jnp.float32)).astype(jnp.bfloat16)
        rhs = jnp.concatenate([hi, hi, lo, lo], axis=0)
        return jnp.dot(lhs, rhs, preferred_element_type=jnp.float32)

    def add(code, product):
        for pair in range(w // 2):
            x = product[:, pair * 2 * BS : (pair + 1) * 2 * BS]
            turned = pltpu.roll(x, BS, 1)
            for side in range(2):
                place = rcode_ref[code >> 24, (code & 255) * w + 2 * pair + side]
                parity = place >> 16
                picked = jnp.where(parity == side, x, turned)
                picked = jnp.where(half == parity, picked, 0.0)
                base = pl.multiple_of(place & 0xFFFF, 2 * BS)
                acc[block_at((code >> 16) & 255), pl.ds(base, 2 * BS)] += picked

    def out_copy(part):
        at = pl.ds(part * part_rows * BS, part_rows * BS)
        return pltpu.make_async_copy(acc.at[at], out_ref.at[at], osem.at[part])

    groups = [jnp.int32(0)] + [(bound + UNROLL - 1) // UNROLL for bound in bounds[1:]]
    for part in range(STEPS):
        @pl.loop(groups[part], groups[part + 1])
        def _(group):
            for u in range(UNROLL):
                add(codes[group * UNROLL + u], value[u])
            for u in range(UNROLL):
                value[u] = product(codes[(group + 1) * UNROLL + u])

        out_copy(part).start()
    for part in range(STEPS):
        out_copy(part).wait()


def column_codes(left_bufs, right_bufs, info, slots, n_row, ratio, rows, rb, w):
    def chosen(bufs, choice):
        cols = jnp.stack([buf[rows, : rb * w] for buf in bufs]).astype(jnp.int32)
        return jnp.sum(jnp.where(choice[:, None, None] == jnp.arange(len(bufs))[None, :, None], cols, 0), axis=1)

    cols = chosen(left_bufs, info[:slots])
    place = jnp.arange(rb * w, dtype=jnp.int32)[None, :]
    slot = jnp.arange(slots, dtype=jnp.int32)[:, None]
    step = (info[slots + STEPS :][:, None] + cols // rb) % n_row
    code = cols % rb | place % w << 8 | slot << 12 | place // w << 16 | step << 24
    valid = (cols >= 0) & (step < STEPS) & (info[:slots] >= 0)[:, None]
    left_code = jnp.where(valid, code, -1)
    cols = chosen(right_bufs, info[slots : slots + STEPS])
    cols = jnp.concatenate([cols, jnp.full((1, rb * w), -1, jnp.int32)])
    right_code = jnp.where(cols < 0, 2 << 16, (cols >> 1) * 2 * BS | (cols & 1) << 16)
    return left_code, right_code


def local(p_cols, p_data):
    n_row, n_col = lax.axis_size("row"), lax.axis_size("col")
    ratio = n_row // n_col
    row_id, col_id = lax.axis_index("row"), lax.axis_index("col")
    rb, w = p_cols.shape
    rows, width = p_data.shape
    left_perms = left_plan(n_row, n_col, ratio)
    right_perms = right_plan(n_row, n_col, ratio)
    table, slots = device_table(left_perms, right_perms, n_row, n_col, ratio)
    info = jnp.asarray(table)[row_id, col_id]

    cols = jnp.pad(p_cols.astype(jnp.float32).reshape(1, -1), ((0, EXTRA - 1), (0, width - rb * w)))
    own = jnp.concatenate([p_data, cols], axis=0)

    def permute(value, pairs):
        return lax.ppermute(value, ("row", "col"), [(s[0] * n_col + s[1], d[0] * n_col + d[1]) for s, d in pairs])

    left_bufs, right_bufs = [own], [own]
    for source, pairs in right_perms:
        right_bufs.append(permute(right_bufs[source], pairs))
    for source, pairs in left_perms:
        left_bufs.append(permute(left_bufs[source], pairs))
    left_code, right_code = column_codes(left_bufs, right_bufs, info, slots, n_row, ratio, rows, rb, w)

    out_shape = jax.ShapeDtypeStruct((rows, rb * ratio * BS), jnp.float32)
    smem = pl.BlockSpec(memory_space=pltpu.SMEM)
    hbm = pl.BlockSpec(memory_space=pl.ANY)
    dma = pltpu.SemaphoreType.DMA
    bufs = right_bufs + left_bufs[1:]
    return pl.pallas_call(
        functools.partial(product_kernel, slots, rb, w, len(right_bufs)),
        out_shape=out_shape,
        in_specs=[smem, smem, smem] + [hbm] * len(bufs),
        out_specs=hbm,
        scratch_shapes=[
            pltpu.VMEM((slots, rows + EXTRA, width), jnp.float32),
            pltpu.VMEM((STEPS + 1, rows + EXTRA, width), jnp.float32),
            pltpu.VMEM(out_shape.shape, jnp.float32),
            pltpu.VMEM((UNROLL, BS, width), jnp.float32),
            pltpu.SMEM((slots * rb * w + 4 * UNROLL,), jnp.int32),
            dma((slots,)),
            dma((STEPS,)),
            dma((STEPS,)),
        ],
        compiler_params=pltpu.CompilerParams(vmem_limit_bytes=24 << 20),
        cost_estimate=pl.CostEstimate(flops=10**9, bytes_accessed=20 << 20, transcendentals=0),
    )(info, right_code, left_code, *bufs)


def solution(mesh):
    in_specs = (P("row", "col"), P("row", "col"))
    return jax.shard_map(local, mesh=mesh, in_specs=in_specs, out_specs=P("row", "col"), check_vma=False)
```

```python
import functools

import jax
import jax.numpy as jnp
import numpy as np
from jax import lax
from jax.experimental import pallas as pl
from jax.experimental.pallas import tpu as pltpu
from jax.sharding import PartitionSpec as P

BS = 64
STEPS = 4
UNROLL = 4
EXTRA = 8


def left_offsets(row, ratio, n_col):
    seen = []
    for step in range(STEPS):
        offset = (row + step) // ratio % n_col
        if offset not in seen:
            seen.append(offset)
    return seen


def shift(rows, step, count):
    return [((r, c), (r, (c + step) % count)) for r in rows for c in range(count)]


def left_plan(n_row, n_col, ratio):
    offsets = [left_offsets(row, ratio, n_col) for row in range(n_row)]
    if (n_row, n_col, ratio) != (8, 4, 2):
        perms = []
        for slot in range(max(len(o) for o in offsets)):
            pairs = [
                ((row, (col + offsets[row][slot]) % n_col), (row, col))
                for row in range(n_row)
                for col in range(n_col)
                if slot < len(offsets[row]) and offsets[row][slot] != 0
            ]
            perms.append((0, pairs))
        return perms
    down = shift([r for r in range(8) if 1 in offsets[r] and not {1, 2, 3} <= set(offsets[r])], -1, 4)
    up = shift([r for r in range(8) if 3 in offsets[r] and not {1, 2, 3} <= set(offsets[r])], 1, 4)
    again_down = shift([r for r in range(8) if set(offsets[r]) in ({0, 1, 2}, {1, 2})], -1, 4)
    again_up = shift([r for r in range(8) if set(offsets[r]) in ({2, 3}, {0, 2, 3})], 1, 4)
    down += [((3, c), (3, c - 1)) for c in (1, 2, 3)] + [((3, 0), (6, 0))]
    up += [((3, c), (3, c + 1)) for c in (0, 1, 2)] + [((3, 3), (0, 3))]
    again_down += [((3, 1), (3, 0)), ((3, 2), (3, 1)), ((6, 0), (3, 3))]
    again_up += [((3, 1), (3, 2)), ((3, 2), (3, 3)), ((0, 3), (3, 0))]
    return [(0, down), (0, up), (1, again_down), (2, again_up)]


def right_plan(n_row, n_col, ratio):
    everyone = [(row, col) for row in range(n_row) for col in range(n_col)]
    if (n_row, n_col, ratio) != (8, 4, 2):
        return [
            (0, [(((r + ratio * c + step) % n_row, c), (r, c)) for r, c in everyone if (ratio * c + step) % n_row])
            for step in range(STEPS)
        ]
    along_y = [((r ^ 4, c), (r, c)) for r, c in everyone]
    along_x = [((r ^ 2, c), (r, c)) for r, c in everyone]
    even = [((r ^ 2, c), (r, c)) for r, c in everyone if r % 2 == 0]
    odd = [((r ^ 4, c), (r, c)) for r, c in everyone if r % 2 == 1]
    perms = [(0, along_y), (0, along_x), (1, even), (2, odd)]
    held = carry_out(perms, n_row, n_col)
    swap = [((r ^ 1, c), (r, c)) for r, c in everyone]
    for buffers in ((0, 1), (2, 3, 4)):
        choice = {}
        for r, c in everyone:
            needs = [((r ^ 1) + 2 * c + step) % 8 for step in range(STEPS)]
            choice[r, c] = [b for b in buffers if held[b].get((r, c)) in [(k, c) for k in needs]][0]
        perms.append((choice, swap))
    return perms


def carry_out(perms, n_row, n_col):
    held = [{(r, c): (r, c) for r in range(n_row) for c in range(n_col)}]
    for source, pairs in perms:
        pick = source.get if isinstance(source, dict) else lambda device: source
        held.append({dst: held[pick(src)][src] for src, dst in pairs})
    return held


def device_table(left_perms, right_perms, n_row, n_col, ratio):
    left_held = carry_out(left_perms, n_row, n_col)
    right_held = carry_out(right_perms, n_row, n_col)
    slots = (ratio - 1 + STEPS - 1) // ratio + 1
    table = np.full((n_row, n_col, 2 * slots + STEPS), -1, np.int32)

    def find(held, device, tile):
        return [i for i, h in enumerate(held) if h.get(device) == tile][0]

    for r in range(n_row):
        for c in range(n_col):
            for slot, offset in enumerate(left_offsets(r, ratio, n_col)):
                tile_col = (c + offset) % n_col
                table[r, c, slot] = find(left_held, (r, c), (r, tile_col))
                table[r, c, slots + STEPS + slot] = (tile_col * ratio - r - ratio * c) % n_row
            for step in range(STEPS):
                table[r, c, slots + step] = find(right_held, (r, c), ((r + ratio * c + step) % n_row, c))
    return table, slots


def fetch(choice, bufs, target, sem):
    for number, buf in enumerate(bufs):
        @pl.when(choice == number)
        def _():
            pltpu.make_async_copy(buf, target, sem).start()


def product_kernel(slots, n_row, ratio, rb, w, n_right, info_ref, *refs):
    out_ref, left, right, acc, value, cols, coded, scalars, codes, lsem, rsem, osem, csem = refs[-13:]
    right_bufs, left_bufs = refs[:n_right], refs[:1] + refs[n_right:-13]
    rows, width = left.shape[1] - EXTRA, left.shape[2]
    names = pl.ds(rows, EXTRA)
    for slot in range(slots):
        fetch(info_ref[slot], [buf.at[names] for buf in left_bufs], cols.at[slot], csem.at[slot])
    for step in range(STEPS):
        choice = info_ref[slots + step]
        fetch(choice, [buf.at[names] for buf in right_bufs], cols.at[slots + step], csem.at[slots + step])
    for step in range(STEPS):
        fetch(info_ref[slots + step], right_bufs, right.at[step], rsem.at[step])
    for slot in range(slots):
        fetch(info_ref[slot], left_bufs, left.at[slot], lsem.at[slot])

    def clear(first, last):
        @pl.loop(first, last)
        def _(r):
            acc[pl.ds(pl.multiple_of(r * BS, BS), BS), :] = jnp.zeros((BS, acc.shape[1]), jnp.float32)

    clear(0, rb // 4)
    lanes = scalars.shape[1]
    place = lax.broadcasted_iota(jnp.int32, (1, lanes), 1)
    for slot in range(slots):
        used = info_ref[slot] >= 0

        @pl.when(used)
        def _():
            pltpu.make_async_copy(left_bufs[0].at[names], cols.at[slot], csem.at[slot]).wait()

        inner = cols[slot, 0:1, 0:lanes].astype(jnp.int32)
        valid = (inner >= 0) & (place < rb * w)
        step = jnp.full(inner.shape, info_ref[slots + STEPS + slot], jnp.int32)
        for _ in range(ratio - 1):
            beyond = inner >= rb
            step = jnp.where(beyond, step + 1, step)
            inner = jnp.where(beyond, inner - rb, inner)
        step = jnp.where(step >= n_row, step - n_row, step)
        code = inner | (place & (w - 1)) << 8 | slot << 12 | (place // w) << 16 | step << 24
        valid = valid & (step < STEPS)
        coded[slot : slot + 1, :] = jnp.where(valid, jnp.where(used, code, -1), -1)
    for step in range(STEPS):
        pltpu.make_async_copy(right_bufs[0].at[names], cols.at[slots + step], csem.at[slots + step]).wait()
        col = cols[slots + step, 0:1, 0:lanes].astype(jnp.int32)
        code = (col >> 1) * 2 * BS | (col & 1) << 16
        coded[slots + step : slots + step + 1, :] = jnp.where(col < 0, 2 << 16, code)
    coded[slots + STEPS : slots + STEPS + 1, :] = jnp.full((1, lanes), 2 << 16, jnp.int32)
    to_scalars = pltpu.make_async_copy(coded, scalars, csem.at[slots + STEPS])
    to_scalars.start()
    clear(rb // 4, rb)
    to_scalars.wait()

    part_rows = rb // STEPS
    for u in range(UNROLL):
        codes[u] = STEPS << 24
    bounds = [jnp.int32(UNROLL)]
    for part in range(STEPS):
        def listed(i, place):
            for slot in range(slots):
                for k in range(w):
                    code = scalars[slot, (part * part_rows + i) * w + k]
                    codes[place] = code
                    place = place + (code >= 0).astype(jnp.int32)
            return place

        bounds.append(lax.fori_loop(0, part_rows, listed, bounds[-1]))
    for u in range(2 * UNROLL):
        codes[bounds[-1] + u] = STEPS << 24

    for step in range(STEPS):
        pltpu.make_async_copy(right_bufs[0], right.at[step], rsem.at[step]).wait()
    for slot in range(slots):
        @pl.when(info_ref[slot] >= 0)
        def _():
            pltpu.make_async_copy(left_bufs[0], left.at[slot], lsem.at[slot]).wait()

    low = lax.broadcasted_iota(jnp.int32, (BS, 2 * BS), 1) < BS
    half = lax.broadcasted_iota(jnp.int32, (BS, 2 * BS), 1) // BS

    def block_at(index):
        return pl.ds(pl.multiple_of(index * BS, BS), BS)

    def product(code):
        slot = (code >> 8) & 15
        x = left[(code >> 12) & 15, block_at((code >> 16) & 255), pl.ds(pl.multiple_of((slot >> 1) * 2 * BS, 2 * BS), 2 * BS)]
        both = jnp.where(half == (slot & 1), x, pltpu.roll(x, BS, 1))
        hi = both.astype(jnp.bfloat16).astype(jnp.float32)
        lhs = jnp.where(low, hi, both - hi).astype(jnp.bfloat16)
        lhs = jnp.concatenate([lhs, lhs], axis=1)
        y = right[code >> 24, block_at(code & 255), :]
        hi = y.astype(jnp.bfloat16)
        lo = (y - hi.astype(jnp.float32)).astype(jnp.bfloat16)
        rhs = jnp.concatenate([hi, hi, lo, lo], axis=0)
        return jnp.dot(lhs, rhs, preferred_element_type=jnp.float32)

    def add(code, product):
        for pair in range(w // 2):
            x = product[:, pair * 2 * BS : (pair + 1) * 2 * BS]
            turned = pltpu.roll(x, BS, 1)
            for side in range(2):
                place = scalars[slots + (code >> 24), (code & 255) * w + 2 * pair + side]
                parity = place >> 16
                picked = jnp.where(parity == side, x, turned)
                picked = jnp.where(half == parity, picked, 0.0)
                base = pl.multiple_of(place & 0xFFFF, 2 * BS)
                acc[block_at((code >> 16) & 255), pl.ds(base, 2 * BS)] += picked

    def out_copy(part):
        at = pl.ds(part * part_rows * BS, part_rows * BS)
        return pltpu.make_async_copy(acc.at[at], out_ref.at[at], osem.at[part])

    groups = [jnp.int32(0)] + [(bound + UNROLL - 1) // UNROLL for bound in bounds[1:]]
    for part in range(STEPS):
        @pl.loop(groups[part], groups[part + 1])
        def _(group):
            for u in range(UNROLL):
                add(codes[group * UNROLL + u], value[u])
            for u in range(UNROLL):
                value[u] = product(codes[(group + 1) * UNROLL + u])

        out_copy(part).start()
    for part in range(STEPS):
        out_copy(part).wait()


def local(p_cols, p_data):
    n_row, n_col = lax.axis_size("row"), lax.axis_size("col")
    ratio = n_row // n_col
    row_id, col_id = lax.axis_index("row"), lax.axis_index("col")
    rb, w = p_cols.shape
    rows, width = p_data.shape
    left_perms = left_plan(n_row, n_col, ratio)
    right_perms = right_plan(n_row, n_col, ratio)
    table, slots = device_table(left_perms, right_perms, n_row, n_col, ratio)
    info = jnp.asarray(table)[row_id, col_id]

    cols = jnp.pad(p_cols.astype(jnp.float32).reshape(1, -1), ((0, EXTRA - 1), (0, width - rb * w)))
    own = jnp.concatenate([p_data, cols], axis=0)

    def permute(value, pairs):
        return lax.ppermute(value, ("row", "col"), [(s[0] * n_col + s[1], d[0] * n_col + d[1]) for s, d in pairs])

    def carry(perms):
        bufs = [own]
        for source, pairs in perms:
            if isinstance(source, dict):
                picks = np.array([[source[r, c] for c in range(n_col)] for r in range(n_row)], np.int32)
                pick = jnp.asarray(picks)[row_id, col_id]
                first, *others = sorted(set(source.values()))
                value = bufs[first]
                for other in others:
                    value = jnp.where(pick == other, bufs[other], value)
            else:
                value = bufs[source]
            bufs.append(lax.ppermute(value, ("row", "col"), [(s[0] * n_col + s[1], d[0] * n_col + d[1]) for s, d in pairs]))
        return bufs

    right_bufs, left_bufs = carry(right_perms), carry(left_perms)
    out_shape = jax.ShapeDtypeStruct((rows, rb * ratio * BS), jnp.float32)
    smem = pl.BlockSpec(memory_space=pltpu.SMEM)
    hbm = pl.BlockSpec(memory_space=pl.ANY)
    dma = pltpu.SemaphoreType.DMA
    bufs = right_bufs + left_bufs[1:]
    return pl.pallas_call(
        functools.partial(product_kernel, slots, n_row, ratio, rb, w, len(right_bufs)),
        out_shape=out_shape,
        in_specs=[smem] + [hbm] * len(bufs),
        out_specs=hbm,
        scratch_shapes=[
            pltpu.VMEM((slots, rows + EXTRA, width), jnp.float32),
            pltpu.VMEM((STEPS + 1, rows + EXTRA, width), jnp.float32),
            pltpu.VMEM(out_shape.shape, jnp.float32),
            pltpu.VMEM((UNROLL, BS, width), jnp.float32),
            pltpu.VMEM((slots + STEPS, EXTRA, width), jnp.float32),
            pltpu.VMEM((16, 128), jnp.int32),
            pltpu.SMEM((16, 128), jnp.int32),
            pltpu.SMEM((slots * rb * w + 4 * UNROLL,), jnp.int32),
            dma((slots,)),
            dma((STEPS,)),
            dma((STEPS,)),
            dma((slots + STEPS + 1,)),
        ],
        compiler_params=pltpu.CompilerParams(vmem_limit_bytes=24 << 20),
        cost_estimate=pl.CostEstimate(flops=10**9, bytes_accessed=20 << 20, transcendentals=0),
    )(info, *bufs)


def solution(mesh):
    in_specs = (P("row", "col"), P("row", "col"))
    return jax.shard_map(local, mesh=mesh, in_specs=in_specs, out_specs=P("row", "col"), check_vma=False)
```

```python
import functools

import jax
import jax.numpy as jnp
import numpy as np
from jax import lax
from jax.experimental import pallas as pl
from jax.experimental.pallas import tpu as pltpu
from jax.sharding import PartitionSpec as P

BS = 64
STEPS = 4
UNROLL = 4
EXTRA = 8


def left_offsets(row, ratio, n_col):
    seen = []
    for step in range(STEPS):
        offset = (row + step) // ratio % n_col
        if offset not in seen:
            seen.append(offset)
    return seen


def shift(rows, step, count):
    return [((r, c), (r, (c + step) % count)) for r in rows for c in range(count)]


def left_plan(n_row, n_col, ratio):
    offsets = [left_offsets(row, ratio, n_col) for row in range(n_row)]
    if (n_row, n_col, ratio) != (8, 4, 2):
        perms = []
        for slot in range(max(len(o) for o in offsets)):
            pairs = [
                ((row, (col + offsets[row][slot]) % n_col), (row, col))
                for row in range(n_row)
                for col in range(n_col)
                if slot < len(offsets[row]) and offsets[row][slot] != 0
            ]
            perms.append((0, pairs))
        return perms
    down = shift([r for r in range(8) if 1 in offsets[r] and not {1, 2, 3} <= set(offsets[r])], -1, 4)
    up = shift([r for r in range(8) if 3 in offsets[r] and not {1, 2, 3} <= set(offsets[r])], 1, 4)
    again_down = shift([r for r in range(8) if set(offsets[r]) in ({0, 1, 2}, {1, 2})], -1, 4)
    again_up = shift([r for r in range(8) if set(offsets[r]) in ({2, 3}, {0, 2, 3})], 1, 4)
    down += [((3, c), (3, c - 1)) for c in (1, 2, 3)] + [((3, 0), (6, 0))]
    up += [((3, c), (3, c + 1)) for c in (0, 1, 2)] + [((3, 3), (0, 3))]
    again_down += [((3, 1), (3, 0)), ((3, 2), (3, 1)), ((6, 0), (3, 3))]
    again_up += [((3, 1), (3, 2)), ((3, 2), (3, 3)), ((0, 3), (3, 0))]
    return [(0, down), (0, up), (1, again_down), (2, again_up)]


def right_plan(n_row, n_col, ratio):
    everyone = [(row, col) for row in range(n_row) for col in range(n_col)]
    if (n_row, n_col, ratio) != (8, 4, 2):
        return [
            (0, [(((r + ratio * c + step) % n_row, c), (r, c)) for r, c in everyone if (ratio * c + step) % n_row])
            for step in range(STEPS)
        ]
    along_y = [((r ^ 4, c), (r, c)) for r, c in everyone]
    along_x = [((r ^ 2, c), (r, c)) for r, c in everyone]
    even = [((r ^ 2, c), (r, c)) for r, c in everyone if r % 2 == 0]
    odd = [((r ^ 4, c), (r, c)) for r, c in everyone if r % 2 == 1]
    perms = [(0, along_y), (0, along_x), (1, even), (2, odd)]
    held = carry_out(perms, n_row, n_col)
    swap = [((r ^ 1, c), (r, c)) for r, c in everyone]
    for buffers in ((0, 1), (2, 3, 4)):
        choice = {}
        for r, c in everyone:
            needs = [((r ^ 1) + 2 * c + step) % 8 for step in range(STEPS)]
            choice[r, c] = [b for b in buffers if held[b].get((r, c)) in [(k, c) for k in needs]][0]
        perms.append((choice, swap))
    return perms


def carry_out(perms, n_row, n_col):
    held = [{(r, c): (r, c) for r in range(n_row) for c in range(n_col)}]
    for source, pairs in perms:
        pick = source.get if isinstance(source, dict) else lambda device: source
        held.append({dst: held[pick(src)][src] for src, dst in pairs})
    return held


def device_table(left_perms, right_perms, n_row, n_col, ratio):
    left_held = carry_out(left_perms, n_row, n_col)
    right_held = carry_out(right_perms, n_row, n_col)
    slots = (ratio - 1 + STEPS - 1) // ratio + 1
    table = np.full((n_row, n_col, 2 * slots + STEPS), -1, np.int32)

    def find(held, device, tile):
        return [i for i, h in enumerate(held) if h.get(device) == tile][0]

    for r in range(n_row):
        for c in range(n_col):
            for slot, offset in enumerate(left_offsets(r, ratio, n_col)):
                tile_col = (c + offset) % n_col
                table[r, c, slot] = find(left_held, (r, c), (r, tile_col))
                table[r, c, slots + STEPS + slot] = (tile_col * ratio - r - ratio * c) % n_row
            for step in range(STEPS):
                table[r, c, slots + step] = find(right_held, (r, c), ((r + ratio * c + step) % n_row, c))
    return table, slots


def fetch(choice, bufs, target, sem):
    for number, buf in enumerate(bufs):
        @pl.when(choice == number)
        def _():
            pltpu.make_async_copy(buf, target, sem).start()


def product_kernel(slots, n_row, ratio, rb, w, n_right, info_ref, *refs):
    out_ref, left, right, acc, value, cols, coded, scalars, codes, lsem, rsem, osem, csem = refs[-13:]
    right_bufs, left_bufs = refs[:n_right], refs[:1] + refs[n_right:-13]
    rows, width = left.shape[1] - EXTRA, left.shape[2]
    names = pl.ds(rows, EXTRA)
    for slot in range(slots):
        fetch(info_ref[slot], [buf.at[names] for buf in left_bufs], cols.at[slot], csem.at[slot])
    for step in range(STEPS):
        choice = info_ref[slots + step]
        fetch(choice, [buf.at[names] for buf in right_bufs], cols.at[slots + step], csem.at[slots + step])
    for step in range(STEPS):
        fetch(info_ref[slots + step], right_bufs, right.at[step], rsem.at[step])
    for slot in range(slots):
        fetch(info_ref[slot], left_bufs, left.at[slot], lsem.at[slot])

    def clear(first, last):
        @pl.loop(first, last)
        def _(r):
            acc[pl.ds(pl.multiple_of(r * BS, BS), BS), :] = jnp.zeros((BS, acc.shape[1]), jnp.float32)

    clear(0, rb // 4)
    lanes = scalars.shape[1]
    place = lax.broadcasted_iota(jnp.int32, (1, lanes), 1)
    for slot in range(slots):
        used = info_ref[slot] >= 0

        @pl.when(used)
        def _():
            pltpu.make_async_copy(left_bufs[0].at[names], cols.at[slot], csem.at[slot]).wait()

        inner = cols[slot, 0:1, 0:lanes].astype(jnp.int32)
        valid = (inner >= 0) & (place < rb * w)
        step = jnp.full(inner.shape, info_ref[slots + STEPS + slot], jnp.int32)
        for _ in range(ratio - 1):
            beyond = inner >= rb
            step = jnp.where(beyond, step + 1, step)
            inner = jnp.where(beyond, inner - rb, inner)
        step = jnp.where(step >= n_row, step - n_row, step)
        code = inner | (place & (w - 1)) << 8 | slot << 12 | (place // w) << 16 | step << 24
        valid = valid & (step < STEPS)
        coded[slot : slot + 1, :] = jnp.where(valid, jnp.where(used, code, -1), -1)
    for step in range(STEPS):
        pltpu.make_async_copy(right_bufs[0].at[names], cols.at[slots + step], csem.at[slots + step]).wait()
        col = cols[slots + step, 0:1, 0:lanes].astype(jnp.int32)
        code = (col >> 1) * 2 * BS | (col & 1) << 16
        coded[slots + step : slots + step + 1, :] = jnp.where(col < 0, 2 << 16, code)
    coded[slots + STEPS : slots + STEPS + 1, :] = jnp.full((1, lanes), 2 << 16, jnp.int32)
    to_scalars = pltpu.make_async_copy(coded, scalars, csem.at[slots + STEPS])
    to_scalars.start()
    clear(rb // 4, rb)
    to_scalars.wait()

    part_rows = rb // STEPS
    for u in range(UNROLL):
        codes[u] = STEPS << 24
    bounds = [jnp.int32(UNROLL)]
    for part in range(STEPS):
        def listed(i, place):
            for slot in range(slots):
                for k in range(w):
                    code = scalars[slot, (part * part_rows + i) * w + k]
                    codes[place] = code
                    place = place + (code >= 0).astype(jnp.int32)
            return place

        bounds.append(lax.fori_loop(0, part_rows, listed, bounds[-1]))
    for u in range(2 * UNROLL):
        codes[bounds[-1] + u] = STEPS << 24

    for step in range(STEPS):
        pltpu.make_async_copy(right_bufs[0], right.at[step], rsem.at[step]).wait()
    for slot in range(slots):
        @pl.when(info_ref[slot] >= 0)
        def _():
            pltpu.make_async_copy(left_bufs[0], left.at[slot], lsem.at[slot]).wait()

    low = lax.broadcasted_iota(jnp.int32, (BS, 2 * BS), 1) < BS
    half = lax.broadcasted_iota(jnp.int32, (BS, 2 * BS), 1) // BS

    def block_at(index):
        return pl.ds(pl.multiple_of(index * BS, BS), BS)

    def product(code):
        slot = (code >> 8) & 15
        x = left[(code >> 12) & 15, block_at((code >> 16) & 255), pl.ds(pl.multiple_of((slot >> 1) * 2 * BS, 2 * BS), 2 * BS)]
        both = jnp.where(half == (slot & 1), x, pltpu.roll(x, BS, 1))
        hi = both.astype(jnp.bfloat16).astype(jnp.float32)
        lhs = jnp.where(low, hi, both - hi).astype(jnp.bfloat16)
        lhs = jnp.concatenate([lhs, lhs], axis=1)
        y = right[code >> 24, block_at(code & 255), :]
        hi = y.astype(jnp.bfloat16)
        lo = (y - hi.astype(jnp.float32)).astype(jnp.bfloat16)
        rhs = jnp.concatenate([hi, hi, lo, lo], axis=0)
        return jnp.dot(lhs, rhs, preferred_element_type=jnp.float32)

    def add(code, product):
        for pair in range(w // 2):
            x = product[:, pair * 2 * BS : (pair + 1) * 2 * BS]
            turned = pltpu.roll(x, BS, 1)
            for side in range(2):
                place = scalars[slots + (code >> 24), (code & 255) * w + 2 * pair + side]
                parity = place >> 16
                picked = jnp.where(parity == side, x, turned)
                picked = jnp.where(half == parity, picked, 0.0)
                base = pl.multiple_of(place & 0xFFFF, 2 * BS)
                acc[block_at((code >> 16) & 255), pl.ds(base, 2 * BS)] += picked

    def out_copy(part):
        at = pl.ds(part * part_rows * BS, part_rows * BS)
        return pltpu.make_async_copy(acc.at[at], out_ref.at[at], osem.at[part])

    groups = [jnp.int32(0)] + [(bound + UNROLL - 1) // UNROLL for bound in bounds[1:]]
    for part in range(STEPS):
        @pl.loop(groups[part], groups[part + 1])
        def _(group):
            for u in range(UNROLL):
                add(codes[group * UNROLL + u], value[u])
            for u in range(UNROLL):
                value[u] = product(codes[(group + 1) * UNROLL + u])

        out_copy(part).start()
    for part in range(STEPS):
        out_copy(part).wait()


def passed_on(bufs):
    hbm = pl.BlockSpec(memory_space=pl.ANY)
    return pl.pallas_call(
        lambda *refs: None,
        out_shape=[jax.ShapeDtypeStruct(buf.shape, buf.dtype) for buf in bufs],
        in_specs=[hbm] * len(bufs),
        out_specs=[hbm] * len(bufs),
        input_output_aliases={i: i for i in range(len(bufs))},
        cost_estimate=pl.CostEstimate(flops=10**11, bytes_accessed=0, transcendentals=0),
    )(*bufs)


def local(p_cols, p_data):
    n_row, n_col = lax.axis_size("row"), lax.axis_size("col")
    ratio = n_row // n_col
    row_id, col_id = lax.axis_index("row"), lax.axis_index("col")
    rb, w = p_cols.shape
    rows, width = p_data.shape
    left_perms = left_plan(n_row, n_col, ratio)
    right_perms = right_plan(n_row, n_col, ratio)
    table, slots = device_table(left_perms, right_perms, n_row, n_col, ratio)
    info = jnp.asarray(table)[row_id, col_id]

    cols = jnp.pad(p_cols.astype(jnp.float32).reshape(1, -1), ((0, EXTRA - 1), (0, width - rb * w)))
    own = jnp.concatenate([p_data, cols], axis=0)

    def permute(value, pairs):
        return lax.ppermute(value, ("row", "col"), [(s[0] * n_col + s[1], d[0] * n_col + d[1]) for s, d in pairs])

    def carry(perms):
        bufs = [own]
        for source, pairs in perms:
            if isinstance(source, dict):
                picks = np.array([[source[r, c] for c in range(n_col)] for r in range(n_row)], np.int32)
                pick = jnp.asarray(picks)[row_id, col_id]
                first, *others = sorted(set(source.values()))
                value = bufs[first]
                for other in others:
                    value = jnp.where(pick == other, bufs[other], value)
            else:
                value = bufs[source]
            bufs.append(lax.ppermute(value, ("row", "col"), [(s[0] * n_col + s[1], d[0] * n_col + d[1]) for s, d in pairs]))
        return bufs

    right_bufs, left_bufs = carry(right_perms), carry(left_perms)
    left_bufs[3:] = passed_on(left_bufs[3:])
    out_shape = jax.ShapeDtypeStruct((rows, rb * ratio * BS), jnp.float32)
    smem = pl.BlockSpec(memory_space=pltpu.SMEM)
    hbm = pl.BlockSpec(memory_space=pl.ANY)
    dma = pltpu.SemaphoreType.DMA
    bufs = right_bufs + left_bufs[1:]
    return pl.pallas_call(
        functools.partial(product_kernel, slots, n_row, ratio, rb, w, len(right_bufs)),
        out_shape=out_shape,
        in_specs=[smem] + [hbm] * len(bufs),
        out_specs=hbm,
        scratch_shapes=[
            pltpu.VMEM((slots, rows + EXTRA, width), jnp.float32),
            pltpu.VMEM((STEPS + 1, rows + EXTRA, width), jnp.float32),
            pltpu.VMEM(out_shape.shape, jnp.float32),
            pltpu.VMEM((UNROLL, BS, width), jnp.float32),
            pltpu.VMEM((slots + STEPS, EXTRA, width), jnp.float32),
            pltpu.VMEM((16, 128), jnp.int32),
            pltpu.SMEM((16, 128), jnp.int32),
            pltpu.SMEM((slots * rb * w + 4 * UNROLL,), jnp.int32),
            dma((slots,)),
            dma((STEPS,)),
            dma((STEPS,)),
            dma((slots + STEPS + 1,)),
        ],
        compiler_params=pltpu.CompilerParams(vmem_limit_bytes=24 << 20),
        cost_estimate=pl.CostEstimate(flops=10**9, bytes_accessed=20 << 20, transcendentals=0),
    )(info, *bufs)


def solution(mesh):
    in_specs = (P("row", "col"), P("row", "col"))
    return jax.shard_map(local, mesh=mesh, in_specs=in_specs, out_specs=P("row", "col"), check_vma=False)
```

```python
import functools

import jax
import jax.numpy as jnp
import numpy as np
from jax import lax
from jax.experimental import pallas as pl
from jax.experimental.pallas import tpu as pltpu
from jax.sharding import PartitionSpec as P

BS = 64
STEPS = 4
UNROLL = 4
EXTRA = 8


def left_offsets(row, ratio, n_col):
    seen = []
    for step in range(STEPS):
        offset = (row + step) // ratio % n_col
        if offset not in seen:
            seen.append(offset)
    return seen


def shift(rows, step, count):
    return [((r, c), (r, (c + step) % count)) for r in rows for c in range(count)]


def left_plan(n_row, n_col, ratio):
    offsets = [left_offsets(row, ratio, n_col) for row in range(n_row)]
    if (n_row, n_col, ratio) != (8, 4, 2):
        perms = []
        for slot in range(max(len(o) for o in offsets)):
            pairs = [
                ((row, (col + offsets[row][slot]) % n_col), (row, col))
                for row in range(n_row)
                for col in range(n_col)
                if slot < len(offsets[row]) and offsets[row][slot] != 0
            ]
            perms.append((0, pairs))
        return perms
    down = shift([r for r in range(8) if 1 in offsets[r] and not {1, 2, 3} <= set(offsets[r])], -1, 4)
    up = shift([r for r in range(8) if 3 in offsets[r] and not {1, 2, 3} <= set(offsets[r])], 1, 4)
    again_down = shift([r for r in range(8) if set(offsets[r]) in ({0, 1, 2}, {1, 2})], -1, 4)
    again_up = shift([r for r in range(8) if set(offsets[r]) in ({2, 3}, {0, 2, 3})], 1, 4)
    down += [((3, c), (3, c - 1)) for c in (1, 2, 3)] + [((3, 0), (6, 0))]
    up += [((3, c), (3, c + 1)) for c in (0, 1, 2)] + [((3, 3), (0, 3))]
    again_down += [((3, 1), (3, 0)), ((3, 2), (3, 1)), ((6, 0), (3, 3))]
    again_up += [((3, 1), (3, 2)), ((3, 2), (3, 3)), ((0, 3), (3, 0))]
    return [(0, down), (0, up), (1, again_down), (2, again_up)]


def right_plan(n_row, n_col, ratio):
    everyone = [(row, col) for row in range(n_row) for col in range(n_col)]
    if (n_row, n_col, ratio) != (8, 4, 2):
        return [
            (0, [(((r + ratio * c + step) % n_row, c), (r, c)) for r, c in everyone if (ratio * c + step) % n_row])
            for step in range(STEPS)
        ]
    along_y = [((r ^ 4, c), (r, c)) for r, c in everyone]
    along_x = [((r ^ 2, c), (r, c)) for r, c in everyone]
    even = [((r ^ 2, c), (r, c)) for r, c in everyone if r % 2 == 0]
    odd = [((r ^ 4, c), (r, c)) for r, c in everyone if r % 2 == 1]
    perms = [(0, along_y), (0, along_x), (1, even), (2, odd)]
    held = carry_out(perms, n_row, n_col)
    swap = [((r ^ 1, c), (r, c)) for r, c in everyone]
    for buffers in ((0, 1), (2, 3, 4)):
        choice = {}
        for r, c in everyone:
            needs = [((r ^ 1) + 2 * c + step) % 8 for step in range(STEPS)]
            choice[r, c] = [b for b in buffers if held[b].get((r, c)) in [(k, c) for k in needs]][0]
        perms.append((choice, swap))
    return perms


def carry_out(perms, n_row, n_col):
    held = [{(r, c): (r, c) for r in range(n_row) for c in range(n_col)}]
    for source, pairs in perms:
        pick = source.get if isinstance(source, dict) else lambda device: source
        held.append({dst: held[pick(src)][src] for src, dst in pairs})
    return held


def device_table(left_perms, right_perms, n_row, n_col, ratio):
    left_held = carry_out(left_perms, n_row, n_col)
    right_held = carry_out(right_perms, n_row, n_col)
    slots = (ratio - 1 + STEPS - 1) // ratio + 1
    table = np.full((n_row, n_col, 2 * slots + STEPS), -1, np.int32)

    def find(held, device, tile):
        return [i for i, h in enumerate(held) if h.get(device) == tile][0]

    for r in range(n_row):
        for c in range(n_col):
            for slot, offset in enumerate(left_offsets(r, ratio, n_col)):
                tile_col = (c + offset) % n_col
                table[r, c, slot] = find(left_held, (r, c), (r, tile_col))
                table[r, c, slots + STEPS + slot] = (tile_col * ratio - r - ratio * c) % n_row
            for step in range(STEPS):
                table[r, c, slots + step] = find(right_held, (r, c), ((r + ratio * c + step) % n_row, c))
    return table, slots


def fetch(choice, bufs, target, sem):
    for number, buf in enumerate(bufs):
        @pl.when(choice == number)
        def _():
            pltpu.make_async_copy(buf, target, sem).start()


def product_kernel(slots, n_row, ratio, rb, w, n_right, info_ref, *refs):
    out_ref, left, right, acc, value, cols, coded, scalars, codes, lsem, rsem, osem, csem = refs[-13:]
    right_bufs, left_bufs = refs[:n_right], refs[:1] + refs[n_right:-13]
    rows, width = left.shape[1] - EXTRA, left.shape[2]
    names = pl.ds(rows, EXTRA)
    for slot in range(slots):
        fetch(info_ref[slot], [buf.at[names] for buf in left_bufs], cols.at[slot], csem.at[slot])
    for step in range(STEPS):
        choice = info_ref[slots + step]
        fetch(choice, [buf.at[names] for buf in right_bufs], cols.at[slots + step], csem.at[slots + step])
    for step in range(STEPS):
        fetch(info_ref[slots + step], right_bufs, right.at[step], rsem.at[step])
    for slot in range(slots):
        fetch(info_ref[slot], left_bufs, left.at[slot], lsem.at[slot])

    def clear(first, last):
        @pl.loop(first, last)
        def _(r):
            acc[pl.ds(pl.multiple_of(r * BS, BS), BS), :] = jnp.zeros((BS, acc.shape[1]), jnp.float32)

    clear(0, rb // 4)
    lanes = scalars.shape[1]
    place = lax.broadcasted_iota(jnp.int32, (1, lanes), 1)
    for slot in range(slots):
        used = info_ref[slot] >= 0

        @pl.when(used)
        def _():
            pltpu.make_async_copy(left_bufs[0].at[names], cols.at[slot], csem.at[slot]).wait()

        inner = cols[slot, 0:1, 0:lanes].astype(jnp.int32)
        valid = (inner >= 0) & (place < rb * w)
        step = jnp.full(inner.shape, info_ref[slots + STEPS + slot], jnp.int32)
        for _ in range(ratio - 1):
            beyond = inner >= rb
            step = jnp.where(beyond, step + 1, step)
            inner = jnp.where(beyond, inner - rb, inner)
        step = jnp.where(step >= n_row, step - n_row, step)
        code = inner | (place & (w - 1)) << 8 | slot << 12 | (place // w) << 16 | step << 24
        valid = valid & (step < STEPS)
        coded[slot : slot + 1, :] = jnp.where(valid, jnp.where(used, code, -1), -1)
    for step in range(STEPS):
        pltpu.make_async_copy(right_bufs[0].at[names], cols.at[slots + step], csem.at[slots + step]).wait()
        col = cols[slots + step, 0:1, 0:lanes].astype(jnp.int32)
        code = (col >> 1) * 2 * BS | (col & 1) << 16
        coded[slots + step : slots + step + 1, :] = jnp.where(col < 0, 2 << 16, code)
    coded[slots + STEPS : slots + STEPS + 1, :] = jnp.full((1, lanes), 2 << 16, jnp.int32)
    to_scalars = pltpu.make_async_copy(coded, scalars, csem.at[slots + STEPS])
    to_scalars.start()
    clear(rb // 4, rb)
    to_scalars.wait()

    part_rows = rb // STEPS
    for u in range(UNROLL):
        codes[u] = STEPS << 24
    bounds = [jnp.int32(UNROLL)]
    for part in range(STEPS):
        def listed(i, place):
            for slot in range(slots):
                for k in range(w):
                    code = scalars[slot, (part * part_rows + i) * w + k]
                    codes[place] = code
                    place = place + (code >= 0).astype(jnp.int32)
            return place

        bounds.append(lax.fori_loop(0, part_rows, listed, bounds[-1]))
    for u in range(2 * UNROLL):
        codes[bounds[-1] + u] = STEPS << 24

    for step in range(STEPS):
        pltpu.make_async_copy(right_bufs[0], right.at[step], rsem.at[step]).wait()
    for slot in range(slots):
        @pl.when(info_ref[slot] >= 0)
        def _():
            pltpu.make_async_copy(left_bufs[0], left.at[slot], lsem.at[slot]).wait()

    low = lax.broadcasted_iota(jnp.int32, (BS, 2 * BS), 1) < BS
    half = lax.broadcasted_iota(jnp.int32, (BS, 2 * BS), 1) // BS

    def block_at(index):
        return pl.ds(pl.multiple_of(index * BS, BS), BS)

    def product(code):
        slot = (code >> 8) & 15
        x = left[(code >> 12) & 15, block_at((code >> 16) & 255), pl.ds(pl.multiple_of((slot >> 1) * 2 * BS, 2 * BS), 2 * BS)]
        both = jnp.where(half == (slot & 1), x, pltpu.roll(x, BS, 1))
        hi = both.astype(jnp.bfloat16).astype(jnp.float32)
        lhs = jnp.where(low, hi, both - hi).astype(jnp.bfloat16)
        lhs = jnp.concatenate([lhs, lhs], axis=1)
        y = right[code >> 24, block_at(code & 255), :]
        hi = y.astype(jnp.bfloat16)
        lo = (y - hi.astype(jnp.float32)).astype(jnp.bfloat16)
        rhs = jnp.concatenate([hi, hi, lo, lo], axis=0)
        return jnp.dot(lhs, rhs, preferred_element_type=jnp.float32)

    def add(code, product):
        for pair in range(w // 2):
            x = product[:, pair * 2 * BS : (pair + 1) * 2 * BS]
            turned = pltpu.roll(x, BS, 1)
            for side in range(2):
                place = scalars[slots + (code >> 24), (code & 255) * w + 2 * pair + side]
                parity = place >> 16
                picked = jnp.where(parity == side, x, turned)
                picked = jnp.where(half == parity, picked, 0.0)
                base = pl.multiple_of(place & 0xFFFF, 2 * BS)
                acc[block_at((code >> 16) & 255), pl.ds(base, 2 * BS)] += picked

    def out_copy(part):
        at = pl.ds(part * part_rows * BS, part_rows * BS)
        return pltpu.make_async_copy(acc.at[at], out_ref.at[at], osem.at[part])

    groups = [jnp.int32(0)] + [(bound + UNROLL - 1) // UNROLL for bound in bounds[1:]]
    for part in range(STEPS):
        @pl.loop(groups[part], groups[part + 1])
        def _(group):
            for u in range(UNROLL):
                add(codes[group * UNROLL + u], value[u])
            for u in range(UNROLL):
                value[u] = product(codes[(group + 1) * UNROLL + u])

        out_copy(part).start()
    for part in range(STEPS):
        out_copy(part).wait()


def passed_on(bufs):
    hbm = pl.BlockSpec(memory_space=pl.ANY)
    return pl.pallas_call(
        lambda *refs: None,
        out_shape=[jax.ShapeDtypeStruct(buf.shape, buf.dtype) for buf in bufs],
        in_specs=[hbm] * len(bufs),
        out_specs=[hbm] * len(bufs),
        input_output_aliases={i: i for i in range(len(bufs))},
        cost_estimate=pl.CostEstimate(flops=10**11, bytes_accessed=0, transcendentals=0),
    )(*bufs)


def local(p_cols, p_data):
    n_row, n_col = lax.axis_size("row"), lax.axis_size("col")
    ratio = n_row // n_col
    row_id, col_id = lax.axis_index("row"), lax.axis_index("col")
    rb, w = p_cols.shape
    rows, width = p_data.shape
    left_perms = left_plan(n_row, n_col, ratio)
    right_perms = right_plan(n_row, n_col, ratio)
    table, slots = device_table(left_perms, right_perms, n_row, n_col, ratio)
    info = jnp.asarray(table)[row_id, col_id]

    cols = jnp.pad(p_cols.astype(jnp.float32).reshape(1, -1), ((0, EXTRA - 1), (0, width - rb * w)))
    own = jnp.concatenate([p_data, cols], axis=0)

    def permute(value, pairs):
        return lax.ppermute(value, ("row", "col"), [(s[0] * n_col + s[1], d[0] * n_col + d[1]) for s, d in pairs])

    def among(devices):
        bits = [sum(1 << c for c in range(n_col) if (r, c) in devices) for r in range(n_row)]
        word = functools.reduce(lambda word, r: jnp.where(row_id == r, bits[r], word), range(1, n_row), jnp.int32(bits[0]))
        return (word >> col_id) & 1 == 1

    def send(value, pairs):
        return lax.ppermute(value, ("row", "col"), [(s[0] * n_col + s[1], d[0] * n_col + d[1]) for s, d in pairs])

    def carry(bufs, perms):
        for source, pairs in perms:
            value = source
            if isinstance(source, dict):
                first, *others = sorted(set(source.values()))
                value = bufs[first]
                for other in others:
                    value = jnp.where(among([d for d in source if source[d] == other]), bufs[other], value)
            else:
                value = bufs[source]
            bufs.append(send(value, pairs))

    left_bufs, right_bufs = [own], [own]
    if len(right_perms) == 6:
        carry(right_bufs, right_perms[:-1])
        carry(left_bufs, left_perms)
        left_bufs[3], left_bufs[4], right_bufs[3], right_bufs[4] = passed_on(left_bufs[3:5] + right_bufs[3:5])
        carry(right_bufs, right_perms[-1:])
    else:
        carry(right_bufs, right_perms)
        carry(left_bufs, left_perms)
    out_shape = jax.ShapeDtypeStruct((rows, rb * ratio * BS), jnp.float32)
    smem = pl.BlockSpec(memory_space=pltpu.SMEM)
    hbm = pl.BlockSpec(memory_space=pl.ANY)
    dma = pltpu.SemaphoreType.DMA
    bufs = right_bufs + left_bufs[1:]
    return pl.pallas_call(
        functools.partial(product_kernel, slots, n_row, ratio, rb, w, len(right_bufs)),
        out_shape=out_shape,
        in_specs=[smem] + [hbm] * len(bufs),
        out_specs=hbm,
        scratch_shapes=[
            pltpu.VMEM((slots, rows + EXTRA, width), jnp.float32),
            pltpu.VMEM((STEPS + 1, rows + EXTRA, width), jnp.float32),
            pltpu.VMEM(out_shape.shape, jnp.float32),
            pltpu.VMEM((UNROLL, BS, width), jnp.float32),
            pltpu.VMEM((slots + STEPS, EXTRA, width), jnp.float32),
            pltpu.VMEM((16, 128), jnp.int32),
            pltpu.SMEM((16, 128), jnp.int32),
            pltpu.SMEM((slots * rb * w + 4 * UNROLL,), jnp.int32),
            dma((slots,)),
            dma((STEPS,)),
            dma((STEPS,)),
            dma((slots + STEPS + 1,)),
        ],
        compiler_params=pltpu.CompilerParams(vmem_limit_bytes=24 << 20),
        cost_estimate=pl.CostEstimate(flops=10**9, bytes_accessed=20 << 20, transcendentals=0),
    )(info, *bufs)


def solution(mesh):
    in_specs = (P("row", "col"), P("row", "col"))
    return jax.shard_map(local, mesh=mesh, in_specs=in_specs, out_specs=P("row", "col"), check_vma=False)
```

```python
import functools

import jax
import jax.numpy as jnp
import numpy as np
from jax import lax
from jax.experimental import pallas as pl
from jax.experimental.pallas import tpu as pltpu
from jax.sharding import PartitionSpec as P

BS = 64
STEPS = 4
UNROLL = 4
EXTRA = 8


def left_offsets(row, ratio, n_col):
    seen = []
    for step in range(STEPS):
        offset = (row + step) // ratio % n_col
        if offset not in seen:
            seen.append(offset)
    return seen


def shift(rows, step, count):
    return [((r, c), (r, (c + step) % count)) for r in rows for c in range(count)]


def left_plan(n_row, n_col, ratio):
    offsets = [left_offsets(row, ratio, n_col) for row in range(n_row)]
    if (n_row, n_col, ratio) != (8, 4, 2):
        perms = []
        for slot in range(max(len(o) for o in offsets)):
            pairs = [
                ((row, (col + offsets[row][slot]) % n_col), (row, col))
                for row in range(n_row)
                for col in range(n_col)
                if slot < len(offsets[row]) and offsets[row][slot] != 0
            ]
            perms.append((0, pairs))
        return perms
    down = shift([r for r in range(8) if 1 in offsets[r] and not {1, 2, 3} <= set(offsets[r])], -1, 4)
    up = shift([r for r in range(8) if 3 in offsets[r] and not {1, 2, 3} <= set(offsets[r])], 1, 4)
    again_down = shift([r for r in range(8) if set(offsets[r]) in ({0, 1, 2}, {1, 2})], -1, 4)
    again_up = shift([r for r in range(8) if set(offsets[r]) in ({2, 3}, {0, 2, 3})], 1, 4)
    down += [((3, c), (3, c - 1)) for c in (1, 2, 3)] + [((3, 0), (6, 0))]
    up += [((3, c), (3, c + 1)) for c in (0, 1, 2)] + [((3, 3), (0, 3))]
    again_down += [((3, 1), (3, 0)), ((3, 2), (3, 1)), ((6, 0), (3, 3))]
    again_up += [((3, 1), (3, 2)), ((3, 2), (3, 3)), ((0, 3), (3, 0))]
    return [(0, down), (0, up), (1, again_down), (2, again_up)]


def right_plan(n_row, n_col, ratio):
    everyone = [(row, col) for row in range(n_row) for col in range(n_col)]
    if (n_row, n_col, ratio) != (8, 4, 2):
        return [
            (0, [(((r + ratio * c + step) % n_row, c), (r, c)) for r, c in everyone if (ratio * c + step) % n_row])
            for step in range(STEPS)
        ]
    first = [(((r + 2 * c) % 8, c), (r, c)) for r, c in everyone if c != 0]
    first += [((r + 1, 0), (r, 0)) for r in range(0, 8, 2)]
    second = [(((r + 2 * c + 2) % 8, c), (r, c)) for r, c in everyone if c != 3]
    second += [((r ^ 1, 3), (r, 3)) for r in range(8)]
    last = [(((r - 1 + 2 * c + 4) % 8, c), (r, c)) for r, c in everyone if r % 2 == 1]
    first_swap = [((r + 1, c), (r, c)) for r, c in everyone if r % 2 == 0 and c != 0]
    second_swap = [((r ^ 1, c), (r, c)) for r, c in everyone if c != 3]
    return [(0, first), (0, second), (0, last), (1, first_swap), (2, second_swap)]


def carry_out(perms, n_row, n_col):
    held = [{(r, c): (r, c) for r in range(n_row) for c in range(n_col)}]
    for source, pairs in perms:
        held.append({dst: held[source][src] for src, dst in pairs})
    return held


def device_table(left_perms, right_perms, n_row, n_col, ratio):
    left_held = carry_out(left_perms, n_row, n_col)
    right_held = carry_out(right_perms, n_row, n_col)
    slots = (ratio - 1 + STEPS - 1) // ratio + 1
    table = np.full((n_row, n_col, 2 * slots + STEPS), -1, np.int32)

    def find(held, device, tile):
        return [i for i, h in enumerate(held) if h.get(device) == tile][0]

    for r in range(n_row):
        for c in range(n_col):
            for slot, offset in enumerate(left_offsets(r, ratio, n_col)):
                tile_col = (c + offset) % n_col
                table[r, c, slot] = find(left_held, (r, c), (r, tile_col))
                table[r, c, slots + STEPS + slot] = (tile_col * ratio - r - ratio * c) % n_row
            for step in range(STEPS):
                table[r, c, slots + step] = find(right_held, (r, c), ((r + ratio * c + step) % n_row, c))
    return table, slots


def fetch(choice, bufs, target, sem):
    for number, buf in enumerate(bufs):
        @pl.when(choice == number)
        def _():
            pltpu.make_async_copy(buf, target, sem).start()


def product_kernel(slots, n_row, ratio, rb, w, n_right, info_ref, *refs):
    out_ref, left, right, acc, value, cols, coded, scalars, codes, lsem, rsem, osem, csem = refs[-13:]
    right_bufs, left_bufs = refs[:n_right], refs[:1] + refs[n_right:-13]
    rows, width = left.shape[1] - EXTRA, left.shape[2]
    names = pl.ds(rows, EXTRA)
    for slot in range(slots):
        fetch(info_ref[slot], [buf.at[names] for buf in left_bufs], cols.at[slot], csem.at[slot])
    for step in range(STEPS):
        choice = info_ref[slots + step]
        fetch(choice, [buf.at[names] for buf in right_bufs], cols.at[slots + step], csem.at[slots + step])
    for step in range(STEPS):
        fetch(info_ref[slots + step], right_bufs, right.at[step], rsem.at[step])
    for slot in range(slots):
        fetch(info_ref[slot], left_bufs, left.at[slot], lsem.at[slot])

    def clear(first, last):
        @pl.loop(first, last)
        def _(r):
            acc[pl.ds(pl.multiple_of(r * BS, BS), BS), :] = jnp.zeros((BS, acc.shape[1]), jnp.float32)

    clear(0, rb // 4)
    lanes = scalars.shape[1]
    place = lax.broadcasted_iota(jnp.int32, (1, lanes), 1)
    for slot in range(slots):
        used = info_ref[slot] >= 0

        @pl.when(used)
        def _():
            pltpu.make_async_copy(left_bufs[0].at[names], cols.at[slot], csem.at[slot]).wait()

        inner = cols[slot, 0:1, 0:lanes].astype(jnp.int32)
        valid = (inner >= 0) & (place < rb * w)
        step = jnp.full(inner.shape, info_ref[slots + STEPS + slot], jnp.int32)
        for _ in range(ratio - 1):
            beyond = inner >= rb
            step = jnp.where(beyond, step + 1, step)
            inner = jnp.where(beyond, inner - rb, inner)
        step = jnp.where(step >= n_row, step - n_row, step)
        code = inner | (place & (w - 1)) << 8 | slot << 12 | (place // w) << 16 | step << 24
        valid = valid & (step < STEPS)
        coded[slot : slot + 1, :] = jnp.where(valid, jnp.where(used, code, -1), -1)
    for step in range(STEPS):
        pltpu.make_async_copy(right_bufs[0].at[names], cols.at[slots + step], csem.at[slots + step]).wait()
        col = cols[slots + step, 0:1, 0:lanes].astype(jnp.int32)
        code = (col >> 1) * 2 * BS | (col & 1) << 16
        coded[slots + step : slots + step + 1, :] = jnp.where(col < 0, 2 << 16, code)
    coded[slots + STEPS : slots + STEPS + 1, :] = jnp.full((1, lanes), 2 << 16, jnp.int32)
    to_scalars = pltpu.make_async_copy(coded, scalars, csem.at[slots + STEPS])
    to_scalars.start()
    clear(rb // 4, rb)
    to_scalars.wait()

    part_rows = rb // STEPS
    for u in range(UNROLL):
        codes[u] = STEPS << 24
    bounds = [jnp.int32(UNROLL)]
    for part in range(STEPS):
        def listed(i, place):
            for slot in range(slots):
                for k in range(w):
                    code = scalars[slot, (part * part_rows + i) * w + k]
                    codes[place] = code
                    place = place + (code >= 0).astype(jnp.int32)
            return place

        bounds.append(lax.fori_loop(0, part_rows, listed, bounds[-1]))
    for u in range(2 * UNROLL):
        codes[bounds[-1] + u] = STEPS << 24

    for step in range(STEPS):
        pltpu.make_async_copy(right_bufs[0], right.at[step], rsem.at[step]).wait()
    for slot in range(slots):
        @pl.when(info_ref[slot] >= 0)
        def _():
            pltpu.make_async_copy(left_bufs[0], left.at[slot], lsem.at[slot]).wait()

    low = lax.broadcasted_iota(jnp.int32, (BS, 2 * BS), 1) < BS
    half = lax.broadcasted_iota(jnp.int32, (BS, 2 * BS), 1) // BS

    def block_at(index):
        return pl.ds(pl.multiple_of(index * BS, BS), BS)

    def product(code):
        slot = (code >> 8) & 15
        x = left[(code >> 12) & 15, block_at((code >> 16) & 255), pl.ds(pl.multiple_of((slot >> 1) * 2 * BS, 2 * BS), 2 * BS)]
        both = jnp.where(half == (slot & 1), x, pltpu.roll(x, BS, 1))
        hi = both.astype(jnp.bfloat16).astype(jnp.float32)
        lhs = jnp.where(low, hi, both - hi).astype(jnp.bfloat16)
        lhs = jnp.concatenate([lhs, lhs], axis=1)
        y = right[code >> 24, block_at(code & 255), :]
        hi = y.astype(jnp.bfloat16)
        lo = (y - hi.astype(jnp.float32)).astype(jnp.bfloat16)
        rhs = jnp.concatenate([hi, hi, lo, lo], axis=0)
        return jnp.dot(lhs, rhs, preferred_element_type=jnp.float32)

    def add(code, product):
        for pair in range(w // 2):
            x = product[:, pair * 2 * BS : (pair + 1) * 2 * BS]
            turned = pltpu.roll(x, BS, 1)
            for side in range(2):
                place = scalars[slots + (code >> 24), (code & 255) * w + 2 * pair + side]
                parity = place >> 16
                picked = jnp.where(parity == side, x, turned)
                picked = jnp.where(half == parity, picked, 0.0)
                base = pl.multiple_of(place & 0xFFFF, 2 * BS)
                acc[block_at((code >> 16) & 255), pl.ds(base, 2 * BS)] += picked

    def out_copy(part):
        at = pl.ds(part * part_rows * BS, part_rows * BS)
        return pltpu.make_async_copy(acc.at[at], out_ref.at[at], osem.at[part])

    groups = [jnp.int32(0)] + [(bound + UNROLL - 1) // UNROLL for bound in bounds[1:]]
    for part in range(STEPS):
        @pl.loop(groups[part], groups[part + 1])
        def _(group):
            for u in range(UNROLL):
                add(codes[group * UNROLL + u], value[u])
            for u in range(UNROLL):
                value[u] = product(codes[(group + 1) * UNROLL + u])

        out_copy(part).start()
    for part in range(STEPS):
        out_copy(part).wait()


def local(p_cols, p_data):
    n_row, n_col = lax.axis_size("row"), lax.axis_size("col")
    ratio = n_row // n_col
    row_id, col_id = lax.axis_index("row"), lax.axis_index("col")
    rb, w = p_cols.shape
    rows, width = p_data.shape
    left_perms = left_plan(n_row, n_col, ratio)
    right_perms = right_plan(n_row, n_col, ratio)
    table, slots = device_table(left_perms, right_perms, n_row, n_col, ratio)
    info = jnp.asarray(table)[row_id, col_id]

    cols = jnp.pad(p_cols.astype(jnp.float32).reshape(1, -1), ((0, EXTRA - 1), (0, width - rb * w)))
    own = jnp.concatenate([p_data, cols], axis=0)

    def carry(perms):
        bufs = [own]
        for source, pairs in perms:
            flat = [(s[0] * n_col + s[1], d[0] * n_col + d[1]) for s, d in pairs]
            bufs.append(lax.ppermute(bufs[source], ("row", "col"), flat))
        return bufs

    left_bufs, right_bufs = carry(left_perms), carry(right_perms)
    out_shape = jax.ShapeDtypeStruct((rows, rb * ratio * BS), jnp.float32)
    smem = pl.BlockSpec(memory_space=pltpu.SMEM)
    hbm = pl.BlockSpec(memory_space=pl.ANY)
    dma = pltpu.SemaphoreType.DMA
    bufs = right_bufs + left_bufs[1:]
    return pl.pallas_call(
        functools.partial(product_kernel, slots, n_row, ratio, rb, w, len(right_bufs)),
        out_shape=out_shape,
        in_specs=[smem] + [hbm] * len(bufs),
        out_specs=hbm,
        scratch_shapes=[
            pltpu.VMEM((slots, rows + EXTRA, width), jnp.float32),
            pltpu.VMEM((STEPS + 1, rows + EXTRA, width), jnp.float32),
            pltpu.VMEM(out_shape.shape, jnp.float32),
            pltpu.VMEM((UNROLL, BS, width), jnp.float32),
            pltpu.VMEM((slots + STEPS, EXTRA, width), jnp.float32),
            pltpu.VMEM((16, 128), jnp.int32),
            pltpu.SMEM((16, 128), jnp.int32),
            pltpu.SMEM((slots * rb * w + 4 * UNROLL,), jnp.int32),
            dma((slots,)),
            dma((STEPS,)),
            dma((STEPS,)),
            dma((slots + STEPS + 1,)),
        ],
        compiler_params=pltpu.CompilerParams(vmem_limit_bytes=24 << 20),
        cost_estimate=pl.CostEstimate(flops=10**9, bytes_accessed=20 << 20, transcendentals=0),
    )(info, *bufs)


def solution(mesh):
    in_specs = (P("row", "col"), P("row", "col"))
    return jax.shard_map(local, mesh=mesh, in_specs=in_specs, out_specs=P("row", "col"), check_vma=False)
```

```python
import functools

import jax
import jax.numpy as jnp
import numpy as np
from jax import lax
from jax.experimental import pallas as pl
from jax.experimental.pallas import tpu as pltpu
from jax.sharding import PartitionSpec as P

BS = 64
STEPS = 4
UNROLL = 4
EXTRA = 8


def left_offsets(row, ratio, n_col):
    seen = []
    for step in range(STEPS):
        offset = (row + step) // ratio % n_col
        if offset not in seen:
            seen.append(offset)
    return seen


def shift(rows, step, count):
    return [((r, c), (r, (c + step) % count)) for r in rows for c in range(count)]


def left_plan(n_row, n_col, ratio):
    offsets = [left_offsets(row, ratio, n_col) for row in range(n_row)]
    if (n_row, n_col, ratio) != (8, 4, 2):
        perms = []
        for slot in range(max(len(o) for o in offsets)):
            pairs = [
                ((row, (col + offsets[row][slot]) % n_col), (row, col))
                for row in range(n_row)
                for col in range(n_col)
                if slot < len(offsets[row]) and offsets[row][slot] != 0
            ]
            perms.append((0, pairs))
        return perms
    whole = [r for r in range(8) if {1, 2, 3} <= set(offsets[r])]
    once, twice = {-1: [], 1: []}, {-1: [], 1: []}
    for r in range(8):
        for offset, step in ((1, -1), (3, 1)):
            if offset in offsets[r] and r not in whole:
                once[step].append(r)
                if 2 in offsets[r]:
                    twice[step].append(r)
    down = shift([r for r in once[-1] if r != 0], -1, 4) + [((3, c), (3, c - 1)) for c in (1, 2, 3)] + [((3, 0), (0, 0))]
    up = shift(once[1], 1, 4) + shift([0], -1, 4) + [((3, c), (3, c + 1)) for c in (0, 1, 2)] + [((3, 3), (1, 3))]
    again_down = shift(twice[-1], -1, 4) + [((3, 1), (3, 0)), ((3, 2), (3, 1)), ((0, 0), (3, 3))]
    again_up = shift(twice[1], 1, 4) + [((3, 1), (3, 2)), ((3, 2), (3, 3)), ((1, 3), (3, 0))]
    return [(0, down), (0, up), (1, again_down), (2, again_up)]


def right_plan(n_row, n_col, ratio):
    everyone = [(row, col) for row in range(n_row) for col in range(n_col)]
    if (n_row, n_col, ratio) != (8, 4, 2):
        return [
            (0, [(((r + ratio * c + step) % n_row, c), (r, c)) for r, c in everyone if (ratio * c + step) % n_row])
            for step in range(STEPS)
        ]
    first = [(((r + 2 * c) % 8, c), (r, c)) for r, c in everyone if c != 0]
    first += [((r + 1, 0), (r, 0)) for r in range(0, 8, 2)]
    second = [(((r + 2 * c + 2) % 8, c), (r, c)) for r, c in everyone if c != 3]
    second += [((r ^ 1, 3), (r, 3)) for r in range(8)]
    last = [(((r - 1 + 2 * c + 4) % 8, c), (r, c)) for r, c in everyone if r % 2 == 1]
    first_swap = [((r + 1, c), (r, c)) for r, c in everyone if r % 2 == 0 and c != 0]
    second_swap = [((r ^ 1, c), (r, c)) for r, c in everyone if c != 3]
    return [(0, first), (0, second), (0, last), (1, first_swap), (2, second_swap)]


def carry_out(perms, n_row, n_col):
    held = [{(r, c): (r, c) for r in range(n_row) for c in range(n_col)}]
    for source, pairs in perms:
        held.append({dst: held[source][src] for src, dst in pairs})
    return held


def device_table(left_perms, right_perms, n_row, n_col, ratio):
    left_held = carry_out(left_perms, n_row, n_col)
    right_held = carry_out(right_perms, n_row, n_col)
    slots = (ratio - 1 + STEPS - 1) // ratio + 1
    table = np.full((n_row, n_col, 2 * slots + STEPS), -1, np.int32)

    def find(held, device, tile):
        return [i for i, h in enumerate(held) if h.get(device) == tile][0]

    for r in range(n_row):
        for c in range(n_col):
            for slot, offset in enumerate(left_offsets(r, ratio, n_col)):
                tile_col = (c + offset) % n_col
                table[r, c, slot] = find(left_held, (r, c), (r, tile_col))
                table[r, c, slots + STEPS + slot] = (tile_col * ratio - r - ratio * c) % n_row
            for step in range(STEPS):
                table[r, c, slots + step] = find(right_held, (r, c), ((r + ratio * c + step) % n_row, c))
    return table, slots


def fetch(choice, bufs, target, sem):
    for number, buf in enumerate(bufs):
        @pl.when(choice == number)
        def _():
            pltpu.make_async_copy(buf, target, sem).start()


def product_kernel(slots, n_row, ratio, rb, w, n_right, info_ref, *refs):
    out_ref, left, right, acc, value, cols, coded, scalars, codes, lsem, rsem, osem, csem = refs[-13:]
    right_bufs, left_bufs = refs[:n_right], refs[:1] + refs[n_right:-13]
    rows, width = left.shape[1] - EXTRA, left.shape[2]
    names = pl.ds(rows, EXTRA)
    for slot in range(slots):
        fetch(info_ref[slot], [buf.at[names] for buf in left_bufs], cols.at[slot], csem.at[slot])
    for step in range(STEPS):
        choice = info_ref[slots + step]
        fetch(choice, [buf.at[names] for buf in right_bufs], cols.at[slots + step], csem.at[slots + step])
    for step in range(STEPS):
        fetch(info_ref[slots + step], right_bufs, right.at[step], rsem.at[step])
    for slot in range(slots):
        fetch(info_ref[slot], left_bufs, left.at[slot], lsem.at[slot])

    def clear(first, last):
        @pl.loop(first, last)
        def _(r):
            acc[pl.ds(pl.multiple_of(r * BS, BS), BS), :] = jnp.zeros((BS, acc.shape[1]), jnp.float32)

    clear(0, rb // 4)
    lanes = scalars.shape[1]
    place = lax.broadcasted_iota(jnp.int32, (1, lanes), 1)
    for slot in range(slots):
        used = info_ref[slot] >= 0

        @pl.when(used)
        def _():
            pltpu.make_async_copy(left_bufs[0].at[names], cols.at[slot], csem.at[slot]).wait()

        inner = cols[slot, 0:1, 0:lanes].astype(jnp.int32)
        valid = (inner >= 0) & (place < rb * w)
        step = jnp.full(inner.shape, info_ref[slots + STEPS + slot], jnp.int32)
        for _ in range(ratio - 1):
            beyond = inner >= rb
            step = jnp.where(beyond, step + 1, step)
            inner = jnp.where(beyond, inner - rb, inner)
        step = jnp.where(step >= n_row, step - n_row, step)
        code = inner | (place & (w - 1)) << 8 | slot << 12 | (place // w) << 16 | step << 24
        valid = valid & (step < STEPS)
        coded[slot : slot + 1, :] = jnp.where(valid, jnp.where(used, code, -1), -1)
    for step in range(STEPS):
        pltpu.make_async_copy(right_bufs[0].at[names], cols.at[slots + step], csem.at[slots + step]).wait()
        col = cols[slots + step, 0:1, 0:lanes].astype(jnp.int32)
        code = (col >> 1) * 2 * BS | (col & 1) << 16
        coded[slots + step : slots + step + 1, :] = jnp.where(col < 0, 2 << 16, code)
    coded[slots + STEPS : slots + STEPS + 1, :] = jnp.full((1, lanes), 2 << 16, jnp.int32)
    to_scalars = pltpu.make_async_copy(coded, scalars, csem.at[slots + STEPS])
    to_scalars.start()
    clear(rb // 4, rb)
    to_scalars.wait()

    part_rows = rb // STEPS
    for u in range(UNROLL):
        codes[u] = STEPS << 24
    bounds = [jnp.int32(UNROLL)]
    for part in range(STEPS):
        def listed(i, place):
            for slot in range(slots):
                for k in range(w):
                    code = scalars[slot, (part * part_rows + i) * w + k]
                    codes[place] = code
                    place = place + (code >= 0).astype(jnp.int32)
            return place

        bounds.append(lax.fori_loop(0, part_rows, listed, bounds[-1]))
    for u in range(2 * UNROLL):
        codes[bounds[-1] + u] = STEPS << 24

    for step in range(STEPS):
        pltpu.make_async_copy(right_bufs[0], right.at[step], rsem.at[step]).wait()
    for slot in range(slots):
        @pl.when(info_ref[slot] >= 0)
        def _():
            pltpu.make_async_copy(left_bufs[0], left.at[slot], lsem.at[slot]).wait()

    low = lax.broadcasted_iota(jnp.int32, (BS, 2 * BS), 1) < BS
    half = lax.broadcasted_iota(jnp.int32, (BS, 2 * BS), 1) // BS

    def block_at(index):
        return pl.ds(pl.multiple_of(index * BS, BS), BS)

    def product(code):
        slot = (code >> 8) & 15
        x = left[(code >> 12) & 15, block_at((code >> 16) & 255), pl.ds(pl.multiple_of((slot >> 1) * 2 * BS, 2 * BS), 2 * BS)]
        both = jnp.where(half == (slot & 1), x, pltpu.roll(x, BS, 1))
        hi = both.astype(jnp.bfloat16).astype(jnp.float32)
        lhs = jnp.where(low, hi, both - hi).astype(jnp.bfloat16)
        lhs = jnp.concatenate([lhs, lhs], axis=1)
        y = right[code >> 24, block_at(code & 255), :]
        hi = y.astype(jnp.bfloat16)
        lo = (y - hi.astype(jnp.float32)).astype(jnp.bfloat16)
        rhs = jnp.concatenate([hi, hi, lo, lo], axis=0)
        return jnp.dot(lhs, rhs, preferred_element_type=jnp.float32)

    def add(code, product):
        for pair in range(w // 2):
            x = product[:, pair * 2 * BS : (pair + 1) * 2 * BS]
            turned = pltpu.roll(x, BS, 1)
            for side in range(2):
                place = scalars[slots + (code >> 24), (code & 255) * w + 2 * pair + side]
                parity = place >> 16
                picked = jnp.where(parity == side, x, turned)
                picked = jnp.where(half == parity, picked, 0.0)
                base = pl.multiple_of(place & 0xFFFF, 2 * BS)
                acc[block_at((code >> 16) & 255), pl.ds(base, 2 * BS)] += picked

    def out_copy(part):
        at = pl.ds(part * part_rows * BS, part_rows * BS)
        return pltpu.make_async_copy(acc.at[at], out_ref.at[at], osem.at[part])

    groups = [jnp.int32(0)] + [(bound + UNROLL - 1) // UNROLL for bound in bounds[1:]]
    for part in range(STEPS):
        @pl.loop(groups[part], groups[part + 1])
        def _(group):
            for u in range(UNROLL):
                add(codes[group * UNROLL + u], value[u])
            for u in range(UNROLL):
                value[u] = product(codes[(group + 1) * UNROLL + u])

        out_copy(part).start()
    for part in range(STEPS):
        out_copy(part).wait()


def local(p_cols, p_data):
    n_row, n_col = lax.axis_size("row"), lax.axis_size("col")
    ratio = n_row // n_col
    row_id, col_id = lax.axis_index("row"), lax.axis_index("col")
    rb, w = p_cols.shape
    rows, width = p_data.shape
    left_perms = left_plan(n_row, n_col, ratio)
    right_perms = right_plan(n_row, n_col, ratio)
    table, slots = device_table(left_perms, right_perms, n_row, n_col, ratio)
    info = jnp.asarray(table)[row_id, col_id]

    cols = jnp.pad(p_cols.astype(jnp.float32).reshape(1, -1), ((0, EXTRA - 1), (0, width - rb * w)))
    own = jnp.concatenate([p_data, cols], axis=0)

    def carry(perms):
        bufs = [own]
        for source, pairs in perms:
            flat = [(s[0] * n_col + s[1], d[0] * n_col + d[1]) for s, d in pairs]
            bufs.append(lax.ppermute(bufs[source], ("row", "col"), flat))
        return bufs

    left_bufs, right_bufs = carry(left_perms), carry(right_perms)
    out_shape = jax.ShapeDtypeStruct((rows, rb * ratio * BS), jnp.float32)
    smem = pl.BlockSpec(memory_space=pltpu.SMEM)
    hbm = pl.BlockSpec(memory_space=pl.ANY)
    dma = pltpu.SemaphoreType.DMA
    bufs = right_bufs + left_bufs[1:]
    return pl.pallas_call(
        functools.partial(product_kernel, slots, n_row, ratio, rb, w, len(right_bufs)),
        out_shape=out_shape,
        in_specs=[smem] + [hbm] * len(bufs),
        out_specs=hbm,
        scratch_shapes=[
            pltpu.VMEM((slots, rows + EXTRA, width), jnp.float32),
            pltpu.VMEM((STEPS + 1, rows + EXTRA, width), jnp.float32),
            pltpu.VMEM(out_shape.shape, jnp.float32),
            pltpu.VMEM((UNROLL, BS, width), jnp.float32),
            pltpu.VMEM((slots + STEPS, EXTRA, width), jnp.float32),
            pltpu.VMEM((16, 128), jnp.int32),
            pltpu.SMEM((16, 128), jnp.int32),
            pltpu.SMEM((slots * rb * w + 4 * UNROLL,), jnp.int32),
            dma((slots,)),
            dma((STEPS,)),
            dma((STEPS,)),
            dma((slots + STEPS + 1,)),
        ],
        compiler_params=pltpu.CompilerParams(vmem_limit_bytes=24 << 20),
        cost_estimate=pl.CostEstimate(flops=10**9, bytes_accessed=20 << 20, transcendentals=0),
    )(info, *bufs)


def solution(mesh):
    in_specs = (P("row", "col"), P("row", "col"))
    return jax.shard_map(local, mesh=mesh, in_specs=in_specs, out_specs=P("row", "col"), check_vma=False)
```

```python
import functools

import jax
import jax.numpy as jnp
import numpy as np
from jax import lax
from jax.experimental import pallas as pl
from jax.experimental.pallas import tpu as pltpu
from jax.sharding import PartitionSpec as P

BS = 64
STEPS = 4
UNROLL = 4
EXTRA = 8
PARTS = 8


def left_offsets(row, ratio, n_col):
    seen = []
    for step in range(STEPS):
        offset = (row + step) // ratio % n_col
        if offset not in seen:
            seen.append(offset)
    return seen


def shift(rows, step, count):
    return [((r, c), (r, (c + step) % count)) for r in rows for c in range(count)]


def left_plan(n_row, n_col, ratio):
    offsets = [left_offsets(row, ratio, n_col) for row in range(n_row)]
    if (n_row, n_col, ratio) != (8, 4, 2):
        perms = []
        for slot in range(max(len(o) for o in offsets)):
            pairs = [
                ((row, (col + offsets[row][slot]) % n_col), (row, col))
                for row in range(n_row)
                for col in range(n_col)
                if slot < len(offsets[row]) and offsets[row][slot] != 0
            ]
            perms.append((0, pairs))
        return perms
    whole = [r for r in range(8) if {1, 2, 3} <= set(offsets[r])]
    once, twice = {-1: [], 1: []}, {-1: [], 1: []}
    for r in range(8):
        for offset, step in ((1, -1), (3, 1)):
            if offset in offsets[r] and r not in whole:
                once[step].append(r)
                if 2 in offsets[r]:
                    twice[step].append(r)
    down = shift([r for r in once[-1] if r != 0], -1, 4) + [((3, c), (3, c - 1)) for c in (1, 2, 3)] + [((3, 0), (0, 0))]
    up = shift(once[1], 1, 4) + shift([0], -1, 4) + [((3, c), (3, c + 1)) for c in (0, 1, 2)] + [((3, 3), (1, 3))]
    again_down = shift(twice[-1], -1, 4) + [((3, 1), (3, 0)), ((3, 2), (3, 1)), ((0, 0), (3, 3))]
    again_up = shift(twice[1], 1, 4) + [((3, 1), (3, 2)), ((3, 2), (3, 3)), ((1, 3), (3, 0))]
    return [(0, down), (0, up), (1, again_down), (2, again_up)]


def right_plan(n_row, n_col, ratio):
    everyone = [(row, col) for row in range(n_row) for col in range(n_col)]
    if (n_row, n_col, ratio) != (8, 4, 2):
        return [
            (0, [(((r + ratio * c + step) % n_row, c), (r, c)) for r, c in everyone if (ratio * c + step) % n_row])
            for step in range(STEPS)
        ]
    first = [(((r + 2 * c) % 8, c), (r, c)) for r, c in everyone if c != 0]
    first += [((r + 1, 0), (r, 0)) for r in range(0, 8, 2)]
    second = [(((r + 2 * c + 2) % 8, c), (r, c)) for r, c in everyone if c != 3]
    second += [((r ^ 1, 3), (r, 3)) for r in range(8)]
    last = [(((r - 1 + 2 * c + 4) % 8, c), (r, c)) for r, c in everyone if r % 2 == 1]
    first_swap = [((r + 1, c), (r, c)) for r, c in everyone if r % 2 == 0 and c != 0]
    second_swap = [((r ^ 1, c), (r, c)) for r, c in everyone if c != 3]
    return [(0, first), (0, second), (0, last), (1, first_swap), (2, second_swap)]


def carry_out(perms, n_row, n_col):
    held = [{(r, c): (r, c) for r in range(n_row) for c in range(n_col)}]
    for source, pairs in perms:
        held.append({dst: held[source][src] for src, dst in pairs})
    return held


def device_table(left_perms, right_perms, n_row, n_col, ratio):
    left_held = carry_out(left_perms, n_row, n_col)
    right_held = carry_out(right_perms, n_row, n_col)
    slots = (ratio - 1 + STEPS - 1) // ratio + 1
    table = np.full((n_row, n_col, 2 * slots + STEPS), -1, np.int32)

    def find(held, device, tile):
        return [i for i, h in enumerate(held) if h.get(device) == tile][0]

    for r in range(n_row):
        for c in range(n_col):
            for slot, offset in enumerate(left_offsets(r, ratio, n_col)):
                tile_col = (c + offset) % n_col
                table[r, c, slot] = find(left_held, (r, c), (r, tile_col))
                table[r, c, slots + STEPS + slot] = (tile_col * ratio - r - ratio * c) % n_row
            for step in range(STEPS):
                table[r, c, slots + step] = find(right_held, (r, c), ((r + ratio * c + step) % n_row, c))
    return table, slots


def fetch(choice, bufs, target, sem):
    for number, buf in enumerate(bufs):
        @pl.when(choice == number)
        def _():
            pltpu.make_async_copy(buf, target, sem).start()


def join_kernel(cols_ref, data_ref, out_ref, tail, sem):
    rows = data_ref.shape[0]
    data_copy = pltpu.make_async_copy(data_ref, out_ref.at[pl.ds(0, rows)], sem.at[0])
    data_copy.start()
    tail[...] = jnp.zeros_like(tail)
    tail[0 : cols_ref.shape[0], 0 : cols_ref.shape[1]] = cols_ref[...].astype(jnp.float32)
    tail_copy = pltpu.make_async_copy(tail, out_ref.at[pl.ds(rows, EXTRA)], sem.at[1])
    tail_copy.start()
    data_copy.wait()
    tail_copy.wait()


def product_kernel(slots, n_row, ratio, rb, w, n_right, info_ref, *refs):
    out_ref, left, right, acc, value, cols, coded, scalars, codes, lsem, rsem, osem, csem = refs[-13:]
    right_bufs, left_bufs = refs[:n_right], refs[:1] + refs[n_right:-13]
    rows, width = left.shape[1] - EXTRA, left.shape[2]
    names = pl.ds(rows, EXTRA)
    for slot in range(slots):
        fetch(info_ref[slot], [buf.at[names] for buf in left_bufs], cols.at[slot], csem.at[slot])
    for step in range(STEPS):
        choice = info_ref[slots + step]
        fetch(choice, [buf.at[names] for buf in right_bufs], cols.at[slots + step], csem.at[slots + step])
    for step in range(STEPS):
        fetch(info_ref[slots + step], right_bufs, right.at[step], rsem.at[step])
    for slot in range(slots):
        fetch(info_ref[slot], left_bufs, left.at[slot], lsem.at[slot])

    def clear(first, last):
        @pl.loop(first, last)
        def _(r):
            acc[pl.ds(pl.multiple_of(r * BS, BS), BS), :] = jnp.zeros((BS, acc.shape[1]), jnp.float32)

    clear(0, rb // 4)
    lanes = scalars.shape[1]
    row = lax.broadcasted_iota(jnp.int32, (w, lanes), 1)
    tile_slot = lax.broadcasted_iota(jnp.int32, (w, lanes), 0)
    for slot in range(slots):
        used = info_ref[slot] >= 0

        @pl.when(used)
        def _():
            pltpu.make_async_copy(left_bufs[0].at[names], cols.at[slot], csem.at[slot]).wait()

        inner = cols[slot, 0:w, 0:lanes].astype(jnp.int32)
        valid = (inner >= 0) & (row < rb)
        step = jnp.full(inner.shape, info_ref[slots + STEPS + slot], jnp.int32)
        for _ in range(ratio - 1):
            beyond = inner >= rb
            step = jnp.where(beyond, step + 1, step)
            inner = jnp.where(beyond, inner - rb, inner)
        step = jnp.where(step >= n_row, step - n_row, step)
        code = inner | tile_slot << 8 | slot << 12 | row << 16 | step << 24
        valid = valid & (step < STEPS)
        coded[slot * w : (slot + 1) * w, :] = jnp.where(valid, jnp.where(used, code, -1), -1)
    for step in range(STEPS):
        pltpu.make_async_copy(right_bufs[0].at[names], cols.at[slots + step], csem.at[slots + step]).wait()
        col = cols[slots + step, 0:w, 0:lanes].astype(jnp.int32)
        code = (col >> 1) * 2 * BS | (col & 1) << 16
        coded[(slots + step) * w : (slots + step + 1) * w, :] = jnp.where(col < 0, 2 << 16, code)
    coded[(slots + STEPS) * w : (slots + STEPS + 1) * w, :] = jnp.full((w, lanes), 2 << 16, jnp.int32)
    to_scalars = pltpu.make_async_copy(coded, scalars, csem.at[slots + STEPS])
    to_scalars.start()
    clear(rb // 4, rb)
    to_scalars.wait()

    part_rows = rb // PARTS
    for u in range(UNROLL):
        codes[u] = STEPS << 24
    bounds = [jnp.int32(UNROLL)]
    for part in range(PARTS):
        def listed(i, place):
            for slot in range(slots):
                for k in range(w):
                    code = scalars[slot * w + k, part * part_rows + i]
                    codes[place] = code
                    place = place + (code >= 0).astype(jnp.int32)
            return place

        bounds.append(lax.fori_loop(0, part_rows, listed, bounds[-1]))
    for u in range(2 * UNROLL):
        codes[bounds[-1] + u] = STEPS << 24

    for step in range(STEPS):
        pltpu.make_async_copy(right_bufs[0], right.at[step], rsem.at[step]).wait()
    for slot in range(slots):
        @pl.when(info_ref[slot] >= 0)
        def _():
            pltpu.make_async_copy(left_bufs[0], left.at[slot], lsem.at[slot]).wait()

    low = lax.broadcasted_iota(jnp.int32, (BS, 2 * BS), 1) < BS
    half = lax.broadcasted_iota(jnp.int32, (BS, 2 * BS), 1) // BS

    def block_at(index):
        return pl.ds(pl.multiple_of(index * BS, BS), BS)

    def product(code):
        slot = (code >> 8) & 15
        x = left[(code >> 12) & 15, block_at((code >> 16) & 255), pl.ds(pl.multiple_of((slot >> 1) * 2 * BS, 2 * BS), 2 * BS)]
        both = jnp.where(half == (slot & 1), x, pltpu.roll(x, BS, 1))
        hi = both.astype(jnp.bfloat16).astype(jnp.float32)
        lhs = jnp.where(low, hi, both - hi).astype(jnp.bfloat16)
        lhs = jnp.concatenate([lhs, lhs], axis=1)
        y = right[code >> 24, block_at(code & 255), :]
        hi = y.astype(jnp.bfloat16)
        lo = (y - hi.astype(jnp.float32)).astype(jnp.bfloat16)
        rhs = jnp.concatenate([hi, hi, lo, lo], axis=0)
        return jnp.dot(lhs, rhs, preferred_element_type=jnp.float32)

    def add(code, product):
        for pair in range(w // 2):
            x = product[:, pair * 2 * BS : (pair + 1) * 2 * BS]
            turned = pltpu.roll(x, BS, 1)
            for side in range(2):
                place = scalars[(slots + (code >> 24)) * w + 2 * pair + side, code & 255]
                parity = place >> 16
                picked = jnp.where(parity == side, x, turned)
                picked = jnp.where(half == parity, picked, 0.0)
                base = pl.multiple_of(place & 0xFFFF, 2 * BS)
                acc[block_at((code >> 16) & 255), pl.ds(base, 2 * BS)] += picked

    def out_copy(part):
        at = pl.ds(part * part_rows * BS, part_rows * BS)
        return pltpu.make_async_copy(acc.at[at], out_ref.at[at], osem.at[part])

    groups = [jnp.int32(0)] + [(bound + UNROLL - 1) // UNROLL for bound in bounds[1:]]
    for part in range(PARTS):
        @pl.loop(groups[part], groups[part + 1])
        def _(group):
            for u in range(UNROLL):
                add(codes[group * UNROLL + u], value[u])
            for u in range(UNROLL):
                value[u] = product(codes[(group + 1) * UNROLL + u])

        out_copy(part).start()
    for part in range(PARTS):
        out_copy(part).wait()


def local(p_cols, p_data):
    n_row, n_col = lax.axis_size("row"), lax.axis_size("col")
    ratio = n_row // n_col
    row_id, col_id = lax.axis_index("row"), lax.axis_index("col")
    rb, w = p_cols.shape
    rows, width = p_data.shape
    left_perms = left_plan(n_row, n_col, ratio)
    right_perms = right_plan(n_row, n_col, ratio)
    table, slots = device_table(left_perms, right_perms, n_row, n_col, ratio)
    info = jnp.asarray(table)[row_id, col_id]

    own = pl.pallas_call(
        join_kernel,
        out_shape=jax.ShapeDtypeStruct((rows + EXTRA, width), jnp.float32),
        in_specs=[pl.BlockSpec(memory_space=pltpu.VMEM), pl.BlockSpec(memory_space=pl.ANY)],
        out_specs=pl.BlockSpec(memory_space=pl.ANY),
        scratch_shapes=[pltpu.VMEM((EXTRA, width), jnp.float32), pltpu.SemaphoreType.DMA((2,))],
        compiler_params=pltpu.CompilerParams(vmem_limit_bytes=2 << 20),
        cost_estimate=pl.CostEstimate(flops=0, bytes_accessed=2 << 20, transcendentals=0),
    )(p_cols.T, p_data)

    def carry(perms):
        bufs = [own]
        for source, pairs in perms:
            flat = [(s[0] * n_col + s[1], d[0] * n_col + d[1]) for s, d in pairs]
            bufs.append(lax.ppermute(bufs[source], ("row", "col"), flat))
        return bufs

    left_bufs, right_bufs = carry(left_perms), carry(right_perms)
    out_shape = jax.ShapeDtypeStruct((rows, rb * ratio * BS), jnp.float32)
    smem = pl.BlockSpec(memory_space=pltpu.SMEM)
    hbm = pl.BlockSpec(memory_space=pl.ANY)
    dma = pltpu.SemaphoreType.DMA
    bufs = right_bufs + left_bufs[1:]
    codings = -(-(slots + STEPS + 1) * w // 8) * 8
    return pl.pallas_call(
        functools.partial(product_kernel, slots, n_row, ratio, rb, w, len(right_bufs)),
        out_shape=out_shape,
        in_specs=[smem] + [hbm] * len(bufs),
        out_specs=hbm,
        scratch_shapes=[
            pltpu.VMEM((slots, rows + EXTRA, width), jnp.float32),
            pltpu.VMEM((STEPS + 1, rows + EXTRA, width), jnp.float32),
            pltpu.VMEM(out_shape.shape, jnp.float32),
            pltpu.VMEM((UNROLL, BS, width), jnp.float32),
            pltpu.VMEM((slots + STEPS, EXTRA, width), jnp.float32),
            pltpu.VMEM((codings, 128), jnp.int32),
            pltpu.SMEM((codings, 128), jnp.int32),
            pltpu.SMEM((slots * rb * w + 4 * UNROLL,), jnp.int32),
            dma((slots,)),
            dma((STEPS,)),
            dma((PARTS,)),
            dma((slots + STEPS + 1,)),
        ],
        compiler_params=pltpu.CompilerParams(vmem_limit_bytes=24 << 20),
        cost_estimate=pl.CostEstimate(flops=10**9, bytes_accessed=20 << 20, transcendentals=0),
    )(info, *bufs)


def solution(mesh):
    in_specs = (P("row", "col"), P("row", "col"))
    return jax.shard_map(local, mesh=mesh, in_specs=in_specs, out_specs=P("row", "col"), check_vma=False)
```

```python
import functools

import jax
import jax.numpy as jnp
import numpy as np
from jax import lax
from jax.experimental import pallas as pl
from jax.experimental.pallas import tpu as pltpu
from jax.sharding import PartitionSpec as P

BS = 64
STEPS = 4
UNROLL = 4
EXTRA = 8
PARTS = 8


def left_offsets(row, ratio, n_col):
    seen = []
    for step in range(STEPS):
        offset = (row + step) // ratio % n_col
        if offset not in seen:
            seen.append(offset)
    return seen


def shift(rows, step, count):
    return [((r, c), (r, (c + step) % count)) for r in rows for c in range(count)]


def left_plan(n_row, n_col, ratio):
    offsets = [left_offsets(row, ratio, n_col) for row in range(n_row)]
    if (n_row, n_col, ratio) != (8, 4, 2):
        perms = []
        for slot in range(max(len(o) for o in offsets)):
            pairs = [
                ((row, (col + offsets[row][slot]) % n_col), (row, col))
                for row in range(n_row)
                for col in range(n_col)
                if slot < len(offsets[row]) and offsets[row][slot] != 0
            ]
            perms.append((0, pairs))
        return perms
    whole = [r for r in range(8) if {1, 2, 3} <= set(offsets[r])]
    once, twice = {-1: [], 1: []}, {-1: [], 1: []}
    for r in range(8):
        for offset, step in ((1, -1), (3, 1)):
            if offset in offsets[r] and r not in whole:
                once[step].append(r)
                if 2 in offsets[r]:
                    twice[step].append(r)
    down = shift([r for r in once[-1] if r != 0], -1, 4) + [((3, c), (3, c - 1)) for c in (1, 2, 3)] + [((3, 0), (0, 0))]
    up = shift(once[1], 1, 4) + shift([0], -1, 4) + [((3, c), (3, c + 1)) for c in (0, 1, 2)] + [((3, 3), (1, 3))]
    again_down = shift(twice[-1], -1, 4) + [((3, 1), (3, 0)), ((3, 2), (3, 1)), ((0, 0), (3, 3))]
    again_up = shift(twice[1], 1, 4) + [((3, 1), (3, 2)), ((3, 2), (3, 3)), ((1, 3), (3, 0))]
    return [(0, down), (0, up), (1, again_down), (2, again_up)]


def right_plan(n_row, n_col, ratio):
    everyone = [(row, col) for row in range(n_row) for col in range(n_col)]
    if (n_row, n_col, ratio) != (8, 4, 2):
        return [
            (0, [(((r + ratio * c + step) % n_row, c), (r, c)) for r, c in everyone if (ratio * c + step) % n_row])
            for step in range(STEPS)
        ]
    first = [(((r + 2 * c) % 8, c), (r, c)) for r, c in everyone if c != 0]
    first += [((r + 1, 0), (r, 0)) for r in range(0, 8, 2)]
    second = [(((r + 2 * c + 2) % 8, c), (r, c)) for r, c in everyone if c != 3]
    second += [((r ^ 1, 3), (r, 3)) for r in range(8)]
    last = [(((r - 1 + 2 * c + 4) % 8, c), (r, c)) for r, c in everyone if r % 2 == 1]
    first_swap = [((r + 1, c), (r, c)) for r, c in everyone if r % 2 == 0 and c != 0]
    second_swap = [((r ^ 1, c), (r, c)) for r, c in everyone if c != 3]
    return [(0, first), (0, second), (0, last), (1, first_swap), (2, second_swap)]


def carry_out(perms, n_row, n_col):
    held = [{(r, c): (r, c) for r in range(n_row) for c in range(n_col)}]
    for source, pairs in perms:
        held.append({dst: held[source][src] for src, dst in pairs})
    return held


def device_table(left_perms, right_perms, n_row, n_col, ratio):
    left_held = carry_out(left_perms, n_row, n_col)
    right_held = carry_out(right_perms, n_row, n_col)
    slots = (ratio - 1 + STEPS - 1) // ratio + 1
    table = np.full((n_row, n_col, 2 * slots + STEPS), -1, np.int32)

    def find(held, device, tile):
        return [i for i, h in enumerate(held) if h.get(device) == tile][0]

    for r in range(n_row):
        for c in range(n_col):
            for slot, offset in enumerate(left_offsets(r, ratio, n_col)):
                tile_col = (c + offset) % n_col
                table[r, c, slot] = find(left_held, (r, c), (r, tile_col))
                table[r, c, slots + STEPS + slot] = (tile_col * ratio - r - ratio * c) % n_row
            for step in range(STEPS):
                table[r, c, slots + step] = find(right_held, (r, c), ((r + ratio * c + step) % n_row, c))
    return table, slots


def fetch(choice, bufs, target, sem):
    for number, buf in enumerate(bufs):
        @pl.when(choice == number)
        def _():
            pltpu.make_async_copy(buf, target, sem).start()


def join_kernel(cols_ref, data_ref, out_ref, cols, tail, sem):
    rows = data_ref.shape[0]
    cols_copy = pltpu.make_async_copy(cols_ref, cols, sem.at[0])
    data_copy = pltpu.make_async_copy(data_ref, out_ref.at[pl.ds(0, rows)], sem.at[1])
    cols_copy.start()
    data_copy.start()
    tail[...] = jnp.zeros_like(tail)
    cols_copy.wait()
    tail[0 : cols.shape[0], 0 : cols.shape[1]] = cols[...].astype(jnp.float32)
    tail_copy = pltpu.make_async_copy(tail, out_ref.at[pl.ds(rows, EXTRA)], sem.at[2])
    tail_copy.start()
    data_copy.wait()
    tail_copy.wait()


def product_kernel(slots, n_row, ratio, rb, w, n_right, info_ref, *refs):
    out_ref, left, right, acc, value, cols, coded, scalars, codes, lsem, rsem, osem, csem = refs[-13:]
    right_bufs, left_bufs = refs[:n_right], refs[:1] + refs[n_right:-13]
    rows, width = left.shape[1] - EXTRA, left.shape[2]
    names = pl.ds(rows, EXTRA)
    for slot in range(slots):
        fetch(info_ref[slot], [buf.at[names] for buf in left_bufs], cols.at[slot], csem.at[slot])
    for step in range(STEPS):
        choice = info_ref[slots + step]
        fetch(choice, [buf.at[names] for buf in right_bufs], cols.at[slots + step], csem.at[slots + step])
    for step in range(STEPS):
        fetch(info_ref[slots + step], right_bufs, right.at[step], rsem.at[step])
    for slot in range(slots):
        fetch(info_ref[slot], left_bufs, left.at[slot], lsem.at[slot])

    def clear(first, last):
        @pl.loop(first, last)
        def _(r):
            acc[pl.ds(pl.multiple_of(r * BS, BS), BS), :] = jnp.zeros((BS, acc.shape[1]), jnp.float32)

    clear(0, rb // 4)
    lanes = scalars.shape[1]
    row = lax.broadcasted_iota(jnp.int32, (w, lanes), 1)
    tile_slot = lax.broadcasted_iota(jnp.int32, (w, lanes), 0)
    for slot in range(slots):
        used = info_ref[slot] >= 0

        @pl.when(used)
        def _():
            pltpu.make_async_copy(left_bufs[0].at[names], cols.at[slot], csem.at[slot]).wait()

        inner = cols[slot, 0:w, 0:lanes].astype(jnp.int32)
        valid = (inner >= 0) & (row < rb)
        step = jnp.full(inner.shape, info_ref[slots + STEPS + slot], jnp.int32)
        for _ in range(ratio - 1):
            beyond = inner >= rb
            step = jnp.where(beyond, step + 1, step)
            inner = jnp.where(beyond, inner - rb, inner)
        step = jnp.where(step >= n_row, step - n_row, step)
        code = inner | tile_slot << 8 | slot << 12 | row << 16 | step << 24
        valid = valid & (step < STEPS)
        coded[slot * w : (slot + 1) * w, :] = jnp.where(valid, jnp.where(used, code, -1), -1)
    for step in range(STEPS):
        pltpu.make_async_copy(right_bufs[0].at[names], cols.at[slots + step], csem.at[slots + step]).wait()
        col = cols[slots + step, 0:w, 0:lanes].astype(jnp.int32)
        code = (col >> 1) * 2 * BS | (col & 1) << 16
        coded[(slots + step) * w : (slots + step + 1) * w, :] = jnp.where(col < 0, 2 << 16, code)
    coded[(slots + STEPS) * w : (slots + STEPS + 1) * w, :] = jnp.full((w, lanes), 2 << 16, jnp.int32)
    to_scalars = pltpu.make_async_copy(coded, scalars, csem.at[slots + STEPS])
    to_scalars.start()
    clear(rb // 4, rb)
    to_scalars.wait()

    part_rows = rb // PARTS
    for u in range(UNROLL):
        codes[u] = STEPS << 24
    bounds = [jnp.int32(UNROLL)]
    for part in range(PARTS):
        def listed(i, place):
            for slot in range(slots):
                for k in range(w):
                    code = scalars[slot * w + k, part * part_rows + i]
                    codes[place] = code
                    place = place + (code >= 0).astype(jnp.int32)
            return place

        bounds.append(lax.fori_loop(0, part_rows, listed, bounds[-1]))
    for u in range(2 * UNROLL):
        codes[bounds[-1] + u] = STEPS << 24

    for step in range(STEPS):
        pltpu.make_async_copy(right_bufs[0], right.at[step], rsem.at[step]).wait()
    for slot in range(slots):
        @pl.when(info_ref[slot] >= 0)
        def _():
            pltpu.make_async_copy(left_bufs[0], left.at[slot], lsem.at[slot]).wait()

    low = lax.broadcasted_iota(jnp.int32, (BS, 2 * BS), 1) < BS
    half = lax.broadcasted_iota(jnp.int32, (BS, 2 * BS), 1) // BS

    def block_at(index):
        return pl.ds(pl.multiple_of(index * BS, BS), BS)

    def product(code):
        slot = (code >> 8) & 15
        x = left[(code >> 12) & 15, block_at((code >> 16) & 255), pl.ds(pl.multiple_of((slot >> 1) * 2 * BS, 2 * BS), 2 * BS)]
        both = jnp.where(half == (slot & 1), x, pltpu.roll(x, BS, 1))
        hi = both.astype(jnp.bfloat16).astype(jnp.float32)
        lhs = jnp.where(low, hi, both - hi).astype(jnp.bfloat16)
        lhs = jnp.concatenate([lhs, lhs], axis=1)
        y = right[code >> 24, block_at(code & 255), :]
        hi = y.astype(jnp.bfloat16)
        lo = (y - hi.astype(jnp.float32)).astype(jnp.bfloat16)
        rhs = jnp.concatenate([hi, hi, lo, lo], axis=0)
        return jnp.dot(lhs, rhs, preferred_element_type=jnp.float32)

    def add(code, product):
        rows_at = block_at((code >> 16) & 255)
        for pair in range(w // 2):
            x = product[:, pair * 2 * BS : (pair + 1) * 2 * BS]
            turned = pltpu.roll(x, BS, 1)
            picked, at = [], []
            for side in range(2):
                place = scalars[(slots + (code >> 24)) * w + 2 * pair + side, code & 255]
                parity = place >> 16
                chosen = jnp.where(parity == side, x, turned)
                picked.append(jnp.where(half == parity, chosen, 0.0))
                at.append(place & 0xFFFF)
            picked[1] = jnp.where(at[0] == at[1], picked[0] + picked[1], picked[1])
            spots = [(rows_at, pl.ds(pl.multiple_of(base, 2 * BS), 2 * BS)) for base in at]
            sums = [acc[spot] + part for spot, part in zip(spots, picked)]
            for spot, total in zip(spots, sums):
                acc[spot] = total

    def out_copy(part):
        at = pl.ds(part * part_rows * BS, part_rows * BS)
        return pltpu.make_async_copy(acc.at[at], out_ref.at[at], osem.at[part])

    groups = [jnp.int32(0)] + [(bound + UNROLL - 1) // UNROLL for bound in bounds[1:]]
    for part in range(PARTS):
        @pl.loop(groups[part], groups[part + 1])
        def _(group):
            for u in range(UNROLL):
                add(codes[group * UNROLL + u], value[u])
            for u in range(UNROLL):
                value[u] = product(codes[(group + 1) * UNROLL + u])

        out_copy(part).start()
    for part in range(PARTS):
        out_copy(part).wait()


def local(p_cols, p_data):
    n_row, n_col = lax.axis_size("row"), lax.axis_size("col")
    ratio = n_row // n_col
    row_id, col_id = lax.axis_index("row"), lax.axis_index("col")
    rb, w = p_cols.shape
    rows, width = p_data.shape
    left_perms = left_plan(n_row, n_col, ratio)
    right_perms = right_plan(n_row, n_col, ratio)
    table, slots = device_table(left_perms, right_perms, n_row, n_col, ratio)
    info = jnp.asarray(table)[row_id, col_id]

    smem = pl.BlockSpec(memory_space=pltpu.SMEM)
    hbm = pl.BlockSpec(memory_space=pl.ANY)
    dma = pltpu.SemaphoreType.DMA
    own = pl.pallas_call(
        join_kernel,
        out_shape=jax.ShapeDtypeStruct((rows + EXTRA, width), jnp.float32),
        in_specs=[hbm, hbm],
        out_specs=hbm,
        scratch_shapes=[pltpu.VMEM((w, rb), jnp.int32), pltpu.VMEM((EXTRA, width), jnp.float32), dma((3,))],
        compiler_params=pltpu.CompilerParams(vmem_limit_bytes=60 << 20),
        cost_estimate=pl.CostEstimate(flops=0, bytes_accessed=2 << 20, transcendentals=0),
    )(p_cols.T, p_data)

    def carry(perms):
        bufs = [own]
        for source, pairs in perms:
            flat = [(s[0] * n_col + s[1], d[0] * n_col + d[1]) for s, d in pairs]
            bufs.append(lax.ppermute(bufs[source], ("row", "col"), flat))
        return bufs

    left_bufs, right_bufs = carry(left_perms), carry(right_perms)
    out_shape = jax.ShapeDtypeStruct((rows, rb * ratio * BS), jnp.float32)
    bufs = right_bufs + left_bufs[1:]
    codings = -(-(slots + STEPS + 1) * w // 8) * 8
    return pl.pallas_call(
        functools.partial(product_kernel, slots, n_row, ratio, rb, w, len(right_bufs)),
        out_shape=out_shape,
        in_specs=[smem] + [hbm] * len(bufs),
        out_specs=hbm,
        scratch_shapes=[
            pltpu.VMEM((slots, rows + EXTRA, width), jnp.float32),
            pltpu.VMEM((STEPS + 1, rows + EXTRA, width), jnp.float32),
            pltpu.VMEM(out_shape.shape, jnp.float32),
            pltpu.VMEM((UNROLL, BS, width), jnp.float32),
            pltpu.VMEM((slots + STEPS, EXTRA, width), jnp.float32),
            pltpu.VMEM((codings, 128), jnp.int32),
            pltpu.SMEM((codings, 128), jnp.int32),
            pltpu.SMEM((slots * rb * w + 4 * UNROLL,), jnp.int32),
            dma((slots,)),
            dma((STEPS,)),
            dma((PARTS,)),
            dma((slots + STEPS + 1,)),
        ],
        compiler_params=pltpu.CompilerParams(vmem_limit_bytes=24 << 20),
        cost_estimate=pl.CostEstimate(flops=10**9, bytes_accessed=20 << 20, transcendentals=0),
    )(info, *bufs)


def solution(mesh):
    in_specs = (P("row", "col"), P("row", "col"))
    return jax.shard_map(local, mesh=mesh, in_specs=in_specs, out_specs=P("row", "col"), check_vma=False)
```

```python
import functools

import jax
import jax.numpy as jnp
import numpy as np
from jax import lax
from jax.experimental import pallas as pl
from jax.experimental.pallas import tpu as pltpu
from jax.sharding import PartitionSpec as P

BS = 64
STEPS = 4
UNROLL = 4
EXTRA = 8
PARTS = 8


def left_offsets(row, ratio, n_col):
    seen = []
    for step in range(STEPS):
        offset = (row + step) // ratio % n_col
        if offset not in seen:
            seen.append(offset)
    return seen


def shift(rows, step, count):
    return [((r, c), (r, (c + step) % count)) for r in rows for c in range(count)]


def left_plan(n_row, n_col, ratio):
    offsets = [left_offsets(row, ratio, n_col) for row in range(n_row)]
    if (n_row, n_col, ratio) != (8, 4, 2):
        perms = []
        for slot in range(max(len(o) for o in offsets)):
            pairs = [
                ((row, (col + offsets[row][slot]) % n_col), (row, col))
                for row in range(n_row)
                for col in range(n_col)
                if slot < len(offsets[row]) and offsets[row][slot] != 0
            ]
            perms.append((0, pairs))
        return perms
    whole = [r for r in range(8) if {1, 2, 3} <= set(offsets[r])]
    once, twice = {-1: [], 1: []}, {-1: [], 1: []}
    for r in range(8):
        for offset, step in ((1, -1), (3, 1)):
            if offset in offsets[r] and r not in whole:
                once[step].append(r)
                if 2 in offsets[r]:
                    twice[step].append(r)
    down = shift([r for r in once[-1] if r != 0], -1, 4) + [((3, c), (3, c - 1)) for c in (1, 2, 3)] + [((3, 0), (0, 0))]
    up = shift(once[1], 1, 4) + shift([0], -1, 4) + [((3, c), (3, c + 1)) for c in (0, 1, 2)] + [((3, 3), (1, 3))]
    again_down = shift(twice[-1], -1, 4) + [((3, 1), (3, 0)), ((3, 2), (3, 1)), ((0, 0), (3, 3))]
    again_up = shift(twice[1], 1, 4) + [((3, 1), (3, 2)), ((3, 2), (3, 3)), ((1, 3), (3, 0))]
    return [(0, down), (0, up), (1, again_down), (2, again_up)]


def right_plan(n_row, n_col, ratio):
    everyone = [(row, col) for row in range(n_row) for col in range(n_col)]
    if (n_row, n_col, ratio) != (8, 4, 2):
        return [
            (0, [(((r + ratio * c + step) % n_row, c), (r, c)) for r, c in everyone if (ratio * c + step) % n_row])
            for step in range(STEPS)
        ]
    first = [(((r + 2 * c) % 8, c), (r, c)) for r, c in everyone if c != 0]
    first += [((r + 1, 0), (r, 0)) for r in range(0, 8, 2)]
    second = [(((r + 2 * c + 2) % 8, c), (r, c)) for r, c in everyone if c != 3]
    second += [((r ^ 1, 3), (r, 3)) for r in range(8)]
    last = [(((r - 1 + 2 * c + 4) % 8, c), (r, c)) for r, c in everyone if r % 2 == 1]
    first_swap = [((r + 1, c), (r, c)) for r, c in everyone if r % 2 == 0 and c != 0]
    second_swap = [((r ^ 1, c), (r, c)) for r, c in everyone if c != 3]
    return [(0, first), (0, second), (0, last), (1, first_swap), (2, second_swap)]


def carry_out(perms, n_row, n_col):
    held = [{(r, c): (r, c) for r in range(n_row) for c in range(n_col)}]
    for source, pairs in perms:
        held.append({dst: held[source][src] for src, dst in pairs})
    return held


def device_table(left_perms, right_perms, n_row, n_col, ratio):
    left_held = carry_out(left_perms, n_row, n_col)
    right_held = carry_out(right_perms, n_row, n_col)
    slots = (ratio - 1 + STEPS - 1) // ratio + 1
    table = np.full((n_row, n_col, 2 * slots + STEPS), -1, np.int32)

    def find(held, device, tile):
        return [i for i, h in enumerate(held) if h.get(device) == tile][0]

    for r in range(n_row):
        for c in range(n_col):
            for slot, offset in enumerate(left_offsets(r, ratio, n_col)):
                tile_col = (c + offset) % n_col
                table[r, c, slot] = find(left_held, (r, c), (r, tile_col))
                table[r, c, slots + STEPS + slot] = (tile_col * ratio - r - ratio * c) % n_row
            for step in range(STEPS):
                table[r, c, slots + step] = find(right_held, (r, c), ((r + ratio * c + step) % n_row, c))
    return table, slots


def fetch(choice, bufs, target, sem):
    for number, buf in enumerate(bufs):
        @pl.when(choice == number)
        def _():
            pltpu.make_async_copy(buf, target, sem).start()


def join_kernel(cols_ref, data_ref, out_ref, sem):
    rows = data_ref.shape[0]
    data_copy = pltpu.make_async_copy(data_ref, out_ref.at[pl.ds(0, rows)], sem.at[0])
    cols_copy = pltpu.make_async_copy(cols_ref, out_ref.at[pl.ds(rows, EXTRA)], sem.at[1])
    data_copy.start()
    cols_copy.start()
    data_copy.wait()
    cols_copy.wait()


def product_kernel(slots, n_row, ratio, rb, w, n_right, info_ref, *refs):
    out_ref, left, right, acc, value, cols, coded, scalars, codes, lsem, rsem, osem, csem = refs[-13:]
    right_bufs, left_bufs = refs[:n_right], refs[:1] + refs[n_right:-13]
    rows, width = left.shape[1] - EXTRA, left.shape[2]
    names = pl.ds(rows, EXTRA)
    for slot in range(slots):
        fetch(info_ref[slot], [buf.at[names] for buf in left_bufs], cols.at[slot], csem.at[slot])
    for step in range(STEPS):
        choice = info_ref[slots + step]
        fetch(choice, [buf.at[names] for buf in right_bufs], cols.at[slots + step], csem.at[slots + step])
    for step in range(STEPS):
        fetch(info_ref[slots + step], right_bufs, right.at[step], rsem.at[step])
    for slot in range(slots):
        fetch(info_ref[slot], left_bufs, left.at[slot], lsem.at[slot])

    def clear(first, last):
        @pl.loop(first, last)
        def _(r):
            acc[pl.ds(pl.multiple_of(r * BS, BS), BS), :] = jnp.zeros((BS, acc.shape[1]), jnp.float32)

    clear(0, rb // 4)
    lanes = scalars.shape[1]
    row = lax.broadcasted_iota(jnp.int32, (w, lanes), 1)
    tile_slot = lax.broadcasted_iota(jnp.int32, (w, lanes), 0)
    for slot in range(slots):
        used = info_ref[slot] >= 0

        @pl.when(used)
        def _():
            pltpu.make_async_copy(left_bufs[0].at[names], cols.at[slot], csem.at[slot]).wait()

        inner = cols[slot, 0:w, 0:lanes].astype(jnp.int32)
        valid = (inner >= 0) & (row < rb)
        step = jnp.full(inner.shape, info_ref[slots + STEPS + slot], jnp.int32)
        for _ in range(ratio - 1):
            beyond = inner >= rb
            step = jnp.where(beyond, step + 1, step)
            inner = jnp.where(beyond, inner - rb, inner)
        step = jnp.where(step >= n_row, step - n_row, step)
        code = inner | tile_slot << 8 | slot << 12 | row << 16 | step << 24
        valid = valid & (step < STEPS)
        coded[slot * w : (slot + 1) * w, :] = jnp.where(valid, jnp.where(used, code, -1), -1)
    for step in range(STEPS):
        pltpu.make_async_copy(right_bufs[0].at[names], cols.at[slots + step], csem.at[slots + step]).wait()
        col = cols[slots + step, 0:w, 0:lanes].astype(jnp.int32)
        code = (col >> 1) * 2 * BS | (col & 1) << 16
        coded[(slots + step) * w : (slots + step + 1) * w, :] = jnp.where(col < 0, 2 << 16, code)
    coded[(slots + STEPS) * w : (slots + STEPS + 1) * w, :] = jnp.full((w, lanes), 2 << 16, jnp.int32)
    to_scalars = pltpu.make_async_copy(coded, scalars, csem.at[slots + STEPS])
    to_scalars.start()
    clear(rb // 4, rb)
    to_scalars.wait()

    part_rows = rb // PARTS
    for u in range(UNROLL):
        codes[u] = STEPS << 24
    bounds = [jnp.int32(UNROLL)]
    for part in range(PARTS):
        def listed(i, place):
            for slot in range(slots):
                for k in range(w):
                    code = scalars[slot * w + k, part * part_rows + i]
                    codes[place] = code
                    place = place + (code >= 0).astype(jnp.int32)
            return place

        bounds.append(lax.fori_loop(0, part_rows, listed, bounds[-1]))
    for u in range(2 * UNROLL):
        codes[bounds[-1] + u] = STEPS << 24

    for step in range(STEPS):
        pltpu.make_async_copy(right_bufs[0], right.at[step], rsem.at[step]).wait()
    for slot in range(slots):
        @pl.when(info_ref[slot] >= 0)
        def _():
            pltpu.make_async_copy(left_bufs[0], left.at[slot], lsem.at[slot]).wait()

    low = lax.broadcasted_iota(jnp.int32, (BS, 2 * BS), 1) < BS
    half = lax.broadcasted_iota(jnp.int32, (BS, 2 * BS), 1) // BS

    def block_at(index):
        return pl.ds(pl.multiple_of(index * BS, BS), BS)

    def product(code):
        slot = (code >> 8) & 15
        x = left[(code >> 12) & 15, block_at((code >> 16) & 255), pl.ds(pl.multiple_of((slot >> 1) * 2 * BS, 2 * BS), 2 * BS)]
        both = jnp.where(half == (slot & 1), x, pltpu.roll(x, BS, 1))
        hi = both.astype(jnp.bfloat16).astype(jnp.float32)
        lhs = jnp.where(low, hi, both - hi).astype(jnp.bfloat16)
        lhs = jnp.concatenate([lhs, lhs], axis=1)
        y = right[code >> 24, block_at(code & 255), :]
        hi = y.astype(jnp.bfloat16)
        lo = (y - hi.astype(jnp.float32)).astype(jnp.bfloat16)
        rhs = jnp.concatenate([hi, hi, lo, lo], axis=0)
        return jnp.dot(lhs, rhs, preferred_element_type=jnp.float32)

    def add(code, product):
        rows_at = block_at((code >> 16) & 255)
        for pair in range(w // 2):
            x = product[:, pair * 2 * BS : (pair + 1) * 2 * BS]
            turned = pltpu.roll(x, BS, 1)
            picked, at = [], []
            for side in range(2):
                place = scalars[(slots + (code >> 24)) * w + 2 * pair + side, code & 255]
                parity = place >> 16
                chosen = jnp.where(parity == side, x, turned)
                picked.append(jnp.where(half == parity, chosen, 0.0))
                at.append(place & 0xFFFF)
            picked[1] = jnp.where(at[0] == at[1], picked[0] + picked[1], picked[1])
            spots = [(rows_at, pl.ds(pl.multiple_of(base, 2 * BS), 2 * BS)) for base in at]
            sums = [acc[spot] + part for spot, part in zip(spots, picked)]
            for spot, total in zip(spots, sums):
                acc[spot] = total

    def out_copy(part):
        at = pl.ds(part * part_rows * BS, part_rows * BS)
        return pltpu.make_async_copy(acc.at[at], out_ref.at[at], osem.at[part])

    groups = [jnp.int32(0)] + [(bound + UNROLL - 1) // UNROLL for bound in bounds[1:]]
    for part in range(PARTS):
        @pl.loop(groups[part], groups[part + 1])
        def _(group):
            for u in range(UNROLL):
                add(codes[group * UNROLL + u], value[u])
            for u in range(UNROLL):
                value[u] = product(codes[(group + 1) * UNROLL + u])

        out_copy(part).start()
    for part in range(PARTS):
        out_copy(part).wait()


def local(p_cols, p_data):
    n_row, n_col = lax.axis_size("row"), lax.axis_size("col")
    ratio = n_row // n_col
    row_id, col_id = lax.axis_index("row"), lax.axis_index("col")
    rb, w = p_cols.shape
    rows, width = p_data.shape
    left_perms = left_plan(n_row, n_col, ratio)
    right_perms = right_plan(n_row, n_col, ratio)
    table, slots = device_table(left_perms, right_perms, n_row, n_col, ratio)
    info = jnp.asarray(table)[row_id, col_id]

    smem = pl.BlockSpec(memory_space=pltpu.SMEM)
    hbm = pl.BlockSpec(memory_space=pl.ANY)
    dma = pltpu.SemaphoreType.DMA
    own = pl.pallas_call(
        join_kernel,
        out_shape=jax.ShapeDtypeStruct((rows + EXTRA, width), jnp.float32),
        in_specs=[hbm, hbm],
        out_specs=hbm,
        scratch_shapes=[dma((2,))],
        compiler_params=pltpu.CompilerParams(vmem_limit_bytes=2 << 20),
        cost_estimate=pl.CostEstimate(flops=0, bytes_accessed=2 << 20, transcendentals=0),
    )(jnp.pad(p_cols.T.astype(jnp.float32), ((0, EXTRA - w), (0, width - rb))), p_data)

    def carry(perms):
        bufs = [own]
        for source, pairs in perms:
            flat = [(s[0] * n_col + s[1], d[0] * n_col + d[1]) for s, d in pairs]
            bufs.append(lax.ppermute(bufs[source], ("row", "col"), flat))
        return bufs

    left_bufs, right_bufs = carry(left_perms), carry(right_perms)
    out_shape = jax.ShapeDtypeStruct((rows, rb * ratio * BS), jnp.float32)
    bufs = right_bufs + left_bufs[1:]
    codings = -(-(slots + STEPS + 1) * w // 8) * 8
    return pl.pallas_call(
        functools.partial(product_kernel, slots, n_row, ratio, rb, w, len(right_bufs)),
        out_shape=out_shape,
        in_specs=[smem] + [hbm] * len(bufs),
        out_specs=hbm,
        scratch_shapes=[
            pltpu.VMEM((slots, rows + EXTRA, width), jnp.float32),
            pltpu.VMEM((STEPS + 1, rows + EXTRA, width), jnp.float32),
            pltpu.VMEM(out_shape.shape, jnp.float32),
            pltpu.VMEM((UNROLL, BS, width), jnp.float32),
            pltpu.VMEM((slots + STEPS, EXTRA, width), jnp.float32),
            pltpu.VMEM((codings, 128), jnp.int32),
            pltpu.SMEM((codings, 128), jnp.int32),
            pltpu.SMEM((slots * rb * w + 4 * UNROLL,), jnp.int32),
            dma((slots,)),
            dma((STEPS,)),
            dma((PARTS,)),
            dma((slots + STEPS + 1,)),
        ],
        compiler_params=pltpu.CompilerParams(vmem_limit_bytes=18 << 20),
        cost_estimate=pl.CostEstimate(flops=10**9, bytes_accessed=20 << 20, transcendentals=0),
    )(info, *bufs)


def solution(mesh):
    in_specs = (P("row", "col"), P("row", "col"))
    return jax.shard_map(local, mesh=mesh, in_specs=in_specs, out_specs=P("row", "col"), check_vma=False)
```

```python
import functools

import jax
import jax.numpy as jnp
import numpy as np
from jax import lax
from jax.experimental import pallas as pl
from jax.experimental.pallas import tpu as pltpu
from jax.sharding import PartitionSpec as P

BS = 64
STEPS = 4
UNROLL = 8
EXTRA = 8
PARTS = 8


def left_offsets(row, ratio, n_col):
    seen = []
    for step in range(STEPS):
        offset = (row + step) // ratio % n_col
        if offset not in seen:
            seen.append(offset)
    return seen


def shift(rows, step, count):
    return [((r, c), (r, (c + step) % count)) for r in rows for c in range(count)]


def left_plan(n_row, n_col, ratio):
    offsets = [left_offsets(row, ratio, n_col) for row in range(n_row)]
    if (n_row, n_col, ratio) != (8, 4, 2):
        perms = []
        for slot in range(max(len(o) for o in offsets)):
            pairs = [
                ((row, (col + offsets[row][slot]) % n_col), (row, col))
                for row in range(n_row)
                for col in range(n_col)
                if slot < len(offsets[row]) and offsets[row][slot] != 0
            ]
            perms.append((0, pairs))
        return perms
    whole = [r for r in range(8) if {1, 2, 3} <= set(offsets[r])]
    once, twice = {-1: [], 1: []}, {-1: [], 1: []}
    for r in range(8):
        for offset, step in ((1, -1), (3, 1)):
            if offset in offsets[r] and r not in whole:
                once[step].append(r)
                if 2 in offsets[r]:
                    twice[step].append(r)
    down = shift([r for r in once[-1] if r != 0], -1, 4) + [((3, c), (3, c - 1)) for c in (1, 2, 3)] + [((3, 0), (0, 0))]
    up = shift(once[1], 1, 4) + shift([0], -1, 4) + [((3, c), (3, c + 1)) for c in (0, 1, 2)] + [((3, 3), (1, 3))]
    again_down = shift(twice[-1], -1, 4) + [((3, 1), (3, 0)), ((3, 2), (3, 1)), ((0, 0), (3, 3))]
    again_up = shift(twice[1], 1, 4) + [((3, 1), (3, 2)), ((3, 2), (3, 3)), ((1, 3), (3, 0))]
    return [(0, down), (0, up), (1, again_down), (2, again_up)]


def right_plan(n_row, n_col, ratio):
    everyone = [(row, col) for row in range(n_row) for col in range(n_col)]
    if (n_row, n_col, ratio) != (8, 4, 2):
        return [
            (0, [(((r + ratio * c + step) % n_row, c), (r, c)) for r, c in everyone if (ratio * c + step) % n_row])
            for step in range(STEPS)
        ]
    first = [(((r + 2 * c) % 8, c), (r, c)) for r, c in everyone if c != 0]
    first += [((r + 1, 0), (r, 0)) for r in range(0, 8, 2)]
    second = [(((r + 2 * c + 2) % 8, c), (r, c)) for r, c in everyone if c != 3]
    second += [((r ^ 1, 3), (r, 3)) for r in range(8)]
    last = [(((r - 1 + 2 * c + 4) % 8, c), (r, c)) for r, c in everyone if r % 2 == 1]
    first_swap = [((r + 1, c), (r, c)) for r, c in everyone if r % 2 == 0 and c != 0]
    second_swap = [((r ^ 1, c), (r, c)) for r, c in everyone if c != 3]
    return [(0, first), (0, second), (0, last), (1, first_swap), (2, second_swap)]


def carry_out(perms, n_row, n_col):
    held = [{(r, c): (r, c) for r in range(n_row) for c in range(n_col)}]
    for source, pairs in perms:
        held.append({dst: held[source][src] for src, dst in pairs})
    return held


def device_table(left_perms, right_perms, n_row, n_col, ratio):
    left_held = carry_out(left_perms, n_row, n_col)
    right_held = carry_out(right_perms, n_row, n_col)
    slots = (ratio - 1 + STEPS - 1) // ratio + 1
    table = np.full((n_row, n_col, 2 * slots + STEPS), -1, np.int32)

    def find(held, device, tile):
        return [i for i, h in enumerate(held) if h.get(device) == tile][0]

    for r in range(n_row):
        for c in range(n_col):
            for slot, offset in enumerate(left_offsets(r, ratio, n_col)):
                tile_col = (c + offset) % n_col
                table[r, c, slot] = find(left_held, (r, c), (r, tile_col))
                table[r, c, slots + STEPS + slot] = (tile_col * ratio - r - ratio * c) % n_row
            for step in range(STEPS):
                table[r, c, slots + step] = find(right_held, (r, c), ((r + ratio * c + step) % n_row, c))
    return table, slots


def fetch(choice, bufs, target, sem):
    for number, buf in enumerate(bufs):
        @pl.when(choice == number)
        def _():
            pltpu.make_async_copy(buf, target, sem).start()


def join_kernel(cols_ref, data_ref, out_ref, cols, sem):
    rows = data_ref.shape[0]
    data_copy = pltpu.make_async_copy(data_ref, out_ref.at[pl.ds(0, rows)], sem.at[0])
    cols_copy = pltpu.make_async_copy(cols_ref, cols, sem.at[1])
    data_copy.start()
    cols_copy.start()
    out_ref[pl.ds(rows, EXTRA), :] = jnp.zeros((EXTRA, out_ref.shape[1]), jnp.float32)
    cols_copy.wait()
    out_ref[pl.ds(rows, cols.shape[0]), pl.ds(0, cols.shape[1])] = cols[...].astype(jnp.float32)
    data_copy.wait()


def product_kernel(slots, n_row, ratio, rb, w, n_right, info_ref, *refs):
    out_ref, left, right, acc, value, cols, coded, scalars, codes, lsem, rsem, osem, csem = refs[-13:]
    right_bufs, left_bufs = refs[:n_right], refs[:1] + refs[n_right:-13]
    rows, width = left.shape[1] - EXTRA, left.shape[2]
    names = pl.ds(rows, EXTRA)
    for slot in range(slots):
        fetch(info_ref[slot], [buf.at[names] for buf in left_bufs], cols.at[slot], csem.at[slot])
    for step in range(STEPS):
        choice = info_ref[slots + step]
        fetch(choice, [buf.at[names] for buf in right_bufs], cols.at[slots + step], csem.at[slots + step])
    for step in range(STEPS):
        fetch(info_ref[slots + step], right_bufs, right.at[step], rsem.at[step])
    for slot in range(slots):
        fetch(info_ref[slot], left_bufs, left.at[slot], lsem.at[slot])

    def clear(first, last):
        @pl.loop(first, last)
        def _(r):
            acc[pl.ds(pl.multiple_of(r * BS, BS), BS), :] = jnp.zeros((BS, acc.shape[1]), jnp.float32)

    clear(0, rb // 4)
    lanes = scalars.shape[1]
    row = lax.broadcasted_iota(jnp.int32, (w, lanes), 1)
    tile_slot = lax.broadcasted_iota(jnp.int32, (w, lanes), 0)
    for slot in range(slots):
        used = info_ref[slot] >= 0

        @pl.when(used)
        def _():
            pltpu.make_async_copy(left_bufs[0].at[names], cols.at[slot], csem.at[slot]).wait()

        inner = cols[slot, 0:w, 0:lanes].astype(jnp.int32)
        valid = (inner >= 0) & (row < rb)
        step = jnp.full(inner.shape, info_ref[slots + STEPS + slot], jnp.int32)
        for _ in range(ratio - 1):
            beyond = inner >= rb
            step = jnp.where(beyond, step + 1, step)
            inner = jnp.where(beyond, inner - rb, inner)
        step = jnp.where(step >= n_row, step - n_row, step)
        code = inner | tile_slot << 8 | slot << 12 | row << 16 | step << 24
        valid = valid & (step < STEPS)
        coded[slot * w : (slot + 1) * w, :] = jnp.where(valid, jnp.where(used, code, -1), -1)
    for step in range(STEPS):
        pltpu.make_async_copy(right_bufs[0].at[names], cols.at[slots + step], csem.at[slots + step]).wait()
        col = cols[slots + step, 0:w, 0:lanes].astype(jnp.int32)
        code = (col >> 1) * 2 * BS | (col & 1) << 16
        coded[(slots + step) * w : (slots + step + 1) * w, :] = jnp.where(col < 0, 2 << 16, code)
    coded[(slots + STEPS) * w : (slots + STEPS + 1) * w, :] = jnp.full((w, lanes), 2 << 16, jnp.int32)
    to_scalars = pltpu.make_async_copy(coded, scalars, csem.at[slots + STEPS])
    to_scalars.start()
    clear(rb // 4, rb)
    to_scalars.wait()

    part_rows = rb // PARTS
    for u in range(UNROLL):
        codes[u] = STEPS << 24
    bounds = [jnp.int32(UNROLL)]
    for part in range(PARTS):
        def listed(i, place):
            for slot in range(slots):
                for k in range(w):
                    code = scalars[slot * w + k, part * part_rows + i]
                    codes[place] = code
                    place = place + (code >= 0).astype(jnp.int32)
            return place

        bounds.append(lax.fori_loop(0, part_rows, listed, bounds[-1]))
    for u in range(2 * UNROLL):
        codes[bounds[-1] + u] = STEPS << 24

    for step in range(STEPS):
        pltpu.make_async_copy(right_bufs[0], right.at[step], rsem.at[step]).wait()
    for slot in range(slots):
        @pl.when(info_ref[slot] >= 0)
        def _():
            pltpu.make_async_copy(left_bufs[0], left.at[slot], lsem.at[slot]).wait()

    low = lax.broadcasted_iota(jnp.int32, (BS, 2 * BS), 1) < BS
    half = lax.broadcasted_iota(jnp.int32, (BS, 2 * BS), 1) // BS

    def block_at(index):
        return pl.ds(pl.multiple_of(index * BS, BS), BS)

    def product(code):
        slot = (code >> 8) & 15
        x = left[(code >> 12) & 15, block_at((code >> 16) & 255), pl.ds(pl.multiple_of((slot >> 1) * 2 * BS, 2 * BS), 2 * BS)]
        both = jnp.where(half == (slot & 1), x, pltpu.roll(x, BS, 1))
        hi = both.astype(jnp.bfloat16).astype(jnp.float32)
        lhs = jnp.where(low, hi, both - hi).astype(jnp.bfloat16)
        lhs = jnp.concatenate([lhs, lhs], axis=1)
        y = right[code >> 24, block_at(code & 255), :]
        hi = y.astype(jnp.bfloat16)
        lo = (y - hi.astype(jnp.float32)).astype(jnp.bfloat16)
        rhs = jnp.concatenate([hi, hi, lo, lo], axis=0)
        return jnp.dot(lhs, rhs, preferred_element_type=jnp.float32)

    def add(code, product):
        rows_at = block_at((code >> 16) & 255)
        for pair in range(w // 2):
            x = product[:, pair * 2 * BS : (pair + 1) * 2 * BS]
            turned = pltpu.roll(x, BS, 1)
            picked, at = [], []
            for side in range(2):
                place = scalars[(slots + (code >> 24)) * w + 2 * pair + side, code & 255]
                parity = place >> 16
                chosen = jnp.where(parity == side, x, turned)
                picked.append(jnp.where(half == parity, chosen, 0.0))
                at.append(place & 0xFFFF)
            picked[1] = jnp.where(at[0] == at[1], picked[0] + picked[1], picked[1])
            spots = [(rows_at, pl.ds(pl.multiple_of(base, 2 * BS), 2 * BS)) for base in at]
            sums = [acc[spot] + part for spot, part in zip(spots, picked)]
            for spot, total in zip(spots, sums):
                acc[spot] = total

    def out_copy(part):
        at = pl.ds(part * part_rows * BS, part_rows * BS)
        return pltpu.make_async_copy(acc.at[at], out_ref.at[at], osem.at[part])

    groups = [jnp.int32(0)] + [(bound + UNROLL - 1) // UNROLL for bound in bounds[1:]]
    for part in range(PARTS):
        @pl.loop(groups[part], groups[part + 1])
        def _(group):
            for u in range(UNROLL):
                add(codes[group * UNROLL + u], value[u])
            for u in range(UNROLL):
                value[u] = product(codes[(group + 1) * UNROLL + u])

        out_copy(part).start()
    for part in range(PARTS):
        out_copy(part).wait()


def local(p_cols, p_data):
    n_row, n_col = lax.axis_size("row"), lax.axis_size("col")
    ratio = n_row // n_col
    row_id, col_id = lax.axis_index("row"), lax.axis_index("col")
    rb, w = p_cols.shape
    rows, width = p_data.shape
    left_perms = left_plan(n_row, n_col, ratio)
    right_perms = right_plan(n_row, n_col, ratio)
    table, slots = device_table(left_perms, right_perms, n_row, n_col, ratio)
    info = jnp.asarray(table)[row_id, col_id]

    smem = pl.BlockSpec(memory_space=pltpu.SMEM)
    hbm = pl.BlockSpec(memory_space=pl.ANY)
    dma = pltpu.SemaphoreType.DMA
    own = pl.pallas_call(
        join_kernel,
        out_shape=jax.ShapeDtypeStruct((rows + EXTRA, width), jnp.float32),
        in_specs=[pl.BlockSpec(memory_space=pltpu.HBM)] * 2,
        out_specs=pl.BlockSpec(memory_space=pltpu.VMEM),
        scratch_shapes=[pltpu.VMEM((w, rb), jnp.int32), dma((2,))],
        compiler_params=pltpu.CompilerParams(vmem_limit_bytes=4 << 20),
        cost_estimate=pl.CostEstimate(flops=0, bytes_accessed=2 << 20, transcendentals=0),
    )(p_cols.T, p_data)

    def carry(perms):
        bufs = [own]
        for source, pairs in perms:
            flat = [(s[0] * n_col + s[1], d[0] * n_col + d[1]) for s, d in pairs]
            bufs.append(lax.ppermute(bufs[source], ("row", "col"), flat))
        return bufs

    left_bufs, right_bufs = carry(left_perms), carry(right_perms)
    out_shape = jax.ShapeDtypeStruct((rows, rb * ratio * BS), jnp.float32)
    bufs = right_bufs + left_bufs[1:]
    codings = -(-(slots + STEPS + 1) * w // 8) * 8
    return pl.pallas_call(
        functools.partial(product_kernel, slots, n_row, ratio, rb, w, len(right_bufs)),
        out_shape=out_shape,
        in_specs=[smem] + [hbm] * len(bufs),
        out_specs=hbm,
        scratch_shapes=[
            pltpu.VMEM((slots, rows + EXTRA, width), jnp.float32),
            pltpu.VMEM((STEPS + 1, rows + EXTRA, width), jnp.float32),
            pltpu.VMEM(out_shape.shape, jnp.float32),
            pltpu.VMEM((UNROLL, BS, width), jnp.float32),
            pltpu.VMEM((slots + STEPS, EXTRA, width), jnp.float32),
            pltpu.VMEM((codings, 128), jnp.int32),
            pltpu.SMEM((codings, 128), jnp.int32),
            pltpu.SMEM((slots * rb * w + 4 * UNROLL,), jnp.int32),
            dma((slots,)),
            dma((STEPS,)),
            dma((PARTS,)),
            dma((slots + STEPS + 1,)),
        ],
        compiler_params=pltpu.CompilerParams(vmem_limit_bytes=18 << 20),
        cost_estimate=pl.CostEstimate(flops=10**9, bytes_accessed=20 << 20, transcendentals=0),
    )(info, *bufs)


def solution(mesh):
    in_specs = (P("row", "col"), P("row", "col"))
    return jax.shard_map(local, mesh=mesh, in_specs=in_specs, out_specs=P("row", "col"), check_vma=False)
```

```python
import functools

import jax
import jax.numpy as jnp
import numpy as np
from jax import lax
from jax.experimental import pallas as pl
from jax.experimental.pallas import tpu as pltpu
from jax.sharding import PartitionSpec as P

BS = 64
STEPS = 4
UNROLL = 16
EXTRA = 8
PARTS = 8


def left_offsets(row, ratio, n_col):
    seen = []
    for step in range(STEPS):
        offset = (row + step) // ratio % n_col
        if offset not in seen:
            seen.append(offset)
    return seen


def shift(rows, step, count):
    return [((r, c), (r, (c + step) % count)) for r in rows for c in range(count)]


def left_plan(n_row, n_col, ratio):
    offsets = [left_offsets(row, ratio, n_col) for row in range(n_row)]
    if (n_row, n_col, ratio) != (8, 4, 2):
        perms = []
        for slot in range(max(len(o) for o in offsets)):
            pairs = [
                ((row, (col + offsets[row][slot]) % n_col), (row, col))
                for row in range(n_row)
                for col in range(n_col)
                if slot < len(offsets[row]) and offsets[row][slot] != 0
            ]
            perms.append((0, pairs))
        return perms
    whole = [r for r in range(8) if {1, 2, 3} <= set(offsets[r])]
    once, twice = {-1: [], 1: []}, {-1: [], 1: []}
    for r in range(8):
        for offset, step in ((1, -1), (3, 1)):
            if offset in offsets[r] and r not in whole:
                once[step].append(r)
                if 2 in offsets[r]:
                    twice[step].append(r)
    down = shift([r for r in once[-1] if r != 0], -1, 4) + [((3, c), (3, c - 1)) for c in (1, 2, 3)] + [((3, 0), (0, 0))]
    up = shift(once[1], 1, 4) + shift([0], -1, 4) + [((3, c), (3, c + 1)) for c in (0, 1, 2)] + [((3, 3), (1, 3))]
    again_down = shift(twice[-1], -1, 4) + [((3, 1), (3, 0)), ((3, 2), (3, 1)), ((0, 0), (3, 3))]
    again_up = shift(twice[1], 1, 4) + [((3, 1), (3, 2)), ((3, 2), (3, 3)), ((1, 3), (3, 0))]
    return [(0, down), (0, up), (1, again_down), (2, again_up)]


def right_plan(n_row, n_col, ratio):
    everyone = [(row, col) for row in range(n_row) for col in range(n_col)]
    if (n_row, n_col, ratio) != (8, 4, 2):
        return [
            (0, [(((r + ratio * c + step) % n_row, c), (r, c)) for r, c in everyone if (ratio * c + step) % n_row])
            for step in range(STEPS)
        ]
    first = [(((r + 2 * c) % 8, c), (r, c)) for r, c in everyone if c != 0]
    first += [((r + 1, 0), (r, 0)) for r in range(0, 8, 2)]
    second = [(((r + 2 * c + 2) % 8, c), (r, c)) for r, c in everyone if c != 3]
    second += [((r ^ 1, 3), (r, 3)) for r in range(8)]
    last = [(((r - 1 + 2 * c + 4) % 8, c), (r, c)) for r, c in everyone if r % 2 == 1]
    first_swap = [((r + 1, c), (r, c)) for r, c in everyone if r % 2 == 0 and c != 0]
    second_swap = [((r ^ 1, c), (r, c)) for r, c in everyone if c != 3]
    return [(0, first), (0, second), (0, last), (1, first_swap), (2, second_swap)]


def carry_out(perms, n_row, n_col):
    held = [{(r, c): (r, c) for r in range(n_row) for c in range(n_col)}]
    for source, pairs in perms:
        held.append({dst: held[source][src] for src, dst in pairs})
    return held


def device_table(left_perms, right_perms, n_row, n_col, ratio):
    left_held = carry_out(left_perms, n_row, n_col)
    right_held = carry_out(right_perms, n_row, n_col)
    slots = (ratio - 1 + STEPS - 1) // ratio + 1
    table = np.full((n_row, n_col, 2 * slots + STEPS), -1, np.int32)

    def find(held, device, tile):
        return [i for i, h in enumerate(held) if h.get(device) == tile][0]

    for r in range(n_row):
        for c in range(n_col):
            for slot, offset in enumerate(left_offsets(r, ratio, n_col)):
                tile_col = (c + offset) % n_col
                table[r, c, slot] = find(left_held, (r, c), (r, tile_col))
                table[r, c, slots + STEPS + slot] = (tile_col * ratio - r - ratio * c) % n_row
            for step in range(STEPS):
                table[r, c, slots + step] = find(right_held, (r, c), ((r + ratio * c + step) % n_row, c))
    return table, slots


def fetch(choice, bufs, target, sem):
    for number, buf in enumerate(bufs):
        @pl.when(choice == number)
        def _():
            pltpu.make_async_copy(buf, target, sem).start()


def join_kernel(cols_ref, data_ref, out_ref, cols, sem):
    rows = data_ref.shape[0]
    data_copy = pltpu.make_async_copy(data_ref, out_ref.at[pl.ds(0, rows)], sem.at[0])
    cols_copy = pltpu.make_async_copy(cols_ref, cols, sem.at[1])
    data_copy.start()
    cols_copy.start()
    out_ref[pl.ds(rows, EXTRA), :] = jnp.zeros((EXTRA, out_ref.shape[1]), jnp.float32)
    cols_copy.wait()
    out_ref[pl.ds(rows, cols.shape[0]), pl.ds(0, cols.shape[1])] = cols[...].astype(jnp.float32)
    data_copy.wait()


def product_kernel(slots, n_row, ratio, rb, w, n_right, info_ref, *refs):
    out_ref, left, right, acc, value, cols, coded, scalars, codes, lsem, rsem, osem, csem = refs[-13:]
    right_bufs, left_bufs = refs[:n_right], refs[:1] + refs[n_right:-13]
    rows, width = left.shape[1] - EXTRA, left.shape[2]
    names = pl.ds(rows, EXTRA)
    for slot in range(slots):
        fetch(info_ref[slot], [buf.at[names] for buf in left_bufs], cols.at[slot], csem.at[slot])
    for step in range(STEPS):
        choice = info_ref[slots + step]
        fetch(choice, [buf.at[names] for buf in right_bufs], cols.at[slots + step], csem.at[slots + step])
    for step in range(STEPS):
        fetch(info_ref[slots + step], right_bufs, right.at[step], rsem.at[step])
    for slot in range(slots):
        fetch(info_ref[slot], left_bufs, left.at[slot], lsem.at[slot])

    def clear(first, last):
        @pl.loop(first, last)
        def _(r):
            acc[pl.ds(pl.multiple_of(r * BS, BS), BS), :] = jnp.zeros((BS, acc.shape[1]), jnp.float32)

    clear(0, rb // 4)
    lanes = scalars.shape[1]
    row = lax.broadcasted_iota(jnp.int32, (w, lanes), 1)
    tile_slot = lax.broadcasted_iota(jnp.int32, (w, lanes), 0)
    for slot in range(slots):
        used = info_ref[slot] >= 0

        @pl.when(used)
        def _():
            pltpu.make_async_copy(left_bufs[0].at[names], cols.at[slot], csem.at[slot]).wait()

        inner = cols[slot, 0:w, 0:lanes].astype(jnp.int32)
        valid = (inner >= 0) & (row < rb)
        step = jnp.full(inner.shape, info_ref[slots + STEPS + slot], jnp.int32)
        for _ in range(ratio - 1):
            beyond = inner >= rb
            step = jnp.where(beyond, step + 1, step)
            inner = jnp.where(beyond, inner - rb, inner)
        step = jnp.where(step >= n_row, step - n_row, step)
        code = inner | tile_slot << 8 | slot << 12 | row << 16 | step << 24
        valid = valid & (step < STEPS)
        coded[slot * w : (slot + 1) * w, :] = jnp.where(valid, jnp.where(used, code, -1), -1)
    for step in range(STEPS):
        pltpu.make_async_copy(right_bufs[0].at[names], cols.at[slots + step], csem.at[slots + step]).wait()
        col = cols[slots + step, 0:w, 0:lanes].astype(jnp.int32)
        code = (col >> 1) * 2 * BS | (col & 1) << 16
        coded[(slots + step) * w : (slots + step + 1) * w, :] = jnp.where(col < 0, 2 << 16, code)
    coded[(slots + STEPS) * w : (slots + STEPS + 1) * w, :] = jnp.full((w, lanes), 2 << 16, jnp.int32)
    to_scalars = pltpu.make_async_copy(coded, scalars, csem.at[slots + STEPS])
    to_scalars.start()
    clear(rb // 4, rb)
    to_scalars.wait()

    part_rows = rb // PARTS
    for u in range(UNROLL):
        codes[u] = STEPS << 24
    bounds = [jnp.int32(UNROLL)]
    for part in range(PARTS):
        def listed(i, place):
            for slot in range(slots):
                for k in range(w):
                    code = scalars[slot * w + k, part * part_rows + i]
                    codes[place] = code
                    place = place + (code >= 0).astype(jnp.int32)
            return place

        bounds.append(lax.fori_loop(0, part_rows, listed, bounds[-1]))
    for u in range(2 * UNROLL):
        codes[bounds[-1] + u] = STEPS << 24

    for step in range(STEPS):
        pltpu.make_async_copy(right_bufs[0], right.at[step], rsem.at[step]).wait()
    for slot in range(slots):
        @pl.when(info_ref[slot] >= 0)
        def _():
            pltpu.make_async_copy(left_bufs[0], left.at[slot], lsem.at[slot]).wait()

    low = lax.broadcasted_iota(jnp.int32, (BS, 2 * BS), 1) < BS
    half = lax.broadcasted_iota(jnp.int32, (BS, 2 * BS), 1) // BS

    def block_at(index):
        return pl.ds(pl.multiple_of(index * BS, BS), BS)

    def product(code):
        slot = (code >> 8) & 15
        x = left[(code >> 12) & 15, block_at((code >> 16) & 255), pl.ds(pl.multiple_of((slot >> 1) * 2 * BS, 2 * BS), 2 * BS)]
        both = jnp.where(half == (slot & 1), x, pltpu.roll(x, BS, 1))
        hi = both.astype(jnp.bfloat16).astype(jnp.float32)
        lhs = jnp.where(low, hi, both - hi).astype(jnp.bfloat16)
        lhs = jnp.concatenate([lhs, lhs], axis=1)
        y = right[code >> 24, block_at(code & 255), :]
        hi = y.astype(jnp.bfloat16)
        lo = (y - hi.astype(jnp.float32)).astype(jnp.bfloat16)
        rhs = jnp.concatenate([hi, hi, lo, lo], axis=0)
        return jnp.dot(lhs, rhs, preferred_element_type=jnp.float32)

    def add(code, product):
        rows_at = block_at((code >> 16) & 255)
        for pair in range(w // 2):
            x = product[:, pair * 2 * BS : (pair + 1) * 2 * BS]
            turned = pltpu.roll(x, BS, 1)
            picked, at = [], []
            for side in range(2):
                place = scalars[(slots + (code >> 24)) * w + 2 * pair + side, code & 255]
                parity = place >> 16
                chosen = jnp.where(parity == side, x, turned)
                picked.append(jnp.where(half == parity, chosen, 0.0))
                at.append(place & 0xFFFF)
            picked[1] = jnp.where(at[0] == at[1], picked[0] + picked[1], picked[1])
            spots = [(rows_at, pl.ds(pl.multiple_of(base, 2 * BS), 2 * BS)) for base in at]
            sums = [acc[spot] + part for spot, part in zip(spots, picked)]
            for spot, total in zip(spots, sums):
                acc[spot] = total

    def out_copy(part):
        at = pl.ds(part * part_rows * BS, part_rows * BS)
        return pltpu.make_async_copy(acc.at[at], out_ref.at[at], osem.at[part])

    groups = [jnp.int32(0)] + [(bound + UNROLL - 1) // UNROLL for bound in bounds[1:]]
    for part in range(PARTS):
        @pl.loop(groups[part], groups[part + 1])
        def _(group):
            for u in range(UNROLL):
                add(codes[group * UNROLL + u], value[u])
            for u in range(UNROLL):
                value[u] = product(codes[(group + 1) * UNROLL + u])

        out_copy(part).start()
    for part in range(PARTS):
        out_copy(part).wait()


def local(p_cols, p_data):
    n_row, n_col = lax.axis_size("row"), lax.axis_size("col")
    ratio = n_row // n_col
    row_id, col_id = lax.axis_index("row"), lax.axis_index("col")
    rb, w = p_cols.shape
    rows, width = p_data.shape
    left_perms = left_plan(n_row, n_col, ratio)
    right_perms = right_plan(n_row, n_col, ratio)
    table, slots = device_table(left_perms, right_perms, n_row, n_col, ratio)
    info = jnp.asarray(table)[row_id, col_id]

    smem = pl.BlockSpec(memory_space=pltpu.SMEM)
    hbm = pl.BlockSpec(memory_space=pl.ANY)
    dma = pltpu.SemaphoreType.DMA
    own = pl.pallas_call(
        join_kernel,
        out_shape=jax.ShapeDtypeStruct((rows + EXTRA, width), jnp.float32),
        in_specs=[pl.BlockSpec(memory_space=pltpu.HBM)] * 2,
        out_specs=pl.BlockSpec(memory_space=pltpu.VMEM),
        scratch_shapes=[pltpu.VMEM((w, rb), jnp.int32), dma((2,))],
        compiler_params=pltpu.CompilerParams(vmem_limit_bytes=4 << 20),
        cost_estimate=pl.CostEstimate(flops=0, bytes_accessed=2 << 20, transcendentals=0),
    )(p_cols.T, p_data)

    def carry(perms):
        bufs = [own]
        for source, pairs in perms:
            flat = [(s[0] * n_col + s[1], d[0] * n_col + d[1]) for s, d in pairs]
            bufs.append(lax.ppermute(bufs[source], ("row", "col"), flat))
        return bufs

    left_bufs, right_bufs = carry(left_perms), carry(right_perms)
    out_shape = jax.ShapeDtypeStruct((rows, rb * ratio * BS), jnp.float32)
    bufs = right_bufs + left_bufs[1:]
    codings = -(-(slots + STEPS + 1) * w // 8) * 8
    return pl.pallas_call(
        functools.partial(product_kernel, slots, n_row, ratio, rb, w, len(right_bufs)),
        out_shape=out_shape,
        in_specs=[smem] + [hbm] * len(bufs),
        out_specs=hbm,
        scratch_shapes=[
            pltpu.VMEM((slots, rows + EXTRA, width), jnp.float32),
            pltpu.VMEM((STEPS + 1, rows + EXTRA, width), jnp.float32),
            pltpu.VMEM(out_shape.shape, jnp.float32),
            pltpu.VMEM((UNROLL, BS, width), jnp.float32),
            pltpu.VMEM((slots + STEPS, EXTRA, width), jnp.float32),
            pltpu.VMEM((codings, 128), jnp.int32),
            pltpu.SMEM((codings, 128), jnp.int32),
            pltpu.SMEM((slots * rb * w + 4 * UNROLL,), jnp.int32),
            dma((slots,)),
            dma((STEPS,)),
            dma((PARTS,)),
            dma((slots + STEPS + 1,)),
        ],
        compiler_params=pltpu.CompilerParams(vmem_limit_bytes=18 << 20),
        cost_estimate=pl.CostEstimate(flops=10**9, bytes_accessed=20 << 20, transcendentals=0),
    )(info, *bufs)


def solution(mesh):
    in_specs = (P("row", "col"), P("row", "col"))
    return jax.shard_map(local, mesh=mesh, in_specs=in_specs, out_specs=P("row", "col"), check_vma=False)
```

```python
import functools

import jax
import jax.numpy as jnp
import numpy as np
from jax import lax
from jax.experimental import pallas as pl
from jax.experimental.pallas import tpu as pltpu
from jax.sharding import PartitionSpec as P

BS = 64
STEPS = 4
UNROLL = 8
EXTRA = 8
PARTS = 8


def left_offsets(row, ratio, n_col):
    seen = []
    for step in range(STEPS):
        offset = (row + step) // ratio % n_col
        if offset not in seen:
            seen.append(offset)
    return seen


def shift(rows, step, count):
    return [((r, c), (r, (c + step) % count)) for r in rows for c in range(count)]


def left_plan(n_row, n_col, ratio):
    offsets = [left_offsets(row, ratio, n_col) for row in range(n_row)]
    if (n_row, n_col, ratio) != (8, 4, 2):
        perms = []
        for slot in range(max(len(o) for o in offsets)):
            pairs = [
                ((row, (col + offsets[row][slot]) % n_col), (row, col))
                for row in range(n_row)
                for col in range(n_col)
                if slot < len(offsets[row]) and offsets[row][slot] != 0
            ]
            perms.append((0, pairs))
        return perms
    whole = [r for r in range(8) if {1, 2, 3} <= set(offsets[r])]
    once, twice = {-1: [], 1: []}, {-1: [], 1: []}
    for r in range(8):
        for offset, step in ((1, -1), (3, 1)):
            if offset in offsets[r] and r not in whole:
                once[step].append(r)
                if 2 in offsets[r]:
                    twice[step].append(r)
    down = shift([r for r in once[-1] if r != 0], -1, 4) + [((3, c), (3, c - 1)) for c in (1, 2, 3)] + [((3, 0), (0, 0))]
    up = shift(once[1], 1, 4) + shift([0], -1, 4) + [((3, c), (3, c + 1)) for c in (0, 1, 2)] + [((3, 3), (1, 3))]
    again_down = shift(twice[-1], -1, 4) + [((3, 1), (3, 0)), ((3, 2), (3, 1)), ((0, 0), (3, 3))]
    again_up = shift(twice[1], 1, 4) + [((3, 1), (3, 2)), ((3, 2), (3, 3)), ((1, 3), (3, 0))]
    return [(0, down), (0, up), (1, again_down), (2, again_up)]


def right_plan(n_row, n_col, ratio):
    everyone = [(row, col) for row in range(n_row) for col in range(n_col)]
    if (n_row, n_col, ratio) != (8, 4, 2):
        return [
            (0, [(((r + ratio * c + step) % n_row, c), (r, c)) for r, c in everyone if (ratio * c + step) % n_row])
            for step in range(STEPS)
        ]
    first = [(((r + 2 * c) % 8, c), (r, c)) for r, c in everyone if c != 0]
    first += [((r + 1, 0), (r, 0)) for r in range(0, 8, 2)]
    second = [(((r + 2 * c + 2) % 8, c), (r, c)) for r, c in everyone if c != 3]
    second += [((r ^ 1, 3), (r, 3)) for r in range(8)]
    last = [(((r - 1 + 2 * c + 4) % 8, c), (r, c)) for r, c in everyone if r % 2 == 1]
    first_swap = [((r + 1, c), (r, c)) for r, c in everyone if r % 2 == 0 and c != 0]
    second_swap = [((r ^ 1, c), (r, c)) for r, c in everyone if c != 3]
    return [(0, first), (0, second), (0, last), (1, first_swap), (2, second_swap)]


def carry_out(perms, n_row, n_col):
    held = [{(r, c): (r, c) for r in range(n_row) for c in range(n_col)}]
    for source, pairs in perms:
        held.append({dst: held[source][src] for src, dst in pairs})
    return held


def device_table(left_perms, right_perms, n_row, n_col, ratio):
    left_held = carry_out(left_perms, n_row, n_col)
    right_held = carry_out(right_perms, n_row, n_col)
    slots = (ratio - 1 + STEPS - 1) // ratio + 1
    table = np.full((n_row, n_col, 2 * slots + STEPS), -1, np.int32)

    def find(held, device, tile):
        return [i for i, h in enumerate(held) if h.get(device) == tile][0]

    for r in range(n_row):
        for c in range(n_col):
            for slot, offset in enumerate(left_offsets(r, ratio, n_col)):
                tile_col = (c + offset) % n_col
                table[r, c, slot] = find(left_held, (r, c), (r, tile_col))
                table[r, c, slots + STEPS + slot] = (tile_col * ratio - r - ratio * c) % n_row
            for step in range(STEPS):
                table[r, c, slots + step] = find(right_held, (r, c), ((r + ratio * c + step) % n_row, c))
    return table, slots


def fetch(choice, among, bufs, target, sem):
    for number in among:
        @pl.when(choice == number)
        def _():
            pltpu.make_async_copy(bufs[number], target, sem).start()


def join_kernel(cols_ref, data_ref, out_ref, cols, sem):
    rows = data_ref.shape[0]
    data_copy = pltpu.make_async_copy(data_ref, out_ref.at[pl.ds(0, rows)], sem.at[0])
    cols_copy = pltpu.make_async_copy(cols_ref, cols, sem.at[1])
    data_copy.start()
    cols_copy.start()
    out_ref[pl.ds(rows, EXTRA), :] = jnp.zeros((EXTRA, out_ref.shape[1]), jnp.float32)
    cols_copy.wait()
    out_ref[pl.ds(rows, cols.shape[0]), pl.ds(0, cols.shape[1])] = cols[...].astype(jnp.float32)
    data_copy.wait()


def code_kernel(slots, n_row, ratio, rb, w, among, info_ref, *refs):
    bufs, code_ref, (cols, sem) = refs[:-3], refs[-3], refs[-2:]
    names = pl.ds(bufs[0].shape[0] - EXTRA, EXTRA)
    for slot in range(slots):
        fetch(info_ref[slot], among[slot], [buf.at[names] for buf in bufs], cols.at[slot], sem.at[slot])
    lanes = code_ref.shape[1]
    row = lax.broadcasted_iota(jnp.int32, (w, lanes), 1)
    tile_slot = lax.broadcasted_iota(jnp.int32, (w, lanes), 0)
    for slot in range(slots):
        used = info_ref[slot] >= 0

        @pl.when(used)
        def _():
            pltpu.make_async_copy(bufs[0].at[names], cols.at[slot], sem.at[slot]).wait()

        inner = cols[slot, 0:w, 0:lanes].astype(jnp.int32)
        valid = (inner >= 0) & (row < rb)
        step = jnp.full(inner.shape, info_ref[slots + STEPS + slot], jnp.int32)
        for _ in range(ratio - 1):
            beyond = inner >= rb
            step = jnp.where(beyond, step + 1, step)
            inner = jnp.where(beyond, inner - rb, inner)
        step = jnp.where(step >= n_row, step - n_row, step)
        code = inner | tile_slot << 8 | slot << 12 | row << 16 | step << 24
        valid = valid & (step < STEPS)
        code_ref[slot * w : (slot + 1) * w, :] = jnp.where(valid, jnp.where(used, code, -1), -1)


def product_kernel(slots, rb, w, n_right, among, info_ref, code_ref, *refs):
    out_ref, left, right, acc, value, cols, places, left_codes, right_places, codes, lsem, rsem, osem, csem = refs[-14:]
    right_bufs, left_bufs = refs[:n_right], refs[:1] + refs[n_right:-14]
    rows, width = left.shape[1] - EXTRA, left.shape[2]
    names = pl.ds(rows, EXTRA)
    left_codes_copy = pltpu.make_async_copy(code_ref, left_codes, csem.at[STEPS])
    left_codes_copy.start()
    for step in range(STEPS):
        choice = info_ref[slots + step]
        fetch(choice, among[slots + step], [buf.at[names] for buf in right_bufs], cols.at[step], csem.at[step])
    for step in range(STEPS):
        fetch(info_ref[slots + step], among[slots + step], right_bufs, right.at[step], rsem.at[step])
    for slot in range(slots):
        fetch(info_ref[slot], among[slot], left_bufs, left.at[slot], lsem.at[slot])

    def clear(first, last):
        @pl.loop(first, last)
        def _(r):
            acc[pl.ds(pl.multiple_of(r * BS, BS), BS), :] = jnp.zeros((BS, acc.shape[1]), jnp.float32)

    clear(0, rb // 2)
    lanes = places.shape[1]
    for step in range(STEPS):
        pltpu.make_async_copy(right_bufs[0].at[names], cols.at[step], csem.at[step]).wait()
        col = cols[step, 0:w, 0:lanes].astype(jnp.int32)
        place = (col >> 1) * 2 * BS | (col & 1) << 16
        places[step * w : (step + 1) * w, :] = jnp.where(col < 0, 2 << 16, place)
    places[STEPS * w : (STEPS + 1) * w, :] = jnp.full((w, lanes), 2 << 16, jnp.int32)
    places_copy = pltpu.make_async_copy(places, right_places, csem.at[STEPS + 1])
    places_copy.start()
    left_codes_copy.wait()

    part_rows = rb // PARTS
    for u in range(UNROLL):
        codes[u] = STEPS << 24
    bounds = [jnp.int32(UNROLL)]
    for part in range(PARTS):
        def listed(i, place):
            for slot in range(slots):
                for k in range(w):
                    code = left_codes[slot * w + k, part * part_rows + i]
                    codes[place] = code
                    place = place + (code >= 0).astype(jnp.int32)
            return place

        bounds.append(lax.fori_loop(0, part_rows, listed, bounds[-1]))
    for u in range(2 * UNROLL):
        codes[bounds[-1] + u] = STEPS << 24

    clear(rb // 2, rb)
    places_copy.wait()
    for step in range(STEPS):
        pltpu.make_async_copy(right_bufs[0], right.at[step], rsem.at[step]).wait()
    for slot in range(slots):
        @pl.when(info_ref[slot] >= 0)
        def _():
            pltpu.make_async_copy(left_bufs[0], left.at[slot], lsem.at[slot]).wait()

    low = lax.broadcasted_iota(jnp.int32, (BS, 2 * BS), 1) < BS
    half = lax.broadcasted_iota(jnp.int32, (BS, 2 * BS), 1) // BS

    def block_at(index):
        return pl.ds(pl.multiple_of(index * BS, BS), BS)

    def product(code):
        slot = (code >> 8) & 15
        x = left[(code >> 12) & 15, block_at((code >> 16) & 255), pl.ds(pl.multiple_of((slot >> 1) * 2 * BS, 2 * BS), 2 * BS)]
        both = jnp.where(half == (slot & 1), x, pltpu.roll(x, BS, 1))
        hi = both.astype(jnp.bfloat16).astype(jnp.float32)
        lhs = jnp.where(low, hi, both - hi).astype(jnp.bfloat16)
        lhs = jnp.concatenate([lhs, lhs], axis=1)
        y = right[code >> 24, block_at(code & 255), :]
        hi = y.astype(jnp.bfloat16)
        lo = (y - hi.astype(jnp.float32)).astype(jnp.bfloat16)
        rhs = jnp.concatenate([hi, hi, lo, lo], axis=0)
        return jnp.dot(lhs, rhs, preferred_element_type=jnp.float32)

    def add(code, product):
        rows_at = block_at((code >> 16) & 255)
        for pair in range(w // 2):
            x = product[:, pair * 2 * BS : (pair + 1) * 2 * BS]
            turned = pltpu.roll(x, BS, 1)
            picked, at = [], []
            for side in range(2):
                place = right_places[(code >> 24) * w + 2 * pair + side, code & 255]
                parity = place >> 16
                chosen = jnp.where(parity == side, x, turned)
                picked.append(jnp.where(half == parity, chosen, 0.0))
                at.append(place & 0xFFFF)
            picked[1] = jnp.where(at[0] == at[1], picked[0] + picked[1], picked[1])
            spots = [(rows_at, pl.ds(pl.multiple_of(base, 2 * BS), 2 * BS)) for base in at]
            sums = [acc[spot] + part for spot, part in zip(spots, picked)]
            for spot, total in zip(spots, sums):
                acc[spot] = total

    def out_copy(part):
        at = pl.ds(part * part_rows * BS, part_rows * BS)
        return pltpu.make_async_copy(acc.at[at], out_ref.at[at], osem.at[part])

    groups = [jnp.int32(0)] + [(bound + UNROLL - 1) // UNROLL for bound in bounds[1:]]
    for part in range(PARTS):
        @pl.loop(groups[part], groups[part + 1])
        def _(group):
            for u in range(UNROLL):
                add(codes[group * UNROLL + u], value[u])
            for u in range(UNROLL):
                value[u] = product(codes[(group + 1) * UNROLL + u])

        out_copy(part).start()
    for part in range(PARTS):
        out_copy(part).wait()


def local(p_cols, p_data):
    n_row, n_col = lax.axis_size("row"), lax.axis_size("col")
    ratio = n_row // n_col
    row_id, col_id = lax.axis_index("row"), lax.axis_index("col")
    rb, w = p_cols.shape
    rows, width = p_data.shape
    left_perms = left_plan(n_row, n_col, ratio)
    right_perms = right_plan(n_row, n_col, ratio)
    table, slots = device_table(left_perms, right_perms, n_row, n_col, ratio)
    info = jnp.asarray(table)[row_id, col_id]

    smem = pl.BlockSpec(memory_space=pltpu.SMEM)
    hbm = pl.BlockSpec(memory_space=pl.ANY)
    dma = pltpu.SemaphoreType.DMA
    own = pl.pallas_call(
        join_kernel,
        out_shape=jax.ShapeDtypeStruct((rows + EXTRA, width), jnp.float32),
        in_specs=[pl.BlockSpec(memory_space=pltpu.HBM)] * 2,
        out_specs=pl.BlockSpec(memory_space=pltpu.VMEM),
        scratch_shapes=[pltpu.VMEM((w, rb), jnp.int32), dma((2,))],
        compiler_params=pltpu.CompilerParams(vmem_limit_bytes=4 << 20),
        cost_estimate=pl.CostEstimate(flops=0, bytes_accessed=2 << 20, transcendentals=0),
    )(p_cols.T, p_data)

    def carry(perms):
        bufs = [own]
        for source, pairs in perms:
            flat = [(s[0] * n_col + s[1], d[0] * n_col + d[1]) for s, d in pairs]
            bufs.append(lax.ppermute(bufs[source], ("row", "col"), flat))
        return bufs

    left_bufs, right_bufs = carry(left_perms), carry(right_perms)
    out_shape = jax.ShapeDtypeStruct((rows, rb * ratio * BS), jnp.float32)
    bufs = right_bufs + left_bufs[1:]
    among = [sorted(set(table[:, :, i].ravel().tolist()) - {-1}) for i in range(slots + STEPS)]
    left_lines, right_lines = -(-slots * w // 8) * 8, -(-(STEPS + 1) * w // 8) * 8
    left_codes = pl.pallas_call(
        functools.partial(code_kernel, slots, n_row, ratio, rb, w, among),
        out_shape=jax.ShapeDtypeStruct((left_lines, 128), jnp.int32),
        in_specs=[smem] + [hbm] * len(left_bufs),
        out_specs=pl.BlockSpec(memory_space=pltpu.VMEM),
        scratch_shapes=[pltpu.VMEM((slots, EXTRA, width), jnp.float32), dma((slots,))],
        compiler_params=pltpu.CompilerParams(vmem_limit_bytes=2 << 20),
        cost_estimate=pl.CostEstimate(flops=10**9, bytes_accessed=1 << 16, transcendentals=0),
    )(info, *left_bufs)
    return pl.pallas_call(
        functools.partial(product_kernel, slots, rb, w, len(right_bufs), among),
        out_shape=out_shape,
        in_specs=[smem] + [hbm] * (1 + len(bufs)),
        out_specs=hbm,
        scratch_shapes=[
            pltpu.VMEM((slots, rows + EXTRA, width), jnp.float32),
            pltpu.VMEM((STEPS + 1, rows + EXTRA, width), jnp.float32),
            pltpu.VMEM(out_shape.shape, jnp.float32),
            pltpu.VMEM((UNROLL, BS, width), jnp.float32),
            pltpu.VMEM((STEPS, EXTRA, width), jnp.float32),
            pltpu.VMEM((right_lines, 128), jnp.int32),
            pltpu.SMEM((left_lines, 128), jnp.int32),
            pltpu.SMEM((right_lines, 128), jnp.int32),
            pltpu.SMEM((slots * rb * w + 4 * UNROLL,), jnp.int32),
            dma((slots,)),
            dma((STEPS,)),
            dma((PARTS,)),
            dma((STEPS + 2,)),
        ],
        compiler_params=pltpu.CompilerParams(vmem_limit_bytes=20 << 20),
        cost_estimate=pl.CostEstimate(flops=10**9, bytes_accessed=20 << 20, transcendentals=0),
    )(info, left_codes, *bufs)


def solution(mesh):
    in_specs = (P("row", "col"), P("row", "col"))
    return jax.shard_map(local, mesh=mesh, in_specs=in_specs, out_specs=P("row", "col"), check_vma=False)
```

```python
import functools

import jax
import jax.numpy as jnp
import numpy as np
from jax import lax
from jax.experimental import pallas as pl
from jax.experimental.pallas import tpu as pltpu
from jax.sharding import PartitionSpec as P

BS = 64
STEPS = 4
UNROLL = 8
EXTRA = 8
PARTS = 8
EARLY = 2


def left_offsets(row, ratio, n_col):
    seen = []
    for step in range(STEPS):
        offset = (row + step) // ratio % n_col
        if offset not in seen:
            seen.append(offset)
    return seen


def shift(rows, step, count):
    return [((r, c), (r, (c + step) % count)) for r in rows for c in range(count)]


def left_plan(n_row, n_col, ratio):
    offsets = [left_offsets(row, ratio, n_col) for row in range(n_row)]
    if (n_row, n_col, ratio) != (8, 4, 2):
        perms = []
        for slot in range(max(len(o) for o in offsets)):
            pairs = [
                ((row, (col + offsets[row][slot]) % n_col), (row, col))
                for row in range(n_row)
                for col in range(n_col)
                if slot < len(offsets[row]) and offsets[row][slot] != 0
            ]
            perms.append((0, pairs))
        return perms
    whole = [r for r in range(8) if {1, 2, 3} <= set(offsets[r])]
    once, twice = {-1: [], 1: []}, {-1: [], 1: []}
    for r in range(8):
        for offset, step in ((1, -1), (3, 1)):
            if offset in offsets[r] and r not in whole:
                once[step].append(r)
                if 2 in offsets[r]:
                    twice[step].append(r)
    down = shift([r for r in once[-1] if r != 0], -1, 4) + [((3, c), (3, c - 1)) for c in (1, 2, 3)] + [((3, 0), (0, 0))]
    up = shift(once[1], 1, 4) + shift([0], -1, 4) + [((3, c), (3, c + 1)) for c in (0, 1, 2)] + [((3, 3), (1, 3))]
    again_down = shift(twice[-1], -1, 4) + [((3, 1), (3, 0)), ((3, 2), (3, 1)), ((0, 0), (3, 3))]
    again_up = shift(twice[1], 1, 4) + [((3, 1), (3, 2)), ((3, 2), (3, 3)), ((1, 3), (3, 0))]
    return [(0, down), (0, up), (1, again_down), (2, again_up)]


def right_plan(n_row, n_col, ratio):
    everyone = [(row, col) for row in range(n_row) for col in range(n_col)]
    if (n_row, n_col, ratio) != (8, 4, 2):
        return [
            (0, [(((r + ratio * c + step) % n_row, c), (r, c)) for r, c in everyone if (ratio * c + step) % n_row])
            for step in range(STEPS)
        ]
    first = [(((r + 2 * c) % 8, c), (r, c)) for r, c in everyone if c != 0]
    first += [((r + 1, 0), (r, 0)) for r in range(0, 8, 2)]
    second = [(((r + 2 * c + 2) % 8, c), (r, c)) for r, c in everyone if c != 3]
    second += [((r ^ 1, 3), (r, 3)) for r in range(8)]
    last = [(((r - 1 + 2 * c + 4) % 8, c), (r, c)) for r, c in everyone if r % 2 == 1]
    first_swap = [((r + 1, c), (r, c)) for r, c in everyone if r % 2 == 0 and c != 0]
    second_swap = [((r ^ 1, c), (r, c)) for r, c in everyone if c != 3]
    return [(0, first), (0, second), (0, last), (1, first_swap), (2, second_swap)]


def carry_out(perms, n_row, n_col):
    held = [{(r, c): (r, c) for r in range(n_row) for c in range(n_col)}]
    for source, pairs in perms:
        held.append({dst: held[source][src] for src, dst in pairs})
    return held


def device_table(left_perms, right_perms, n_row, n_col, ratio):
    left_held = carry_out(left_perms, n_row, n_col)
    right_held = carry_out(right_perms, n_row, n_col)
    slots = (ratio - 1 + STEPS - 1) // ratio + 1
    table = np.full((n_row, n_col, 2 * slots + STEPS), -1, np.int32)

    def find(held, device, tile):
        return [i for i, h in enumerate(held) if h.get(device) == tile][0]

    for r in range(n_row):
        for c in range(n_col):
            for slot, offset in enumerate(left_offsets(r, ratio, n_col)):
                tile_col = (c + offset) % n_col
                table[r, c, slot] = find(left_held, (r, c), (r, tile_col))
                table[r, c, slots + STEPS + slot] = (tile_col * ratio - r - ratio * c) % n_row
            for step in range(STEPS):
                table[r, c, slots + step] = find(right_held, (r, c), ((r + ratio * c + step) % n_row, c))
    return table, slots


def fetch(choice, among, bufs, target, sem):
    for number in among:
        @pl.when(choice == number)
        def _():
            pltpu.make_async_copy(bufs[number], target, sem).start()


def join_kernel(cols_ref, data_ref, out_ref, cols, sem):
    rows = data_ref.shape[0]
    data_copy = pltpu.make_async_copy(data_ref, out_ref.at[pl.ds(0, rows)], sem.at[0])
    cols_copy = pltpu.make_async_copy(cols_ref, cols, sem.at[1])
    data_copy.start()
    cols_copy.start()
    out_ref[pl.ds(rows, EXTRA), :] = jnp.zeros((EXTRA, out_ref.shape[1]), jnp.float32)
    cols_copy.wait()
    out_ref[pl.ds(rows, cols.shape[0]), pl.ds(0, cols.shape[1])] = cols[...].astype(jnp.float32)
    data_copy.wait()


def product_kernel(slots, n_row, ratio, rb, w, n_right, among, info_ref, *refs):
    out_ref, left, right, acc, value, cols, coded, scalars, codes, lsem, rsem, osem, csem = refs[-13:]
    right_bufs, left_bufs = refs[:n_right], refs[:1] + refs[n_right:-13]
    rows, width = left.shape[1] - EXTRA, left.shape[2]
    names = pl.ds(rows, EXTRA)
    def fetch_left(slot):
        fetch(info_ref[slot], among[slot], left_bufs, left.at[slot], lsem.at[slot])

    def fetch_right(step):
        fetch(info_ref[slots + step], among[slots + step], right_bufs, right.at[step], rsem.at[step])

    for slot in range(slots):
        fetch(info_ref[slot], among[slot], [buf.at[names] for buf in left_bufs], cols.at[slot], csem.at[slot])
    for step in range(STEPS):
        at = slots + step
        fetch(info_ref[at], among[at], [buf.at[names] for buf in right_bufs], cols.at[at], csem.at[at])
    for step in range(EARLY):
        fetch_right(step)
    for slot in range(slots):
        fetch_left(slot)
    for step in range(EARLY, STEPS):
        fetch_right(step)

    def clear(first, last):
        @pl.loop(first, last)
        def _(r):
            acc[pl.ds(pl.multiple_of(r * BS, BS), BS), :] = jnp.zeros((BS, acc.shape[1]), jnp.float32)

    clear(0, rb // 4)
    lanes = scalars.shape[1]
    row = lax.broadcasted_iota(jnp.int32, (w, lanes), 1)
    tile_slot = lax.broadcasted_iota(jnp.int32, (w, lanes), 0)
    for slot in range(slots):
        used = info_ref[slot] >= 0

        @pl.when(used)
        def _():
            pltpu.make_async_copy(left_bufs[0].at[names], cols.at[slot], csem.at[slot]).wait()

        inner = cols[slot, 0:w, 0:lanes].astype(jnp.int32)
        valid = (inner >= 0) & (row < rb)
        step = jnp.full(inner.shape, info_ref[slots + STEPS + slot], jnp.int32)
        for _ in range(ratio - 1):
            beyond = inner >= rb
            step = jnp.where(beyond, step + 1, step)
            inner = jnp.where(beyond, inner - rb, inner)
        step = jnp.where(step >= n_row, step - n_row, step)
        code = inner | tile_slot << 8 | slot << 12 | row << 16 | step << 24
        valid = valid & (step < STEPS)
        coded[slot * w : (slot + 1) * w, :] = jnp.where(valid, jnp.where(used, code, -1), -1)
    for step in range(STEPS):
        pltpu.make_async_copy(right_bufs[0].at[names], cols.at[slots + step], csem.at[slots + step]).wait()
        col = cols[slots + step, 0:w, 0:lanes].astype(jnp.int32)
        code = (col >> 1) * 2 * BS | (col & 1) << 16
        coded[(slots + step) * w : (slots + step + 1) * w, :] = jnp.where(col < 0, 2 << 16, code)
    coded[(slots + STEPS) * w : (slots + STEPS + 1) * w, :] = jnp.full((w, lanes), 2 << 16, jnp.int32)
    to_scalars = pltpu.make_async_copy(coded, scalars, csem.at[slots + STEPS])
    to_scalars.start()
    clear(rb // 4, rb)
    to_scalars.wait()

    part_rows = rb // PARTS
    dummy, late = STEPS << 24, EARLY << 24
    for u in range(UNROLL):
        codes[u] = dummy

    def listing(first_row, rows_count, wanted, place):
        def listed(i, place):
            for slot in range(slots):
                for k in range(w):
                    code = scalars[slot * w + k, first_row + i]
                    codes[place] = code
                    place = place + wanted(code).astype(jnp.int32)
            return place

        return lax.fori_loop(0, rows_count, listed, place)

    early_end = listing(0, rb, lambda code: (code >= 0) & (code < late), jnp.int32(UNROLL))
    for u in range(UNROLL - 1):
        codes[early_end + u] = dummy
    early_groups = (early_end + UNROLL - 1) // UNROLL - 1
    bounds = [(early_groups + 1) * UNROLL]
    for part in range(PARTS):
        bounds.append(listing(part * part_rows, part_rows, lambda code: code >= late, bounds[-1]))
    for u in range(2 * UNROLL):
        codes[bounds[-1] + u] = dummy

    def wait_right(step):
        pltpu.make_async_copy(right_bufs[0], right.at[step], rsem.at[step]).wait()

    for step in range(EARLY):
        wait_right(step)
    for slot in range(slots):
        @pl.when(info_ref[slot] >= 0)
        def _():
            pltpu.make_async_copy(left_bufs[0], left.at[slot], lsem.at[slot]).wait()

    low = lax.broadcasted_iota(jnp.int32, (BS, 2 * BS), 1) < BS
    half = lax.broadcasted_iota(jnp.int32, (BS, 2 * BS), 1) // BS

    def block_at(index):
        return pl.ds(pl.multiple_of(index * BS, BS), BS)

    def product(code):
        slot = (code >> 8) & 15
        x = left[(code >> 12) & 15, block_at((code >> 16) & 255), pl.ds(pl.multiple_of((slot >> 1) * 2 * BS, 2 * BS), 2 * BS)]
        both = jnp.where(half == (slot & 1), x, pltpu.roll(x, BS, 1))
        hi = both.astype(jnp.bfloat16).astype(jnp.float32)
        lhs = jnp.where(low, hi, both - hi).astype(jnp.bfloat16)
        lhs = jnp.concatenate([lhs, lhs], axis=1)
        y = right[code >> 24, block_at(code & 255), :]
        hi = y.astype(jnp.bfloat16)
        lo = (y - hi.astype(jnp.float32)).astype(jnp.bfloat16)
        rhs = jnp.concatenate([hi, hi, lo, lo], axis=0)
        return jnp.dot(lhs, rhs, preferred_element_type=jnp.float32)

    def add(code, product):
        rows_at = block_at((code >> 16) & 255)
        for pair in range(w // 2):
            x = product[:, pair * 2 * BS : (pair + 1) * 2 * BS]
            turned = pltpu.roll(x, BS, 1)
            picked, at = [], []
            for side in range(2):
                place = scalars[(slots + (code >> 24)) * w + 2 * pair + side, code & 255]
                parity = place >> 16
                chosen = jnp.where(parity == side, x, turned)
                picked.append(jnp.where(half == parity, chosen, 0.0))
                at.append(place & 0xFFFF)
            picked[1] = jnp.where(at[0] == at[1], picked[0] + picked[1], picked[1])
            spots = [(rows_at, pl.ds(pl.multiple_of(base, 2 * BS), 2 * BS)) for base in at]
            sums = [acc[spot] + part for spot, part in zip(spots, picked)]
            for spot, total in zip(spots, sums):
                acc[spot] = total

    def out_copy(part):
        at = pl.ds(part * part_rows * BS, part_rows * BS)
        return pltpu.make_async_copy(acc.at[at], out_ref.at[at], osem.at[part])

    def group_step(group):
        for u in range(UNROLL):
            add(codes[group * UNROLL + u], value[u])
        for u in range(UNROLL):
            value[u] = product(codes[(group + 1) * UNROLL + u])

    pl.loop(0, early_groups)(group_step)
    for step in range(EARLY, STEPS):
        wait_right(step)
    groups = [early_groups] + [(bound + UNROLL - 1) // UNROLL for bound in bounds[1:]]
    for part in range(PARTS):
        pl.loop(groups[part], groups[part + 1])(group_step)
        out_copy(part).start()
    for part in range(PARTS):
        out_copy(part).wait()


def local(p_cols, p_data):
    n_row, n_col = lax.axis_size("row"), lax.axis_size("col")
    ratio = n_row // n_col
    row_id, col_id = lax.axis_index("row"), lax.axis_index("col")
    rb, w = p_cols.shape
    rows, width = p_data.shape
    left_perms = left_plan(n_row, n_col, ratio)
    right_perms = right_plan(n_row, n_col, ratio)
    table, slots = device_table(left_perms, right_perms, n_row, n_col, ratio)
    info = jnp.asarray(table)[row_id, col_id]

    smem = pl.BlockSpec(memory_space=pltpu.SMEM)
    hbm = pl.BlockSpec(memory_space=pl.ANY)
    dma = pltpu.SemaphoreType.DMA
    own = pl.pallas_call(
        join_kernel,
        out_shape=jax.ShapeDtypeStruct((rows + EXTRA, width), jnp.float32),
        in_specs=[pl.BlockSpec(memory_space=pltpu.HBM)] * 2,
        out_specs=pl.BlockSpec(memory_space=pltpu.VMEM),
        scratch_shapes=[pltpu.VMEM((w, rb), jnp.int32), dma((2,))],
        compiler_params=pltpu.CompilerParams(vmem_limit_bytes=4 << 20),
        cost_estimate=pl.CostEstimate(flops=0, bytes_accessed=2 << 20, transcendentals=0),
    )(p_cols.T, p_data)

    def carry(perms):
        bufs = [own]
        for source, pairs in perms:
            flat = [(s[0] * n_col + s[1], d[0] * n_col + d[1]) for s, d in pairs]
            bufs.append(lax.ppermute(bufs[source], ("row", "col"), flat))
        return bufs

    left_bufs, right_bufs = carry(left_perms), carry(right_perms)
    out_shape = jax.ShapeDtypeStruct((rows, rb * ratio * BS), jnp.float32)
    bufs = right_bufs + left_bufs[1:]
    among = [sorted(set(table[:, :, i].ravel().tolist()) - {-1}) for i in range(slots + STEPS)]
    codings = -(-(slots + STEPS + 1) * w // 8) * 8
    return pl.pallas_call(
        functools.partial(product_kernel, slots, n_row, ratio, rb, w, len(right_bufs), among),
        out_shape=out_shape,
        in_specs=[smem] + [hbm] * len(bufs),
        out_specs=hbm,
        scratch_shapes=[
            pltpu.VMEM((slots, rows + EXTRA, width), jnp.float32),
            pltpu.VMEM((STEPS + 1, rows + EXTRA, width), jnp.float32),
            pltpu.VMEM(out_shape.shape, jnp.float32),
            pltpu.VMEM((UNROLL, BS, width), jnp.float32),
            pltpu.VMEM((slots + STEPS, EXTRA, width), jnp.float32),
            pltpu.VMEM((codings, 128), jnp.int32),
            pltpu.SMEM((codings, 128), jnp.int32),
            pltpu.SMEM((slots * rb * w + 5 * UNROLL,), jnp.int32),
            dma((slots,)),
            dma((STEPS,)),
            dma((PARTS,)),
            dma((slots + STEPS + 1,)),
        ],
        compiler_params=pltpu.CompilerParams(vmem_limit_bytes=18 << 20),
        cost_estimate=pl.CostEstimate(flops=10**9, bytes_accessed=20 << 20, transcendentals=0),
    )(info, *bufs)


def solution(mesh):
    in_specs = (P("row", "col"), P("row", "col"))
    return jax.shard_map(local, mesh=mesh, in_specs=in_specs, out_specs=P("row", "col"), check_vma=False)
```

```python
import functools

import jax
import jax.numpy as jnp
import numpy as np
from jax import lax
from jax.experimental import pallas as pl
from jax.experimental.pallas import tpu as pltpu
from jax.sharding import PartitionSpec as P

BS = 64
STEPS = 4
UNROLL = 8
EXTRA = 8
PARTS = 8


def left_offsets(row, ratio, n_col):
    seen = []
    for step in range(STEPS):
        offset = (row + step) // ratio % n_col
        if offset not in seen:
            seen.append(offset)
    return seen


def shift(rows, step, count):
    return [((r, c), (r, (c + step) % count)) for r in rows for c in range(count)]


def left_plan(n_row, n_col, ratio):
    offsets = [left_offsets(row, ratio, n_col) for row in range(n_row)]
    if (n_row, n_col, ratio) != (8, 4, 2):
        perms = []
        for slot in range(max(len(o) for o in offsets)):
            pairs = [
                ((row, (col + offsets[row][slot]) % n_col), (row, col))
                for row in range(n_row)
                for col in range(n_col)
                if slot < len(offsets[row]) and offsets[row][slot] != 0
            ]
            perms.append((0, pairs))
        return perms
    whole = [r for r in range(8) if {1, 2, 3} <= set(offsets[r])]
    once, twice = {-1: [], 1: []}, {-1: [], 1: []}
    for r in range(8):
        for offset, step in ((1, -1), (3, 1)):
            if offset in offsets[r] and r not in whole:
                once[step].append(r)
                if 2 in offsets[r]:
                    twice[step].append(r)
    down = shift([r for r in once[-1] if r != 0], -1, 4) + [((3, c), (3, c - 1)) for c in (1, 2, 3)] + [((3, 0), (0, 0))]
    up = shift(once[1], 1, 4) + shift([0], -1, 4) + [((3, c), (3, c + 1)) for c in (0, 1, 2)] + [((3, 3), (1, 3))]
    again_down = shift(twice[-1], -1, 4) + [((3, 1), (3, 0)), ((3, 2), (3, 1)), ((0, 0), (3, 3))]
    again_up = shift(twice[1], 1, 4) + [((3, 1), (3, 2)), ((3, 2), (3, 3)), ((1, 3), (3, 0))]
    return [(0, down), (0, up), (1, again_down), (2, again_up)]


def right_plan(n_row, n_col, ratio):
    everyone = [(row, col) for row in range(n_row) for col in range(n_col)]
    if (n_row, n_col, ratio) != (8, 4, 2):
        return [
            (0, [(((r + ratio * c + step) % n_row, c), (r, c)) for r, c in everyone if (ratio * c + step) % n_row])
            for step in range(STEPS)
        ]
    first = [(((r + 2 * c) % 8, c), (r, c)) for r, c in everyone if c != 0]
    first += [((r + 1, 0), (r, 0)) for r in range(0, 8, 2)]
    second = [(((r + 2 * c + 2) % 8, c), (r, c)) for r, c in everyone if c != 3]
    second += [((r ^ 1, 3), (r, 3)) for r in range(8)]
    last = [(((r - 1 + 2 * c + 4) % 8, c), (r, c)) for r, c in everyone if r % 2 == 1]
    first_swap = [((r + 1, c), (r, c)) for r, c in everyone if r % 2 == 0 and c != 0]
    second_swap = [((r ^ 1, c), (r, c)) for r, c in everyone if c != 3]
    return [(0, first), (0, second), (0, last), (1, first_swap), (2, second_swap)]


def carry_out(perms, n_row, n_col):
    held = [{(r, c): (r, c) for r in range(n_row) for c in range(n_col)}]
    for source, pairs in perms:
        held.append({dst: held[source][src] for src, dst in pairs})
    return held


def device_table(left_perms, right_perms, n_row, n_col, ratio):
    left_held = carry_out(left_perms, n_row, n_col)
    right_held = carry_out(right_perms, n_row, n_col)
    slots = (ratio - 1 + STEPS - 1) // ratio + 1
    table = np.full((n_row, n_col, 2 * slots + STEPS), -1, np.int32)

    def find(held, device, tile):
        return [i for i, h in enumerate(held) if h.get(device) == tile][0]

    for r in range(n_row):
        for c in range(n_col):
            for slot, offset in enumerate(left_offsets(r, ratio, n_col)):
                tile_col = (c + offset) % n_col
                table[r, c, slot] = find(left_held, (r, c), (r, tile_col))
                table[r, c, slots + STEPS + slot] = (tile_col * ratio - r - ratio * c) % n_row
            for step in range(STEPS):
                table[r, c, slots + step] = find(right_held, (r, c), ((r + ratio * c + step) % n_row, c))
    return table, slots


def fetch(choice, among, bufs, target, sem):
    for number in among:
        @pl.when(choice == number)
        def _():
            pltpu.make_async_copy(bufs[number], target, sem).start()


def join_kernel(cols_ref, data_ref, out_ref, cols, sem):
    rows = data_ref.shape[0]
    data_copy = pltpu.make_async_copy(data_ref, out_ref.at[pl.ds(0, rows)], sem.at[0])
    cols_copy = pltpu.make_async_copy(cols_ref, cols, sem.at[1])
    data_copy.start()
    cols_copy.start()
    out_ref[pl.ds(rows, EXTRA), :] = jnp.zeros((EXTRA, out_ref.shape[1]), jnp.float32)
    cols_copy.wait()
    out_ref[pl.ds(rows, cols.shape[0]), pl.ds(0, cols.shape[1])] = cols[...].astype(jnp.float32)
    data_copy.wait()


def product_kernel(slots, n_row, ratio, rb, w, n_right, among, info_ref, *refs):
    out_ref, left, right, acc, value, cols, coded, scalars, codes, lsem, rsem, osem, csem = refs[-13:]
    right_bufs, left_bufs = refs[:n_right], refs[:1] + refs[n_right:-13]
    rows, width = left.shape[1] - EXTRA, left.shape[2]
    names = pl.ds(rows, EXTRA)
    for slot in range(slots):
        fetch(info_ref[slot], among[slot], [buf.at[names] for buf in left_bufs], cols.at[slot], csem.at[slot])
    for step in range(STEPS):
        at = slots + step
        fetch(info_ref[at], among[at], [buf.at[names] for buf in right_bufs], cols.at[at], csem.at[at])
    for step in range(STEPS):
        fetch(info_ref[slots + step], among[slots + step], right_bufs, right.at[step], rsem.at[step])
    for slot in range(slots):
        fetch(info_ref[slot], among[slot], left_bufs, left.at[slot], lsem.at[slot])

    def clear(first, last):
        @pl.loop(first, last)
        def _(r):
            acc[pl.ds(pl.multiple_of(r * BS, BS), BS), :] = jnp.zeros((BS, acc.shape[1]), jnp.float32)

    clear(0, rb // 4)
    lanes = scalars.shape[1]
    row = lax.broadcasted_iota(jnp.int32, (w, lanes), 1)
    tile_slot = lax.broadcasted_iota(jnp.int32, (w, lanes), 0)
    for slot in range(slots):
        used = info_ref[slot] >= 0

        @pl.when(used)
        def _():
            pltpu.make_async_copy(left_bufs[0].at[names], cols.at[slot], csem.at[slot]).wait()

        inner = cols[slot, 0:w, 0:lanes].astype(jnp.int32)
        valid = (inner >= 0) & (row < rb)
        step = jnp.full(inner.shape, info_ref[slots + STEPS + slot], jnp.int32)
        for _ in range(ratio - 1):
            beyond = inner >= rb
            step = jnp.where(beyond, step + 1, step)
            inner = jnp.where(beyond, inner - rb, inner)
        step = jnp.where(step >= n_row, step - n_row, step)
        code = inner | tile_slot << 8 | slot << 12 | row << 16 | step << 24
        valid = valid & (step < STEPS)
        coded[slot * w : (slot + 1) * w, :] = jnp.where(valid, jnp.where(used, code, -1), -1)
    for step in range(STEPS):
        pltpu.make_async_copy(right_bufs[0].at[names], cols.at[slots + step], csem.at[slots + step]).wait()
        col = cols[slots + step, 0:w, 0:lanes].astype(jnp.int32)
        code = (col >> 1) * 2 * BS | (col & 1) << 16
        coded[(slots + step) * w : (slots + step + 1) * w, :] = jnp.where(col < 0, 2 << 16, code)
    coded[(slots + STEPS) * w : (slots + STEPS + 1) * w, :] = jnp.full((w, lanes), 2 << 16, jnp.int32)
    to_scalars = pltpu.make_async_copy(coded, scalars, csem.at[slots + STEPS])
    to_scalars.start()
    clear(rb // 4, rb)
    to_scalars.wait()

    part_rows = rb // PARTS
    for u in range(UNROLL):
        codes[u] = STEPS << 24
    bounds = [jnp.int32(UNROLL)]
    for part in range(PARTS):
        def listed(i, place):
            row_codes = [scalars[line, part * part_rows + i] for line in range(slots * w)]
            for code in row_codes:
                codes[place] = code
                place = place + (code >= 0).astype(jnp.int32)
            return place

        bounds.append(lax.fori_loop(0, part_rows, listed, bounds[-1]))
    for u in range(2 * UNROLL):
        codes[bounds[-1] + u] = STEPS << 24

    for step in range(STEPS):
        pltpu.make_async_copy(right_bufs[0], right.at[step], rsem.at[step]).wait()
    for slot in range(slots):
        @pl.when(info_ref[slot] >= 0)
        def _():
            pltpu.make_async_copy(left_bufs[0], left.at[slot], lsem.at[slot]).wait()

    low = lax.broadcasted_iota(jnp.int32, (BS, 2 * BS), 1) < BS
    half = lax.broadcasted_iota(jnp.int32, (BS, 2 * BS), 1) // BS

    def block_at(index):
        return pl.ds(pl.multiple_of(index * BS, BS), BS)

    def product(code):
        slot = (code >> 8) & 15
        x = left[(code >> 12) & 15, block_at((code >> 16) & 255), pl.ds(pl.multiple_of((slot >> 1) * 2 * BS, 2 * BS), 2 * BS)]
        both = jnp.where(half == (slot & 1), x, pltpu.roll(x, BS, 1))
        hi = both.astype(jnp.bfloat16).astype(jnp.float32)
        lhs = jnp.where(low, hi, both - hi).astype(jnp.bfloat16)
        lhs = jnp.concatenate([lhs, lhs], axis=1)
        y = right[code >> 24, block_at(code & 255), :]
        hi = y.astype(jnp.bfloat16)
        lo = (y - hi.astype(jnp.float32)).astype(jnp.bfloat16)
        rhs = jnp.concatenate([hi, hi, lo, lo], axis=0)
        return jnp.dot(lhs, rhs, preferred_element_type=jnp.float32)

    def add(code, product):
        rows_at = block_at((code >> 16) & 255)
        for pair in range(w // 2):
            x = product[:, pair * 2 * BS : (pair + 1) * 2 * BS]
            turned = pltpu.roll(x, BS, 1)
            picked, at = [], []
            for side in range(2):
                place = scalars[(slots + (code >> 24)) * w + 2 * pair + side, code & 255]
                parity = place >> 16
                chosen = jnp.where(parity == side, x, turned)
                picked.append(jnp.where(half == parity, chosen, 0.0))
                at.append(place & 0xFFFF)
            picked[1] = jnp.where(at[0] == at[1], picked[0] + picked[1], picked[1])
            spots = [(rows_at, pl.ds(pl.multiple_of(base, 2 * BS), 2 * BS)) for base in at]
            sums = [acc[spot] + part for spot, part in zip(spots, picked)]
            for spot, total in zip(spots, sums):
                acc[spot] = total

    def out_copy(part):
        at = pl.ds(part * part_rows * BS, part_rows * BS)
        return pltpu.make_async_copy(acc.at[at], out_ref.at[at], osem.at[part])

    groups = [jnp.int32(0)] + [(bound + UNROLL - 1) // UNROLL for bound in bounds[1:]]
    for part in range(PARTS):
        @pl.loop(groups[part], groups[part + 1])
        def _(group):
            for u in range(UNROLL):
                add(codes[group * UNROLL + u], value[u])
            for u in range(UNROLL):
                value[u] = product(codes[(group + 1) * UNROLL + u])

        out_copy(part).start()
    for part in range(PARTS):
        out_copy(part).wait()


def local(p_cols, p_data):
    n_row, n_col = lax.axis_size("row"), lax.axis_size("col")
    ratio = n_row // n_col
    row_id, col_id = lax.axis_index("row"), lax.axis_index("col")
    rb, w = p_cols.shape
    rows, width = p_data.shape
    left_perms = left_plan(n_row, n_col, ratio)
    right_perms = right_plan(n_row, n_col, ratio)
    table, slots = device_table(left_perms, right_perms, n_row, n_col, ratio)
    info = jnp.asarray(table)[row_id, col_id]

    smem = pl.BlockSpec(memory_space=pltpu.SMEM)
    hbm = pl.BlockSpec(memory_space=pl.ANY)
    dma = pltpu.SemaphoreType.DMA
    own = pl.pallas_call(
        join_kernel,
        out_shape=jax.ShapeDtypeStruct((rows + EXTRA, width), jnp.float32),
        in_specs=[pl.BlockSpec(memory_space=pltpu.HBM)] * 2,
        out_specs=pl.BlockSpec(memory_space=pltpu.VMEM),
        scratch_shapes=[pltpu.VMEM((w, rb), jnp.int32), dma((2,))],
        compiler_params=pltpu.CompilerParams(vmem_limit_bytes=4 << 20),
        cost_estimate=pl.CostEstimate(flops=0, bytes_accessed=2 << 20, transcendentals=0),
    )(p_cols.T, p_data)

    def carry(perms):
        bufs = [own]
        for source, pairs in perms:
            flat = [(s[0] * n_col + s[1], d[0] * n_col + d[1]) for s, d in pairs]
            bufs.append(lax.ppermute(bufs[source], ("row", "col"), flat))
        return bufs

    left_bufs, right_bufs = carry(left_perms), carry(right_perms)
    out_shape = jax.ShapeDtypeStruct((rows, rb * ratio * BS), jnp.float32)
    bufs = right_bufs + left_bufs[1:]
    among = [sorted(set(table[:, :, i].ravel().tolist()) - {-1}) for i in range(slots + STEPS)]
    codings = -(-(slots + STEPS + 1) * w // 8) * 8
    return pl.pallas_call(
        functools.partial(product_kernel, slots, n_row, ratio, rb, w, len(right_bufs), among),
        out_shape=out_shape,
        in_specs=[smem] + [hbm] * len(bufs),
        out_specs=hbm,
        scratch_shapes=[
            pltpu.VMEM((slots, rows + EXTRA, width), jnp.float32),
            pltpu.VMEM((STEPS + 1, rows + EXTRA, width), jnp.float32),
            pltpu.VMEM(out_shape.shape, jnp.float32),
            pltpu.VMEM((UNROLL, BS, width), jnp.float32),
            pltpu.VMEM((slots + STEPS, EXTRA, width), jnp.float32),
            pltpu.VMEM((codings, 128), jnp.int32),
            pltpu.SMEM((codings, 128), jnp.int32),
            pltpu.SMEM((slots * rb * w + 4 * UNROLL,), jnp.int32),
            dma((slots,)),
            dma((STEPS,)),
            dma((PARTS,)),
            dma((slots + STEPS + 1,)),
        ],
        compiler_params=pltpu.CompilerParams(vmem_limit_bytes=18 << 20),
        cost_estimate=pl.CostEstimate(flops=10**9, bytes_accessed=20 << 20, transcendentals=0),
    )(info, *bufs)


def solution(mesh):
    in_specs = (P("row", "col"), P("row", "col"))
    return jax.shard_map(local, mesh=mesh, in_specs=in_specs, out_specs=P("row", "col"), check_vma=False)
```

```python
import functools

import jax
import jax.numpy as jnp
import numpy as np
from jax import lax
from jax.experimental import pallas as pl
from jax.experimental.pallas import tpu as pltpu
from jax.sharding import PartitionSpec as P

BS = 64
STEPS = 4
UNROLL = 8
EXTRA = 8
PARTS = 8


def left_offsets(row, ratio, n_col):
    seen = []
    for step in range(STEPS):
        offset = (row + step) // ratio % n_col
        if offset not in seen:
            seen.append(offset)
    return seen


def shift(rows, step, count):
    return [((r, c), (r, (c + step) % count)) for r in rows for c in range(count)]


def left_plan(n_row, n_col, ratio):
    offsets = [left_offsets(row, ratio, n_col) for row in range(n_row)]
    if (n_row, n_col, ratio) != (8, 4, 2):
        perms = []
        for slot in range(max(len(o) for o in offsets)):
            pairs = [
                ((row, (col + offsets[row][slot]) % n_col), (row, col))
                for row in range(n_row)
                for col in range(n_col)
                if slot < len(offsets[row]) and offsets[row][slot] != 0
            ]
            perms.append((0, pairs))
        return perms
    whole = [r for r in range(8) if {1, 2, 3} <= set(offsets[r])]
    once, twice = {-1: [], 1: []}, {-1: [], 1: []}
    for r in range(8):
        for offset, step in ((1, -1), (3, 1)):
            if offset in offsets[r] and r not in whole:
                once[step].append(r)
                if 2 in offsets[r]:
                    twice[step].append(r)
    down = shift([r for r in once[-1] if r != 0], -1, 4) + [((3, c), (3, c - 1)) for c in (1, 2, 3)] + [((3, 0), (0, 0))]
    up = shift(once[1], 1, 4) + shift([0], -1, 4) + [((3, c), (3, c + 1)) for c in (0, 1, 2)] + [((3, 3), (1, 3))]
    again_down = shift(twice[-1], -1, 4) + [((3, 1), (3, 0)), ((3, 2), (3, 1)), ((0, 0), (3, 3))]
    again_up = shift(twice[1], 1, 4) + [((3, 1), (3, 2)), ((3, 2), (3, 3)), ((1, 3), (3, 0))]
    return [(0, down), (0, up), (1, again_down), (2, again_up)]


def right_plan(n_row, n_col, ratio):
    everyone = [(row, col) for row in range(n_row) for col in range(n_col)]
    if (n_row, n_col, ratio) != (8, 4, 2):
        return [
            (0, [(((r + ratio * c + step) % n_row, c), (r, c)) for r, c in everyone if (ratio * c + step) % n_row])
            for step in range(STEPS)
        ]
    first = [(((r + 2 * c) % 8, c), (r, c)) for r, c in everyone if c != 0]
    first += [((r + 1, 0), (r, 0)) for r in range(0, 8, 2)]
    second = [(((r + 2 * c + 2) % 8, c), (r, c)) for r, c in everyone if c != 3]
    second += [((r ^ 1, 3), (r, 3)) for r in range(8)]
    last = [(((r - 1 + 2 * c + 4) % 8, c), (r, c)) for r, c in everyone if r % 2 == 1]
    first_swap = [((r + 1, c), (r, c)) for r, c in everyone if r % 2 == 0 and c != 0]
    second_swap = [((r ^ 1, c), (r, c)) for r, c in everyone if c != 3]
    return [(0, first), (0, second), (0, last), (1, first_swap), (2, second_swap)]


def carry_out(perms, n_row, n_col):
    held = [{(r, c): (r, c) for r in range(n_row) for c in range(n_col)}]
    for source, pairs in perms:
        held.append({dst: held[source][src] for src, dst in pairs})
    return held


def device_table(left_perms, right_perms, n_row, n_col, ratio):
    left_held = carry_out(left_perms, n_row, n_col)
    right_held = carry_out(right_perms, n_row, n_col)
    slots = (ratio - 1 + STEPS - 1) // ratio + 1
    table = np.full((n_row, n_col, 2 * slots + STEPS), -1, np.int32)

    def find(held, device, tile):
        return [i for i, h in enumerate(held) if h.get(device) == tile][0]

    for r in range(n_row):
        for c in range(n_col):
            for slot, offset in enumerate(left_offsets(r, ratio, n_col)):
                tile_col = (c + offset) % n_col
                table[r, c, slot] = find(left_held, (r, c), (r, tile_col))
                table[r, c, slots + STEPS + slot] = (tile_col * ratio - r - ratio * c) % n_row
            for step in range(STEPS):
                table[r, c, slots + step] = find(right_held, (r, c), ((r + ratio * c + step) % n_row, c))
    return table, slots


def fetch(choice, among, bufs, target, sem):
    for number in among:
        @pl.when(choice == number)
        def _():
            pltpu.make_async_copy(bufs[number], target, sem).start()


def join_kernel(cols_ref, data_ref, out_ref, cols, sem):
    rows = data_ref.shape[0]
    data_copy = pltpu.make_async_copy(data_ref, out_ref.at[pl.ds(0, rows)], sem.at[0])
    cols_copy = pltpu.make_async_copy(cols_ref, cols, sem.at[1])
    data_copy.start()
    cols_copy.start()
    out_ref[pl.ds(rows, EXTRA), :] = jnp.zeros((EXTRA, out_ref.shape[1]), jnp.float32)
    cols_copy.wait()
    out_ref[pl.ds(rows, cols.shape[0]), pl.ds(0, cols.shape[1])] = cols[...].astype(jnp.float32)
    data_copy.wait()


def product_kernel(slots, n_row, ratio, rb, w, n_right, among, info_ref, *refs):
    out_ref, left, right, acc, value, cols, coded, scalars, codes, lsem, rsem, osem, csem = refs[-13:]
    right_bufs, left_bufs = refs[:n_right], refs[:1] + refs[n_right:-13]
    rows, width = left.shape[1] - EXTRA, left.shape[2]
    names = pl.ds(rows, EXTRA)
    for slot in range(slots):
        fetch(info_ref[slot], among[slot], [buf.at[names] for buf in left_bufs], cols.at[slot], csem.at[slot])
    for step in range(STEPS):
        at = slots + step
        fetch(info_ref[at], among[at], [buf.at[names] for buf in right_bufs], cols.at[at], csem.at[at])
    for step in range(STEPS):
        fetch(info_ref[slots + step], among[slots + step], right_bufs, right.at[step], rsem.at[step])
    for slot in range(slots):
        fetch(info_ref[slot], among[slot], left_bufs, left.at[slot], lsem.at[slot])

    def clear(first, last):
        @pl.loop(first, last)
        def _(r):
            acc[pl.ds(pl.multiple_of(r * BS, BS), BS), :] = jnp.zeros((BS, acc.shape[1]), jnp.float32)

    clear(0, rb // 4)
    lanes = scalars.shape[1]
    row = lax.broadcasted_iota(jnp.int32, (w, lanes), 1)
    tile_slot = lax.broadcasted_iota(jnp.int32, (w, lanes), 0)
    for slot in range(slots):
        used = info_ref[slot] >= 0

        @pl.when(used)
        def _():
            pltpu.make_async_copy(left_bufs[0].at[names], cols.at[slot], csem.at[slot]).wait()

        inner = cols[slot, 0:w, 0:lanes].astype(jnp.int32)
        valid = (inner >= 0) & (row < rb)
        step = jnp.full(inner.shape, info_ref[slots + STEPS + slot], jnp.int32)
        for _ in range(ratio - 1):
            beyond = inner >= rb
            step = jnp.where(beyond, step + 1, step)
            inner = jnp.where(beyond, inner - rb, inner)
        step = jnp.where(step >= n_row, step - n_row, step)
        code = inner | tile_slot << 8 | slot << 12 | row << 16 | step << 24
        valid = valid & (step < STEPS)
        coded[slot * w : (slot + 1) * w, :] = jnp.where(valid, jnp.where(used, code, -1), -1)
    for step in range(STEPS):
        pltpu.make_async_copy(right_bufs[0].at[names], cols.at[slots + step], csem.at[slots + step]).wait()
        col = cols[slots + step, 0:w, 0:lanes].astype(jnp.int32)
        code = (col >> 1) * 2 * BS | (col & 1) << 16
        coded[(slots + step) * w : (slots + step + 1) * w, :] = jnp.where(col < 0, 2 << 16, code)
    coded[(slots + STEPS) * w : (slots + STEPS + 1) * w, :] = jnp.full((w, lanes), 2 << 16, jnp.int32)
    to_scalars = pltpu.make_async_copy(coded, scalars, csem.at[slots + STEPS])
    to_scalars.start()
    clear(rb // 4, rb)
    to_scalars.wait()

    part_rows = rb // PARTS
    bounds = [jnp.int32(0)]
    for part in range(PARTS):
        def listed(i, place):
            row_codes = [scalars[line, part * part_rows + i] for line in range(slots * w)]
            for code in row_codes:
                codes[place] = code
                place = place + (code >= 0).astype(jnp.int32)
            return place

        bounds.append(lax.fori_loop(0, part_rows, listed, bounds[-1]))
    for u in range(UNROLL):
        codes[bounds[-1] + u] = STEPS << 24

    for step in range(STEPS):
        pltpu.make_async_copy(right_bufs[0], right.at[step], rsem.at[step]).wait()
    for slot in range(slots):
        @pl.when(info_ref[slot] >= 0)
        def _():
            pltpu.make_async_copy(left_bufs[0], left.at[slot], lsem.at[slot]).wait()

    half = lax.broadcasted_iota(jnp.int32, (BS, 2 * BS), 1) // BS

    def block_at(index):
        return pl.ds(pl.multiple_of(index * BS, BS), BS)

    def product(code):
        slot = (code >> 8) & 15
        x = left[(code >> 12) & 15, block_at((code >> 16) & 255), pl.ds(pl.multiple_of((slot >> 1) * 2 * BS, 2 * BS), 2 * BS)]
        both = jnp.where(half == (slot & 1), x, pltpu.roll(x, BS, 1))
        hi = both.astype(jnp.bfloat16)
        lo = (both - hi.astype(jnp.float32)).astype(jnp.bfloat16)
        y = right[code >> 24, block_at(code & 255), :]
        right_hi = y.astype(jnp.bfloat16)
        right_lo = (y - right_hi.astype(jnp.float32)).astype(jnp.bfloat16)
        lhs = jnp.concatenate([hi, lo], axis=0)
        rhs = jnp.concatenate([right_hi, right_lo], axis=0)
        terms = jnp.dot(lhs, rhs, preferred_element_type=jnp.float32)
        return terms[:BS] + terms[BS:]

    def add(code, product):
        rows_at = block_at((code >> 16) & 255)
        for pair in range(w // 2):
            x = product[:, pair * 2 * BS : (pair + 1) * 2 * BS]
            turned = pltpu.roll(x, BS, 1)
            picked, at = [], []
            for side in range(2):
                place = scalars[(slots + (code >> 24)) * w + 2 * pair + side, code & 255]
                parity = place >> 16
                chosen = jnp.where(parity == side, x, turned)
                picked.append(jnp.where(half == parity, chosen, 0.0))
                at.append(place & 0xFFFF)
            picked[1] = jnp.where(at[0] == at[1], picked[0] + picked[1], picked[1])
            spots = [(rows_at, pl.ds(pl.multiple_of(base, 2 * BS), 2 * BS)) for base in at]
            sums = [acc[spot] + part for spot, part in zip(spots, picked)]
            for spot, total in zip(spots, sums):
                acc[spot] = total

    def out_copy(part):
        at = pl.ds(part * part_rows * BS, part_rows * BS)
        return pltpu.make_async_copy(acc.at[at], out_ref.at[at], osem.at[part])

    def products(group):
        for u in range(UNROLL):
            value[u] = product(codes[group * UNROLL + u])

    def sums(group):
        for u in range(UNROLL):
            add(codes[group * UNROLL + u], value[u])

    ends = [(bound + UNROLL - 1) // UNROLL for bound in bounds]
    last = jnp.maximum(ends[-1] - 1, 0)
    products(0)
    for part in range(PARTS):
        @pl.loop(jnp.minimum(ends[part], last), jnp.minimum(ends[part + 1], last))
        def _(group):
            sums(group)
            products(group + 1)

        @pl.when(ends[part + 1] <= last)
        def _():
            out_copy(part).start()
    sums(last)
    for part in range(PARTS):
        @pl.when(ends[part + 1] > last)
        def _():
            out_copy(part).start()
    for part in range(PARTS):
        out_copy(part).wait()


def local(p_cols, p_data):
    n_row, n_col = lax.axis_size("row"), lax.axis_size("col")
    ratio = n_row // n_col
    row_id, col_id = lax.axis_index("row"), lax.axis_index("col")
    rb, w = p_cols.shape
    rows, width = p_data.shape
    left_perms = left_plan(n_row, n_col, ratio)
    right_perms = right_plan(n_row, n_col, ratio)
    table, slots = device_table(left_perms, right_perms, n_row, n_col, ratio)
    info = jnp.asarray(table)[row_id, col_id]

    smem = pl.BlockSpec(memory_space=pltpu.SMEM)
    hbm = pl.BlockSpec(memory_space=pl.ANY)
    dma = pltpu.SemaphoreType.DMA
    own = pl.pallas_call(
        join_kernel,
        out_shape=jax.ShapeDtypeStruct((rows + EXTRA, width), jnp.float32),
        in_specs=[pl.BlockSpec(memory_space=pltpu.HBM)] * 2,
        out_specs=pl.BlockSpec(memory_space=pltpu.VMEM),
        scratch_shapes=[pltpu.VMEM((w, rb), jnp.int32), dma((2,))],
        compiler_params=pltpu.CompilerParams(vmem_limit_bytes=4 << 20),
        cost_estimate=pl.CostEstimate(flops=0, bytes_accessed=2 << 20, transcendentals=0),
    )(p_cols.T, p_data)

    def carry(perms):
        bufs = [own]
        for source, pairs in perms:
            flat = [(s[0] * n_col + s[1], d[0] * n_col + d[1]) for s, d in pairs]
            bufs.append(lax.ppermute(bufs[source], ("row", "col"), flat))
        return bufs

    left_bufs, right_bufs = carry(left_perms), carry(right_perms)
    out_shape = jax.ShapeDtypeStruct((rows, rb * ratio * BS), jnp.float32)
    bufs = right_bufs + left_bufs[1:]
    among = [sorted(set(table[:, :, i].ravel().tolist()) - {-1}) for i in range(slots + STEPS)]
    codings = -(-(slots + STEPS + 1) * w // 8) * 8
    return pl.pallas_call(
        functools.partial(product_kernel, slots, n_row, ratio, rb, w, len(right_bufs), among),
        out_shape=out_shape,
        in_specs=[smem] + [hbm] * len(bufs),
        out_specs=hbm,
        scratch_shapes=[
            pltpu.VMEM((slots, rows + EXTRA, width), jnp.float32),
            pltpu.VMEM((STEPS + 1, rows + EXTRA, width), jnp.float32),
            pltpu.VMEM(out_shape.shape, jnp.float32),
            pltpu.VMEM((UNROLL, BS, width), jnp.float32),
            pltpu.VMEM((slots + STEPS, EXTRA, width), jnp.float32),
            pltpu.VMEM((codings, 128), jnp.int32),
            pltpu.SMEM((codings, 128), jnp.int32),
            pltpu.SMEM((slots * rb * w + 4 * UNROLL,), jnp.int32),
            dma((slots,)),
            dma((STEPS,)),
            dma((PARTS,)),
            dma((slots + STEPS + 1,)),
        ],
        compiler_params=pltpu.CompilerParams(vmem_limit_bytes=18 << 20),
        cost_estimate=pl.CostEstimate(flops=10**9, bytes_accessed=20 << 20, transcendentals=0),
    )(info, *bufs)


def solution(mesh):
    in_specs = (P("row", "col"), P("row", "col"))
    return jax.shard_map(local, mesh=mesh, in_specs=in_specs, out_specs=P("row", "col"), check_vma=False)
```

```python
import functools

import jax
import jax.numpy as jnp
import numpy as np
from jax import lax
from jax.experimental import pallas as pl
from jax.experimental.pallas import tpu as pltpu
from jax.sharding import PartitionSpec as P

BS = 64
STEPS = 4
UNROLL = 8
EXTRA = 8
PARTS = 8


def left_offsets(row, ratio, n_col):
    seen = []
    for step in range(STEPS):
        offset = (row + step) // ratio % n_col
        if offset not in seen:
            seen.append(offset)
    return seen


def shift(rows, step, count):
    return [((r, c), (r, (c + step) % count)) for r in rows for c in range(count)]


def left_plan(n_row, n_col, ratio):
    offsets = [left_offsets(row, ratio, n_col) for row in range(n_row)]
    if (n_row, n_col, ratio) != (8, 4, 2):
        perms = []
        for slot in range(max(len(o) for o in offsets)):
            pairs = [
                ((row, (col + offsets[row][slot]) % n_col), (row, col))
                for row in range(n_row)
                for col in range(n_col)
                if slot < len(offsets[row]) and offsets[row][slot] != 0
            ]
            perms.append((0, pairs))
        return perms
    whole = [r for r in range(8) if {1, 2, 3} <= set(offsets[r])]
    once, twice = {-1: [], 1: []}, {-1: [], 1: []}
    for r in range(8):
        for offset, step in ((1, -1), (3, 1)):
            if offset in offsets[r] and r not in whole:
                once[step].append(r)
                if 2 in offsets[r]:
                    twice[step].append(r)
    down = shift([r for r in once[-1] if r != 0], -1, 4) + [((3, c), (3, c - 1)) for c in (1, 2, 3)] + [((3, 0), (0, 0))]
    up = shift(once[1], 1, 4) + shift([0], -1, 4) + [((3, c), (3, c + 1)) for c in (0, 1, 2)] + [((3, 3), (1, 3))]
    again_down = shift(twice[-1], -1, 4) + [((3, 1), (3, 0)), ((3, 2), (3, 1)), ((0, 0), (3, 3))]
    again_up = shift(twice[1], 1, 4) + [((3, 1), (3, 2)), ((3, 2), (3, 3)), ((1, 3), (3, 0))]
    return [(0, down), (0, up), (1, again_down), (2, again_up)]


def right_plan(n_row, n_col, ratio):
    everyone = [(row, col) for row in range(n_row) for col in range(n_col)]
    if (n_row, n_col, ratio) != (8, 4, 2):
        return [
            (0, [(((r + ratio * c + step) % n_row, c), (r, c)) for r, c in everyone if (ratio * c + step) % n_row])
            for step in range(STEPS)
        ]
    first = [(((r + 2 * c) % 8, c), (r, c)) for r, c in everyone if c != 0]
    first += [((r + 1, 0), (r, 0)) for r in range(0, 8, 2)]
    second = [(((r + 2 * c + 2) % 8, c), (r, c)) for r, c in everyone if c != 3]
    second += [((r ^ 1, 3), (r, 3)) for r in range(8)]
    last = [(((r - 1 + 2 * c + 4) % 8, c), (r, c)) for r, c in everyone if r % 2 == 1]
    first_swap = [((r + 1, c), (r, c)) for r, c in everyone if r % 2 == 0 and c != 0]
    second_swap = [((r ^ 1, c), (r, c)) for r, c in everyone if c != 3]
    return [(0, first), (0, second), (0, last), (1, first_swap), (2, second_swap)]


def carry_out(perms, n_row, n_col):
    held = [{(r, c): (r, c) for r in range(n_row) for c in range(n_col)}]
    for source, pairs in perms:
        held.append({dst: held[source][src] for src, dst in pairs})
    return held


def device_table(left_perms, right_perms, n_row, n_col, ratio):
    left_held = carry_out(left_perms, n_row, n_col)
    right_held = carry_out(right_perms, n_row, n_col)
    slots = (ratio - 1 + STEPS - 1) // ratio + 1
    table = np.full((n_row, n_col, 2 * slots + STEPS), -1, np.int32)

    def find(held, device, tile):
        return [i for i, h in enumerate(held) if h.get(device) == tile][0]

    for r in range(n_row):
        for c in range(n_col):
            for slot, offset in enumerate(left_offsets(r, ratio, n_col)):
                tile_col = (c + offset) % n_col
                table[r, c, slot] = find(left_held, (r, c), (r, tile_col))
                table[r, c, slots + STEPS + slot] = (tile_col * ratio - r - ratio * c) % n_row
            for step in range(STEPS):
                table[r, c, slots + step] = find(right_held, (r, c), ((r + ratio * c + step) % n_row, c))
    return table, slots


def fetch(choice, among, bufs, target, sem):
    for number in among:
        @pl.when(choice == number)
        def _():
            pltpu.make_async_copy(bufs[number], target, sem).start()


def join_kernel(cols_ref, data_ref, out_ref, cols, sem):
    rows = data_ref.shape[0]
    data_copy = pltpu.make_async_copy(data_ref, out_ref.at[pl.ds(0, rows)], sem.at[0])
    cols_copy = pltpu.make_async_copy(cols_ref, cols, sem.at[1])
    data_copy.start()
    cols_copy.start()
    out_ref[pl.ds(rows, EXTRA), :] = jnp.zeros((EXTRA, out_ref.shape[1]), jnp.float32)
    cols_copy.wait()
    out_ref[pl.ds(rows, cols.shape[0]), pl.ds(0, cols.shape[1])] = cols[...].astype(jnp.float32)
    data_copy.wait()


def product_kernel(slots, n_row, ratio, rb, w, n_right, among, info_ref, *refs):
    out_ref, left, right, acc, value, cols, coded, scalars, codes, lsem, rsem, osem, csem = refs[-13:]
    right_bufs, left_bufs = refs[:n_right], refs[:1] + refs[n_right:-13]
    rows, width = left.shape[1] - EXTRA, left.shape[2]
    names = pl.ds(rows, EXTRA)
    for slot in range(slots):
        fetch(info_ref[slot], among[slot], [buf.at[names] for buf in left_bufs], cols.at[slot], csem.at[slot])
    for step in range(STEPS):
        at = slots + step
        fetch(info_ref[at], among[at], [buf.at[names] for buf in right_bufs], cols.at[at], csem.at[at])
    for step in range(STEPS):
        fetch(info_ref[slots + step], among[slots + step], right_bufs, right.at[step], rsem.at[step])
    for slot in range(slots):
        fetch(info_ref[slot], among[slot], left_bufs, left.at[slot], lsem.at[slot])

    def clear(first, last):
        @pl.loop(first, last)
        def _(r):
            acc[pl.ds(pl.multiple_of(r * BS, BS), BS), :] = jnp.zeros((BS, acc.shape[1]), jnp.float32)

    clear(0, rb // 4)
    lanes = scalars.shape[1]
    row = lax.broadcasted_iota(jnp.int32, (w, lanes), 1)
    tile_slot = lax.broadcasted_iota(jnp.int32, (w, lanes), 0)
    for slot in range(slots):
        used = info_ref[slot] >= 0

        @pl.when(used)
        def _():
            pltpu.make_async_copy(left_bufs[0].at[names], cols.at[slot], csem.at[slot]).wait()

        inner = cols[slot, 0:w, 0:lanes].astype(jnp.int32)
        valid = (inner >= 0) & (row < rb)
        step = jnp.full(inner.shape, info_ref[slots + STEPS + slot], jnp.int32)
        for _ in range(ratio - 1):
            beyond = inner >= rb
            step = jnp.where(beyond, step + 1, step)
            inner = jnp.where(beyond, inner - rb, inner)
        step = jnp.where(step >= n_row, step - n_row, step)
        code = inner | tile_slot << 8 | slot << 12 | row << 16 | step << 24
        valid = valid & (step < STEPS)
        coded[slot * w : (slot + 1) * w, :] = jnp.where(valid, jnp.where(used, code, -1), -1)
    for step in range(STEPS):
        pltpu.make_async_copy(right_bufs[0].at[names], cols.at[slots + step], csem.at[slots + step]).wait()
        col = cols[slots + step, 0:w, 0:lanes].astype(jnp.int32)
        code = (col >> 1) * 2 * BS | (col & 1) << 16
        coded[(slots + step) * w : (slots + step + 1) * w, :] = jnp.where(col < 0, 2 << 16, code)
    coded[(slots + STEPS) * w : (slots + STEPS + 1) * w, :] = jnp.full((w, lanes), 2 << 16, jnp.int32)
    to_scalars = pltpu.make_async_copy(coded, scalars, csem.at[slots + STEPS])
    to_scalars.start()
    clear(rb // 4, rb)
    to_scalars.wait()

    part_rows = rb // PARTS
    bounds = [jnp.int32(0)]
    for part in range(PARTS):
        def listed(i, place):
            row_codes = [scalars[line, part * part_rows + i] for line in range(slots * w)]
            for code in row_codes:
                codes[place] = code
                place = place + (code >= 0).astype(jnp.int32)
            return place

        bounds.append(lax.fori_loop(0, part_rows, listed, bounds[-1]))
    for u in range(UNROLL):
        codes[bounds[-1] + u] = STEPS << 24

    for step in range(STEPS):
        pltpu.make_async_copy(right_bufs[0], right.at[step], rsem.at[step]).wait()
    for slot in range(slots):
        @pl.when(info_ref[slot] >= 0)
        def _():
            pltpu.make_async_copy(left_bufs[0], left.at[slot], lsem.at[slot]).wait()

    half = lax.broadcasted_iota(jnp.int32, (BS, 2 * BS), 1) // BS

    def block_at(index):
        return pl.ds(pl.multiple_of(index * BS, BS), BS)

    def product(code):
        slot = (code >> 8) & 15
        x = left[(code >> 12) & 15, block_at((code >> 16) & 255), pl.ds(pl.multiple_of((slot >> 1) * 2 * BS, 2 * BS), 2 * BS)]
        both = jnp.where(half == (slot & 1), x, pltpu.roll(x, BS, 1))
        hi = both.astype(jnp.bfloat16).astype(jnp.float32)
        lhs = jnp.where(half == 0, hi, both - hi).astype(jnp.bfloat16)
        y = right[code >> 24, block_at(code & 255), :]
        hi = y.astype(jnp.bfloat16)
        lo = (y - hi.astype(jnp.float32)).astype(jnp.bfloat16)
        lhs = jnp.concatenate([lhs, lhs], axis=1)
        rhs = jnp.concatenate([hi, hi, lo, lo], axis=0)
        return jnp.dot(lhs, rhs, preferred_element_type=jnp.float32)

    def add(code, product):
        rows_at = block_at((code >> 16) & 255)
        for pair in range(w // 2):
            x = product[:, pair * 2 * BS : (pair + 1) * 2 * BS]
            turned = pltpu.roll(x, BS, 1)
            picked, at = [], []
            for side in range(2):
                place = scalars[(slots + (code >> 24)) * w + 2 * pair + side, code & 255]
                parity = place >> 16
                chosen = jnp.where(parity == side, x, turned)
                picked.append(jnp.where(half == parity, chosen, 0.0))
                at.append(place & 0xFFFF)
            picked[1] = jnp.where(at[0] == at[1], picked[0] + picked[1], picked[1])
            spots = [(rows_at, pl.ds(pl.multiple_of(base, 2 * BS), 2 * BS)) for base in at]
            sums = [acc[spot] + part for spot, part in zip(spots, picked)]
            for spot, total in zip(spots, sums):
                acc[spot] = total

    def out_copy(part):
        at = pl.ds(part * part_rows * BS, part_rows * BS)
        return pltpu.make_async_copy(acc.at[at], out_ref.at[at], osem.at[part])

    def products(group):
        for u in range(UNROLL):
            value[u] = product(codes[group * UNROLL + u])

    def sums(group):
        for u in range(UNROLL):
            add(codes[group * UNROLL + u], value[u])

    ends = [(bound + UNROLL - 1) // UNROLL for bound in bounds]
    last = jnp.maximum(ends[-1] - 1, 0)
    products(0)
    for part in range(PARTS):
        @pl.loop(jnp.minimum(ends[part], last), jnp.minimum(ends[part + 1], last))
        def _(group):
            sums(group)
            products(group + 1)

        @pl.when(ends[part + 1] <= last)
        def _():
            out_copy(part).start()
    sums(last)
    for part in range(PARTS):
        @pl.when(ends[part + 1] > last)
        def _():
            out_copy(part).start()
    for part in range(PARTS):
        out_copy(part).wait()


def local(p_cols, p_data):
    n_row, n_col = lax.axis_size("row"), lax.axis_size("col")
    ratio = n_row // n_col
    row_id, col_id = lax.axis_index("row"), lax.axis_index("col")
    rb, w = p_cols.shape
    rows, width = p_data.shape
    left_perms = left_plan(n_row, n_col, ratio)
    right_perms = right_plan(n_row, n_col, ratio)
    table, slots = device_table(left_perms, right_perms, n_row, n_col, ratio)
    info = jnp.asarray(table)[row_id, col_id]

    smem = pl.BlockSpec(memory_space=pltpu.SMEM)
    hbm = pl.BlockSpec(memory_space=pl.ANY)
    dma = pltpu.SemaphoreType.DMA
    own = pl.pallas_call(
        join_kernel,
        out_shape=jax.ShapeDtypeStruct((rows + EXTRA, width), jnp.float32),
        in_specs=[pl.BlockSpec(memory_space=pltpu.HBM)] * 2,
        out_specs=pl.BlockSpec(memory_space=pltpu.VMEM),
        scratch_shapes=[pltpu.VMEM((w, rb), jnp.int32), dma((2,))],
        compiler_params=pltpu.CompilerParams(vmem_limit_bytes=4 << 20),
        cost_estimate=pl.CostEstimate(flops=0, bytes_accessed=2 << 20, transcendentals=0),
    )(p_cols.T, p_data)

    def carry(perms):
        bufs = [own]
        for source, pairs in perms:
            flat = [(s[0] * n_col + s[1], d[0] * n_col + d[1]) for s, d in pairs]
            bufs.append(lax.ppermute(bufs[source], ("row", "col"), flat))
        return bufs

    left_bufs, right_bufs = carry(left_perms), carry(right_perms)
    out_shape = jax.ShapeDtypeStruct((rows, rb * ratio * BS), jnp.float32)
    bufs = right_bufs + left_bufs[1:]
    among = [sorted(set(table[:, :, i].ravel().tolist()) - {-1}) for i in range(slots + STEPS)]
    codings = -(-(slots + STEPS + 1) * w // 8) * 8
    return pl.pallas_call(
        functools.partial(product_kernel, slots, n_row, ratio, rb, w, len(right_bufs), among),
        out_shape=out_shape,
        in_specs=[smem] + [hbm] * len(bufs),
        out_specs=hbm,
        scratch_shapes=[
            pltpu.VMEM((slots, rows + EXTRA, width), jnp.float32),
            pltpu.VMEM((STEPS + 1, rows + EXTRA, width), jnp.float32),
            pltpu.VMEM(out_shape.shape, jnp.float32),
            pltpu.VMEM((UNROLL, BS, width), jnp.float32),
            pltpu.VMEM((slots + STEPS, EXTRA, width), jnp.float32),
            pltpu.VMEM((codings, 128), jnp.int32),
            pltpu.SMEM((codings, 128), jnp.int32),
            pltpu.SMEM((slots * rb * w + 4 * UNROLL,), jnp.int32),
            dma((slots,)),
            dma((STEPS,)),
            dma((PARTS,)),
            dma((slots + STEPS + 1,)),
        ],
        compiler_params=pltpu.CompilerParams(vmem_limit_bytes=18 << 20),
        cost_estimate=pl.CostEstimate(flops=10**9, bytes_accessed=20 << 20, transcendentals=0),
    )(info, *bufs)


def solution(mesh):
    in_specs = (P("row", "col"), P("row", "col"))
    return jax.shard_map(local, mesh=mesh, in_specs=in_specs, out_specs=P("row", "col"), check_vma=False)
```

```python
import functools

import jax
import jax.numpy as jnp
import numpy as np
from jax import lax
from jax.experimental import pallas as pl
from jax.experimental.pallas import tpu as pltpu
from jax.sharding import PartitionSpec as P

BS = 64
STEPS = 4
UNROLL = 8
EXTRA = 8
PARTS = 8


def left_offsets(row, ratio, n_col):
    seen = []
    for step in range(STEPS):
        offset = (row + step) // ratio % n_col
        if offset not in seen:
            seen.append(offset)
    return seen


def shift(rows, step, count):
    return [((r, c), (r, (c + step) % count)) for r in rows for c in range(count)]


def left_plan(n_row, n_col, ratio):
    offsets = [left_offsets(row, ratio, n_col) for row in range(n_row)]
    if (n_row, n_col, ratio) != (8, 4, 2):
        perms = []
        for slot in range(max(len(o) for o in offsets)):
            pairs = [
                ((row, (col + offsets[row][slot]) % n_col), (row, col))
                for row in range(n_row)
                for col in range(n_col)
                if slot < len(offsets[row]) and offsets[row][slot] != 0
            ]
            perms.append((0, pairs))
        return perms
    whole = [r for r in range(8) if {1, 2, 3} <= set(offsets[r])]
    once, twice = {-1: [], 1: []}, {-1: [], 1: []}
    for r in range(8):
        for offset, step in ((1, -1), (3, 1)):
            if offset in offsets[r] and r not in whole:
                once[step].append(r)
                if 2 in offsets[r]:
                    twice[step].append(r)
    down = shift([r for r in once[-1] if r != 0], -1, 4) + [((3, c), (3, c - 1)) for c in (1, 2, 3)] + [((3, 0), (0, 0))]
    up = shift(once[1], 1, 4) + shift([0], -1, 4) + [((3, c), (3, c + 1)) for c in (0, 1, 2)] + [((3, 3), (1, 3))]
    again_down = shift(twice[-1], -1, 4) + [((3, 1), (3, 0)), ((3, 2), (3, 1)), ((0, 0), (3, 3))]
    again_up = shift(twice[1], 1, 4) + [((3, 1), (3, 2)), ((3, 2), (3, 3)), ((1, 3), (3, 0))]
    return [(0, down), (0, up), (1, again_down), (2, again_up)]


def right_plan(n_row, n_col, ratio):
    everyone = [(row, col) for row in range(n_row) for col in range(n_col)]
    if (n_row, n_col, ratio) != (8, 4, 2):
        return [
            (0, [(((r + ratio * c + step) % n_row, c), (r, c)) for r, c in everyone if (ratio * c + step) % n_row])
            for step in range(STEPS)
        ]
    first = [(((r + 2 * c) % 8, c), (r, c)) for r, c in everyone if c != 0]
    first += [((r + 1, 0), (r, 0)) for r in range(0, 8, 2)]
    second = [(((r + 2 * c + 2) % 8, c), (r, c)) for r, c in everyone if c != 3]
    second += [((r ^ 1, 3), (r, 3)) for r in range(8)]
    last = [(((r - 1 + 2 * c + 4) % 8, c), (r, c)) for r, c in everyone if r % 2 == 1]
    first_swap = [((r + 1, c), (r, c)) for r, c in everyone if r % 2 == 0 and c != 0]
    second_swap = [((r ^ 1, c), (r, c)) for r, c in everyone if c != 3]
    return [(0, first), (0, second), (0, last), (1, first_swap), (2, second_swap)]


def carry_out(perms, n_row, n_col):
    held = [{(r, c): (r, c) for r in range(n_row) for c in range(n_col)}]
    for source, pairs in perms:
        held.append({dst: held[source][src] for src, dst in pairs})
    return held


def device_table(left_perms, right_perms, n_row, n_col, ratio):
    left_held = carry_out(left_perms, n_row, n_col)
    right_held = carry_out(right_perms, n_row, n_col)
    slots = (ratio - 1 + STEPS - 1) // ratio + 1
    table = np.full((n_row, n_col, 2 * slots + STEPS), -1, np.int32)

    def find(held, device, tile):
        return [i for i, h in enumerate(held) if h.get(device) == tile][0]

    for r in range(n_row):
        for c in range(n_col):
            for slot, offset in enumerate(left_offsets(r, ratio, n_col)):
                tile_col = (c + offset) % n_col
                table[r, c, slot] = find(left_held, (r, c), (r, tile_col))
                table[r, c, slots + STEPS + slot] = (tile_col * ratio - r - ratio * c) % n_row
            for step in range(STEPS):
                table[r, c, slots + step] = find(right_held, (r, c), ((r + ratio * c + step) % n_row, c))
    return table, slots


def fetch(choice, among, bufs, target, sem):
    for number in among:
        @pl.when(choice == number)
        def _():
            pltpu.make_async_copy(bufs[number], target, sem).start()


def join_kernel(cols_ref, data_ref, out_ref, cols, sem):
    rows = data_ref.shape[0]
    data_copy = pltpu.make_async_copy(data_ref, out_ref.at[pl.ds(0, rows)], sem.at[0])
    cols_copy = pltpu.make_async_copy(cols_ref, cols, sem.at[1])
    data_copy.start()
    cols_copy.start()
    out_ref[pl.ds(rows, EXTRA), :] = jnp.zeros((EXTRA, out_ref.shape[1]), jnp.float32)
    cols_copy.wait()
    out_ref[pl.ds(rows, cols.shape[0]), pl.ds(0, cols.shape[1])] = cols[...].astype(jnp.float32)
    data_copy.wait()


def product_kernel(slots, n_row, ratio, rb, w, n_right, among, info_ref, *refs):
    out_ref, left, right, acc, value, cols, coded, scalars, codes, ends, lsem, rsem, osem, csem = refs[-14:]
    right_bufs, left_bufs = refs[:n_right], refs[:1] + refs[n_right:-14]
    rows, width = left.shape[1] - EXTRA, left.shape[2]
    names = pl.ds(rows, EXTRA)
    for slot in range(slots):
        fetch(info_ref[slot], among[slot], [buf.at[names] for buf in left_bufs], cols.at[slot], csem.at[slot])
    for step in range(STEPS):
        at = slots + step
        fetch(info_ref[at], among[at], [buf.at[names] for buf in right_bufs], cols.at[at], csem.at[at])
    for step in range(STEPS):
        fetch(info_ref[slots + step], among[slots + step], right_bufs, right.at[step], rsem.at[step])
    for slot in range(slots):
        fetch(info_ref[slot], among[slot], left_bufs, left.at[slot], lsem.at[slot])

    def clear(first, last):
        @pl.loop(first, last)
        def _(r):
            acc[pl.ds(pl.multiple_of(r * BS, BS), BS), :] = jnp.zeros((BS, acc.shape[1]), jnp.float32)

    clear(0, rb // 4)
    lanes = scalars.shape[1]
    row = lax.broadcasted_iota(jnp.int32, (w, lanes), 1)
    tile_slot = lax.broadcasted_iota(jnp.int32, (w, lanes), 0)
    for slot in range(slots):
        used = info_ref[slot] >= 0

        @pl.when(used)
        def _():
            pltpu.make_async_copy(left_bufs[0].at[names], cols.at[slot], csem.at[slot]).wait()

        inner = cols[slot, 0:w, 0:lanes].astype(jnp.int32)
        valid = (inner >= 0) & (row < rb)
        step = jnp.full(inner.shape, info_ref[slots + STEPS + slot], jnp.int32)
        for _ in range(ratio - 1):
            beyond = inner >= rb
            step = jnp.where(beyond, step + 1, step)
            inner = jnp.where(beyond, inner - rb, inner)
        step = jnp.where(step >= n_row, step - n_row, step)
        code = inner | tile_slot << 8 | slot << 12 | row << 16 | step << 24
        valid = valid & (step < STEPS)
        coded[slot * w : (slot + 1) * w, :] = jnp.where(valid, jnp.where(used, code, -1), -1)
    for step in range(STEPS):
        pltpu.make_async_copy(right_bufs[0].at[names], cols.at[slots + step], csem.at[slots + step]).wait()
        col = cols[slots + step, 0:w, 0:lanes].astype(jnp.int32)
        code = (col >> 1) * 2 * BS | (col & 1) << 16
        coded[(slots + step) * w : (slots + step + 1) * w, :] = jnp.where(col < 0, 2 << 16, code)
    coded[(slots + STEPS) * w : (slots + STEPS + 1) * w, :] = jnp.full((w, lanes), 2 << 16, jnp.int32)
    to_scalars = pltpu.make_async_copy(coded, scalars, csem.at[slots + STEPS])
    to_scalars.start()
    clear(rb // 4, rb)
    to_scalars.wait()

    part_rows = rb // PARTS

    def listed(row, place):
        for code in [scalars[line, row] for line in range(slots * w)]:
            codes[place] = code
            place = place + (code >= 0).astype(jnp.int32)
        ends[row] = (place + UNROLL - 1) // UNROLL
        return place

    listed_end = lax.fori_loop(0, rb, listed, jnp.int32(0))
    for u in range(UNROLL):
        codes[listed_end + u] = STEPS << 24

    for step in range(STEPS):
        pltpu.make_async_copy(right_bufs[0], right.at[step], rsem.at[step]).wait()
    for slot in range(slots):
        @pl.when(info_ref[slot] >= 0)
        def _():
            pltpu.make_async_copy(left_bufs[0], left.at[slot], lsem.at[slot]).wait()

    half = lax.broadcasted_iota(jnp.int32, (BS, 2 * BS), 1) // BS

    def block_at(index):
        return pl.ds(pl.multiple_of(index * BS, BS), BS)

    def product(code):
        slot = (code >> 8) & 15
        x = left[(code >> 12) & 15, block_at((code >> 16) & 255), pl.ds(pl.multiple_of((slot >> 1) * 2 * BS, 2 * BS), 2 * BS)]
        both = jnp.where(half == (slot & 1), x, pltpu.roll(x, BS, 1))
        hi = both.astype(jnp.bfloat16).astype(jnp.float32)
        lhs = jnp.where(half == 0, hi, both - hi).astype(jnp.bfloat16)
        y = right[code >> 24, block_at(code & 255), :]
        hi = y.astype(jnp.bfloat16)
        lo = (y - hi.astype(jnp.float32)).astype(jnp.bfloat16)
        lhs = jnp.concatenate([lhs, lhs], axis=1)
        rhs = jnp.concatenate([hi, hi, lo, lo], axis=0)
        return jnp.dot(lhs, rhs, preferred_element_type=jnp.float32)

    def add(code, product):
        rows_at = block_at((code >> 16) & 255)
        for pair in range(w // 2):
            x = product[:, pair * 2 * BS : (pair + 1) * 2 * BS]
            turned = pltpu.roll(x, BS, 1)
            picked, at = [], []
            for side in range(2):
                place = scalars[(slots + (code >> 24)) * w + 2 * pair + side, code & 255]
                parity = place >> 16
                chosen = jnp.where(parity == side, x, turned)
                picked.append(jnp.where(half == parity, chosen, 0.0))
                at.append(place & 0xFFFF)
            picked[1] = jnp.where(at[0] == at[1], picked[0] + picked[1], picked[1])
            spots = [(rows_at, pl.ds(pl.multiple_of(base, 2 * BS), 2 * BS)) for base in at]
            sums = [acc[spot] + part for spot, part in zip(spots, picked)]
            for spot, total in zip(spots, sums):
                acc[spot] = total

    def out_copy(part):
        at = pl.ds(part * part_rows * BS, part_rows * BS)
        return pltpu.make_async_copy(acc.at[at], out_ref.at[at], osem.at[part])

    def products(group):
        for u in range(UNROLL):
            value[u] = product(codes[group * UNROLL + u])

    def sums(group):
        for u in range(UNROLL):
            add(codes[group * UNROLL + u], value[u])

    last = jnp.maximum(ends[rb - 1] - 1, 0)

    def leave(group):
        for part in range(PARTS):
            @pl.when(jnp.maximum(ends[(part + 1) * part_rows - 1] - 1, 0) == group)
            def _():
                out_copy(part).start()

    products(0)

    @pl.loop(0, last)
    def _(group):
        sums(group)
        products(group + 1)
        leave(group)

    sums(last)
    leave(last)
    for part in range(PARTS):
        out_copy(part).wait()


def local(p_cols, p_data):
    n_row, n_col = lax.axis_size("row"), lax.axis_size("col")
    ratio = n_row // n_col
    row_id, col_id = lax.axis_index("row"), lax.axis_index("col")
    rb, w = p_cols.shape
    rows, width = p_data.shape
    left_perms = left_plan(n_row, n_col, ratio)
    right_perms = right_plan(n_row, n_col, ratio)
    table, slots = device_table(left_perms, right_perms, n_row, n_col, ratio)
    info = jnp.asarray(table)[row_id, col_id]

    smem = pl.BlockSpec(memory_space=pltpu.SMEM)
    hbm = pl.BlockSpec(memory_space=pl.ANY)
    dma = pltpu.SemaphoreType.DMA
    own = pl.pallas_call(
        join_kernel,
        out_shape=jax.ShapeDtypeStruct((rows + EXTRA, width), jnp.float32),
        in_specs=[pl.BlockSpec(memory_space=pltpu.HBM)] * 2,
        out_specs=pl.BlockSpec(memory_space=pltpu.VMEM),
        scratch_shapes=[pltpu.VMEM((w, rb), jnp.int32), dma((2,))],
        compiler_params=pltpu.CompilerParams(vmem_limit_bytes=4 << 20),
        cost_estimate=pl.CostEstimate(flops=0, bytes_accessed=2 << 20, transcendentals=0),
    )(p_cols.T, p_data)

    def carry(perms):
        bufs = [own]
        for source, pairs in perms:
            flat = [(s[0] * n_col + s[1], d[0] * n_col + d[1]) for s, d in pairs]
            bufs.append(lax.ppermute(bufs[source], ("row", "col"), flat))
        return bufs

    left_bufs, right_bufs = carry(left_perms), carry(right_perms)
    out_shape = jax.ShapeDtypeStruct((rows, rb * ratio * BS), jnp.float32)
    bufs = right_bufs + left_bufs[1:]
    among = [sorted(set(table[:, :, i].ravel().tolist()) - {-1}) for i in range(slots + STEPS)]
    codings = -(-(slots + STEPS + 1) * w // 8) * 8
    return pl.pallas_call(
        functools.partial(product_kernel, slots, n_row, ratio, rb, w, len(right_bufs), among),
        out_shape=out_shape,
        in_specs=[smem] + [hbm] * len(bufs),
        out_specs=hbm,
        scratch_shapes=[
            pltpu.VMEM((slots, rows + EXTRA, width), jnp.float32),
            pltpu.VMEM((STEPS + 1, rows + EXTRA, width), jnp.float32),
            pltpu.VMEM(out_shape.shape, jnp.float32),
            pltpu.VMEM((UNROLL, BS, width), jnp.float32),
            pltpu.VMEM((slots + STEPS, EXTRA, width), jnp.float32),
            pltpu.VMEM((codings, 128), jnp.int32),
            pltpu.SMEM((codings, 128), jnp.int32),
            pltpu.SMEM((slots * rb * w + UNROLL,), jnp.int32),
            pltpu.SMEM((rb,), jnp.int32),
            dma((slots,)),
            dma((STEPS,)),
            dma((PARTS,)),
            dma((slots + STEPS + 1,)),
        ],
        compiler_params=pltpu.CompilerParams(vmem_limit_bytes=18 << 20),
        cost_estimate=pl.CostEstimate(flops=10**9, bytes_accessed=20 << 20, transcendentals=0),
    )(info, *bufs)


def solution(mesh):
    in_specs = (P("row", "col"), P("row", "col"))
    return jax.shard_map(local, mesh=mesh, in_specs=in_specs, out_specs=P("row", "col"), check_vma=False)
```

```python
import functools

import jax
import jax.numpy as jnp
import numpy as np
from jax import lax
from jax.experimental import pallas as pl
from jax.experimental.pallas import tpu as pltpu
from jax.sharding import PartitionSpec as P

BS = 64
STEPS = 4
UNROLL = 8
EXTRA = 8
PARTS = 8


def left_offsets(row, ratio, n_col):
    seen = []
    for step in range(STEPS):
        offset = (row + step) // ratio % n_col
        if offset not in seen:
            seen.append(offset)
    return seen


def shift(rows, step, count):
    return [((r, c), (r, (c + step) % count)) for r in rows for c in range(count)]


def left_plan(n_row, n_col, ratio):
    offsets = [left_offsets(row, ratio, n_col) for row in range(n_row)]
    if (n_row, n_col, ratio) != (8, 4, 2):
        perms = []
        for slot in range(max(len(o) for o in offsets)):
            pairs = [
                ((row, (col + offsets[row][slot]) % n_col), (row, col))
                for row in range(n_row)
                for col in range(n_col)
                if slot < len(offsets[row]) and offsets[row][slot] != 0
            ]
            perms.append((0, pairs))
        return perms
    whole = [r for r in range(8) if {1, 2, 3} <= set(offsets[r])]
    once, twice = {-1: [], 1: []}, {-1: [], 1: []}
    for r in range(8):
        for offset, step in ((1, -1), (3, 1)):
            if offset in offsets[r] and r not in whole:
                once[step].append(r)
                if 2 in offsets[r]:
                    twice[step].append(r)
    down = shift([r for r in once[-1] if r != 0], -1, 4) + [((3, c), (3, c - 1)) for c in (1, 2, 3)] + [((3, 0), (0, 0))]
    up = shift(once[1], 1, 4) + shift([0], -1, 4) + [((3, c), (3, c + 1)) for c in (0, 1, 2)] + [((3, 3), (1, 3))]
    again_down = shift(twice[-1], -1, 4) + [((3, 1), (3, 0)), ((3, 2), (3, 1)), ((0, 0), (3, 3))]
    again_up = shift(twice[1], 1, 4) + [((3, 1), (3, 2)), ((3, 2), (3, 3)), ((1, 3), (3, 0))]
    return [(0, down), (0, up), (1, again_down), (2, again_up)]


def right_plan(n_row, n_col, ratio):
    everyone = [(row, col) for row in range(n_row) for col in range(n_col)]
    if (n_row, n_col, ratio) != (8, 4, 2):
        return [
            (0, [(((r + ratio * c + step) % n_row, c), (r, c)) for r, c in everyone if (ratio * c + step) % n_row])
            for step in range(STEPS)
        ]
    first = [(((r + 2 * c) % 8, c), (r, c)) for r, c in everyone if c != 0]
    first += [((r + 1, 0), (r, 0)) for r in range(0, 8, 2)]
    second = [(((r + 2 * c + 2) % 8, c), (r, c)) for r, c in everyone if c != 3]
    second += [((r ^ 1, 3), (r, 3)) for r in range(8)]
    last = [(((r - 1 + 2 * c + 4) % 8, c), (r, c)) for r, c in everyone if r % 2 == 1]
    first_swap = [((r + 1, c), (r, c)) for r, c in everyone if r % 2 == 0 and c != 0]
    second_swap = [((r ^ 1, c), (r, c)) for r, c in everyone if c != 3]
    return [(0, first), (0, second), (0, last), (1, first_swap), (2, second_swap)]


def carry_out(perms, n_row, n_col):
    held = [{(r, c): (r, c) for r in range(n_row) for c in range(n_col)}]
    for source, pairs in perms:
        held.append({dst: held[source][src] for src, dst in pairs})
    return held


def device_table(left_perms, right_perms, n_row, n_col, ratio):
    left_held = carry_out(left_perms, n_row, n_col)
    right_held = carry_out(right_perms, n_row, n_col)
    slots = (ratio - 1 + STEPS - 1) // ratio + 1
    table = np.full((n_row, n_col, 2 * slots + STEPS), -1, np.int32)

    def find(held, device, tile):
        return [i for i, h in enumerate(held) if h.get(device) == tile][0]

    for r in range(n_row):
        for c in range(n_col):
            for slot, offset in enumerate(left_offsets(r, ratio, n_col)):
                tile_col = (c + offset) % n_col
                table[r, c, slot] = find(left_held, (r, c), (r, tile_col))
                table[r, c, slots + STEPS + slot] = (tile_col * ratio - r - ratio * c) % n_row
            for step in range(STEPS):
                table[r, c, slots + step] = find(right_held, (r, c), ((r + ratio * c + step) % n_row, c))
    return table, slots


def fetch(choice, among, bufs, target, sem):
    for number in among:
        @pl.when(choice == number)
        def _():
            pltpu.make_async_copy(bufs[number], target, sem).start()


def join_kernel(cols_ref, data_ref, out_ref, cols, sem):
    rows = data_ref.shape[0]
    data_copy = pltpu.make_async_copy(data_ref, out_ref.at[pl.ds(0, rows)], sem.at[0])
    cols_copy = pltpu.make_async_copy(cols_ref, cols, sem.at[1])
    data_copy.start()
    cols_copy.start()
    out_ref[pl.ds(rows, EXTRA), :] = jnp.zeros((EXTRA, out_ref.shape[1]), jnp.float32)
    cols_copy.wait()
    out_ref[pl.ds(rows, cols.shape[0]), pl.ds(0, cols.shape[1])] = cols[...].astype(jnp.float32)
    data_copy.wait()


def product_kernel(slots, n_row, ratio, rb, w, n_right, among, info_ref, *refs):
    out_ref, left, right, acc, value, cols, coded, scalars, codes, ends, lsem, rsem, osem, csem = refs[-14:]
    right_bufs, left_bufs = refs[:n_right], refs[:1] + refs[n_right:-14]
    rows, width = left.shape[1] - EXTRA, left.shape[2]
    names = pl.ds(rows, EXTRA)
    for slot in range(slots):
        fetch(info_ref[slot], among[slot], [buf.at[names] for buf in left_bufs], cols.at[slot], csem.at[slot])
    for step in range(STEPS):
        at = slots + step
        fetch(info_ref[at], among[at], [buf.at[names] for buf in right_bufs], cols.at[at], csem.at[at])
    for step in range(STEPS):
        fetch(info_ref[slots + step], among[slots + step], right_bufs, right.at[step], rsem.at[step])
    for slot in range(slots):
        fetch(info_ref[slot], among[slot], left_bufs, left.at[slot], lsem.at[slot])

    def clear(first, last):
        @pl.loop(first, last)
        def _(r):
            acc[pl.ds(pl.multiple_of(r * BS, BS), BS), :] = jnp.zeros((BS, acc.shape[1]), jnp.float32)

    clear(0, rb // 4)
    lanes = scalars.shape[1]
    row = lax.broadcasted_iota(jnp.int32, (w, lanes), 1)
    tile_slot = lax.broadcasted_iota(jnp.int32, (w, lanes), 0)
    for slot in range(slots):
        used = info_ref[slot] >= 0

        @pl.when(used)
        def _():
            pltpu.make_async_copy(left_bufs[0].at[names], cols.at[slot], csem.at[slot]).wait()

        inner = cols[slot, 0:w, 0:lanes].astype(jnp.int32)
        valid = (inner >= 0) & (row < rb)
        step = jnp.full(inner.shape, info_ref[slots + STEPS + slot], jnp.int32)
        for _ in range(ratio - 1):
            beyond = inner >= rb
            step = jnp.where(beyond, step + 1, step)
            inner = jnp.where(beyond, inner - rb, inner)
        step = jnp.where(step >= n_row, step - n_row, step)
        code = inner | tile_slot << 8 | slot << 12 | row << 16 | step << 24
        valid = valid & (step < STEPS)
        coded[slot * w : (slot + 1) * w, :] = jnp.where(valid, jnp.where(used, code, -1), -1)
    for step in range(STEPS):
        pltpu.make_async_copy(right_bufs[0].at[names], cols.at[slots + step], csem.at[slots + step]).wait()
        col = cols[slots + step, 0:w, 0:lanes].astype(jnp.int32)
        code = (col >> 1) * 2 * BS | (col & 1) << 16
        coded[(slots + step) * w : (slots + step + 1) * w, :] = jnp.where(col < 0, 2 << 16, code)
    coded[(slots + STEPS) * w : (slots + STEPS + 1) * w, :] = jnp.full((w, lanes), 2 << 16, jnp.int32)
    to_scalars = pltpu.make_async_copy(coded, scalars, csem.at[slots + STEPS])
    to_scalars.start()
    clear(rb // 4, rb)
    to_scalars.wait()

    part_rows = rb // PARTS

    def listed(row, place):
        for code in [scalars[line, row] for line in range(slots * w)]:
            codes[place] = code
            place = place + (code >= 0).astype(jnp.int32)
        ends[row] = (place + UNROLL - 1) // UNROLL
        return place

    listed_end = lax.fori_loop(0, rb, listed, jnp.int32(0))
    for u in range(UNROLL):
        codes[listed_end + u] = STEPS << 24

    for step in range(STEPS):
        pltpu.make_async_copy(right_bufs[0], right.at[step], rsem.at[step]).wait()
    for slot in range(slots):
        @pl.when(info_ref[slot] >= 0)
        def _():
            pltpu.make_async_copy(left_bufs[0], left.at[slot], lsem.at[slot]).wait()

    half = lax.broadcasted_iota(jnp.int32, (8, 2 * BS), 1) // BS

    def block_at(index):
        return pl.ds(pl.multiple_of(index * BS, BS), BS)

    def in_half(side, kept, other):
        tall = lambda x: x.reshape(BS // 8, 8, 2 * BS) if jnp.ndim(x) else x
        return jnp.where((half == side)[None], tall(kept), tall(other)).reshape(BS, 2 * BS)

    def product(code):
        slot = (code >> 8) & 15
        x = left[(code >> 12) & 15, block_at((code >> 16) & 255), pl.ds(pl.multiple_of((slot >> 1) * 2 * BS, 2 * BS), 2 * BS)]
        both = in_half(slot & 1, x, pltpu.roll(x, BS, 1))
        hi = both.astype(jnp.bfloat16).astype(jnp.float32)
        lhs = in_half(0, hi, both - hi).astype(jnp.bfloat16)
        y = right[code >> 24, block_at(code & 255), :]
        hi = y.astype(jnp.bfloat16)
        lo = (y - hi.astype(jnp.float32)).astype(jnp.bfloat16)
        lhs = jnp.concatenate([lhs, lhs], axis=1)
        rhs = jnp.concatenate([hi, hi, lo, lo], axis=0)
        return jnp.dot(lhs, rhs, preferred_element_type=jnp.float32)

    def add(code, u):
        rows_at = block_at((code >> 16) & 255)
        for pair in range(w // 2):
            lanes_at = pl.ds(pair * 2 * BS, 2 * BS)
            picked, at = [], []
            for side in range(2):
                place = scalars[(slots + (code >> 24)) * w + 2 * pair + side, code & 255]
                parity = place >> 16
                picked.append(in_half(parity, value[u, (parity ^ side) & 1, :, lanes_at], 0.0))
                at.append(place & 0xFFFF)
            picked[1] = jnp.where(at[0] == at[1], picked[0] + picked[1], picked[1])
            spots = [(rows_at, pl.ds(pl.multiple_of(base, 2 * BS), 2 * BS)) for base in at]
            sums = [acc[spot] + part for spot, part in zip(spots, picked)]
            for spot, total in zip(spots, sums):
                acc[spot] = total

    def out_copy(part):
        at = pl.ds(part * part_rows * BS, part_rows * BS)
        return pltpu.make_async_copy(acc.at[at], out_ref.at[at], osem.at[part])

    def products(group):
        for u in range(UNROLL):
            result = product(codes[group * UNROLL + u])
            value[u, 0] = result
            for pair in range(w // 2):
                lanes_at = slice(pair * 2 * BS, (pair + 1) * 2 * BS)
                value[u, 1, :, lanes_at] = pltpu.roll(result[:, lanes_at], BS, 1)

    def sums(group):
        for u in range(UNROLL):
            add(codes[group * UNROLL + u], u)

    last = jnp.maximum(ends[rb - 1] - 1, 0)

    def leave(group):
        for part in range(PARTS):
            @pl.when(jnp.maximum(ends[(part + 1) * part_rows - 1] - 1, 0) == group)
            def _():
                out_copy(part).start()

    products(0)

    @pl.loop(0, last)
    def _(group):
        sums(group)
        products(group + 1)
        leave(group)

    sums(last)
    leave(last)
    for part in range(PARTS):
        out_copy(part).wait()


def local(p_cols, p_data):
    n_row, n_col = lax.axis_size("row"), lax.axis_size("col")
    ratio = n_row // n_col
    row_id, col_id = lax.axis_index("row"), lax.axis_index("col")
    rb, w = p_cols.shape
    rows, width = p_data.shape
    left_perms = left_plan(n_row, n_col, ratio)
    right_perms = right_plan(n_row, n_col, ratio)
    table, slots = device_table(left_perms, right_perms, n_row, n_col, ratio)
    info = jnp.asarray(table)[row_id, col_id]

    smem = pl.BlockSpec(memory_space=pltpu.SMEM)
    hbm = pl.BlockSpec(memory_space=pl.ANY)
    dma = pltpu.SemaphoreType.DMA
    own = pl.pallas_call(
        join_kernel,
        out_shape=jax.ShapeDtypeStruct((rows + EXTRA, width), jnp.float32),
        in_specs=[pl.BlockSpec(memory_space=pltpu.HBM)] * 2,
        out_specs=pl.BlockSpec(memory_space=pltpu.VMEM),
        scratch_shapes=[pltpu.VMEM((w, rb), jnp.int32), dma((2,))],
        compiler_params=pltpu.CompilerParams(vmem_limit_bytes=4 << 20),
        cost_estimate=pl.CostEstimate(flops=0, bytes_accessed=2 << 20, transcendentals=0),
    )(p_cols.T, p_data)

    def carry(perms):
        bufs = [own]
        for source, pairs in perms:
            flat = [(s[0] * n_col + s[1], d[0] * n_col + d[1]) for s, d in pairs]
            bufs.append(lax.ppermute(bufs[source], ("row", "col"), flat))
        return bufs

    left_bufs, right_bufs = carry(left_perms), carry(right_perms)
    out_shape = jax.ShapeDtypeStruct((rows, rb * ratio * BS), jnp.float32)
    bufs = right_bufs + left_bufs[1:]
    among = [sorted(set(table[:, :, i].ravel().tolist()) - {-1}) for i in range(slots + STEPS)]
    codings = -(-(slots + STEPS + 1) * w // 8) * 8
    return pl.pallas_call(
        functools.partial(product_kernel, slots, n_row, ratio, rb, w, len(right_bufs), among),
        out_shape=out_shape,
        in_specs=[smem] + [hbm] * len(bufs),
        out_specs=hbm,
        scratch_shapes=[
            pltpu.VMEM((slots, rows + EXTRA, width), jnp.float32),
            pltpu.VMEM((STEPS + 1, rows + EXTRA, width), jnp.float32),
            pltpu.VMEM(out_shape.shape, jnp.float32),
            pltpu.VMEM((UNROLL, 2, BS, width), jnp.float32),
            pltpu.VMEM((slots + STEPS, EXTRA, width), jnp.float32),
            pltpu.VMEM((codings, 128), jnp.int32),
            pltpu.SMEM((codings, 128), jnp.int32),
            pltpu.SMEM((slots * rb * w + UNROLL,), jnp.int32),
            pltpu.SMEM((rb,), jnp.int32),
            dma((slots,)),
            dma((STEPS,)),
            dma((PARTS,)),
            dma((slots + STEPS + 1,)),
        ],
        compiler_params=pltpu.CompilerParams(vmem_limit_bytes=18 << 20),
        cost_estimate=pl.CostEstimate(flops=10**9, bytes_accessed=20 << 20, transcendentals=0),
    )(info, *bufs)


def solution(mesh):
    in_specs = (P("row", "col"), P("row", "col"))
    return jax.shard_map(local, mesh=mesh, in_specs=in_specs, out_specs=P("row", "col"), check_vma=False)
```

```python
import functools

import jax
import jax.numpy as jnp
import numpy as np
from jax import lax
from jax.experimental import pallas as pl
from jax.experimental.pallas import tpu as pltpu
from jax.sharding import PartitionSpec as P

BS = 64
STEPS = 4
UNROLL = 8
AHEAD = 2
EXTRA = 8
PARTS = 8


def left_offsets(row, ratio, n_col):
    seen = []
    for step in range(STEPS):
        offset = (row + step) // ratio % n_col
        if offset not in seen:
            seen.append(offset)
    return seen


def shift(rows, step, count):
    return [((r, c), (r, (c + step) % count)) for r in rows for c in range(count)]


def left_plan(n_row, n_col, ratio):
    offsets = [left_offsets(row, ratio, n_col) for row in range(n_row)]
    if (n_row, n_col, ratio) != (8, 4, 2):
        perms = []
        for slot in range(max(len(o) for o in offsets)):
            pairs = [
                ((row, (col + offsets[row][slot]) % n_col), (row, col))
                for row in range(n_row)
                for col in range(n_col)
                if slot < len(offsets[row]) and offsets[row][slot] != 0
            ]
            perms.append((0, pairs))
        return perms
    whole = [r for r in range(8) if {1, 2, 3} <= set(offsets[r])]
    once, twice = {-1: [], 1: []}, {-1: [], 1: []}
    for r in range(8):
        for offset, step in ((1, -1), (3, 1)):
            if offset in offsets[r] and r not in whole:
                once[step].append(r)
                if 2 in offsets[r]:
                    twice[step].append(r)
    down = shift([r for r in once[-1] if r != 0], -1, 4) + [((3, c), (3, c - 1)) for c in (1, 2, 3)] + [((3, 0), (0, 0))]
    up = shift(once[1], 1, 4) + shift([0], -1, 4) + [((3, c), (3, c + 1)) for c in (0, 1, 2)] + [((3, 3), (1, 3))]
    again_down = shift(twice[-1], -1, 4) + [((3, 1), (3, 0)), ((3, 2), (3, 1)), ((0, 0), (3, 3))]
    again_up = shift(twice[1], 1, 4) + [((3, 1), (3, 2)), ((3, 2), (3, 3)), ((1, 3), (3, 0))]
    return [(0, down), (0, up), (1, again_down), (2, again_up)]


def right_plan(n_row, n_col, ratio):
    everyone = [(row, col) for row in range(n_row) for col in range(n_col)]
    if (n_row, n_col, ratio) != (8, 4, 2):
        return [
            (0, [(((r + ratio * c + step) % n_row, c), (r, c)) for r, c in everyone if (ratio * c + step) % n_row])
            for step in range(STEPS)
        ]
    first = [(((r + 2 * c) % 8, c), (r, c)) for r, c in everyone if c != 0]
    first += [((r + 1, 0), (r, 0)) for r in range(0, 8, 2)]
    second = [(((r + 2 * c + 2) % 8, c), (r, c)) for r, c in everyone if c != 3]
    second += [((r ^ 1, 3), (r, 3)) for r in range(8)]
    last = [(((r - 1 + 2 * c + 4) % 8, c), (r, c)) for r, c in everyone if r % 2 == 1]
    first_swap = [((r + 1, c), (r, c)) for r, c in everyone if r % 2 == 0 and c != 0]
    second_swap = [((r ^ 1, c), (r, c)) for r, c in everyone if c != 3]
    return [(0, first), (0, second), (0, last), (1, first_swap), (2, second_swap)]


def carry_out(perms, n_row, n_col):
    held = [{(r, c): (r, c) for r in range(n_row) for c in range(n_col)}]
    for source, pairs in perms:
        held.append({dst: held[source][src] for src, dst in pairs})
    return held


def device_table(left_perms, right_perms, n_row, n_col, ratio):
    left_held = carry_out(left_perms, n_row, n_col)
    right_held = carry_out(right_perms, n_row, n_col)
    slots = (ratio - 1 + STEPS - 1) // ratio + 1
    table = np.full((n_row, n_col, 2 * slots + STEPS), -1, np.int32)

    def find(held, device, tile):
        return [i for i, h in enumerate(held) if h.get(device) == tile][0]

    for r in range(n_row):
        for c in range(n_col):
            for slot, offset in enumerate(left_offsets(r, ratio, n_col)):
                tile_col = (c + offset) % n_col
                table[r, c, slot] = find(left_held, (r, c), (r, tile_col))
                table[r, c, slots + STEPS + slot] = (tile_col * ratio - r - ratio * c) % n_row
            for step in range(STEPS):
                table[r, c, slots + step] = find(right_held, (r, c), ((r + ratio * c + step) % n_row, c))
    return table, slots


def fetch(choice, among, bufs, target, sem):
    for number in among:
        @pl.when(choice == number)
        def _():
            pltpu.make_async_copy(bufs[number], target, sem).start()


def join_kernel(cols_ref, data_ref, out_ref, cols, sem):
    rows = data_ref.shape[0]
    data_copy = pltpu.make_async_copy(data_ref, out_ref.at[pl.ds(0, rows)], sem.at[0])
    cols_copy = pltpu.make_async_copy(cols_ref, cols, sem.at[1])
    data_copy.start()
    cols_copy.start()
    out_ref[pl.ds(rows, EXTRA), :] = jnp.zeros((EXTRA, out_ref.shape[1]), jnp.float32)
    cols_copy.wait()
    out_ref[pl.ds(rows, cols.shape[0]), pl.ds(0, cols.shape[1])] = cols[...].astype(jnp.float32)
    data_copy.wait()


def product_kernel(slots, n_row, ratio, rb, w, n_right, among, info_ref, *refs):
    out_ref, left, right, acc, value, cols, coded, scalars, codes, ends, lsem, rsem, osem, csem = refs[-14:]
    right_bufs, left_bufs = refs[:n_right], refs[:1] + refs[n_right:-14]
    rows, width = left.shape[1] - EXTRA, left.shape[2]
    names = pl.ds(rows, EXTRA)
    for slot in range(slots):
        fetch(info_ref[slot], among[slot], [buf.at[names] for buf in left_bufs], cols.at[slot], csem.at[slot])
    for step in range(STEPS):
        at = slots + step
        fetch(info_ref[at], among[at], [buf.at[names] for buf in right_bufs], cols.at[at], csem.at[at])
    for step in range(STEPS):
        fetch(info_ref[slots + step], among[slots + step], right_bufs, right.at[step], rsem.at[step])
    for slot in range(slots):
        fetch(info_ref[slot], among[slot], left_bufs, left.at[slot], lsem.at[slot])

    def clear(first, last):
        @pl.loop(first, last)
        def _(r):
            acc[pl.ds(pl.multiple_of(r * BS, BS), BS), :] = jnp.zeros((BS, acc.shape[1]), jnp.float32)

    clear(0, rb // 4)
    lanes = scalars.shape[1]
    row = lax.broadcasted_iota(jnp.int32, (w, lanes), 1)
    tile_slot = lax.broadcasted_iota(jnp.int32, (w, lanes), 0)
    for slot in range(slots):
        used = info_ref[slot] >= 0

        @pl.when(used)
        def _():
            pltpu.make_async_copy(left_bufs[0].at[names], cols.at[slot], csem.at[slot]).wait()

        inner = cols[slot, 0:w, 0:lanes].astype(jnp.int32)
        valid = (inner >= 0) & (row < rb)
        step = jnp.full(inner.shape, info_ref[slots + STEPS + slot], jnp.int32)
        for _ in range(ratio - 1):
            beyond = inner >= rb
            step = jnp.where(beyond, step + 1, step)
            inner = jnp.where(beyond, inner - rb, inner)
        step = jnp.where(step >= n_row, step - n_row, step)
        code = inner | tile_slot << 8 | slot << 12 | row << 16 | step << 24
        valid = valid & (step < STEPS)
        coded[slot * w : (slot + 1) * w, :] = jnp.where(valid, jnp.where(used, code, -1), -1)
    for step in range(STEPS):
        pltpu.make_async_copy(right_bufs[0].at[names], cols.at[slots + step], csem.at[slots + step]).wait()
        col = cols[slots + step, 0:w, 0:lanes].astype(jnp.int32)
        code = (col >> 1) * 2 * BS | (col & 1) << 16
        coded[(slots + step) * w : (slots + step + 1) * w, :] = jnp.where(col < 0, 2 << 16, code)
    coded[(slots + STEPS) * w : (slots + STEPS + 1) * w, :] = jnp.full((w, lanes), 2 << 16, jnp.int32)
    to_scalars = pltpu.make_async_copy(coded, scalars, csem.at[slots + STEPS])
    to_scalars.start()
    clear(rb // 4, rb)
    to_scalars.wait()

    part_rows = rb // PARTS

    def listed(row, place):
        for code in [scalars[line, row] for line in range(slots * w)]:
            codes[place] = code
            place = place + (code >= 0).astype(jnp.int32)
        ends[row] = (place + UNROLL - 1) // UNROLL
        return place

    listed_end = lax.fori_loop(0, rb, listed, jnp.int32(0))
    for u in range(UNROLL):
        codes[listed_end + u] = STEPS << 24

    for step in range(STEPS):
        pltpu.make_async_copy(right_bufs[0], right.at[step], rsem.at[step]).wait()
    for slot in range(slots):
        @pl.when(info_ref[slot] >= 0)
        def _():
            pltpu.make_async_copy(left_bufs[0], left.at[slot], lsem.at[slot]).wait()

    half = lax.broadcasted_iota(jnp.int32, (BS, 2 * BS), 1) // BS

    def block_at(index):
        return pl.ds(pl.multiple_of(index * BS, BS), BS)

    def product(code):
        slot = (code >> 8) & 15
        x = left[(code >> 12) & 15, block_at((code >> 16) & 255), pl.ds(pl.multiple_of((slot >> 1) * 2 * BS, 2 * BS), 2 * BS)]
        both = jnp.where(half == (slot & 1), x, pltpu.roll(x, BS, 1))
        hi = both.astype(jnp.bfloat16).astype(jnp.float32)
        lhs = jnp.where(half == 0, hi, both - hi).astype(jnp.bfloat16)
        y = right[code >> 24, block_at(code & 255), :]
        hi = y.astype(jnp.bfloat16)
        lo = (y - hi.astype(jnp.float32)).astype(jnp.bfloat16)
        lhs = jnp.concatenate([lhs, lhs], axis=1)
        rhs = jnp.concatenate([hi, hi, lo, lo], axis=0)
        return jnp.dot(lhs, rhs, preferred_element_type=jnp.float32)

    def add(code, product):
        rows_at = block_at((code >> 16) & 255)
        for pair in range(w // 2):
            x = product[:, pair * 2 * BS : (pair + 1) * 2 * BS]
            turned = pltpu.roll(x, BS, 1)
            picked, at = [], []
            for side in range(2):
                place = scalars[(slots + (code >> 24)) * w + 2 * pair + side, code & 255]
                parity = place >> 16
                chosen = jnp.where(parity == side, x, turned)
                picked.append(jnp.where(half == parity, chosen, 0.0))
                at.append(place & 0xFFFF)
            picked[1] = jnp.where(at[0] == at[1], picked[0] + picked[1], picked[1])
            spots = [(rows_at, pl.ds(pl.multiple_of(base, 2 * BS), 2 * BS)) for base in at]
            sums = [acc[spot] + part for spot, part in zip(spots, picked)]
            for spot, total in zip(spots, sums):
                acc[spot] = total

    def out_copy(part):
        at = pl.ds(part * part_rows * BS, part_rows * BS)
        return pltpu.make_async_copy(acc.at[at], out_ref.at[at], osem.at[part])

    def first_products(group):
        for u in range(AHEAD):
            value[u] = product(codes[group * UNROLL + u])

    def sums(group, more):
        waiting = [value[u] for u in range(AHEAD)]
        for u in range(UNROLL):
            if u + AHEAD < UNROLL or more:
                waiting.append(product(codes[group * UNROLL + u + AHEAD]))
            add(codes[group * UNROLL + u], waiting[u])
        for u in range(AHEAD if more else 0):
            value[u] = waiting[UNROLL + u]

    last = jnp.maximum(ends[rb - 1] - 1, 0)

    def leave(group):
        for part in range(PARTS):
            @pl.when(jnp.maximum(ends[(part + 1) * part_rows - 1] - 1, 0) == group)
            def _():
                out_copy(part).start()

    first_products(0)

    @pl.loop(0, last)
    def _(group):
        sums(group, True)
        leave(group)

    sums(last, False)
    leave(last)
    for part in range(PARTS):
        out_copy(part).wait()


def local(p_cols, p_data):
    n_row, n_col = lax.axis_size("row"), lax.axis_size("col")
    ratio = n_row // n_col
    row_id, col_id = lax.axis_index("row"), lax.axis_index("col")
    rb, w = p_cols.shape
    rows, width = p_data.shape
    left_perms = left_plan(n_row, n_col, ratio)
    right_perms = right_plan(n_row, n_col, ratio)
    table, slots = device_table(left_perms, right_perms, n_row, n_col, ratio)
    info = jnp.asarray(table)[row_id, col_id]

    smem = pl.BlockSpec(memory_space=pltpu.SMEM)
    hbm = pl.BlockSpec(memory_space=pl.ANY)
    dma = pltpu.SemaphoreType.DMA
    own = pl.pallas_call(
        join_kernel,
        out_shape=jax.ShapeDtypeStruct((rows + EXTRA, width), jnp.float32),
        in_specs=[pl.BlockSpec(memory_space=pltpu.HBM)] * 2,
        out_specs=pl.BlockSpec(memory_space=pltpu.VMEM),
        scratch_shapes=[pltpu.VMEM((w, rb), jnp.int32), dma((2,))],
        compiler_params=pltpu.CompilerParams(vmem_limit_bytes=4 << 20),
        cost_estimate=pl.CostEstimate(flops=0, bytes_accessed=2 << 20, transcendentals=0),
    )(p_cols.T, p_data)

    def carry(perms):
        bufs = [own]
        for source, pairs in perms:
            flat = [(s[0] * n_col + s[1], d[0] * n_col + d[1]) for s, d in pairs]
            bufs.append(lax.ppermute(bufs[source], ("row", "col"), flat))
        return bufs

    left_bufs, right_bufs = carry(left_perms), carry(right_perms)
    out_shape = jax.ShapeDtypeStruct((rows, rb * ratio * BS), jnp.float32)
    bufs = right_bufs + left_bufs[1:]
    among = [sorted(set(table[:, :, i].ravel().tolist()) - {-1}) for i in range(slots + STEPS)]
    codings = -(-(slots + STEPS + 1) * w // 8) * 8
    return pl.pallas_call(
        functools.partial(product_kernel, slots, n_row, ratio, rb, w, len(right_bufs), among),
        out_shape=out_shape,
        in_specs=[smem] + [hbm] * len(bufs),
        out_specs=hbm,
        scratch_shapes=[
            pltpu.VMEM((slots, rows + EXTRA, width), jnp.float32),
            pltpu.VMEM((STEPS + 1, rows + EXTRA, width), jnp.float32),
            pltpu.VMEM(out_shape.shape, jnp.float32),
            pltpu.VMEM((AHEAD, BS, width), jnp.float32),
            pltpu.VMEM((slots + STEPS, EXTRA, width), jnp.float32),
            pltpu.VMEM((codings, 128), jnp.int32),
            pltpu.SMEM((codings, 128), jnp.int32),
            pltpu.SMEM((slots * rb * w + UNROLL,), jnp.int32),
            pltpu.SMEM((rb,), jnp.int32),
            dma((slots,)),
            dma((STEPS,)),
            dma((PARTS,)),
            dma((slots + STEPS + 1,)),
        ],
        compiler_params=pltpu.CompilerParams(vmem_limit_bytes=18 << 20),
        cost_estimate=pl.CostEstimate(flops=10**9, bytes_accessed=20 << 20, transcendentals=0),
    )(info, *bufs)


def solution(mesh):
    in_specs = (P("row", "col"), P("row", "col"))
    return jax.shard_map(local, mesh=mesh, in_specs=in_specs, out_specs=P("row", "col"), check_vma=False)
```

```python
import functools

import jax
import jax.numpy as jnp
import numpy as np
from jax import lax
from jax.experimental import pallas as pl
from jax.experimental.pallas import tpu as pltpu
from jax.sharding import PartitionSpec as P

BS = 64
STEPS = 4
UNROLL = 8
EXTRA = 8
PARTS = 8


def left_offsets(row, ratio, n_col):
    seen = []
    for step in range(STEPS):
        offset = (row + step) // ratio % n_col
        if offset not in seen:
            seen.append(offset)
    return seen


def shift(rows, step, count):
    return [((r, c), (r, (c + step) % count)) for r in rows for c in range(count)]


def left_plan(n_row, n_col, ratio):
    offsets = [left_offsets(row, ratio, n_col) for row in range(n_row)]
    if (n_row, n_col, ratio) != (8, 4, 2):
        perms = []
        for slot in range(max(len(o) for o in offsets)):
            pairs = [
                ((row, (col + offsets[row][slot]) % n_col), (row, col))
                for row in range(n_row)
                for col in range(n_col)
                if slot < len(offsets[row]) and offsets[row][slot] != 0
            ]
            perms.append((0, pairs))
        return perms
    whole = [r for r in range(8) if {1, 2, 3} <= set(offsets[r])]
    once, twice = {-1: [], 1: []}, {-1: [], 1: []}
    for r in range(8):
        for offset, step in ((1, -1), (3, 1)):
            if offset in offsets[r] and r not in whole:
                once[step].append(r)
                if 2 in offsets[r]:
                    twice[step].append(r)
    down = shift([r for r in once[-1] if r != 0], -1, 4) + [((3, c), (3, c - 1)) for c in (1, 2, 3)] + [((3, 0), (0, 0))]
    up = shift(once[1], 1, 4) + shift([0], -1, 4) + [((3, c), (3, c + 1)) for c in (0, 1, 2)] + [((3, 3), (1, 3))]
    again_down = shift(twice[-1], -1, 4) + [((3, 1), (3, 0)), ((3, 2), (3, 1)), ((0, 0), (3, 3))]
    again_up = shift(twice[1], 1, 4) + [((3, 1), (3, 2)), ((3, 2), (3, 3)), ((1, 3), (3, 0))]
    return [(0, down), (0, up), (1, again_down), (2, again_up)]


def right_plan(n_row, n_col, ratio):
    everyone = [(row, col) for row in range(n_row) for col in range(n_col)]
    if (n_row, n_col, ratio) != (8, 4, 2):
        return [
            (0, [(((r + ratio * c + step) % n_row, c), (r, c)) for r, c in everyone if (ratio * c + step) % n_row])
            for step in range(STEPS)
        ]
    first = [(((r + 2 * c) % 8, c), (r, c)) for r, c in everyone if c != 0]
    first += [((r + 1, 0), (r, 0)) for r in range(0, 8, 2)]
    second = [(((r + 2 * c + 2) % 8, c), (r, c)) for r, c in everyone if c != 3]
    second += [((r ^ 1, 3), (r, 3)) for r in range(8)]
    last = [(((r - 1 + 2 * c + 4) % 8, c), (r, c)) for r, c in everyone if r % 2 == 1]
    first_swap = [((r ^ 1, c), (r, c)) for r, c in everyone]
    second_swap = [((r ^ 1, c), (r, c)) for r, c in everyone if c != 3]
    return [(0, first), (0, second), (0, last), (1, first_swap), (2, second_swap)]


def carry_out(perms, n_row, n_col):
    held = [{(r, c): (r, c) for r in range(n_row) for c in range(n_col)}]
    for source, pairs in perms:
        held.append({dst: held[source][src] for src, dst in pairs if src in held[source]})
    return held


def device_table(left_perms, right_perms, n_row, n_col, ratio):
    left_held = carry_out(left_perms, n_row, n_col)
    right_held = carry_out(right_perms, n_row, n_col)
    slots = (ratio - 1 + STEPS - 1) // ratio + 1
    table = np.full((n_row, n_col, 2 * slots + STEPS), -1, np.int32)

    def find(held, device, tile):
        return [i for i, h in enumerate(held) if h.get(device) == tile][0]

    for r in range(n_row):
        for c in range(n_col):
            for slot, offset in enumerate(left_offsets(r, ratio, n_col)):
                tile_col = (c + offset) % n_col
                table[r, c, slot] = find(left_held, (r, c), (r, tile_col))
                table[r, c, slots + STEPS + slot] = (tile_col * ratio - r - ratio * c) % n_row
            for step in range(STEPS):
                table[r, c, slots + step] = find(right_held, (r, c), ((r + ratio * c + step) % n_row, c))
    return table, slots


def fetch(choice, among, bufs, target, sem):
    for number in among:
        @pl.when(choice == number)
        def _():
            pltpu.make_async_copy(bufs[number], target, sem).start()


def join_kernel(cols_ref, data_ref, out_ref, cols, sem):
    rows = data_ref.shape[0]
    data_copy = pltpu.make_async_copy(data_ref, out_ref.at[pl.ds(0, rows)], sem.at[0])
    cols_copy = pltpu.make_async_copy(cols_ref, cols, sem.at[1])
    data_copy.start()
    cols_copy.start()
    out_ref[pl.ds(rows, EXTRA), :] = jnp.zeros((EXTRA, out_ref.shape[1]), jnp.float32)
    cols_copy.wait()
    out_ref[pl.ds(rows, cols.shape[0]), pl.ds(0, cols.shape[1])] = cols[...].astype(jnp.float32)
    data_copy.wait()


def product_kernel(slots, n_row, ratio, rb, w, n_right, among, info_ref, *refs):
    out_ref, left, right, acc, value, cols, coded, scalars, codes, ends, lsem, rsem, osem, csem = refs[-14:]
    right_bufs, left_bufs = refs[:n_right], refs[:1] + refs[n_right:-14]
    rows, width = left.shape[1] - EXTRA, left.shape[2]
    names = pl.ds(rows, EXTRA)
    for slot in range(slots):
        fetch(info_ref[slot], among[slot], [buf.at[names] for buf in left_bufs], cols.at[slot], csem.at[slot])
    for step in range(STEPS):
        at = slots + step
        fetch(info_ref[at], among[at], [buf.at[names] for buf in right_bufs], cols.at[at], csem.at[at])
    for step in range(STEPS):
        fetch(info_ref[slots + step], among[slots + step], right_bufs, right.at[step], rsem.at[step])
    for slot in range(slots):
        fetch(info_ref[slot], among[slot], left_bufs, left.at[slot], lsem.at[slot])

    def clear(first, last):
        @pl.loop(first, last)
        def _(r):
            acc[pl.ds(pl.multiple_of(r * BS, BS), BS), :] = jnp.zeros((BS, acc.shape[1]), jnp.float32)

    clear(0, rb // 4)
    lanes = scalars.shape[1]
    row = lax.broadcasted_iota(jnp.int32, (w, lanes), 1)
    tile_slot = lax.broadcasted_iota(jnp.int32, (w, lanes), 0)
    for slot in range(slots):
        used = info_ref[slot] >= 0

        @pl.when(used)
        def _():
            pltpu.make_async_copy(left_bufs[0].at[names], cols.at[slot], csem.at[slot]).wait()

        inner = cols[slot, 0:w, 0:lanes].astype(jnp.int32)
        valid = (inner >= 0) & (row < rb)
        step = jnp.full(inner.shape, info_ref[slots + STEPS + slot], jnp.int32)
        for _ in range(ratio - 1):
            beyond = inner >= rb
            step = jnp.where(beyond, step + 1, step)
            inner = jnp.where(beyond, inner - rb, inner)
        step = jnp.where(step >= n_row, step - n_row, step)
        code = inner | tile_slot << 8 | slot << 12 | row << 16 | step << 24
        valid = valid & (step < STEPS)
        coded[slot * w : (slot + 1) * w, :] = jnp.where(valid, jnp.where(used, code, -1), -1)
    for step in range(STEPS):
        pltpu.make_async_copy(right_bufs[0].at[names], cols.at[slots + step], csem.at[slots + step]).wait()
        col = cols[slots + step, 0:w, 0:lanes].astype(jnp.int32)
        code = (col >> 1) * 2 * BS | (col & 1) << 16
        coded[(slots + step) * w : (slots + step + 1) * w, :] = jnp.where(col < 0, 2 << 16, code)
    coded[(slots + STEPS) * w : (slots + STEPS + 1) * w, :] = jnp.full((w, lanes), 2 << 16, jnp.int32)
    to_scalars = pltpu.make_async_copy(coded, scalars, csem.at[slots + STEPS])
    to_scalars.start()
    clear(rb // 4, rb)
    to_scalars.wait()

    part_rows = rb // PARTS

    def listed(row, place):
        for code in [scalars[line, row] for line in range(slots * w)]:
            codes[place] = code
            place = place + (code >= 0).astype(jnp.int32)
        ends[row] = (place + UNROLL - 1) // UNROLL
        return place

    listed_end = lax.fori_loop(0, rb, listed, jnp.int32(0))
    for u in range(UNROLL):
        codes[listed_end + u] = STEPS << 24

    for step in range(STEPS):
        pltpu.make_async_copy(right_bufs[0], right.at[step], rsem.at[step]).wait()
    for slot in range(slots):
        @pl.when(info_ref[slot] >= 0)
        def _():
            pltpu.make_async_copy(left_bufs[0], left.at[slot], lsem.at[slot]).wait()

    half = lax.broadcasted_iota(jnp.int32, (BS, 2 * BS), 1) // BS

    def block_at(index):
        return pl.ds(pl.multiple_of(index * BS, BS), BS)

    def product(code):
        slot = (code >> 8) & 15
        x = left[(code >> 12) & 15, block_at((code >> 16) & 255), pl.ds(pl.multiple_of((slot >> 1) * 2 * BS, 2 * BS), 2 * BS)]
        both = jnp.where(half == (slot & 1), x, pltpu.roll(x, BS, 1))
        hi = both.astype(jnp.bfloat16).astype(jnp.float32)
        lhs = jnp.where(half == 0, hi, both - hi).astype(jnp.bfloat16)
        y = right[code >> 24, block_at(code & 255), :]
        hi = y.astype(jnp.bfloat16)
        lo = (y - hi.astype(jnp.float32)).astype(jnp.bfloat16)
        lhs = jnp.concatenate([lhs, lhs], axis=1)
        rhs = jnp.concatenate([hi, hi, lo, lo], axis=0)
        return jnp.dot(lhs, rhs, preferred_element_type=jnp.float32)

    def add(code, product):
        rows_at = block_at((code >> 16) & 255)
        for pair in range(w // 2):
            x = product[:, pair * 2 * BS : (pair + 1) * 2 * BS]
            turned = pltpu.roll(x, BS, 1)
            picked, at = [], []
            for side in range(2):
                place = scalars[(slots + (code >> 24)) * w + 2 * pair + side, code & 255]
                parity = place >> 16
                chosen = jnp.where(parity == side, x, turned)
                picked.append(jnp.where(half == parity, chosen, 0.0))
                at.append(place & 0xFFFF)
            picked[1] = jnp.where(at[0] == at[1], picked[0] + picked[1], picked[1])
            spots = [(rows_at, pl.ds(pl.multiple_of(base, 2 * BS), 2 * BS)) for base in at]
            sums = [acc[spot] + part for spot, part in zip(spots, picked)]
            for spot, total in zip(spots, sums):
                acc[spot] = total

    def out_copy(part):
        at = pl.ds(part * part_rows * BS, part_rows * BS)
        return pltpu.make_async_copy(acc.at[at], out_ref.at[at], osem.at[part])

    def products(group):
        for u in range(UNROLL):
            value[u] = product(codes[group * UNROLL + u])

    def sums(group):
        for u in range(UNROLL):
            add(codes[group * UNROLL + u], value[u])

    last = jnp.maximum(ends[rb - 1] - 1, 0)

    def leave(group):
        for part in range(PARTS):
            @pl.when(jnp.maximum(ends[(part + 1) * part_rows - 1] - 1, 0) == group)
            def _():
                out_copy(part).start()

    products(0)

    @pl.loop(0, last)
    def _(group):
        sums(group)
        products(group + 1)
        leave(group)

    sums(last)
    leave(last)
    for part in range(PARTS):
        out_copy(part).wait()


def local(p_cols, p_data):
    n_row, n_col = lax.axis_size("row"), lax.axis_size("col")
    ratio = n_row // n_col
    row_id, col_id = lax.axis_index("row"), lax.axis_index("col")
    rb, w = p_cols.shape
    rows, width = p_data.shape
    left_perms = left_plan(n_row, n_col, ratio)
    right_perms = right_plan(n_row, n_col, ratio)
    table, slots = device_table(left_perms, right_perms, n_row, n_col, ratio)
    info = jnp.asarray(table)[row_id, col_id]

    smem = pl.BlockSpec(memory_space=pltpu.SMEM)
    hbm = pl.BlockSpec(memory_space=pl.ANY)
    dma = pltpu.SemaphoreType.DMA
    own = pl.pallas_call(
        join_kernel,
        out_shape=jax.ShapeDtypeStruct((rows + EXTRA, width), jnp.float32),
        in_specs=[pl.BlockSpec(memory_space=pltpu.HBM)] * 2,
        out_specs=pl.BlockSpec(memory_space=pltpu.VMEM),
        scratch_shapes=[pltpu.VMEM((w, rb), jnp.int32), dma((2,))],
        compiler_params=pltpu.CompilerParams(vmem_limit_bytes=4 << 20),
        cost_estimate=pl.CostEstimate(flops=0, bytes_accessed=2 << 20, transcendentals=0),
    )(p_cols.T, p_data)

    def carry(perms):
        bufs = [own]
        for source, pairs in perms:
            flat = [(s[0] * n_col + s[1], d[0] * n_col + d[1]) for s, d in pairs]
            bufs.append(lax.ppermute(bufs[source], ("row", "col"), flat))
        return bufs

    left_bufs, right_bufs = carry(left_perms), carry(right_perms)
    out_shape = jax.ShapeDtypeStruct((rows, rb * ratio * BS), jnp.float32)
    bufs = right_bufs + left_bufs[1:]
    among = [sorted(set(table[:, :, i].ravel().tolist()) - {-1}) for i in range(slots + STEPS)]
    codings = -(-(slots + STEPS + 1) * w // 8) * 8
    return pl.pallas_call(
        functools.partial(product_kernel, slots, n_row, ratio, rb, w, len(right_bufs), among),
        out_shape=out_shape,
        in_specs=[smem] + [hbm] * len(bufs),
        out_specs=hbm,
        scratch_shapes=[
            pltpu.VMEM((slots, rows + EXTRA, width), jnp.float32),
            pltpu.VMEM((STEPS + 1, rows + EXTRA, width), jnp.float32),
            pltpu.VMEM(out_shape.shape, jnp.float32),
            pltpu.VMEM((UNROLL, BS, width), jnp.float32),
            pltpu.VMEM((slots + STEPS, EXTRA, width), jnp.float32),
            pltpu.VMEM((codings, 128), jnp.int32),
            pltpu.SMEM((codings, 128), jnp.int32),
            pltpu.SMEM((slots * rb * w + UNROLL,), jnp.int32),
            pltpu.SMEM((rb,), jnp.int32),
            dma((slots,)),
            dma((STEPS,)),
            dma((PARTS,)),
            dma((slots + STEPS + 1,)),
        ],
        compiler_params=pltpu.CompilerParams(vmem_limit_bytes=18 << 20),
        cost_estimate=pl.CostEstimate(flops=10**9, bytes_accessed=20 << 20, transcendentals=0),
    )(info, *bufs)


def solution(mesh):
    in_specs = (P("row", "col"), P("row", "col"))
    return jax.shard_map(local, mesh=mesh, in_specs=in_specs, out_specs=P("row", "col"), check_vma=False)
```

```python
import functools

import jax
import jax.numpy as jnp
import numpy as np
from jax import lax
from jax.experimental import pallas as pl
from jax.experimental.pallas import tpu as pltpu
from jax.sharding import PartitionSpec as P

BS = 64
STEPS = 4
UNROLL = 8
EXTRA = 8
PARTS = 8


def left_offsets(row, ratio, n_col):
    seen = []
    for step in range(STEPS):
        offset = (row + step) // ratio % n_col
        if offset not in seen:
            seen.append(offset)
    return seen


def shift(rows, step, count):
    return [((r, c), (r, (c + step) % count)) for r in rows for c in range(count)]


def left_plan(n_row, n_col, ratio):
    offsets = [left_offsets(row, ratio, n_col) for row in range(n_row)]
    if (n_row, n_col, ratio) != (8, 4, 2):
        perms = []
        for slot in range(max(len(o) for o in offsets)):
            pairs = [
                ((row, (col + offsets[row][slot]) % n_col), (row, col))
                for row in range(n_row)
                for col in range(n_col)
                if slot < len(offsets[row]) and offsets[row][slot] != 0
            ]
            perms.append((0, pairs))
        return perms
    whole = [r for r in range(8) if {1, 2, 3} <= set(offsets[r])]
    once, twice = {-1: [], 1: []}, {-1: [], 1: []}
    for r in range(8):
        for offset, step in ((1, -1), (3, 1)):
            if offset in offsets[r] and r not in whole:
                once[step].append(r)
                if 2 in offsets[r]:
                    twice[step].append(r)
    down = shift([r for r in once[-1] if r != 0], -1, 4) + [((3, c), (3, c - 1)) for c in (1, 2, 3)] + [((3, 0), (0, 0))]
    up = shift(once[1], 1, 4) + shift([0], -1, 4) + [((3, c), (3, c + 1)) for c in (0, 1, 2)] + [((3, 3), (1, 3))]
    again_down = shift(twice[-1], -1, 4) + [((3, 1), (3, 0)), ((3, 2), (3, 1)), ((0, 0), (3, 3))]
    again_up = shift(twice[1], 1, 4) + [((3, 1), (3, 2)), ((3, 2), (3, 3)), ((1, 3), (3, 0))]
    return [(0, up), (0, down), (1, again_up), (2, again_down)]


def right_plan(n_row, n_col, ratio):
    everyone = [(row, col) for row in range(n_row) for col in range(n_col)]
    if (n_row, n_col, ratio) != (8, 4, 2):
        return [
            (0, [(((r + ratio * c + step) % n_row, c), (r, c)) for r, c in everyone if (ratio * c + step) % n_row])
            for step in range(STEPS)
        ]
    first = [(((r + 2 * c) % 8, c), (r, c)) for r, c in everyone if c != 0]
    first += [((r ^ 1, 0), (r, 0)) for r in range(8)]
    second = [(((r + 2 * c + 2) % 8, c), (r, c)) for r, c in everyone if c != 3]
    second += [((r ^ 1, 3), (r, 3)) for r in range(8)]
    last = [(((r - 1 + 2 * c + 4) % 8, c), (r, c)) for r, c in everyone if r % 2 == 1]
    last += [((r + 1, c), (r, c)) for r, c in everyone if r % 2 == 0]
    swap = [((r ^ 1, c), (r, c)) for r, c in everyone]
    return [(0, first), (0, second), (0, last), (1, swap), (2, swap)]


def carry_out(perms, n_row, n_col):
    held = [{(r, c): (r, c) for r in range(n_row) for c in range(n_col)}]
    for source, pairs in perms:
        held.append({dst: held[source][src] for src, dst in pairs if src in held[source]})
    return held


def device_table(left_perms, right_perms, n_row, n_col, ratio):
    left_held = carry_out(left_perms, n_row, n_col)
    right_held = carry_out(right_perms, n_row, n_col)
    slots = (ratio - 1 + STEPS - 1) // ratio + 1
    table = np.full((n_row, n_col, 2 * slots + STEPS), -1, np.int32)

    def find(held, device, tile):
        return [i for i, h in enumerate(held) if h.get(device) == tile][0]

    for r in range(n_row):
        for c in range(n_col):
            for slot, offset in enumerate(left_offsets(r, ratio, n_col)):
                tile_col = (c + offset) % n_col
                table[r, c, slot] = find(left_held, (r, c), (r, tile_col))
                table[r, c, slots + STEPS + slot] = (tile_col * ratio - r - ratio * c) % n_row
            for step in range(STEPS):
                table[r, c, slots + step] = find(right_held, (r, c), ((r + ratio * c + step) % n_row, c))
    return table, slots


def fetch(choice, among, bufs, target, sem):
    for number in among:
        @pl.when(choice == number)
        def _():
            pltpu.make_async_copy(bufs[number], target, sem).start()


def join_kernel(cols_ref, data_ref, out_ref, cols, sem):
    rows = data_ref.shape[0]
    data_copy = pltpu.make_async_copy(data_ref, out_ref.at[pl.ds(0, rows)], sem.at[0])
    cols_copy = pltpu.make_async_copy(cols_ref, cols, sem.at[1])
    data_copy.start()
    cols_copy.start()
    out_ref[pl.ds(rows, EXTRA), :] = jnp.zeros((EXTRA, out_ref.shape[1]), jnp.float32)
    cols_copy.wait()
    out_ref[pl.ds(rows, cols.shape[0]), pl.ds(0, cols.shape[1])] = cols[...].astype(jnp.float32)
    data_copy.wait()


def product_kernel(slots, n_row, ratio, rb, w, n_right, among, info_ref, *refs):
    out_ref, left, right, acc, value, cols, coded, scalars, codes, ends, lsem, rsem, osem, csem = refs[-14:]
    right_bufs, left_bufs = refs[:n_right], refs[:1] + refs[n_right:-14]
    rows, width = left.shape[1] - EXTRA, left.shape[2]
    names = pl.ds(rows, EXTRA)
    for slot in range(slots):
        fetch(info_ref[slot], among[slot], [buf.at[names] for buf in left_bufs], cols.at[slot], csem.at[slot])
    for step in range(STEPS):
        at = slots + step
        fetch(info_ref[at], among[at], [buf.at[names] for buf in right_bufs], cols.at[at], csem.at[at])
    for step in range(STEPS):
        fetch(info_ref[slots + step], among[slots + step], right_bufs, right.at[step], rsem.at[step])
    for slot in range(slots):
        fetch(info_ref[slot], among[slot], left_bufs, left.at[slot], lsem.at[slot])

    def clear(first, last):
        @pl.loop(first, last)
        def _(r):
            acc[pl.ds(pl.multiple_of(r * BS, BS), BS), :] = jnp.zeros((BS, acc.shape[1]), jnp.float32)

    clear(0, rb // 4)
    lanes = scalars.shape[1]
    row = lax.broadcasted_iota(jnp.int32, (w, lanes), 1)
    tile_slot = lax.broadcasted_iota(jnp.int32, (w, lanes), 0)
    for slot in range(slots):
        used = info_ref[slot] >= 0

        @pl.when(used)
        def _():
            pltpu.make_async_copy(left_bufs[0].at[names], cols.at[slot], csem.at[slot]).wait()

        inner = cols[slot, 0:w, 0:lanes].astype(jnp.int32)
        valid = (inner >= 0) & (row < rb)
        step = jnp.full(inner.shape, info_ref[slots + STEPS + slot], jnp.int32)
        for _ in range(ratio - 1):
            beyond = inner >= rb
            step = jnp.where(beyond, step + 1, step)
            inner = jnp.where(beyond, inner - rb, inner)
        step = jnp.where(step >= n_row, step - n_row, step)
        code = inner | tile_slot << 8 | slot << 12 | row << 16 | step << 24
        valid = valid & (step < STEPS)
        coded[slot * w : (slot + 1) * w, :] = jnp.where(valid, jnp.where(used, code, -1), -1)
    for step in range(STEPS):
        pltpu.make_async_copy(right_bufs[0].at[names], cols.at[slots + step], csem.at[slots + step]).wait()
        col = cols[slots + step, 0:w, 0:lanes].astype(jnp.int32)
        code = (col >> 1) * 2 * BS | (col & 1) << 16
        coded[(slots + step) * w : (slots + step + 1) * w, :] = jnp.where(col < 0, 2 << 16, code)
    coded[(slots + STEPS) * w : (slots + STEPS + 1) * w, :] = jnp.full((w, lanes), 2 << 16, jnp.int32)
    to_scalars = pltpu.make_async_copy(coded, scalars, csem.at[slots + STEPS])
    to_scalars.start()
    clear(rb // 4, rb)
    to_scalars.wait()

    part_rows = rb // PARTS

    def listed(row, place):
        for code in [scalars[line, row] for line in range(slots * w)]:
            codes[place] = code
            place = place + (code >= 0).astype(jnp.int32)
        ends[row] = (place + UNROLL - 1) // UNROLL
        return place

    listed_end = lax.fori_loop(0, rb, listed, jnp.int32(0))
    for u in range(UNROLL):
        codes[listed_end + u] = STEPS << 24

    for step in range(STEPS):
        pltpu.make_async_copy(right_bufs[0], right.at[step], rsem.at[step]).wait()
    for slot in range(slots):
        @pl.when(info_ref[slot] >= 0)
        def _():
            pltpu.make_async_copy(left_bufs[0], left.at[slot], lsem.at[slot]).wait()

    half = lax.broadcasted_iota(jnp.int32, (BS, 2 * BS), 1) // BS

    def block_at(index):
        return pl.ds(pl.multiple_of(index * BS, BS), BS)

    def product(code):
        slot = (code >> 8) & 15
        x = left[(code >> 12) & 15, block_at((code >> 16) & 255), pl.ds(pl.multiple_of((slot >> 1) * 2 * BS, 2 * BS), 2 * BS)]
        both = jnp.where(half == (slot & 1), x, pltpu.roll(x, BS, 1))
        hi = both.astype(jnp.bfloat16).astype(jnp.float32)
        lhs = jnp.where(half == 0, hi, both - hi).astype(jnp.bfloat16)
        y = right[code >> 24, block_at(code & 255), :]
        hi = y.astype(jnp.bfloat16)
        lo = (y - hi.astype(jnp.float32)).astype(jnp.bfloat16)
        lhs = jnp.concatenate([lhs, lhs], axis=1)
        rhs = jnp.concatenate([hi, hi, lo, lo], axis=0)
        return jnp.dot(lhs, rhs, preferred_element_type=jnp.float32)

    def add(code, product):
        rows_at = block_at((code >> 16) & 255)
        for pair in range(w // 2):
            x = product[:, pair * 2 * BS : (pair + 1) * 2 * BS]
            turned = pltpu.roll(x, BS, 1)
            picked, at = [], []
            for side in range(2):
                place = scalars[(slots + (code >> 24)) * w + 2 * pair + side, code & 255]
                parity = place >> 16
                chosen = jnp.where(parity == side, x, turned)
                picked.append(jnp.where(half == parity, chosen, 0.0))
                at.append(place & 0xFFFF)
            picked[1] = jnp.where(at[0] == at[1], picked[0] + picked[1], picked[1])
            spots = [(rows_at, pl.ds(pl.multiple_of(base, 2 * BS), 2 * BS)) for base in at]
            sums = [acc[spot] + part for spot, part in zip(spots, picked)]
            for spot, total in zip(spots, sums):
                acc[spot] = total

    def out_copy(part):
        at = pl.ds(part * part_rows * BS, part_rows * BS)
        return pltpu.make_async_copy(acc.at[at], out_ref.at[at], osem.at[part])

    def products(group):
        for u in range(UNROLL):
            value[u] = product(codes[group * UNROLL + u])

    def sums(group):
        for u in range(UNROLL):
            add(codes[group * UNROLL + u], value[u])

    last = jnp.maximum(ends[rb - 1] - 1, 0)

    def leave(group):
        for part in range(PARTS):
            @pl.when(jnp.maximum(ends[(part + 1) * part_rows - 1] - 1, 0) == group)
            def _():
                out_copy(part).start()

    products(0)

    @pl.loop(0, last)
    def _(group):
        sums(group)
        products(group + 1)
        leave(group)

    sums(last)
    leave(last)
    for part in range(PARTS):
        out_copy(part).wait()


def local(p_cols, p_data):
    n_row, n_col = lax.axis_size("row"), lax.axis_size("col")
    ratio = n_row // n_col
    row_id, col_id = lax.axis_index("row"), lax.axis_index("col")
    rb, w = p_cols.shape
    rows, width = p_data.shape
    left_perms = left_plan(n_row, n_col, ratio)
    right_perms = right_plan(n_row, n_col, ratio)
    table, slots = device_table(left_perms, right_perms, n_row, n_col, ratio)
    info = jnp.asarray(table)[row_id, col_id]

    smem = pl.BlockSpec(memory_space=pltpu.SMEM)
    hbm = pl.BlockSpec(memory_space=pl.ANY)
    dma = pltpu.SemaphoreType.DMA
    own = pl.pallas_call(
        join_kernel,
        out_shape=jax.ShapeDtypeStruct((rows + EXTRA, width), jnp.float32),
        in_specs=[pl.BlockSpec(memory_space=pltpu.HBM)] * 2,
        out_specs=pl.BlockSpec(memory_space=pltpu.VMEM),
        scratch_shapes=[pltpu.VMEM((w, rb), jnp.int32), dma((2,))],
        compiler_params=pltpu.CompilerParams(vmem_limit_bytes=4 << 20),
        cost_estimate=pl.CostEstimate(flops=0, bytes_accessed=2 << 20, transcendentals=0),
    )(p_cols.T, p_data)

    def carry(perms):
        bufs = [own]
        for source, pairs in perms:
            flat = [(s[0] * n_col + s[1], d[0] * n_col + d[1]) for s, d in pairs]
            bufs.append(lax.ppermute(bufs[source], ("row", "col"), flat))
        return bufs

    left_bufs, right_bufs = carry(left_perms), carry(right_perms)
    out_shape = jax.ShapeDtypeStruct((rows, rb * ratio * BS), jnp.float32)
    bufs = right_bufs + left_bufs[1:]
    among = [sorted(set(table[:, :, i].ravel().tolist()) - {-1}) for i in range(slots + STEPS)]
    codings = -(-(slots + STEPS + 1) * w // 8) * 8
    return pl.pallas_call(
        functools.partial(product_kernel, slots, n_row, ratio, rb, w, len(right_bufs), among),
        out_shape=out_shape,
        in_specs=[smem] + [hbm] * len(bufs),
        out_specs=hbm,
        scratch_shapes=[
            pltpu.VMEM((slots, rows + EXTRA, width), jnp.float32),
            pltpu.VMEM((STEPS + 1, rows + EXTRA, width), jnp.float32),
            pltpu.VMEM(out_shape.shape, jnp.float32),
            pltpu.VMEM((UNROLL, BS, width), jnp.float32),
            pltpu.VMEM((slots + STEPS, EXTRA, width), jnp.float32),
            pltpu.VMEM((codings, 128), jnp.int32),
            pltpu.SMEM((codings, 128), jnp.int32),
            pltpu.SMEM((slots * rb * w + UNROLL,), jnp.int32),
            pltpu.SMEM((rb,), jnp.int32),
            dma((slots,)),
            dma((STEPS,)),
            dma((PARTS,)),
            dma((slots + STEPS + 1,)),
        ],
        compiler_params=pltpu.CompilerParams(vmem_limit_bytes=18 << 20),
        cost_estimate=pl.CostEstimate(flops=10**9, bytes_accessed=20 << 20, transcendentals=0),
    )(info, *bufs)


def solution(mesh):
    in_specs = (P("row", "col"), P("row", "col"))
    return jax.shard_map(local, mesh=mesh, in_specs=in_specs, out_specs=P("row", "col"), check_vma=False)
```

```python
import functools

import jax
import jax.numpy as jnp
import numpy as np
from jax import lax
from jax.experimental import pallas as pl
from jax.experimental.pallas import tpu as pltpu
from jax.sharding import PartitionSpec as P

BS = 64
STEPS = 4
UNROLL = 8
EXTRA = 8
PARTS = 16


def left_offsets(row, ratio, n_col):
    seen = []
    for step in range(STEPS):
        offset = (row + step) // ratio % n_col
        if offset not in seen:
            seen.append(offset)
    return seen


def shift(rows, step, count):
    return [((r, c), (r, (c + step) % count)) for r in rows for c in range(count)]


def left_plan(n_row, n_col, ratio):
    offsets = [left_offsets(row, ratio, n_col) for row in range(n_row)]
    if (n_row, n_col, ratio) != (8, 4, 2):
        perms = []
        for slot in range(max(len(o) for o in offsets)):
            pairs = [
                ((row, (col + offsets[row][slot]) % n_col), (row, col))
                for row in range(n_row)
                for col in range(n_col)
                if slot < len(offsets[row]) and offsets[row][slot] != 0
            ]
            perms.append((0, pairs))
        return perms
    whole = [r for r in range(8) if {1, 2, 3} <= set(offsets[r])]
    once, twice = {-1: [], 1: []}, {-1: [], 1: []}
    for r in range(8):
        for offset, step in ((1, -1), (3, 1)):
            if offset in offsets[r] and r not in whole:
                once[step].append(r)
                if 2 in offsets[r]:
                    twice[step].append(r)
    down = shift([r for r in once[-1] if r != 0], -1, 4) + [((3, c), (3, c - 1)) for c in (1, 2, 3)] + [((3, 0), (0, 0))]
    up = shift(once[1], 1, 4) + shift([0], -1, 4) + [((3, c), (3, c + 1)) for c in (0, 1, 2)] + [((3, 3), (1, 3))]
    again_down = shift(twice[-1], -1, 4) + [((3, 1), (3, 0)), ((3, 2), (3, 1)), ((0, 0), (3, 3))]
    again_up = shift(twice[1], 1, 4) + [((3, 1), (3, 2)), ((3, 2), (3, 3)), ((1, 3), (3, 0))]
    return [(0, up), (0, down), (1, again_up), (2, again_down)]


def right_plan(n_row, n_col, ratio):
    everyone = [(row, col) for row in range(n_row) for col in range(n_col)]
    if (n_row, n_col, ratio) != (8, 4, 2):
        return [
            (0, [(((r + ratio * c + step) % n_row, c), (r, c)) for r, c in everyone if (ratio * c + step) % n_row])
            for step in range(STEPS)
        ]
    first = [(((r + 2 * c) % 8, c), (r, c)) for r, c in everyone if c != 0]
    first += [((r ^ 1, 0), (r, 0)) for r in range(8)]
    second = [(((r + 2 * c + 2) % 8, c), (r, c)) for r, c in everyone if c != 3]
    second += [((r ^ 1, 3), (r, 3)) for r in range(8)]
    last = [(((r - 1 + 2 * c + 4) % 8, c), (r, c)) for r, c in everyone if r % 2 == 1]
    last += [((r + 1, c), (r, c)) for r, c in everyone if r % 2 == 0]
    swap = [((r ^ 1, c), (r, c)) for r, c in everyone]
    return [(0, first), (0, second), (0, last), (1, swap), (2, swap)]


def carry_out(perms, n_row, n_col):
    held = [{(r, c): (r, c) for r in range(n_row) for c in range(n_col)}]
    for source, pairs in perms:
        held.append({dst: held[source][src] for src, dst in pairs if src in held[source]})
    return held


def device_table(left_perms, right_perms, n_row, n_col, ratio):
    left_held = carry_out(left_perms, n_row, n_col)
    right_held = carry_out(right_perms, n_row, n_col)
    slots = (ratio - 1 + STEPS - 1) // ratio + 1
    table = np.full((n_row, n_col, 2 * slots + STEPS), -1, np.int32)

    def find(held, device, tile):
        return [i for i, h in enumerate(held) if h.get(device) == tile][0]

    for r in range(n_row):
        for c in range(n_col):
            for slot, offset in enumerate(left_offsets(r, ratio, n_col)):
                tile_col = (c + offset) % n_col
                table[r, c, slot] = find(left_held, (r, c), (r, tile_col))
                table[r, c, slots + STEPS + slot] = (tile_col * ratio - r - ratio * c) % n_row
            for step in range(STEPS):
                table[r, c, slots + step] = find(right_held, (r, c), ((r + ratio * c + step) % n_row, c))
    return table, slots


def fetch(choice, among, bufs, target, sem):
    for number in among:
        @pl.when(choice == number)
        def _():
            pltpu.make_async_copy(bufs[number], target, sem).start()


def join_kernel(cols_ref, data_ref, out_ref, cols, sem):
    rows = data_ref.shape[0]
    data_copy = pltpu.make_async_copy(data_ref, out_ref.at[pl.ds(0, rows)], sem.at[0])
    cols_copy = pltpu.make_async_copy(cols_ref, cols, sem.at[1])
    data_copy.start()
    cols_copy.start()
    out_ref[pl.ds(rows, EXTRA), :] = jnp.zeros((EXTRA, out_ref.shape[1]), jnp.float32)
    cols_copy.wait()
    out_ref[pl.ds(rows, cols.shape[0]), pl.ds(0, cols.shape[1])] = cols[...].astype(jnp.float32)
    data_copy.wait()


def product_kernel(slots, n_row, ratio, rb, w, n_right, among, info_ref, *refs):
    out_ref, left, right, acc, value, cols, coded, scalars, codes, ends, lsem, rsem, osem, csem = refs[-14:]
    right_bufs, left_bufs = refs[:n_right], refs[:1] + refs[n_right:-14]
    rows, width = left.shape[1] - EXTRA, left.shape[2]
    names = pl.ds(rows, EXTRA)
    for slot in range(slots):
        fetch(info_ref[slot], among[slot], [buf.at[names] for buf in left_bufs], cols.at[slot], csem.at[slot])
    for step in range(STEPS):
        at = slots + step
        fetch(info_ref[at], among[at], [buf.at[names] for buf in right_bufs], cols.at[at], csem.at[at])
    for step in range(STEPS):
        fetch(info_ref[slots + step], among[slots + step], right_bufs, right.at[step], rsem.at[step])
    for slot in range(slots):
        fetch(info_ref[slot], among[slot], left_bufs, left.at[slot], lsem.at[slot])

    def clear(first, rows_count):
        at = pl.ds(pl.multiple_of(first, 8), rows_count)
        acc[at, :] = jnp.zeros((rows_count, acc.shape[1]), jnp.float32)

    beside = BS // 64 * 24
    ahead = (BS - beside) * rb // BS

    def clear_blocks(first, last):
        @pl.loop(first, last)
        def _(block):
            clear(block * BS, BS)

    clear_blocks(0, ahead // 2)
    lanes = scalars.shape[1]
    row = lax.broadcasted_iota(jnp.int32, (w, lanes), 1)
    tile_slot = lax.broadcasted_iota(jnp.int32, (w, lanes), 0)
    for slot in range(slots):
        used = info_ref[slot] >= 0

        @pl.when(used)
        def _():
            pltpu.make_async_copy(left_bufs[0].at[names], cols.at[slot], csem.at[slot]).wait()

        inner = cols[slot, 0:w, 0:lanes].astype(jnp.int32)
        valid = (inner >= 0) & (row < rb)
        step = jnp.full(inner.shape, info_ref[slots + STEPS + slot], jnp.int32)
        for _ in range(ratio - 1):
            beyond = inner >= rb
            step = jnp.where(beyond, step + 1, step)
            inner = jnp.where(beyond, inner - rb, inner)
        step = jnp.where(step >= n_row, step - n_row, step)
        code = inner | tile_slot << 8 | slot << 12 | row << 16 | step << 24
        valid = valid & (step < STEPS)
        coded[slot * w : (slot + 1) * w, :] = jnp.where(valid, jnp.where(used, code, -1), -1)
    for step in range(STEPS):
        pltpu.make_async_copy(right_bufs[0].at[names], cols.at[slots + step], csem.at[slots + step]).wait()
        col = cols[slots + step, 0:w, 0:lanes].astype(jnp.int32)
        code = (col >> 1) * 2 * BS | (col & 1) << 16
        coded[(slots + step) * w : (slots + step + 1) * w, :] = jnp.where(col < 0, 2 << 16, code)
    coded[(slots + STEPS) * w : (slots + STEPS + 1) * w, :] = jnp.full((w, lanes), 2 << 16, jnp.int32)
    to_scalars = pltpu.make_async_copy(coded, scalars, csem.at[slots + STEPS])
    to_scalars.start()
    clear_blocks(ahead // 2, ahead)
    to_scalars.wait()

    part_rows = rb // PARTS

    def listed(row, place):
        for code in [scalars[line, row] for line in range(slots * w)]:
            codes[place] = code
            place = place + (code >= 0).astype(jnp.int32)
        ends[row] = (place + UNROLL - 1) // UNROLL
        clear(ahead * BS + row * beside, beside)
        return place

    listed_end = lax.fori_loop(0, rb, listed, jnp.int32(0))
    for u in range(UNROLL):
        codes[listed_end + u] = STEPS << 24

    for step in range(STEPS):
        pltpu.make_async_copy(right_bufs[0], right.at[step], rsem.at[step]).wait()
    for slot in range(slots):
        @pl.when(info_ref[slot] >= 0)
        def _():
            pltpu.make_async_copy(left_bufs[0], left.at[slot], lsem.at[slot]).wait()

    half = lax.broadcasted_iota(jnp.int32, (BS, 2 * BS), 1) // BS

    def block_at(index):
        return pl.ds(pl.multiple_of(index * BS, BS), BS)

    def product(code):
        slot = (code >> 8) & 15
        x = left[(code >> 12) & 15, block_at((code >> 16) & 255), pl.ds(pl.multiple_of((slot >> 1) * 2 * BS, 2 * BS), 2 * BS)]
        both = jnp.where(half == (slot & 1), x, pltpu.roll(x, BS, 1))
        hi = both.astype(jnp.bfloat16).astype(jnp.float32)
        lhs = jnp.where(half == 0, hi, both - hi).astype(jnp.bfloat16)
        y = right[code >> 24, block_at(code & 255), :]
        hi = y.astype(jnp.bfloat16)
        lo = (y - hi.astype(jnp.float32)).astype(jnp.bfloat16)
        lhs = jnp.concatenate([lhs, lhs], axis=1)
        rhs = jnp.concatenate([hi, hi, lo, lo], axis=0)
        return jnp.dot(lhs, rhs, preferred_element_type=jnp.float32)

    def add(code, product):
        rows_at = block_at((code >> 16) & 255)
        for pair in range(w // 2):
            x = product[:, pair * 2 * BS : (pair + 1) * 2 * BS]
            turned = pltpu.roll(x, BS, 1)
            picked, at = [], []
            for side in range(2):
                place = scalars[(slots + (code >> 24)) * w + 2 * pair + side, code & 255]
                parity = place >> 16
                chosen = jnp.where(parity == side, x, turned)
                picked.append(jnp.where(half == parity, chosen, 0.0))
                at.append(place & 0xFFFF)
            picked[1] = jnp.where(at[0] == at[1], picked[0] + picked[1], picked[1])
            spots = [(rows_at, pl.ds(pl.multiple_of(base, 2 * BS), 2 * BS)) for base in at]
            sums = [acc[spot] + part for spot, part in zip(spots, picked)]
            for spot, total in zip(spots, sums):
                acc[spot] = total

    def out_copy(part):
        at = pl.ds(part * part_rows * BS, part_rows * BS)
        return pltpu.make_async_copy(acc.at[at], out_ref.at[at], osem.at[part])

    def products(group):
        for u in range(UNROLL):
            value[u] = product(codes[group * UNROLL + u])

    def sums(group):
        for u in range(UNROLL):
            add(codes[group * UNROLL + u], value[u])

    last = jnp.maximum(ends[rb - 1] - 1, 0)

    def leave(group):
        for part in range(PARTS):
            @pl.when(jnp.maximum(ends[(part + 1) * part_rows - 1] - 1, 0) == group)
            def _():
                out_copy(part).start()

    products(0)

    @pl.loop(0, last)
    def _(group):
        sums(group)
        products(group + 1)
        leave(group)

    sums(last)
    leave(last)
    for part in range(PARTS):
        out_copy(part).wait()


def local(p_cols, p_data):
    n_row, n_col = lax.axis_size("row"), lax.axis_size("col")
    ratio = n_row // n_col
    row_id, col_id = lax.axis_index("row"), lax.axis_index("col")
    rb, w = p_cols.shape
    rows, width = p_data.shape
    left_perms = left_plan(n_row, n_col, ratio)
    right_perms = right_plan(n_row, n_col, ratio)
    table, slots = device_table(left_perms, right_perms, n_row, n_col, ratio)
    info = jnp.asarray(table)[row_id, col_id]

    smem = pl.BlockSpec(memory_space=pltpu.SMEM)
    hbm = pl.BlockSpec(memory_space=pl.ANY)
    dma = pltpu.SemaphoreType.DMA
    own = pl.pallas_call(
        join_kernel,
        out_shape=jax.ShapeDtypeStruct((rows + EXTRA, width), jnp.float32),
        in_specs=[pl.BlockSpec(memory_space=pltpu.HBM)] * 2,
        out_specs=pl.BlockSpec(memory_space=pltpu.VMEM),
        scratch_shapes=[pltpu.VMEM((w, rb), jnp.int32), dma((2,))],
        compiler_params=pltpu.CompilerParams(vmem_limit_bytes=4 << 20),
        cost_estimate=pl.CostEstimate(flops=0, bytes_accessed=2 << 20, transcendentals=0),
    )(p_cols.T, p_data)

    def carry(perms):
        bufs = [own]
        for source, pairs in perms:
            flat = [(s[0] * n_col + s[1], d[0] * n_col + d[1]) for s, d in pairs]
            bufs.append(lax.ppermute(bufs[source], ("row", "col"), flat))
        return bufs

    left_bufs, right_bufs = carry(left_perms), carry(right_perms)
    out_shape = jax.ShapeDtypeStruct((rows, rb * ratio * BS), jnp.float32)
    bufs = right_bufs + left_bufs[1:]
    among = [sorted(set(table[:, :, i].ravel().tolist()) - {-1}) for i in range(slots + STEPS)]
    codings = -(-(slots + STEPS + 1) * w // 8) * 8
    return pl.pallas_call(
        functools.partial(product_kernel, slots, n_row, ratio, rb, w, len(right_bufs), among),
        out_shape=out_shape,
        in_specs=[smem] + [hbm] * len(bufs),
        out_specs=hbm,
        scratch_shapes=[
            pltpu.VMEM((slots, rows + EXTRA, width), jnp.float32),
            pltpu.VMEM((STEPS + 1, rows + EXTRA, width), jnp.float32),
            pltpu.VMEM(out_shape.shape, jnp.float32),
            pltpu.VMEM((UNROLL, BS, width), jnp.float32),
            pltpu.VMEM((slots + STEPS, EXTRA, width), jnp.float32),
            pltpu.VMEM((codings, 128), jnp.int32),
            pltpu.SMEM((codings, 128), jnp.int32),
            pltpu.SMEM((slots * rb * w + UNROLL,), jnp.int32),
            pltpu.SMEM((rb,), jnp.int32),
            dma((slots,)),
            dma((STEPS,)),
            dma((PARTS,)),
            dma((slots + STEPS + 1,)),
        ],
        compiler_params=pltpu.CompilerParams(vmem_limit_bytes=18 << 20),
        cost_estimate=pl.CostEstimate(flops=10**9, bytes_accessed=20 << 20, transcendentals=0),
    )(info, *bufs)


def solution(mesh):
    in_specs = (P("row", "col"), P("row", "col"))
    return jax.shard_map(local, mesh=mesh, in_specs=in_specs, out_specs=P("row", "col"), check_vma=False)
```

```python
import functools

import jax
import jax.numpy as jnp
import numpy as np
from jax import lax
from jax.experimental import pallas as pl
from jax.experimental.pallas import tpu as pltpu
from jax.sharding import PartitionSpec as P

BS = 64
STEPS = 4
UNROLL = 8
EXTRA = 8
PARTS = 16


def left_offsets(row, ratio, n_col):
    seen = []
    for step in range(STEPS):
        offset = (row + step) // ratio % n_col
        if offset not in seen:
            seen.append(offset)
    return seen


def shift(rows, step, count):
    return [((r, c), (r, (c + step) % count)) for r in rows for c in range(count)]


def left_plan(n_row, n_col, ratio):
    offsets = [left_offsets(row, ratio, n_col) for row in range(n_row)]
    if (n_row, n_col, ratio) != (8, 4, 2):
        perms = []
        for slot in range(max(len(o) for o in offsets)):
            pairs = [
                ((row, (col + offsets[row][slot]) % n_col), (row, col))
                for row in range(n_row)
                for col in range(n_col)
                if slot < len(offsets[row]) and offsets[row][slot] != 0
            ]
            perms.append((0, pairs))
        return perms
    whole = [r for r in range(8) if {1, 2, 3} <= set(offsets[r])]
    once, twice = {-1: [], 1: []}, {-1: [], 1: []}
    for r in range(8):
        for offset, step in ((1, -1), (3, 1)):
            if offset in offsets[r] and r not in whole:
                once[step].append(r)
                if 2 in offsets[r]:
                    twice[step].append(r)
    down = shift([r for r in once[-1] if r != 0], -1, 4) + [((3, c), (3, c - 1)) for c in (1, 2, 3)] + [((3, 0), (0, 0))]
    up = shift(once[1], 1, 4) + shift([0], -1, 4) + [((3, c), (3, c + 1)) for c in (0, 1, 2)] + [((3, 3), (1, 3))]
    again_down = shift(twice[-1], -1, 4) + [((3, 1), (3, 0)), ((3, 2), (3, 1)), ((0, 0), (3, 3))]
    again_up = shift(twice[1], 1, 4) + [((3, 1), (3, 2)), ((3, 2), (3, 3)), ((1, 3), (3, 0))]
    return [(0, up), (0, down), (1, again_up), (2, again_down)]


def right_plan(n_row, n_col, ratio):
    everyone = [(row, col) for row in range(n_row) for col in range(n_col)]
    if (n_row, n_col, ratio) != (8, 4, 2):
        return [
            (0, [(((r + ratio * c + step) % n_row, c), (r, c)) for r, c in everyone if (ratio * c + step) % n_row])
            for step in range(STEPS)
        ]
    first = [(((r + 2 * c) % 8, c), (r, c)) for r, c in everyone if c != 0]
    first += [((r ^ 1, 0), (r, 0)) for r in range(8)]
    second = [(((r + 2 * c + 2) % 8, c), (r, c)) for r, c in everyone if c != 3]
    second += [((r ^ 1, 3), (r, 3)) for r in range(8)]
    last = [(((r - 1 + 2 * c + 4) % 8, c), (r, c)) for r, c in everyone if r % 2 == 1]
    last += [((r + 1, c), (r, c)) for r, c in everyone if r % 2 == 0]
    swap = [((r ^ 1, c), (r, c)) for r, c in everyone]
    return [(0, first), (0, second), (0, last), (1, swap), (2, swap)]


def carry_out(perms, n_row, n_col):
    held = [{(r, c): (r, c) for r in range(n_row) for c in range(n_col)}]
    for source, pairs in perms:
        held.append({dst: held[source][src] for src, dst in pairs if src in held[source]})
    return held


def device_table(left_perms, right_perms, n_row, n_col, ratio):
    left_held = carry_out(left_perms, n_row, n_col)
    right_held = carry_out(right_perms, n_row, n_col)
    slots = (ratio - 1 + STEPS - 1) // ratio + 1
    table = np.full((n_row, n_col, 2 * slots + STEPS), -1, np.int32)

    def find(held, device, tile):
        return [i for i, h in enumerate(held) if h.get(device) == tile][0]

    for r in range(n_row):
        for c in range(n_col):
            for slot, offset in enumerate(left_offsets(r, ratio, n_col)):
                tile_col = (c + offset) % n_col
                table[r, c, slot] = find(left_held, (r, c), (r, tile_col))
                table[r, c, slots + STEPS + slot] = (tile_col * ratio - r - ratio * c) % n_row
            for step in range(STEPS):
                table[r, c, slots + step] = find(right_held, (r, c), ((r + ratio * c + step) % n_row, c))
    return table, slots


def fetch(choice, among, bufs, target, sem):
    for number in among:
        @pl.when(choice == number)
        def _():
            pltpu.make_async_copy(bufs[number], target, sem).start()


def join_kernel(cols_ref, data_ref, out_ref, cols, sem):
    rows = data_ref.shape[0]
    data_copy = pltpu.make_async_copy(data_ref, out_ref.at[pl.ds(0, rows)], sem.at[0])
    cols_copy = pltpu.make_async_copy(cols_ref, cols, sem.at[1])
    data_copy.start()
    cols_copy.start()
    out_ref[pl.ds(rows, EXTRA), :] = jnp.zeros((EXTRA, out_ref.shape[1]), jnp.float32)
    cols_copy.wait()
    out_ref[pl.ds(rows, cols.shape[0]), pl.ds(0, cols.shape[1])] = cols[...].astype(jnp.float32)
    data_copy.wait()


def product_kernel(slots, n_row, ratio, rb, w, n_right, among, info_ref, *refs):
    out_ref, left, right, acc, value, cols, coded, scalars, codes, ends, lsem, rsem, osem, csem = refs[-14:]
    right_bufs, left_bufs = refs[:n_right], refs[:1] + refs[n_right:-14]
    rows, width = left.shape[1] - EXTRA, left.shape[2]
    names = pl.ds(rows, EXTRA)
    for slot in range(slots):
        fetch(info_ref[slot], among[slot], [buf.at[names] for buf in left_bufs], cols.at[slot], csem.at[slot])
    for step in range(STEPS):
        at = slots + step
        fetch(info_ref[at], among[at], [buf.at[names] for buf in right_bufs], cols.at[at], csem.at[at])
    for step in range(STEPS):
        fetch(info_ref[slots + step], among[slots + step], right_bufs, right.at[step], rsem.at[step])
    for slot in range(slots):
        fetch(info_ref[slot], among[slot], left_bufs, left.at[slot], lsem.at[slot])

    def clear(first, rows_count):
        at = pl.ds(pl.multiple_of(first, 8), rows_count)
        acc[at, :] = jnp.zeros((rows_count, acc.shape[1]), jnp.float32)

    beside = BS // 64 * 24
    ahead = (BS - beside) * rb // BS

    def clear_blocks(first, last):
        @pl.loop(first, last)
        def _(block):
            clear(block * BS, BS)

    clear_blocks(0, ahead // 2)
    lanes = scalars.shape[1]
    row = lax.broadcasted_iota(jnp.int32, (w, lanes), 1)
    tile_slot = lax.broadcasted_iota(jnp.int32, (w, lanes), 0)
    for slot in range(slots):
        used = info_ref[slot] >= 0

        @pl.when(used)
        def _():
            pltpu.make_async_copy(left_bufs[0].at[names], cols.at[slot], csem.at[slot]).wait()

        inner = cols[slot, 0:w, 0:lanes].astype(jnp.int32)
        valid = (inner >= 0) & (row < rb)
        step = jnp.full(inner.shape, info_ref[slots + STEPS + slot], jnp.int32)
        for _ in range(ratio - 1):
            beyond = inner >= rb
            step = jnp.where(beyond, step + 1, step)
            inner = jnp.where(beyond, inner - rb, inner)
        step = jnp.where(step >= n_row, step - n_row, step)
        code = inner | tile_slot << 8 | slot << 12 | row << 16 | step << 24
        valid = valid & (step < STEPS)
        coded[slot * w : (slot + 1) * w, :] = jnp.where(valid, jnp.where(used, code, -1), -1)
    for step in range(STEPS):
        pltpu.make_async_copy(right_bufs[0].at[names], cols.at[slots + step], csem.at[slots + step]).wait()
        col = cols[slots + step, 0:w, 0:lanes].astype(jnp.int32)
        code = (col >> 1) * 2 * BS | (col & 1) << 16
        coded[(slots + step) * w : (slots + step + 1) * w, :] = jnp.where(col < 0, 2 << 16, code)
    coded[(slots + STEPS) * w : (slots + STEPS + 1) * w, :] = jnp.full((w, lanes), 2 << 16, jnp.int32)
    to_scalars = pltpu.make_async_copy(coded, scalars, csem.at[slots + STEPS])
    to_scalars.start()
    clear_blocks(ahead // 2, ahead)
    to_scalars.wait()

    part_rows = rb // PARTS

    def listed(row, place):
        for code in [scalars[line, row] for line in range(slots * w)]:
            codes[place] = code
            place = place + (code >= 0).astype(jnp.int32)
        ends[row] = (place + UNROLL - 1) // UNROLL
        clear(ahead * BS + row * beside, beside)
        return place

    listed_end = lax.fori_loop(0, rb, listed, jnp.int32(0))
    for u in range(UNROLL):
        codes[listed_end + u] = STEPS << 24

    for step in range(STEPS):
        pltpu.make_async_copy(right_bufs[0], right.at[step], rsem.at[step]).wait()
    for slot in range(slots):
        @pl.when(info_ref[slot] >= 0)
        def _():
            pltpu.make_async_copy(left_bufs[0], left.at[slot], lsem.at[slot]).wait()

    half = lax.broadcasted_iota(jnp.int32, (BS, 2 * BS), 1) // BS

    def block_at(index):
        return pl.ds(pl.multiple_of(index * BS, BS), BS)

    def product(code):
        slot = (code >> 8) & 15
        x = left[(code >> 12) & 15, block_at((code >> 16) & 255), pl.ds(pl.multiple_of((slot >> 1) * 2 * BS, 2 * BS), 2 * BS)]
        both = jnp.where(half == (slot & 1), x, pltpu.roll(x, BS, 1))
        hi = both.astype(jnp.bfloat16).astype(jnp.float32)
        lhs = jnp.where(half == 0, hi, both - hi).astype(jnp.bfloat16)
        y = right[code >> 24, block_at(code & 255), :]
        hi = y.astype(jnp.bfloat16)
        lo = (y - hi.astype(jnp.float32)).astype(jnp.bfloat16)
        lhs = jnp.concatenate([lhs, lhs], axis=1)
        rhs = jnp.concatenate([hi, hi, lo, lo], axis=0)
        return jnp.dot(lhs, rhs, preferred_element_type=jnp.float32)

    def add(code, product):
        rows_at = block_at((code >> 16) & 255)
        for pair in range(w // 2):
            x = product[:, pair * 2 * BS : (pair + 1) * 2 * BS]
            turned = pltpu.roll(x, BS, 1)
            picked, at = [], []
            for side in range(2):
                place = scalars[(slots + (code >> 24)) * w + 2 * pair + side, code & 255]
                parity = place >> 16
                chosen = jnp.where(parity == side, x, turned)
                picked.append(jnp.where(half == parity, chosen, 0.0))
                at.append(place & 0xFFFF)
            picked[1] = jnp.where(at[0] == at[1], picked[0] + picked[1], picked[1])
            spots = [(rows_at, pl.ds(pl.multiple_of(base, 2 * BS), 2 * BS)) for base in at]
            sums = [acc[spot] + part for spot, part in zip(spots, picked)]
            for spot, total in zip(spots, sums):
                acc[spot] = total

    def out_copy(part):
        at = pl.ds(part * part_rows * BS, part_rows * BS)
        return pltpu.make_async_copy(acc.at[at], out_ref.at[at], osem.at[part])

    def step_of(group, adds, multiplies):
        for u in range(UNROLL):
            if adds:
                add(codes[group * UNROLL + u], value[u])
            if multiplies:
                value[u] = product(codes[(group + 1) * UNROLL + u])

    last = jnp.maximum(ends[rb - 1] - 1, 0)

    def leave(group):
        for part in range(PARTS):
            @pl.when(jnp.maximum(ends[(part + 1) * part_rows - 1] - 1, 0) == group)
            def _():
                out_copy(part).start()

    step_of(-1, False, True)

    @pl.loop(0, last)
    def _(group):
        step_of(group, True, True)
        leave(group)

    step_of(last, True, False)
    leave(last)
    for part in range(PARTS):
        out_copy(part).wait()


def local(p_cols, p_data):
    n_row, n_col = lax.axis_size("row"), lax.axis_size("col")
    ratio = n_row // n_col
    row_id, col_id = lax.axis_index("row"), lax.axis_index("col")
    rb, w = p_cols.shape
    rows, width = p_data.shape
    left_perms = left_plan(n_row, n_col, ratio)
    right_perms = right_plan(n_row, n_col, ratio)
    table, slots = device_table(left_perms, right_perms, n_row, n_col, ratio)
    info = jnp.asarray(table)[row_id, col_id]

    smem = pl.BlockSpec(memory_space=pltpu.SMEM)
    hbm = pl.BlockSpec(memory_space=pl.ANY)
    dma = pltpu.SemaphoreType.DMA
    own = pl.pallas_call(
        join_kernel,
        out_shape=jax.ShapeDtypeStruct((rows + EXTRA, width), jnp.float32),
        in_specs=[pl.BlockSpec(memory_space=pltpu.HBM)] * 2,
        out_specs=pl.BlockSpec(memory_space=pltpu.VMEM),
        scratch_shapes=[pltpu.VMEM((w, rb), jnp.int32), dma((2,))],
        compiler_params=pltpu.CompilerParams(vmem_limit_bytes=4 << 20),
        cost_estimate=pl.CostEstimate(flops=0, bytes_accessed=2 << 20, transcendentals=0),
    )(p_cols.T, p_data)

    def carry(perms):
        bufs = [own]
        for source, pairs in perms:
            flat = [(s[0] * n_col + s[1], d[0] * n_col + d[1]) for s, d in pairs]
            bufs.append(lax.ppermute(bufs[source], ("row", "col"), flat))
        return bufs

    left_bufs, right_bufs = carry(left_perms), carry(right_perms)
    out_shape = jax.ShapeDtypeStruct((rows, rb * ratio * BS), jnp.float32)
    bufs = right_bufs + left_bufs[1:]
    among = [sorted(set(table[:, :, i].ravel().tolist()) - {-1}) for i in range(slots + STEPS)]
    codings = -(-(slots + STEPS + 1) * w // 8) * 8
    return pl.pallas_call(
        functools.partial(product_kernel, slots, n_row, ratio, rb, w, len(right_bufs), among),
        out_shape=out_shape,
        in_specs=[smem] + [hbm] * len(bufs),
        out_specs=hbm,
        scratch_shapes=[
            pltpu.VMEM((slots, rows + EXTRA, width), jnp.float32),
            pltpu.VMEM((STEPS + 1, rows + EXTRA, width), jnp.float32),
            pltpu.VMEM(out_shape.shape, jnp.float32),
            pltpu.VMEM((UNROLL, BS, width), jnp.float32),
            pltpu.VMEM((slots + STEPS, EXTRA, width), jnp.float32),
            pltpu.VMEM((codings, 128), jnp.int32),
            pltpu.SMEM((codings, 128), jnp.int32),
            pltpu.SMEM((slots * rb * w + UNROLL,), jnp.int32),
            pltpu.SMEM((rb,), jnp.int32),
            dma((slots,)),
            dma((STEPS,)),
            dma((PARTS,)),
            dma((slots + STEPS + 1,)),
        ],
        compiler_params=pltpu.CompilerParams(vmem_limit_bytes=18 << 20),
        cost_estimate=pl.CostEstimate(flops=10**9, bytes_accessed=20 << 20, transcendentals=0),
    )(info, *bufs)


def solution(mesh):
    in_specs = (P("row", "col"), P("row", "col"))
    return jax.shard_map(local, mesh=mesh, in_specs=in_specs, out_specs=P("row", "col"), check_vma=False)
```

```python
import functools

import jax
import jax.numpy as jnp
import numpy as np
from jax import lax
from jax.experimental import pallas as pl
from jax.experimental.pallas import tpu as pltpu
from jax.sharding import PartitionSpec as P

BS = 64
STEPS = 4
UNROLL = 8
EXTRA = 8
PARTS = 16


def left_offsets(row, ratio, n_col):
    seen = []
    for step in range(STEPS):
        offset = (row + step) // ratio % n_col
        if offset not in seen:
            seen.append(offset)
    return seen


def shift(rows, step, count):
    return [((r, c), (r, (c + step) % count)) for r in rows for c in range(count)]


def left_plan(n_row, n_col, ratio):
    offsets = [left_offsets(row, ratio, n_col) for row in range(n_row)]
    if (n_row, n_col, ratio) != (8, 4, 2):
        perms = []
        for slot in range(max(len(o) for o in offsets)):
            pairs = [
                ((row, (col + offsets[row][slot]) % n_col), (row, col))
                for row in range(n_row)
                for col in range(n_col)
                if slot < len(offsets[row]) and offsets[row][slot] != 0
            ]
            perms.append((0, pairs))
        return perms
    whole = [r for r in range(8) if {1, 2, 3} <= set(offsets[r])]
    once, twice = {-1: [], 1: []}, {-1: [], 1: []}
    for r in range(8):
        for offset, step in ((1, -1), (3, 1)):
            if offset in offsets[r] and r not in whole:
                once[step].append(r)
                if 2 in offsets[r]:
                    twice[step].append(r)
    down = shift([r for r in once[-1] if r != 0], -1, 4) + [((3, c), (3, c - 1)) for c in (1, 2, 3)] + [((3, 0), (0, 0))]
    up = shift(once[1], 1, 4) + shift([0], -1, 4) + [((3, c), (3, c + 1)) for c in (0, 1, 2)] + [((3, 3), (1, 3))]
    again_down = shift(twice[-1], -1, 4) + [((3, 1), (3, 0)), ((3, 2), (3, 1)), ((0, 0), (3, 3))]
    again_up = shift(twice[1], 1, 4) + [((3, 1), (3, 2)), ((3, 2), (3, 3)), ((1, 3), (3, 0))]
    return [(0, up), (0, down), (1, again_up), (2, again_down)]


def right_plan(n_row, n_col, ratio):
    everyone = [(row, col) for row in range(n_row) for col in range(n_col)]
    if (n_row, n_col, ratio) != (8, 4, 2):
        return [
            (0, [(((r + ratio * c + step) % n_row, c), (r, c)) for r, c in everyone if (ratio * c + step) % n_row])
            for step in range(STEPS)
        ]
    first = [(((r + 2 * c) % 8, c), (r, c)) for r, c in everyone if c != 0]
    first += [((r ^ 1, 0), (r, 0)) for r in range(8)]
    second = [(((r + 2 * c + 2) % 8, c), (r, c)) for r, c in everyone if c != 3]
    second += [((r ^ 1, 3), (r, 3)) for r in range(8)]
    last = [(((r - 1 + 2 * c + 4) % 8, c), (r, c)) for r, c in everyone if r % 2 == 1]
    last += [((r + 1, c), (r, c)) for r, c in everyone if r % 2 == 0]
    swap = [((r ^ 1, c), (r, c)) for r, c in everyone]
    return [(0, first), (0, second), (0, last), (1, swap), (2, swap)]


def carry_out(perms, n_row, n_col):
    held = [{(r, c): (r, c) for r in range(n_row) for c in range(n_col)}]
    for source, pairs in perms:
        held.append({dst: held[source][src] for src, dst in pairs if src in held[source]})
    return held


def device_table(left_perms, right_perms, n_row, n_col, ratio):
    left_held = carry_out(left_perms, n_row, n_col)
    right_held = carry_out(right_perms, n_row, n_col)
    slots = (ratio - 1 + STEPS - 1) // ratio + 1
    table = np.full((n_row, n_col, 2 * slots + STEPS), -1, np.int32)

    def find(held, device, tile):
        return [i for i, h in enumerate(held) if h.get(device) == tile][0]

    for r in range(n_row):
        for c in range(n_col):
            for slot, offset in enumerate(left_offsets(r, ratio, n_col)):
                tile_col = (c + offset) % n_col
                table[r, c, slot] = find(left_held, (r, c), (r, tile_col))
                table[r, c, slots + STEPS + slot] = (tile_col * ratio - r - ratio * c) % n_row
            for step in range(STEPS):
                table[r, c, slots + step] = find(right_held, (r, c), ((r + ratio * c + step) % n_row, c))
    return table, slots


def fetch(choice, among, bufs, target, sem):
    for number in among:
        @pl.when(choice == number)
        def _():
            pltpu.make_async_copy(bufs[number], target, sem).start()


def join_kernel(cols_ref, data_ref, out_ref, cols, sem):
    rows = data_ref.shape[0]
    data_copy = pltpu.make_async_copy(data_ref, out_ref.at[pl.ds(0, rows)], sem.at[0])
    cols_copy = pltpu.make_async_copy(cols_ref, cols, sem.at[1])
    data_copy.start()
    cols_copy.start()
    out_ref[pl.ds(rows, EXTRA), :] = jnp.zeros((EXTRA, out_ref.shape[1]), jnp.float32)
    cols_copy.wait()
    out_ref[pl.ds(rows, cols.shape[0]), pl.ds(0, cols.shape[1])] = cols[...].astype(jnp.float32)
    data_copy.wait()


def product_kernel(slots, n_row, ratio, rb, w, n_right, among, info_ref, *refs):
    out_ref, left, right, acc, value, cols, coded, scalars, codes, ends, lsem, rsem, osem, csem = refs[-14:]
    right_bufs, left_bufs = refs[:n_right], refs[:1] + refs[n_right:-14]
    rows, width = left.shape[1] - EXTRA, left.shape[2]
    names = pl.ds(rows, EXTRA)
    for slot in range(slots):
        fetch(info_ref[slot], among[slot], [buf.at[names] for buf in left_bufs], cols.at[slot], csem.at[slot])
    for step in range(STEPS):
        at = slots + step
        fetch(info_ref[at], among[at], [buf.at[names] for buf in right_bufs], cols.at[at], csem.at[at])
    for step in range(STEPS):
        fetch(info_ref[slots + step], among[slots + step], right_bufs, right.at[step], rsem.at[step])
    for slot in range(slots):
        fetch(info_ref[slot], among[slot], left_bufs, left.at[slot], lsem.at[slot])

    def clear(first, rows_count):
        at = pl.ds(pl.multiple_of(first, 8), rows_count)
        acc[at, :] = jnp.zeros((rows_count, acc.shape[1]), jnp.float32)

    beside = BS // 64 * 24
    ahead = (BS - beside) * rb // BS

    def clear_blocks(first, last):
        @pl.loop(first, last)
        def _(block):
            clear(block * BS, BS)

    clear_blocks(0, ahead // 2)
    lanes = scalars.shape[1]
    row = lax.broadcasted_iota(jnp.int32, (w, lanes), 1)
    tile_slot = lax.broadcasted_iota(jnp.int32, (w, lanes), 0)
    for slot in range(slots):
        used = info_ref[slot] >= 0

        @pl.when(used)
        def _():
            pltpu.make_async_copy(left_bufs[0].at[names], cols.at[slot], csem.at[slot]).wait()

        inner = cols[slot, 0:w, 0:lanes].astype(jnp.int32)
        valid = (inner >= 0) & (row < rb)
        step = jnp.full(inner.shape, info_ref[slots + STEPS + slot], jnp.int32)
        for _ in range(ratio - 1):
            beyond = inner >= rb
            step = jnp.where(beyond, step + 1, step)
            inner = jnp.where(beyond, inner - rb, inner)
        step = jnp.where(step >= n_row, step - n_row, step)
        code = inner | tile_slot << 8 | slot << 12 | row << 16 | step << 24
        valid = valid & (step < STEPS)
        coded[slot * w : (slot + 1) * w, :] = jnp.where(valid, jnp.where(used, code, -1), -1)
    for step in range(STEPS):
        pltpu.make_async_copy(right_bufs[0].at[names], cols.at[slots + step], csem.at[slots + step]).wait()
        col = cols[slots + step, 0:w, 0:lanes].astype(jnp.int32)
        code = (col >> 1) * 2 * BS | (col & 1) << 16
        coded[(slots + step) * w : (slots + step + 1) * w, :] = jnp.where(col < 0, 2 << 16, code)
    coded[(slots + STEPS) * w : (slots + STEPS + 1) * w, :] = jnp.full((w, lanes), 2 << 16, jnp.int32)
    to_scalars = pltpu.make_async_copy(coded, scalars, csem.at[slots + STEPS])
    to_scalars.start()
    clear_blocks(ahead // 2, ahead)
    to_scalars.wait()

    part_rows = rb // PARTS

    def listed(row, place):
        for code in [scalars[line, row] for line in range(slots * w)]:
            codes[place] = code
            place = place + (code >= 0).astype(jnp.int32)
        ends[row] = (place + UNROLL - 1) // UNROLL
        clear(ahead * BS + row * beside, beside)
        return place

    listed_end = lax.fori_loop(0, rb, listed, jnp.int32(0))
    for u in range(UNROLL):
        codes[listed_end + u] = STEPS << 24

    for step in range(STEPS):
        pltpu.make_async_copy(right_bufs[0], right.at[step], rsem.at[step]).wait()
    for slot in range(slots):
        @pl.when(info_ref[slot] >= 0)
        def _():
            pltpu.make_async_copy(left_bufs[0], left.at[slot], lsem.at[slot]).wait()

    half = lax.broadcasted_iota(jnp.int32, (8, 2 * BS), 1) // BS

    def block_at(index):
        return pl.ds(pl.multiple_of(index * BS, BS), BS)

    def in_half(side, kept, other):
        tall = lambda x: x.reshape(BS // 8, 8, 2 * BS) if jnp.ndim(x) else x
        return jnp.where((half == side)[None], tall(kept), tall(other)).reshape(BS, 2 * BS)

    def product(code):
        slot = (code >> 8) & 15
        x = left[(code >> 12) & 15, block_at((code >> 16) & 255), pl.ds(pl.multiple_of((slot >> 1) * 2 * BS, 2 * BS), 2 * BS)]
        both = in_half(slot & 1, x, pltpu.roll(x, BS, 1))
        hi = both.astype(jnp.bfloat16).astype(jnp.float32)
        lhs = in_half(0, hi, both - hi).astype(jnp.bfloat16)
        y = right[code >> 24, block_at(code & 255), :]
        hi = y.astype(jnp.bfloat16)
        lo = (y - hi.astype(jnp.float32)).astype(jnp.bfloat16)
        lhs = jnp.concatenate([lhs, lhs], axis=1)
        rhs = jnp.concatenate([hi, hi, lo, lo], axis=0)
        return jnp.dot(lhs, rhs, preferred_element_type=jnp.float32)

    def add(code, product):
        rows_at = block_at((code >> 16) & 255)
        for pair in range(w // 2):
            x = product[:, pair * 2 * BS : (pair + 1) * 2 * BS]
            turned = pltpu.roll(x, BS, 1)
            picked, at = [], []
            for side in range(2):
                place = scalars[(slots + (code >> 24)) * w + 2 * pair + side, code & 255]
                parity = place >> 16
                chosen = jnp.where(parity == side, x, turned)
                picked.append(in_half(parity, chosen, 0.0))
                at.append(place & 0xFFFF)
            picked[1] = jnp.where(at[0] == at[1], picked[0] + picked[1], picked[1])
            spots = [(rows_at, pl.ds(pl.multiple_of(base, 2 * BS), 2 * BS)) for base in at]
            sums = [acc[spot] + part for spot, part in zip(spots, picked)]
            for spot, total in zip(spots, sums):
                acc[spot] = total

    def out_copy(part):
        at = pl.ds(part * part_rows * BS, part_rows * BS)
        return pltpu.make_async_copy(acc.at[at], out_ref.at[at], osem.at[part])

    def products(group):
        for u in range(UNROLL):
            value[u] = product(codes[group * UNROLL + u])

    def sums(group):
        for u in range(UNROLL):
            add(codes[group * UNROLL + u], value[u])

    last = jnp.maximum(ends[rb - 1] - 1, 0)

    def leave(group):
        for part in range(PARTS):
            @pl.when(jnp.maximum(ends[(part + 1) * part_rows - 1] - 1, 0) == group)
            def _():
                out_copy(part).start()

    products(0)

    @pl.loop(0, last)
    def _(group):
        sums(group)
        products(group + 1)
        leave(group)

    sums(last)
    leave(last)
    for part in range(PARTS):
        out_copy(part).wait()


def local(p_cols, p_data):
    n_row, n_col = lax.axis_size("row"), lax.axis_size("col")
    ratio = n_row // n_col
    row_id, col_id = lax.axis_index("row"), lax.axis_index("col")
    rb, w = p_cols.shape
    rows, width = p_data.shape
    left_perms = left_plan(n_row, n_col, ratio)
    right_perms = right_plan(n_row, n_col, ratio)
    table, slots = device_table(left_perms, right_perms, n_row, n_col, ratio)
    info = jnp.asarray(table)[row_id, col_id]

    smem = pl.BlockSpec(memory_space=pltpu.SMEM)
    hbm = pl.BlockSpec(memory_space=pl.ANY)
    dma = pltpu.SemaphoreType.DMA
    own = pl.pallas_call(
        join_kernel,
        out_shape=jax.ShapeDtypeStruct((rows + EXTRA, width), jnp.float32),
        in_specs=[pl.BlockSpec(memory_space=pltpu.HBM)] * 2,
        out_specs=pl.BlockSpec(memory_space=pltpu.VMEM),
        scratch_shapes=[pltpu.VMEM((w, rb), jnp.int32), dma((2,))],
        compiler_params=pltpu.CompilerParams(vmem_limit_bytes=4 << 20),
        cost_estimate=pl.CostEstimate(flops=0, bytes_accessed=2 << 20, transcendentals=0),
    )(p_cols.T, p_data)

    def carry(perms):
        bufs = [own]
        for source, pairs in perms:
            flat = [(s[0] * n_col + s[1], d[0] * n_col + d[1]) for s, d in pairs]
            bufs.append(lax.ppermute(bufs[source], ("row", "col"), flat))
        return bufs

    left_bufs, right_bufs = carry(left_perms), carry(right_perms)
    out_shape = jax.ShapeDtypeStruct((rows, rb * ratio * BS), jnp.float32)
    bufs = right_bufs + left_bufs[1:]
    among = [sorted(set(table[:, :, i].ravel().tolist()) - {-1}) for i in range(slots + STEPS)]
    codings = -(-(slots + STEPS + 1) * w // 8) * 8
    return pl.pallas_call(
        functools.partial(product_kernel, slots, n_row, ratio, rb, w, len(right_bufs), among),
        out_shape=out_shape,
        in_specs=[smem] + [hbm] * len(bufs),
        out_specs=hbm,
        scratch_shapes=[
            pltpu.VMEM((slots, rows + EXTRA, width), jnp.float32),
            pltpu.VMEM((STEPS + 1, rows + EXTRA, width), jnp.float32),
            pltpu.VMEM(out_shape.shape, jnp.float32),
            pltpu.VMEM((UNROLL, BS, width), jnp.float32),
            pltpu.VMEM((slots + STEPS, EXTRA, width), jnp.float32),
            pltpu.VMEM((codings, 128), jnp.int32),
            pltpu.SMEM((codings, 128), jnp.int32),
            pltpu.SMEM((slots * rb * w + UNROLL,), jnp.int32),
            pltpu.SMEM((rb,), jnp.int32),
            dma((slots,)),
            dma((STEPS,)),
            dma((PARTS,)),
            dma((slots + STEPS + 1,)),
        ],
        compiler_params=pltpu.CompilerParams(vmem_limit_bytes=18 << 20),
        cost_estimate=pl.CostEstimate(flops=10**9, bytes_accessed=20 << 20, transcendentals=0),
    )(info, *bufs)


def solution(mesh):
    in_specs = (P("row", "col"), P("row", "col"))
    return jax.shard_map(local, mesh=mesh, in_specs=in_specs, out_specs=P("row", "col"), check_vma=False)
```

```python
import functools

import jax
import jax.numpy as jnp
import numpy as np
from jax import lax
from jax.experimental import pallas as pl
from jax.experimental.pallas import tpu as pltpu
from jax.sharding import PartitionSpec as P

BS = 64
STEPS = 4
UNROLL = 8
EXTRA = 8
PARTS = 16


def left_offsets(row, ratio, n_col):
    seen = []
    for step in range(STEPS):
        offset = (row + step) // ratio % n_col
        if offset not in seen:
            seen.append(offset)
    return seen


def shift(rows, step, count):
    return [((r, c), (r, (c + step) % count)) for r in rows for c in range(count)]


def left_plan(n_row, n_col, ratio):
    offsets = [left_offsets(row, ratio, n_col) for row in range(n_row)]
    if (n_row, n_col, ratio) != (8, 4, 2):
        perms = []
        for slot in range(max(len(o) for o in offsets)):
            pairs = [
                ((row, (col + offsets[row][slot]) % n_col), (row, col))
                for row in range(n_row)
                for col in range(n_col)
                if slot < len(offsets[row]) and offsets[row][slot] != 0
            ]
            perms.append((0, pairs))
        return perms
    whole = [r for r in range(8) if {1, 2, 3} <= set(offsets[r])]
    once, twice = {-1: [], 1: []}, {-1: [], 1: []}
    for r in range(8):
        for offset, step in ((1, -1), (3, 1)):
            if offset in offsets[r] and r not in whole:
                once[step].append(r)
                if 2 in offsets[r]:
                    twice[step].append(r)
    down = shift([r for r in once[-1] if r != 0], -1, 4) + [((3, c), (3, c - 1)) for c in (1, 2, 3)] + [((3, 0), (0, 0))]
    up = shift(once[1], 1, 4) + shift([0], -1, 4) + [((3, c), (3, c + 1)) for c in (0, 1, 2)] + [((3, 3), (1, 3))]
    again_down = shift(twice[-1], -1, 4) + [((3, 1), (3, 0)), ((3, 2), (3, 1)), ((0, 0), (3, 3))]
    again_up = shift(twice[1], 1, 4) + [((3, 1), (3, 2)), ((3, 2), (3, 3)), ((1, 3), (3, 0))]
    return [(0, up), (0, down), (1, again_up), (2, again_down)]


def right_plan(n_row, n_col, ratio):
    everyone = [(row, col) for row in range(n_row) for col in range(n_col)]
    if (n_row, n_col, ratio) != (8, 4, 2):
        return [
            (0, [(((r + ratio * c + step) % n_row, c), (r, c)) for r, c in everyone if (ratio * c + step) % n_row])
            for step in range(STEPS)
        ]
    first = [(((r + 2 * c) % 8, c), (r, c)) for r, c in everyone if c != 0]
    first += [((r ^ 1, 0), (r, 0)) for r in range(8)]
    second = [(((r + 2 * c + 2) % 8, c), (r, c)) for r, c in everyone if c != 3]
    second += [((r ^ 1, 3), (r, 3)) for r in range(8)]
    last = [(((r - 1 + 2 * c + 4) % 8, c), (r, c)) for r, c in everyone if r % 2 == 1]
    last += [((r + 1, c), (r, c)) for r, c in everyone if r % 2 == 0]
    swap = [((r ^ 1, c), (r, c)) for r, c in everyone]
    return [(0, first), (0, second), (0, last), (1, swap), (2, swap)]


def carry_out(perms, n_row, n_col):
    held = [{(r, c): (r, c) for r in range(n_row) for c in range(n_col)}]
    for source, pairs in perms:
        held.append({dst: held[source][src] for src, dst in pairs if src in held[source]})
    return held


def device_table(left_perms, right_perms, n_row, n_col, ratio):
    left_held = carry_out(left_perms, n_row, n_col)
    right_held = carry_out(right_perms, n_row, n_col)
    slots = (ratio - 1 + STEPS - 1) // ratio + 1
    table = np.full((n_row, n_col, 2 * slots + STEPS), -1, np.int32)

    def find(held, device, tile):
        return [i for i, h in enumerate(held) if h.get(device) == tile][0]

    for r in range(n_row):
        for c in range(n_col):
            for slot, offset in enumerate(left_offsets(r, ratio, n_col)):
                tile_col = (c + offset) % n_col
                table[r, c, slot] = find(left_held, (r, c), (r, tile_col))
                table[r, c, slots + STEPS + slot] = (tile_col * ratio - r - ratio * c) % n_row
            for step in range(STEPS):
                table[r, c, slots + step] = find(right_held, (r, c), ((r + ratio * c + step) % n_row, c))
    return table, slots


def fetch(choice, among, bufs, target, sem):
    for number in among:
        @pl.when(choice == number)
        def _():
            pltpu.make_async_copy(bufs[number], target, sem).start()


def join_kernel(cols_ref, data_ref, out_ref, cols, sem):
    rows = data_ref.shape[0]
    data_copy = pltpu.make_async_copy(data_ref, out_ref.at[pl.ds(0, rows)], sem.at[0])
    cols_copy = pltpu.make_async_copy(cols_ref, cols, sem.at[1])
    data_copy.start()
    cols_copy.start()
    out_ref[pl.ds(rows, EXTRA), :] = jnp.zeros((EXTRA, out_ref.shape[1]), jnp.float32)
    cols_copy.wait()
    out_ref[pl.ds(rows, cols.shape[0]), pl.ds(0, cols.shape[1])] = cols[...].astype(jnp.float32)
    data_copy.wait()


def product_kernel(slots, n_row, ratio, rb, w, n_right, among, info_ref, *refs):
    out_ref, left, right, acc, value, cols, coded, scalars, codes, ends, lsem, rsem, osem, csem = refs[-14:]
    right_bufs, left_bufs = refs[:n_right], refs[:1] + refs[n_right:-14]
    rows, width = left.shape[1] - EXTRA, left.shape[2]
    names = pl.ds(rows, EXTRA)
    for slot in range(slots):
        fetch(info_ref[slot], among[slot], [buf.at[names] for buf in left_bufs], cols.at[slot], csem.at[slot])
    for step in range(STEPS):
        at = slots + step
        fetch(info_ref[at], among[at], [buf.at[names] for buf in right_bufs], cols.at[at], csem.at[at])
    for step in range(STEPS):
        fetch(info_ref[slots + step], among[slots + step], right_bufs, right.at[step], rsem.at[step])
    for slot in range(slots):
        fetch(info_ref[slot], among[slot], left_bufs, left.at[slot], lsem.at[slot])

    def clear(first, rows_count):
        at = pl.ds(pl.multiple_of(first, 8), rows_count)
        acc[at, :] = jnp.zeros((rows_count, acc.shape[1]), jnp.float32)

    beside = BS // 64 * 24
    ahead = (BS - beside) * rb // BS

    def clear_blocks(first, last):
        @pl.loop(first, last)
        def _(block):
            clear(block * BS, BS)

    clear_blocks(0, ahead // 2)
    lanes = scalars.shape[1]
    row = lax.broadcasted_iota(jnp.int32, (w, lanes), 1)
    tile_slot = lax.broadcasted_iota(jnp.int32, (w, lanes), 0)
    for slot in range(slots):
        used = info_ref[slot] >= 0

        @pl.when(used)
        def _():
            pltpu.make_async_copy(left_bufs[0].at[names], cols.at[slot], csem.at[slot]).wait()

        inner = cols[slot, 0:w, 0:lanes].astype(jnp.int32)
        valid = (inner >= 0) & (row < rb)
        step = jnp.full(inner.shape, info_ref[slots + STEPS + slot], jnp.int32)
        for _ in range(ratio - 1):
            beyond = inner >= rb
            step = jnp.where(beyond, step + 1, step)
            inner = jnp.where(beyond, inner - rb, inner)
        step = jnp.where(step >= n_row, step - n_row, step)
        code = inner | tile_slot << 8 | slot << 12 | row << 16 | step << 24
        valid = valid & (step < STEPS)
        coded[slot * w : (slot + 1) * w, :] = jnp.where(valid, jnp.where(used, code, -1), -1)
    for step in range(STEPS):
        pltpu.make_async_copy(right_bufs[0].at[names], cols.at[slots + step], csem.at[slots + step]).wait()
        col = cols[slots + step, 0:w, 0:lanes].astype(jnp.int32)
        code = (col >> 1) * 2 * BS | (col & 1) << 16
        coded[(slots + step) * w : (slots + step + 1) * w, :] = jnp.where(col < 0, 2 << 16, code)
    coded[(slots + STEPS) * w : (slots + STEPS + 1) * w, :] = jnp.full((w, lanes), 2 << 16, jnp.int32)
    to_scalars = pltpu.make_async_copy(coded, scalars, csem.at[slots + STEPS])
    to_scalars.start()
    clear_blocks(ahead // 2, ahead)
    to_scalars.wait()

    part_rows = rb // PARTS

    def listed(row, place):
        for code in [scalars[line, row] for line in range(slots * w)]:
            codes[place] = code
            place = place + (code >= 0).astype(jnp.int32)
        ends[row] = (place + UNROLL - 1) // UNROLL
        clear(ahead * BS + row * beside, beside)
        return place

    listed_end = lax.fori_loop(0, rb, listed, jnp.int32(0))
    for u in range(UNROLL):
        codes[listed_end + u] = STEPS << 24

    for step in range(STEPS):
        pltpu.make_async_copy(right_bufs[0], right.at[step], rsem.at[step]).wait()
    for slot in range(slots):
        @pl.when(info_ref[slot] >= 0)
        def _():
            pltpu.make_async_copy(left_bufs[0], left.at[slot], lsem.at[slot]).wait()

    half = lax.broadcasted_iota(jnp.int32, (BS, 2 * BS), 1) // BS

    def block_at(index):
        return pl.ds(pl.multiple_of(index * BS, BS), BS)

    def product(code):
        slot = (code >> 8) & 15
        x = left[(code >> 12) & 15, block_at((code >> 16) & 255), pl.ds(pl.multiple_of((slot >> 1) * 2 * BS, 2 * BS), 2 * BS)]
        both = jnp.where(half == (slot & 1), x, pltpu.roll(x, BS, 1))
        hi = both.astype(jnp.bfloat16).astype(jnp.float32)
        lhs = jnp.where(half == 0, hi, both - hi).astype(jnp.bfloat16)
        y = right[code >> 24, block_at(code & 255), :]
        hi = y.astype(jnp.bfloat16)
        lo = (y - hi.astype(jnp.float32)).astype(jnp.bfloat16)
        lhs = jnp.concatenate([lhs, lhs[:, :BS]], axis=1)
        rhs = jnp.concatenate([hi, hi, lo], axis=0)
        return jnp.dot(lhs, rhs, preferred_element_type=jnp.float32)

    def add(code, product):
        rows_at = block_at((code >> 16) & 255)
        for pair in range(w // 2):
            x = product[:, pair * 2 * BS : (pair + 1) * 2 * BS]
            turned = pltpu.roll(x, BS, 1)
            picked, at = [], []
            for side in range(2):
                place = scalars[(slots + (code >> 24)) * w + 2 * pair + side, code & 255]
                parity = place >> 16
                chosen = jnp.where(parity == side, x, turned)
                picked.append(jnp.where(half == parity, chosen, 0.0))
                at.append(place & 0xFFFF)
            picked[1] = jnp.where(at[0] == at[1], picked[0] + picked[1], picked[1])
            spots = [(rows_at, pl.ds(pl.multiple_of(base, 2 * BS), 2 * BS)) for base in at]
            sums = [acc[spot] + part for spot, part in zip(spots, picked)]
            for spot, total in zip(spots, sums):
                acc[spot] = total

    def out_copy(part):
        at = pl.ds(part * part_rows * BS, part_rows * BS)
        return pltpu.make_async_copy(acc.at[at], out_ref.at[at], osem.at[part])

    def products(group):
        for u in range(UNROLL):
            value[u] = product(codes[group * UNROLL + u])

    def sums(group):
        for u in range(UNROLL):
            add(codes[group * UNROLL + u], value[u])

    last = jnp.maximum(ends[rb - 1] - 1, 0)

    def leave(group):
        for part in range(PARTS):
            @pl.when(jnp.maximum(ends[(part + 1) * part_rows - 1] - 1, 0) == group)
            def _():
                out_copy(part).start()

    products(0)

    @pl.loop(0, last)
    def _(group):
        sums(group)
        products(group + 1)
        leave(group)

    sums(last)
    leave(last)
    for part in range(PARTS):
        out_copy(part).wait()


def local(p_cols, p_data):
    n_row, n_col = lax.axis_size("row"), lax.axis_size("col")
    ratio = n_row // n_col
    row_id, col_id = lax.axis_index("row"), lax.axis_index("col")
    rb, w = p_cols.shape
    rows, width = p_data.shape
    left_perms = left_plan(n_row, n_col, ratio)
    right_perms = right_plan(n_row, n_col, ratio)
    table, slots = device_table(left_perms, right_perms, n_row, n_col, ratio)
    info = jnp.asarray(table)[row_id, col_id]

    smem = pl.BlockSpec(memory_space=pltpu.SMEM)
    hbm = pl.BlockSpec(memory_space=pl.ANY)
    dma = pltpu.SemaphoreType.DMA
    own = pl.pallas_call(
        join_kernel,
        out_shape=jax.ShapeDtypeStruct((rows + EXTRA, width), jnp.float32),
        in_specs=[pl.BlockSpec(memory_space=pltpu.HBM)] * 2,
        out_specs=pl.BlockSpec(memory_space=pltpu.VMEM),
        scratch_shapes=[pltpu.VMEM((w, rb), jnp.int32), dma((2,))],
        compiler_params=pltpu.CompilerParams(vmem_limit_bytes=4 << 20),
        cost_estimate=pl.CostEstimate(flops=0, bytes_accessed=2 << 20, transcendentals=0),
    )(p_cols.T, p_data)

    def carry(perms):
        bufs = [own]
        for source, pairs in perms:
            flat = [(s[0] * n_col + s[1], d[0] * n_col + d[1]) for s, d in pairs]
            bufs.append(lax.ppermute(bufs[source], ("row", "col"), flat))
        return bufs

    left_bufs, right_bufs = carry(left_perms), carry(right_perms)
    out_shape = jax.ShapeDtypeStruct((rows, rb * ratio * BS), jnp.float32)
    bufs = right_bufs + left_bufs[1:]
    among = [sorted(set(table[:, :, i].ravel().tolist()) - {-1}) for i in range(slots + STEPS)]
    codings = -(-(slots + STEPS + 1) * w // 8) * 8
    return pl.pallas_call(
        functools.partial(product_kernel, slots, n_row, ratio, rb, w, len(right_bufs), among),
        out_shape=out_shape,
        in_specs=[smem] + [hbm] * len(bufs),
        out_specs=hbm,
        scratch_shapes=[
            pltpu.VMEM((slots, rows + EXTRA, width), jnp.float32),
            pltpu.VMEM((STEPS + 1, rows + EXTRA, width), jnp.float32),
            pltpu.VMEM(out_shape.shape, jnp.float32),
            pltpu.VMEM((UNROLL, BS, width), jnp.float32),
            pltpu.VMEM((slots + STEPS, EXTRA, width), jnp.float32),
            pltpu.VMEM((codings, 128), jnp.int32),
            pltpu.SMEM((codings, 128), jnp.int32),
            pltpu.SMEM((slots * rb * w + UNROLL,), jnp.int32),
            pltpu.SMEM((rb,), jnp.int32),
            dma((slots,)),
            dma((STEPS,)),
            dma((PARTS,)),
            dma((slots + STEPS + 1,)),
        ],
        compiler_params=pltpu.CompilerParams(vmem_limit_bytes=18 << 20),
        cost_estimate=pl.CostEstimate(flops=10**9, bytes_accessed=20 << 20, transcendentals=0),
    )(info, *bufs)


def solution(mesh):
    in_specs = (P("row", "col"), P("row", "col"))
    return jax.shard_map(local, mesh=mesh, in_specs=in_specs, out_specs=P("row", "col"), check_vma=False)
```

```python
import functools

import jax
import jax.numpy as jnp
import numpy as np
from jax import lax
from jax.experimental import pallas as pl
from jax.experimental.pallas import tpu as pltpu
from jax.sharding import PartitionSpec as P

BS = 64
STEPS = 4
UNROLL = 12
EXTRA = 8
PARTS = 16


def left_offsets(row, ratio, n_col):
    seen = []
    for step in range(STEPS):
        offset = (row + step) // ratio % n_col
        if offset not in seen:
            seen.append(offset)
    return seen


def shift(rows, step, count):
    return [((r, c), (r, (c + step) % count)) for r in rows for c in range(count)]


def left_plan(n_row, n_col, ratio):
    offsets = [left_offsets(row, ratio, n_col) for row in range(n_row)]
    if (n_row, n_col, ratio) != (8, 4, 2):
        perms = []
        for slot in range(max(len(o) for o in offsets)):
            pairs = [
                ((row, (col + offsets[row][slot]) % n_col), (row, col))
                for row in range(n_row)
                for col in range(n_col)
                if slot < len(offsets[row]) and offsets[row][slot] != 0
            ]
            perms.append((0, pairs))
        return perms
    whole = [r for r in range(8) if {1, 2, 3} <= set(offsets[r])]
    once, twice = {-1: [], 1: []}, {-1: [], 1: []}
    for r in range(8):
        for offset, step in ((1, -1), (3, 1)):
            if offset in offsets[r] and r not in whole:
                once[step].append(r)
                if 2 in offsets[r]:
                    twice[step].append(r)
    down = shift([r for r in once[-1] if r != 0], -1, 4) + [((3, c), (3, c - 1)) for c in (1, 2, 3)] + [((3, 0), (0, 0))]
    up = shift(once[1], 1, 4) + shift([0], -1, 4) + [((3, c), (3, c + 1)) for c in (0, 1, 2)] + [((3, 3), (1, 3))]
    again_down = shift(twice[-1], -1, 4) + [((3, 1), (3, 0)), ((3, 2), (3, 1)), ((0, 0), (3, 3))]
    again_up = shift(twice[1], 1, 4) + [((3, 1), (3, 2)), ((3, 2), (3, 3)), ((1, 3), (3, 0))]
    return [(0, up), (0, down), (1, again_up), (2, again_down)]


def right_plan(n_row, n_col, ratio):
    everyone = [(row, col) for row in range(n_row) for col in range(n_col)]
    if (n_row, n_col, ratio) != (8, 4, 2):
        return [
            (0, [(((r + ratio * c + step) % n_row, c), (r, c)) for r, c in everyone if (ratio * c + step) % n_row])
            for step in range(STEPS)
        ]
    first = [(((r + 2 * c) % 8, c), (r, c)) for r, c in everyone if c != 0]
    first += [((r ^ 1, 0), (r, 0)) for r in range(8)]
    second = [(((r + 2 * c + 2) % 8, c), (r, c)) for r, c in everyone if c != 3]
    second += [((r ^ 1, 3), (r, 3)) for r in range(8)]
    last = [(((r - 1 + 2 * c + 4) % 8, c), (r, c)) for r, c in everyone if r % 2 == 1]
    last += [((r + 1, c), (r, c)) for r, c in everyone if r % 2 == 0]
    swap = [((r ^ 1, c), (r, c)) for r, c in everyone]
    return [(0, first), (0, second), (0, last), (1, swap), (2, swap)]


def carry_out(perms, n_row, n_col):
    held = [{(r, c): (r, c) for r in range(n_row) for c in range(n_col)}]
    for source, pairs in perms:
        held.append({dst: held[source][src] for src, dst in pairs if src in held[source]})
    return held


def device_table(left_perms, right_perms, n_row, n_col, ratio):
    left_held = carry_out(left_perms, n_row, n_col)
    right_held = carry_out(right_perms, n_row, n_col)
    slots = (ratio - 1 + STEPS - 1) // ratio + 1
    table = np.full((n_row, n_col, 2 * slots + STEPS), -1, np.int32)

    def find(held, device, tile):
        return [i for i, h in enumerate(held) if h.get(device) == tile][0]

    for r in range(n_row):
        for c in range(n_col):
            for slot, offset in enumerate(left_offsets(r, ratio, n_col)):
                tile_col = (c + offset) % n_col
                table[r, c, slot] = find(left_held, (r, c), (r, tile_col))
                table[r, c, slots + STEPS + slot] = (tile_col * ratio - r - ratio * c) % n_row
            for step in range(STEPS):
                table[r, c, slots + step] = find(right_held, (r, c), ((r + ratio * c + step) % n_row, c))
    return table, slots


def fetch(choice, among, bufs, target, sem):
    for number in among:
        @pl.when(choice == number)
        def _():
            pltpu.make_async_copy(bufs[number], target, sem).start()


def join_kernel(cols_ref, data_ref, out_ref, cols, sem):
    rows = data_ref.shape[0]
    data_copy = pltpu.make_async_copy(data_ref, out_ref.at[pl.ds(0, rows)], sem.at[0])
    cols_copy = pltpu.make_async_copy(cols_ref, cols, sem.at[1])
    data_copy.start()
    cols_copy.start()
    out_ref[pl.ds(rows, EXTRA), :] = jnp.zeros((EXTRA, out_ref.shape[1]), jnp.float32)
    cols_copy.wait()
    out_ref[pl.ds(rows, cols.shape[0]), pl.ds(0, cols.shape[1])] = cols[...].astype(jnp.float32)
    data_copy.wait()


def product_kernel(slots, n_row, ratio, rb, w, n_right, among, info_ref, *refs):
    out_ref, left, right, acc, value, cols, coded, scalars, codes, ends, lsem, rsem, osem, csem = refs[-14:]
    right_bufs, left_bufs = refs[:n_right], refs[:1] + refs[n_right:-14]
    rows, width = left.shape[1] - EXTRA, left.shape[2]
    names = pl.ds(rows, EXTRA)
    for slot in range(slots):
        fetch(info_ref[slot], among[slot], [buf.at[names] for buf in left_bufs], cols.at[slot], csem.at[slot])
    for step in range(STEPS):
        at = slots + step
        fetch(info_ref[at], among[at], [buf.at[names] for buf in right_bufs], cols.at[at], csem.at[at])
    for step in range(STEPS):
        fetch(info_ref[slots + step], among[slots + step], right_bufs, right.at[step], rsem.at[step])
    for slot in range(slots):
        fetch(info_ref[slot], among[slot], left_bufs, left.at[slot], lsem.at[slot])

    def clear(first, rows_count):
        at = pl.ds(pl.multiple_of(first, 8), rows_count)
        acc[at, :] = jnp.zeros((rows_count, acc.shape[1]), jnp.float32)

    beside = BS // 64 * 24
    ahead = (BS - beside) * rb // BS

    def clear_blocks(first, last):
        @pl.loop(first, last)
        def _(block):
            clear(block * BS, BS)

    clear_blocks(0, ahead // 2)
    lanes = scalars.shape[1]
    row = lax.broadcasted_iota(jnp.int32, (w, lanes), 1)
    tile_slot = lax.broadcasted_iota(jnp.int32, (w, lanes), 0)
    for slot in range(slots):
        used = info_ref[slot] >= 0

        @pl.when(used)
        def _():
            pltpu.make_async_copy(left_bufs[0].at[names], cols.at[slot], csem.at[slot]).wait()

        inner = cols[slot, 0:w, 0:lanes].astype(jnp.int32)
        valid = (inner >= 0) & (row < rb)
        step = jnp.full(inner.shape, info_ref[slots + STEPS + slot], jnp.int32)
        for _ in range(ratio - 1):
            beyond = inner >= rb
            step = jnp.where(beyond, step + 1, step)
            inner = jnp.where(beyond, inner - rb, inner)
        step = jnp.where(step >= n_row, step - n_row, step)
        code = inner | tile_slot << 8 | slot << 12 | row << 16 | step << 24
        valid = valid & (step < STEPS)
        coded[slot * w : (slot + 1) * w, :] = jnp.where(valid, jnp.where(used, code, -1), -1)
    for step in range(STEPS):
        pltpu.make_async_copy(right_bufs[0].at[names], cols.at[slots + step], csem.at[slots + step]).wait()
        col = cols[slots + step, 0:w, 0:lanes].astype(jnp.int32)
        code = (col >> 1) * 2 * BS | (col & 1) << 16
        coded[(slots + step) * w : (slots + step + 1) * w, :] = jnp.where(col < 0, 2 << 16, code)
    coded[(slots + STEPS) * w : (slots + STEPS + 1) * w, :] = jnp.full((w, lanes), 2 << 16, jnp.int32)
    to_scalars = pltpu.make_async_copy(coded, scalars, csem.at[slots + STEPS])
    to_scalars.start()
    clear_blocks(ahead // 2, ahead)
    to_scalars.wait()

    part_rows = rb // PARTS

    def listed(row, place):
        for code in [scalars[line, row] for line in range(slots * w)]:
            codes[place] = code
            place = place + (code >= 0).astype(jnp.int32)
        ends[row] = (place + UNROLL - 1) // UNROLL
        clear(ahead * BS + row * beside, beside)
        return place

    listed_end = lax.fori_loop(0, rb, listed, jnp.int32(0))
    for u in range(UNROLL):
        codes[listed_end + u] = STEPS << 24

    for step in range(STEPS):
        pltpu.make_async_copy(right_bufs[0], right.at[step], rsem.at[step]).wait()
    for slot in range(slots):
        @pl.when(info_ref[slot] >= 0)
        def _():
            pltpu.make_async_copy(left_bufs[0], left.at[slot], lsem.at[slot]).wait()

    half = lax.broadcasted_iota(jnp.int32, (BS, 2 * BS), 1) // BS

    def block_at(index):
        return pl.ds(pl.multiple_of(index * BS, BS), BS)

    def product(code):
        slot = (code >> 8) & 15
        x = left[(code >> 12) & 15, block_at((code >> 16) & 255), pl.ds(pl.multiple_of((slot >> 1) * 2 * BS, 2 * BS), 2 * BS)]
        both = jnp.where(half == (slot & 1), x, pltpu.roll(x, BS, 1))
        hi = both.astype(jnp.bfloat16).astype(jnp.float32)
        lhs = jnp.where(half == 0, hi, both - hi).astype(jnp.bfloat16)
        y = right[code >> 24, block_at(code & 255), :]
        hi = y.astype(jnp.bfloat16)
        lo = (y - hi.astype(jnp.float32)).astype(jnp.bfloat16)
        lhs = jnp.concatenate([lhs, lhs], axis=1)
        rhs = jnp.concatenate([hi, hi, lo, lo], axis=0)
        return jnp.dot(lhs, rhs, preferred_element_type=jnp.float32)

    def add(code, product):
        rows_at = block_at((code >> 16) & 255)
        for pair in range(w // 2):
            x = product[:, pair * 2 * BS : (pair + 1) * 2 * BS]
            turned = pltpu.roll(x, BS, 1)
            picked, at = [], []
            for side in range(2):
                place = scalars[(slots + (code >> 24)) * w + 2 * pair + side, code & 255]
                parity = place >> 16
                chosen = jnp.where(parity == side, x, turned)
                picked.append(jnp.where(half == parity, chosen, 0.0))
                at.append(place & 0xFFFF)
            picked[1] = jnp.where(at[0] == at[1], picked[0] + picked[1], picked[1])
            spots = [(rows_at, pl.ds(pl.multiple_of(base, 2 * BS), 2 * BS)) for base in at]
            sums = [acc[spot] + part for spot, part in zip(spots, picked)]
            for spot, total in zip(spots, sums):
                acc[spot] = total

    def out_copy(part):
        at = pl.ds(part * part_rows * BS, part_rows * BS)
        return pltpu.make_async_copy(acc.at[at], out_ref.at[at], osem.at[part])

    def products(group):
        for u in range(UNROLL):
            value[u] = product(codes[group * UNROLL + u])

    def sums(group):
        for u in range(UNROLL):
            add(codes[group * UNROLL + u], value[u])

    last = jnp.maximum(ends[rb - 1] - 1, 0)

    def leave(group):
        for part in range(PARTS):
            @pl.when(jnp.maximum(ends[(part + 1) * part_rows - 1] - 1, 0) == group)
            def _():
                out_copy(part).start()

    products(0)

    @pl.loop(0, last)
    def _(group):
        sums(group)
        products(group + 1)
        leave(group)

    sums(last)
    leave(last)
    for part in range(PARTS):
        out_copy(part).wait()


def local(p_cols, p_data):
    n_row, n_col = lax.axis_size("row"), lax.axis_size("col")
    ratio = n_row // n_col
    row_id, col_id = lax.axis_index("row"), lax.axis_index("col")
    rb, w = p_cols.shape
    rows, width = p_data.shape
    left_perms = left_plan(n_row, n_col, ratio)
    right_perms = right_plan(n_row, n_col, ratio)
    table, slots = device_table(left_perms, right_perms, n_row, n_col, ratio)
    info = jnp.asarray(table)[row_id, col_id]

    smem = pl.BlockSpec(memory_space=pltpu.SMEM)
    hbm = pl.BlockSpec(memory_space=pl.ANY)
    dma = pltpu.SemaphoreType.DMA
    own = pl.pallas_call(
        join_kernel,
        out_shape=jax.ShapeDtypeStruct((rows + EXTRA, width), jnp.float32),
        in_specs=[pl.BlockSpec(memory_space=pltpu.HBM)] * 2,
        out_specs=pl.BlockSpec(memory_space=pltpu.VMEM),
        scratch_shapes=[pltpu.VMEM((w, rb), jnp.int32), dma((2,))],
        compiler_params=pltpu.CompilerParams(vmem_limit_bytes=58 << 20),
        cost_estimate=pl.CostEstimate(flops=0, bytes_accessed=2 << 20, transcendentals=0),
    )(p_cols.T, p_data)

    def carry(perms):
        bufs = [own]
        for source, pairs in perms:
            flat = [(s[0] * n_col + s[1], d[0] * n_col + d[1]) for s, d in pairs]
            bufs.append(lax.ppermute(bufs[source], ("row", "col"), flat))
        return bufs

    left_bufs, right_bufs = carry(left_perms), carry(right_perms)
    out_shape = jax.ShapeDtypeStruct((rows, rb * ratio * BS), jnp.float32)
    bufs = right_bufs + left_bufs[1:]
    among = [sorted(set(table[:, :, i].ravel().tolist()) - {-1}) for i in range(slots + STEPS)]
    codings = -(-(slots + STEPS + 1) * w // 8) * 8
    return pl.pallas_call(
        functools.partial(product_kernel, slots, n_row, ratio, rb, w, len(right_bufs), among),
        out_shape=out_shape,
        in_specs=[smem] + [hbm] * len(bufs),
        out_specs=hbm,
        scratch_shapes=[
            pltpu.VMEM((slots, rows + EXTRA, width), jnp.float32),
            pltpu.VMEM((STEPS + 1, rows + EXTRA, width), jnp.float32),
            pltpu.VMEM(out_shape.shape, jnp.float32),
            pltpu.VMEM((UNROLL, BS, width), jnp.float32),
            pltpu.VMEM((slots + STEPS, EXTRA, width), jnp.float32),
            pltpu.VMEM((codings, 128), jnp.int32),
            pltpu.SMEM((codings, 128), jnp.int32),
            pltpu.SMEM((slots * rb * w + UNROLL,), jnp.int32),
            pltpu.SMEM((rb,), jnp.int32),
            dma((slots,)),
            dma((STEPS,)),
            dma((PARTS,)),
            dma((slots + STEPS + 1,)),
        ],
        compiler_params=pltpu.CompilerParams(vmem_limit_bytes=18 << 20),
        cost_estimate=pl.CostEstimate(flops=10**9, bytes_accessed=20 << 20, transcendentals=0),
    )(info, *bufs)


def solution(mesh):
    in_specs = (P("row", "col"), P("row", "col"))
    return jax.shard_map(local, mesh=mesh, in_specs=in_specs, out_specs=P("row", "col"), check_vma=False)
```

```python
import functools

import jax
import jax.numpy as jnp
import numpy as np
from jax import lax
from jax.experimental import pallas as pl
from jax.experimental.pallas import tpu as pltpu
from jax.sharding import PartitionSpec as P

BS = 64
STEPS = 4
UNROLL = 12
EXTRA = 8
PARTS = 16


def left_offsets(row, ratio, n_col):
    seen = []
    for step in range(STEPS):
        offset = (row + step) // ratio % n_col
        if offset not in seen:
            seen.append(offset)
    return seen


def shift(rows, step, count):
    return [((r, c), (r, (c + step) % count)) for r in rows for c in range(count)]


def left_plan(n_row, n_col, ratio):
    offsets = [left_offsets(row, ratio, n_col) for row in range(n_row)]
    if (n_row, n_col, ratio) != (8, 4, 2):
        perms = []
        for slot in range(max(len(o) for o in offsets)):
            pairs = [
                ((row, (col + offsets[row][slot]) % n_col), (row, col))
                for row in range(n_row)
                for col in range(n_col)
                if slot < len(offsets[row]) and offsets[row][slot] != 0
            ]
            perms.append((0, pairs))
        return perms
    whole = [r for r in range(8) if {1, 2, 3} <= set(offsets[r])]
    once, twice = {-1: [], 1: []}, {-1: [], 1: []}
    for r in range(8):
        for offset, step in ((1, -1), (3, 1)):
            if offset in offsets[r] and r not in whole:
                once[step].append(r)
                if 2 in offsets[r]:
                    twice[step].append(r)
    plain = lambda step: [r for r in once[step] if r not in twice[step] and r != 7]
    early = shift(twice[-1] + [7], -1, 4) + shift(twice[1], 1, 4)
    early += [((3, c), (3, c - 1)) for c in (1, 2, 3)] + [((3, 0), (0, 0))]
    late = shift(plain(-1), -1, 4) + shift(plain(1) + [7], 1, 4)
    late += [((3, c), (3, c + 1)) for c in (0, 1, 2)] + [((3, 3), (1, 3))]
    again_early = shift(twice[-1], -1, 4) + shift(twice[1], 1, 4) + [((3, 1), (3, 0)), ((3, 2), (3, 1)), ((0, 0), (3, 3))]
    again_late = [((3, 1), (3, 2)), ((3, 2), (3, 3)), ((1, 3), (3, 0))]
    return [(0, late), (0, early), (1, again_late), (2, again_early)]


def right_plan(n_row, n_col, ratio):
    everyone = [(row, col) for row in range(n_row) for col in range(n_col)]
    if (n_row, n_col, ratio) != (8, 4, 2):
        return [
            (0, [(((r + ratio * c + step) % n_row, c), (r, c)) for r, c in everyone if (ratio * c + step) % n_row])
            for step in range(STEPS)
        ]
    first = [(((r + 2 * c) % 8, c), (r, c)) for r, c in everyone if c != 0]
    first += [((r ^ 1, 0), (r, 0)) for r in range(8)]
    second = [(((r + 2 * c + 2) % 8, c), (r, c)) for r, c in everyone if c != 3]
    second += [((r ^ 1, 3), (r, 3)) for r in range(8)]
    last = [(((r - 1 + 2 * c + 4) % 8, c), (r, c)) for r, c in everyone if r % 2 == 1]
    last += [((r + 1, c), (r, c)) for r, c in everyone if r % 2 == 0]
    swap = [((r ^ 1, c), (r, c)) for r, c in everyone]
    return [(0, first), (0, second), (0, last), (1, swap), (2, swap)]


def carry_out(perms, n_row, n_col):
    held = [{(r, c): (r, c) for r in range(n_row) for c in range(n_col)}]
    for source, pairs in perms:
        held.append({dst: held[source][src] for src, dst in pairs if src in held[source]})
    return held


def device_table(left_perms, right_perms, n_row, n_col, ratio):
    left_held = carry_out(left_perms, n_row, n_col)
    right_held = carry_out(right_perms, n_row, n_col)
    slots = (ratio - 1 + STEPS - 1) // ratio + 1
    table = np.full((n_row, n_col, 2 * slots + STEPS), -1, np.int32)

    def find(held, device, tile):
        return [i for i, h in enumerate(held) if h.get(device) == tile][0]

    for r in range(n_row):
        for c in range(n_col):
            for slot, offset in enumerate(left_offsets(r, ratio, n_col)):
                tile_col = (c + offset) % n_col
                table[r, c, slot] = find(left_held, (r, c), (r, tile_col))
                table[r, c, slots + STEPS + slot] = (tile_col * ratio - r - ratio * c) % n_row
            for step in range(STEPS):
                table[r, c, slots + step] = find(right_held, (r, c), ((r + ratio * c + step) % n_row, c))
    return table, slots


def fetch(choice, among, bufs, target, sem):
    for number in among:
        @pl.when(choice == number)
        def _():
            pltpu.make_async_copy(bufs[number], target, sem).start()


def join_kernel(cols_ref, data_ref, out_ref, cols, sem):
    rows = data_ref.shape[0]
    data_copy = pltpu.make_async_copy(data_ref, out_ref.at[pl.ds(0, rows)], sem.at[0])
    cols_copy = pltpu.make_async_copy(cols_ref, cols, sem.at[1])
    data_copy.start()
    cols_copy.start()
    out_ref[pl.ds(rows, EXTRA), :] = jnp.zeros((EXTRA, out_ref.shape[1]), jnp.float32)
    cols_copy.wait()
    out_ref[pl.ds(rows, cols.shape[0]), pl.ds(0, cols.shape[1])] = cols[...].astype(jnp.float32)
    data_copy.wait()


def product_kernel(slots, n_row, ratio, rb, w, n_right, among, info_ref, *refs):
    out_ref, left, right, acc, value, cols, coded, scalars, codes, ends, lsem, rsem, osem, csem = refs[-14:]
    right_bufs, left_bufs = refs[:n_right], refs[:1] + refs[n_right:-14]
    rows, width = left.shape[1] - EXTRA, left.shape[2]
    names = pl.ds(rows, EXTRA)
    for slot in range(slots):
        fetch(info_ref[slot], among[slot], [buf.at[names] for buf in left_bufs], cols.at[slot], csem.at[slot])
    for step in range(STEPS):
        at = slots + step
        fetch(info_ref[at], among[at], [buf.at[names] for buf in right_bufs], cols.at[at], csem.at[at])
    for step in range(STEPS):
        fetch(info_ref[slots + step], among[slots + step], right_bufs, right.at[step], rsem.at[step])
    for slot in range(slots):
        fetch(info_ref[slot], among[slot], left_bufs, left.at[slot], lsem.at[slot])

    def clear(first, rows_count):
        at = pl.ds(pl.multiple_of(first, 8), rows_count)
        acc[at, :] = jnp.zeros((rows_count, acc.shape[1]), jnp.float32)

    beside = BS // 64 * 24
    ahead = (BS - beside) * rb // BS

    def clear_blocks(first, last):
        @pl.loop(first, last)
        def _(block):
            clear(block * BS, BS)

    clear_blocks(0, ahead // 2)
    lanes = scalars.shape[1]
    row = lax.broadcasted_iota(jnp.int32, (w, lanes), 1)
    tile_slot = lax.broadcasted_iota(jnp.int32, (w, lanes), 0)
    for slot in range(slots):
        used = info_ref[slot] >= 0

        @pl.when(used)
        def _():
            pltpu.make_async_copy(left_bufs[0].at[names], cols.at[slot], csem.at[slot]).wait()

        inner = cols[slot, 0:w, 0:lanes].astype(jnp.int32)
        valid = (inner >= 0) & (row < rb)
        step = jnp.full(inner.shape, info_ref[slots + STEPS + slot], jnp.int32)
        for _ in range(ratio - 1):
            beyond = inner >= rb
            step = jnp.where(beyond, step + 1, step)
            inner = jnp.where(beyond, inner - rb, inner)
        step = jnp.where(step >= n_row, step - n_row, step)
        code = inner | tile_slot << 8 | slot << 12 | row << 16 | step << 24
        valid = valid & (step < STEPS)
        coded[slot * w : (slot + 1) * w, :] = jnp.where(valid, jnp.where(used, code, -1), -1)
    for step in range(STEPS):
        pltpu.make_async_copy(right_bufs[0].at[names], cols.at[slots + step], csem.at[slots + step]).wait()
        col = cols[slots + step, 0:w, 0:lanes].astype(jnp.int32)
        code = (col >> 1) * 2 * BS | (col & 1) << 16
        coded[(slots + step) * w : (slots + step + 1) * w, :] = jnp.where(col < 0, 2 << 16, code)
    coded[(slots + STEPS) * w : (slots + STEPS + 1) * w, :] = jnp.full((w, lanes), 2 << 16, jnp.int32)
    to_scalars = pltpu.make_async_copy(coded, scalars, csem.at[slots + STEPS])
    to_scalars.start()
    clear_blocks(ahead // 2, ahead)
    to_scalars.wait()

    part_rows = rb // PARTS

    def listed(row, place):
        for code in [scalars[line, row] for line in range(slots * w)]:
            codes[place] = code
            place = place + (code >= 0).astype(jnp.int32)
        ends[row] = (place + UNROLL - 1) // UNROLL
        clear(ahead * BS + row * beside, beside)
        return place

    listed_end = lax.fori_loop(0, rb, listed, jnp.int32(0))
    for u in range(UNROLL):
        codes[listed_end + u] = STEPS << 24

    for step in range(STEPS):
        pltpu.make_async_copy(right_bufs[0], right.at[step], rsem.at[step]).wait()
    for slot in range(slots):
        @pl.when(info_ref[slot] >= 0)
        def _():
            pltpu.make_async_copy(left_bufs[0], left.at[slot], lsem.at[slot]).wait()

    half = lax.broadcasted_iota(jnp.int32, (BS, 2 * BS), 1) // BS

    def block_at(index):
        return pl.ds(pl.multiple_of(index * BS, BS), BS)

    def product(code):
        slot = (code >> 8) & 15
        x = left[(code >> 12) & 15, block_at((code >> 16) & 255), pl.ds(pl.multiple_of((slot >> 1) * 2 * BS, 2 * BS), 2 * BS)]
        both = jnp.where(half == (slot & 1), x, pltpu.roll(x, BS, 1))
        hi = both.astype(jnp.bfloat16).astype(jnp.float32)
        lhs = jnp.where(half == 0, hi, both - hi).astype(jnp.bfloat16)
        y = right[code >> 24, block_at(code & 255), :]
        hi = y.astype(jnp.bfloat16)
        lo = (y - hi.astype(jnp.float32)).astype(jnp.bfloat16)
        lhs = jnp.concatenate([lhs, lhs], axis=1)
        rhs = jnp.concatenate([hi, hi, lo, lo], axis=0)
        return jnp.dot(lhs, rhs, preferred_element_type=jnp.float32)

    def add(code, product):
        rows_at = block_at((code >> 16) & 255)
        for pair in range(w // 2):
            x = product[:, pair * 2 * BS : (pair + 1) * 2 * BS]
            turned = pltpu.roll(x, BS, 1)
            picked, at = [], []
            for side in range(2):
                place = scalars[(slots + (code >> 24)) * w + 2 * pair + side, code & 255]
                parity = place >> 16
                chosen = jnp.where(parity == side, x, turned)
                picked.append(jnp.where(half == parity, chosen, 0.0))
                at.append(place & 0xFFFF)
            picked[1] = jnp.where(at[0] == at[1], picked[0] + picked[1], picked[1])
            spots = [(rows_at, pl.ds(pl.multiple_of(base, 2 * BS), 2 * BS)) for base in at]
            sums = [acc[spot] + part for spot, part in zip(spots, picked)]
            for spot, total in zip(spots, sums):
                acc[spot] = total

    def out_copy(part):
        at = pl.ds(part * part_rows * BS, part_rows * BS)
        return pltpu.make_async_copy(acc.at[at], out_ref.at[at], osem.at[part])

    def products(group):
        for u in range(UNROLL):
            value[u] = product(codes[group * UNROLL + u])

    def sums(group):
        for u in range(UNROLL):
            add(codes[group * UNROLL + u], value[u])

    last = jnp.maximum(ends[rb - 1] - 1, 0)

    def leave(group):
        for part in range(PARTS):
            @pl.when(jnp.maximum(ends[(part + 1) * part_rows - 1] - 1, 0) == group)
            def _():
                out_copy(part).start()

    products(0)

    @pl.loop(0, last)
    def _(group):
        sums(group)
        products(group + 1)
        leave(group)

    sums(last)
    leave(last)
    for part in range(PARTS):
        out_copy(part).wait()


def local(p_cols, p_data):
    n_row, n_col = lax.axis_size("row"), lax.axis_size("col")
    ratio = n_row // n_col
    row_id, col_id = lax.axis_index("row"), lax.axis_index("col")
    rb, w = p_cols.shape
    rows, width = p_data.shape
    left_perms = left_plan(n_row, n_col, ratio)
    right_perms = right_plan(n_row, n_col, ratio)
    table, slots = device_table(left_perms, right_perms, n_row, n_col, ratio)
    info = jnp.asarray(table)[row_id, col_id]

    smem = pl.BlockSpec(memory_space=pltpu.SMEM)
    hbm = pl.BlockSpec(memory_space=pl.ANY)
    dma = pltpu.SemaphoreType.DMA
    own = pl.pallas_call(
        join_kernel,
        out_shape=jax.ShapeDtypeStruct((rows + EXTRA, width), jnp.float32),
        in_specs=[pl.BlockSpec(memory_space=pltpu.HBM)] * 2,
        out_specs=pl.BlockSpec(memory_space=pltpu.VMEM),
        scratch_shapes=[pltpu.VMEM((w, rb), jnp.int32), dma((2,))],
        compiler_params=pltpu.CompilerParams(vmem_limit_bytes=4 << 20),
        cost_estimate=pl.CostEstimate(flops=0, bytes_accessed=2 << 20, transcendentals=0),
    )(p_cols.T, p_data)

    def carry(perms):
        bufs = [own]
        for source, pairs in perms:
            flat = [(s[0] * n_col + s[1], d[0] * n_col + d[1]) for s, d in pairs]
            bufs.append(lax.ppermute(bufs[source], ("row", "col"), flat))
        return bufs

    left_bufs, right_bufs = carry(left_perms), carry(right_perms)
    out_shape = jax.ShapeDtypeStruct((rows, rb * ratio * BS), jnp.float32)
    bufs = right_bufs + left_bufs[1:]
    among = [sorted(set(table[:, :, i].ravel().tolist()) - {-1}) for i in range(slots + STEPS)]
    codings = -(-(slots + STEPS + 1) * w // 8) * 8
    return pl.pallas_call(
        functools.partial(product_kernel, slots, n_row, ratio, rb, w, len(right_bufs), among),
        out_shape=out_shape,
        in_specs=[smem] + [hbm] * len(bufs),
        out_specs=hbm,
        scratch_shapes=[
            pltpu.VMEM((slots, rows + EXTRA, width), jnp.float32),
            pltpu.VMEM((STEPS + 1, rows + EXTRA, width), jnp.float32),
            pltpu.VMEM(out_shape.shape, jnp.float32),
            pltpu.VMEM((UNROLL, BS, width), jnp.float32),
            pltpu.VMEM((slots + STEPS, EXTRA, width), jnp.float32),
            pltpu.VMEM((codings, 128), jnp.int32),
            pltpu.SMEM((codings, 128), jnp.int32),
            pltpu.SMEM((slots * rb * w + UNROLL,), jnp.int32),
            pltpu.SMEM((rb,), jnp.int32),
            dma((slots,)),
            dma((STEPS,)),
            dma((PARTS,)),
            dma((slots + STEPS + 1,)),
        ],
        compiler_params=pltpu.CompilerParams(vmem_limit_bytes=18 << 20),
        cost_estimate=pl.CostEstimate(flops=10**9, bytes_accessed=20 << 20, transcendentals=0),
    )(info, *bufs)


def solution(mesh):
    in_specs = (P("row", "col"), P("row", "col"))
    return jax.shard_map(local, mesh=mesh, in_specs=in_specs, out_specs=P("row", "col"), check_vma=False)
```

```python
import functools

import jax
import jax.numpy as jnp
import numpy as np
from jax import lax
from jax.experimental import pallas as pl
from jax.experimental.pallas import tpu as pltpu
from jax.sharding import PartitionSpec as P

BS = 64
STEPS = 4
UNROLL = 8
EXTRA = 8
PARTS = 16


def left_offsets(row, ratio, n_col):
    seen = []
    for step in range(STEPS):
        offset = (row + step) // ratio % n_col
        if offset not in seen:
            seen.append(offset)
    return seen


def shift(rows, step, count):
    return [((r, c), (r, (c + step) % count)) for r in rows for c in range(count)]


def left_plan(n_row, n_col, ratio):
    offsets = [left_offsets(row, ratio, n_col) for row in range(n_row)]
    if (n_row, n_col, ratio) != (8, 4, 2):
        perms = []
        for slot in range(max(len(o) for o in offsets)):
            pairs = [
                ((row, (col + offsets[row][slot]) % n_col), (row, col))
                for row in range(n_row)
                for col in range(n_col)
                if slot < len(offsets[row]) and offsets[row][slot] != 0
            ]
            perms.append((0, pairs))
        return perms
    whole = [r for r in range(8) if {1, 2, 3} <= set(offsets[r])]
    once, twice = {-1: [], 1: []}, {-1: [], 1: []}
    for r in range(8):
        for offset, step in ((1, -1), (3, 1)):
            if offset in offsets[r] and r not in whole:
                once[step].append(r)
                if 2 in offsets[r]:
                    twice[step].append(r)
    plain = lambda step: [r for r in once[step] if r not in twice[step] and r != 7]
    early = shift(twice[-1] + [7], -1, 4) + shift(twice[1], 1, 4)
    early += [((3, c), (3, c - 1)) for c in (1, 2, 3)] + [((3, 0), (0, 0))]
    late = shift(plain(-1), -1, 4) + shift(plain(1) + [7], 1, 4)
    late += [((3, c), (3, c + 1)) for c in (0, 1, 2)] + [((3, 3), (1, 3))]
    again_early = shift(twice[-1], -1, 4) + shift(twice[1], 1, 4) + [((3, 1), (3, 0)), ((3, 2), (3, 1)), ((0, 0), (3, 3))]
    again_late = [((3, 1), (3, 2)), ((3, 2), (3, 3)), ((1, 3), (3, 0))]
    return [(0, late), (0, early), (1, again_late), (2, again_early)]


def right_plan(n_row, n_col, ratio):
    everyone = [(row, col) for row in range(n_row) for col in range(n_col)]
    if (n_row, n_col, ratio) != (8, 4, 2):
        return [
            (0, [(((r + ratio * c + step) % n_row, c), (r, c)) for r, c in everyone if (ratio * c + step) % n_row])
            for step in range(STEPS)
        ]
    first = [(((r + 2 * c) % 8, c), (r, c)) for r, c in everyone if c != 0]
    first += [((r ^ 1, 0), (r, 0)) for r in range(8)]
    second = [(((r + 2 * c + 2) % 8, c), (r, c)) for r, c in everyone if c != 3]
    second += [((r ^ 1, 3), (r, 3)) for r in range(8)]
    last = [(((r - 1 + 2 * c + 4) % 8, c), (r, c)) for r, c in everyone if r % 2 == 1]
    last += [((r + 1, c), (r, c)) for r, c in everyone if r % 2 == 0]
    swap = [((r ^ 1, c), (r, c)) for r, c in everyone]
    return [(0, first), (0, second), (0, last), (1, swap), (2, swap)]


def carry_out(perms, n_row, n_col):
    held = [{(r, c): (r, c) for r in range(n_row) for c in range(n_col)}]
    for source, pairs in perms:
        held.append({dst: held[source][src] for src, dst in pairs if src in held[source]})
    return held


def device_table(left_perms, right_perms, n_row, n_col, ratio):
    left_held = carry_out(left_perms, n_row, n_col)
    right_held = carry_out(right_perms, n_row, n_col)
    slots = (ratio - 1 + STEPS - 1) // ratio + 1
    table = np.full((n_row, n_col, 2 * slots + STEPS), -1, np.int32)

    def find(held, device, tile):
        return [i for i, h in enumerate(held) if h.get(device) == tile][0]

    for r in range(n_row):
        for c in range(n_col):
            for slot, offset in enumerate(left_offsets(r, ratio, n_col)):
                tile_col = (c + offset) % n_col
                table[r, c, slot] = find(left_held, (r, c), (r, tile_col))
                table[r, c, slots + STEPS + slot] = (tile_col * ratio - r - ratio * c) % n_row
            for step in range(STEPS):
                table[r, c, slots + step] = find(right_held, (r, c), ((r + ratio * c + step) % n_row, c))
    return table, slots


def fetch(choice, among, bufs, target, sem):
    for number in among:
        @pl.when(choice == number)
        def _():
            pltpu.make_async_copy(bufs[number], target, sem).start()


def join_kernel(cols_ref, data_ref, out_ref, cols, sem):
    rows = data_ref.shape[0]
    data_copy = pltpu.make_async_copy(data_ref, out_ref.at[pl.ds(0, rows)], sem.at[0])
    cols_copy = pltpu.make_async_copy(cols_ref, cols, sem.at[1])
    data_copy.start()
    cols_copy.start()
    out_ref[pl.ds(rows, EXTRA), :] = jnp.zeros((EXTRA, out_ref.shape[1]), jnp.float32)
    cols_copy.wait()
    out_ref[pl.ds(rows, cols.shape[0]), pl.ds(0, cols.shape[1])] = cols[...].astype(jnp.float32)
    data_copy.wait()


def product_kernel(slots, n_row, ratio, rb, w, n_right, among, info_ref, *refs):
    out_ref, left, right, acc, value, cols, coded, scalars, codes, ends, lsem, rsem, osem, csem = refs[-14:]
    right_bufs, left_bufs = refs[:n_right], refs[:1] + refs[n_right:-14]
    rows, width = left.shape[1] - EXTRA, left.shape[2]
    names = pl.ds(rows, EXTRA)
    for slot in range(slots):
        fetch(info_ref[slot], among[slot], [buf.at[names] for buf in left_bufs], cols.at[slot], csem.at[slot])
    for step in range(STEPS):
        at = slots + step
        fetch(info_ref[at], among[at], [buf.at[names] for buf in right_bufs], cols.at[at], csem.at[at])
    for step in range(STEPS):
        fetch(info_ref[slots + step], among[slots + step], right_bufs, right.at[step], rsem.at[step])
    for slot in range(slots):
        fetch(info_ref[slot], among[slot], left_bufs, left.at[slot], lsem.at[slot])

    def clear(first, rows_count):
        at = pl.ds(pl.multiple_of(first, 8), rows_count)
        acc[at, :] = jnp.zeros((rows_count, acc.shape[1]), jnp.float32)

    beside = BS // 64 * 24
    ahead = (BS - beside) * rb // BS

    def clear_blocks(first, last):
        @pl.loop(first, last)
        def _(block):
            clear(block * BS, BS)

    clear_blocks(0, ahead // 2)
    lanes = scalars.shape[1]
    row = lax.broadcasted_iota(jnp.int32, (w, lanes), 1)
    tile_slot = lax.broadcasted_iota(jnp.int32, (w, lanes), 0)
    for slot in range(slots):
        used = info_ref[slot] >= 0

        @pl.when(used)
        def _():
            pltpu.make_async_copy(left_bufs[0].at[names], cols.at[slot], csem.at[slot]).wait()

        inner = cols[slot, 0:w, 0:lanes].astype(jnp.int32)
        valid = (inner >= 0) & (row < rb)
        step = jnp.full(inner.shape, info_ref[slots + STEPS + slot], jnp.int32)
        for _ in range(ratio - 1):
            beyond = inner >= rb
            step = jnp.where(beyond, step + 1, step)
            inner = jnp.where(beyond, inner - rb, inner)
        step = jnp.where(step >= n_row, step - n_row, step)
        code = inner | tile_slot << 8 | slot << 12 | row << 16 | step << 24
        valid = valid & (step < STEPS)
        coded[slot * w : (slot + 1) * w, :] = jnp.where(valid, jnp.where(used, code, -1), -1)
    for step in range(STEPS):
        pltpu.make_async_copy(right_bufs[0].at[names], cols.at[slots + step], csem.at[slots + step]).wait()
        col = cols[slots + step, 0:w, 0:lanes].astype(jnp.int32)
        code = (col >> 1) * 2 * BS | (col & 1) << 16
        coded[(slots + step) * w : (slots + step + 1) * w, :] = jnp.where(col < 0, 2 << 16, code)
    coded[(slots + STEPS) * w : (slots + STEPS + 1) * w, :] = jnp.full((w, lanes), 2 << 16, jnp.int32)
    to_scalars = pltpu.make_async_copy(coded, scalars, csem.at[slots + STEPS])
    to_scalars.start()
    clear_blocks(ahead // 2, ahead)
    to_scalars.wait()

    part_rows = rb // PARTS

    def listed(row, place):
        for code in [scalars[line, row] for line in range(slots * w)]:
            codes[place] = code
            place = place + (code >= 0).astype(jnp.int32)
        ends[row] = (place + UNROLL - 1) // UNROLL
        clear(ahead * BS + row * beside, beside)
        return place

    listed_end = lax.fori_loop(0, rb, listed, jnp.int32(0))
    for u in range(UNROLL):
        codes[listed_end + u] = STEPS << 24

    for step in range(STEPS):
        pltpu.make_async_copy(right_bufs[0], right.at[step], rsem.at[step]).wait()
    for slot in range(slots):
        @pl.when(info_ref[slot] >= 0)
        def _():
            pltpu.make_async_copy(left_bufs[0], left.at[slot], lsem.at[slot]).wait()

    half = lax.broadcasted_iota(jnp.int32, (BS, 2 * BS), 1) // BS

    def block_at(index):
        return pl.ds(pl.multiple_of(index * BS, BS), BS)

    def product(code):
        slot = (code >> 8) & 15
        x = left[(code >> 12) & 15, block_at((code >> 16) & 255), pl.ds(pl.multiple_of((slot >> 1) * 2 * BS, 2 * BS), 2 * BS)]
        both = jnp.where(half == (slot & 1), x, pltpu.roll(x, BS, 1))
        hi = both.astype(jnp.bfloat16).astype(jnp.float32)
        lhs = jnp.where(half == 0, hi, both - hi).astype(jnp.bfloat16)
        y = right[code >> 24, block_at(code & 255), :]
        hi = y.astype(jnp.bfloat16)
        lo = (y - hi.astype(jnp.float32)).astype(jnp.bfloat16)
        lhs = jnp.concatenate([lhs, lhs], axis=1)
        rhs = jnp.concatenate([hi, hi, lo, lo], axis=0)
        return jnp.dot(lhs, rhs, preferred_element_type=jnp.float32)

    def add(code, product):
        rows_at = block_at((code >> 16) & 255)
        for pair in range(w // 2):
            x = product[:, pair * 2 * BS : (pair + 1) * 2 * BS]
            turned = pltpu.roll(x, BS, 1)
            picked, at = [], []
            for side in range(2):
                place = scalars[(slots + (code >> 24)) * w + 2 * pair + side, code & 255]
                parity = place >> 16
                chosen = jnp.where(parity == side, x, turned)
                picked.append(jnp.where(half == parity, chosen, 0.0))
                at.append(place & 0xFFFF)
            picked[1] = jnp.where(at[0] == at[1], picked[0] + picked[1], picked[1])
            spots = [(rows_at, pl.ds(pl.multiple_of(base, 2 * BS), 2 * BS)) for base in at]
            sums = [acc[spot] + part for spot, part in zip(spots, picked)]
            for spot, total in zip(spots, sums):
                acc[spot] = total

    def out_copy(part):
        at = pl.ds(part * part_rows * BS, part_rows * BS)
        return pltpu.make_async_copy(acc.at[at], out_ref.at[at], osem.at[part])

    def products(group):
        for u in range(UNROLL):
            value[u] = product(codes[group * UNROLL + u])

    def sums(group):
        for u in range(UNROLL):
            add(codes[group * UNROLL + u], value[u])

    last = jnp.maximum(ends[rb - 1] - 1, 0)

    def leave(group):
        for part in range(PARTS):
            @pl.when(jnp.maximum(ends[(part + 1) * part_rows - 1] - 1, 0) == group)
            def _():
                out_copy(part).start()

    products(0)

    @pl.loop(0, last)
    def _(group):
        sums(group)
        products(group + 1)
        leave(group)

    sums(last)
    leave(last)
    for part in range(PARTS):
        out_copy(part).wait()


def local(p_cols, p_data):
    n_row, n_col = lax.axis_size("row"), lax.axis_size("col")
    ratio = n_row // n_col
    row_id, col_id = lax.axis_index("row"), lax.axis_index("col")
    rb, w = p_cols.shape
    rows, width = p_data.shape
    left_perms = left_plan(n_row, n_col, ratio)
    right_perms = right_plan(n_row, n_col, ratio)
    table, slots = device_table(left_perms, right_perms, n_row, n_col, ratio)
    info = jnp.asarray(table)[row_id, col_id]

    smem = pl.BlockSpec(memory_space=pltpu.SMEM)
    hbm = pl.BlockSpec(memory_space=pl.ANY)
    dma = pltpu.SemaphoreType.DMA
    own = pl.pallas_call(
        join_kernel,
        out_shape=jax.ShapeDtypeStruct((rows + EXTRA, width), jnp.float32),
        in_specs=[pl.BlockSpec(memory_space=pltpu.HBM)] * 2,
        out_specs=pl.BlockSpec(memory_space=pltpu.VMEM),
        scratch_shapes=[pltpu.VMEM((w, rb), jnp.int32), dma((2,))],
        compiler_params=pltpu.CompilerParams(vmem_limit_bytes=4 << 20),
        cost_estimate=pl.CostEstimate(flops=0, bytes_accessed=2 << 20, transcendentals=0),
    )(p_cols.T, p_data)

    def carry(perms):
        bufs = [own]
        for source, pairs in perms:
            flat = [(s[0] * n_col + s[1], d[0] * n_col + d[1]) for s, d in pairs]
            bufs.append(lax.ppermute(bufs[source], ("row", "col"), flat))
        return bufs

    left_bufs, right_bufs = carry(left_perms), carry(right_perms)
    out_shape = jax.ShapeDtypeStruct((rows, rb * ratio * BS), jnp.float32)
    bufs = right_bufs + left_bufs[1:]
    among = [sorted(set(table[:, :, i].ravel().tolist()) - {-1}) for i in range(slots + STEPS)]
    codings = -(-(slots + STEPS + 1) * w // 8) * 8
    return pl.pallas_call(
        functools.partial(product_kernel, slots, n_row, ratio, rb, w, len(right_bufs), among),
        out_shape=out_shape,
        in_specs=[smem] + [hbm] * len(bufs),
        out_specs=hbm,
        scratch_shapes=[
            pltpu.VMEM((slots, rows + EXTRA, width), jnp.float32),
            pltpu.VMEM((STEPS + 1, rows + EXTRA, width), jnp.float32),
            pltpu.VMEM(out_shape.shape, jnp.float32),
            pltpu.VMEM((UNROLL, BS, width), jnp.float32),
            pltpu.VMEM((slots + STEPS, EXTRA, width), jnp.float32),
            pltpu.VMEM((codings, 128), jnp.int32),
            pltpu.SMEM((codings, 128), jnp.int32),
            pltpu.SMEM((slots * rb * w + UNROLL,), jnp.int32),
            pltpu.SMEM((rb,), jnp.int32),
            dma((slots,)),
            dma((STEPS,)),
            dma((PARTS,)),
            dma((slots + STEPS + 1,)),
        ],
        compiler_params=pltpu.CompilerParams(vmem_limit_bytes=18 << 20),
        cost_estimate=pl.CostEstimate(flops=10**9, bytes_accessed=20 << 20, transcendentals=0),
    )(info, *bufs)


def solution(mesh):
    in_specs = (P("row", "col"), P("row", "col"))
    return jax.shard_map(local, mesh=mesh, in_specs=in_specs, out_specs=P("row", "col"), check_vma=False)
```

```python
import functools

import jax
import jax.numpy as jnp
import numpy as np
from jax import lax
from jax.experimental import pallas as pl
from jax.experimental.pallas import tpu as pltpu
from jax.sharding import PartitionSpec as P

BS = 64
STEPS = 4
UNROLL = 8
EXTRA = 8
PARTS = 16


def left_offsets(row, ratio, n_col):
    seen = []
    for step in range(STEPS):
        offset = (row + step) // ratio % n_col
        if offset not in seen:
            seen.append(offset)
    return seen


def shift(rows, step, count):
    return [((r, c), (r, (c + step) % count)) for r in rows for c in range(count)]


def left_plan(n_row, n_col, ratio):
    offsets = [left_offsets(row, ratio, n_col) for row in range(n_row)]
    if (n_row, n_col, ratio) != (8, 4, 2):
        perms = []
        for slot in range(max(len(o) for o in offsets)):
            pairs = [
                ((row, (col + offsets[row][slot]) % n_col), (row, col))
                for row in range(n_row)
                for col in range(n_col)
                if slot < len(offsets[row]) and offsets[row][slot] != 0
            ]
            perms.append((0, pairs))
        return perms
    whole = [r for r in range(8) if {1, 2, 3} <= set(offsets[r])]
    once, twice = {-1: [], 1: []}, {-1: [], 1: []}
    for r in range(8):
        for offset, step in ((1, -1), (3, 1)):
            if offset in offsets[r] and r not in whole:
                once[step].append(r)
                if 2 in offsets[r]:
                    twice[step].append(r)
    down = shift([r for r in once[-1] if r != 0], -1, 4) + [((3, c), (3, c - 1)) for c in (1, 2, 3)] + [((3, 0), (0, 0))]
    up = shift(once[1], 1, 4) + shift([0], -1, 4) + [((3, c), (3, c + 1)) for c in (0, 1, 2)] + [((3, 3), (1, 3))]
    again_down = shift(twice[-1], -1, 4) + [((3, 1), (3, 0)), ((3, 2), (3, 1)), ((0, 0), (3, 3))]
    again_up = shift(twice[1], 1, 4) + [((3, 1), (3, 2)), ((3, 2), (3, 3)), ((1, 3), (3, 0))]
    return [(0, up), (0, down), (1, again_up), (2, again_down)]


def right_plan(n_row, n_col, ratio):
    everyone = [(row, col) for row in range(n_row) for col in range(n_col)]
    if (n_row, n_col, ratio) != (8, 4, 2):
        return [
            (0, [(((r + ratio * c + step) % n_row, c), (r, c)) for r, c in everyone if (ratio * c + step) % n_row])
            for step in range(STEPS)
        ]
    first = [(((r + 2 * c) % 8, c), (r, c)) for r, c in everyone if c != 0]
    first += [((r ^ 1, 0), (r, 0)) for r in range(8)]
    second = [(((r + 2 * c + 2) % 8, c), (r, c)) for r, c in everyone if c != 3]
    second += [((r ^ 1, 3), (r, 3)) for r in range(8)]
    last = [(((r - 1 + 2 * c + 4) % 8, c), (r, c)) for r, c in everyone if r % 2 == 1]
    last += [((r + 1, c), (r, c)) for r, c in everyone if r % 2 == 0]
    swap = [((r ^ 1, c), (r, c)) for r, c in everyone]
    return [(0, first), (0, second), (0, last), (1, swap), (2, swap)]


def carry_out(perms, n_row, n_col):
    held = [{(r, c): (r, c) for r in range(n_row) for c in range(n_col)}]
    for source, pairs in perms:
        held.append({dst: held[source][src] for src, dst in pairs if src in held[source]})
    return held


def device_table(left_perms, right_perms, n_row, n_col, ratio):
    left_held = carry_out(left_perms, n_row, n_col)
    right_held = carry_out(right_perms, n_row, n_col)
    slots = (ratio - 1 + STEPS - 1) // ratio + 1
    table = np.full((n_row, n_col, 2 * slots + STEPS), -1, np.int32)

    def find(held, device, tile):
        return [i for i, h in enumerate(held) if h.get(device) == tile][0]

    for r in range(n_row):
        for c in range(n_col):
            for slot, offset in enumerate(left_offsets(r, ratio, n_col)):
                tile_col = (c + offset) % n_col
                table[r, c, slot] = find(left_held, (r, c), (r, tile_col))
                table[r, c, slots + STEPS + slot] = (tile_col * ratio - r - ratio * c) % n_row
            for step in range(STEPS):
                table[r, c, slots + step] = find(right_held, (r, c), ((r + ratio * c + step) % n_row, c))
    return table, slots


def fetch(choice, among, bufs, target, sem):
    for number in among:
        @pl.when(choice == number)
        def _():
            pltpu.make_async_copy(bufs[number], target, sem).start()


def join_kernel(cols_ref, data_ref, out_ref, cols, sem):
    rows = data_ref.shape[0]
    data_copy = pltpu.make_async_copy(data_ref, out_ref.at[pl.ds(0, rows)], sem.at[0])
    cols_copy = pltpu.make_async_copy(cols_ref, cols, sem.at[1])
    data_copy.start()
    cols_copy.start()
    out_ref[pl.ds(rows, EXTRA), :] = jnp.zeros((EXTRA, out_ref.shape[1]), jnp.float32)
    cols_copy.wait()
    out_ref[pl.ds(rows, cols.shape[0]), pl.ds(0, cols.shape[1])] = cols[...].astype(jnp.float32)
    data_copy.wait()


def bufs_rows(bufs):
    return bufs[0].shape[0] - EXTRA


def product_kernel(slots, n_row, ratio, rb, w, n_right, among, info_ref, *refs):
    out_ref, left, right, acc, value, cols, coded, scalars, codes, ends, lsem, rsem, osem, csem = refs[-14:]
    right_bufs, left_bufs = refs[:n_right], refs[:1] + refs[n_right:-14]
    rows, width = bufs_rows(right_bufs), left.shape[1]
    names, tile = pl.ds(rows, EXTRA), pl.ds(0, rows)
    place_of = lambda ref, index: ref.at[pl.ds(index * rows, rows)]
    for slot in range(slots):
        fetch(info_ref[slot], among[slot], [buf.at[names] for buf in left_bufs], cols.at[slot], csem.at[slot])
    for step in range(STEPS):
        at = slots + step
        fetch(info_ref[at], among[at], [buf.at[names] for buf in right_bufs], cols.at[at], csem.at[at])
    for step in range(STEPS):
        fetch(info_ref[slots + step], among[slots + step], [buf.at[tile] for buf in right_bufs], place_of(right, step), rsem.at[step])
    for slot in range(slots):
        fetch(info_ref[slot], among[slot], [buf.at[tile] for buf in left_bufs], place_of(left, slot), lsem.at[slot])

    def clear(first, rows_count):
        at = pl.ds(pl.multiple_of(first, 8), rows_count)
        acc[at, :] = jnp.zeros((rows_count, acc.shape[1]), jnp.float32)

    beside = BS // 64 * 24
    ahead = (BS - beside) * rb // BS

    def clear_blocks(first, last):
        @pl.loop(first, last)
        def _(block):
            clear(block * BS, BS)

    clear_blocks(0, ahead // 2)
    lanes = scalars.shape[1]
    row = lax.broadcasted_iota(jnp.int32, (w, lanes), 1)
    tile_slot = lax.broadcasted_iota(jnp.int32, (w, lanes), 0)
    for slot in range(slots):
        used = info_ref[slot] >= 0

        @pl.when(used)
        def _():
            pltpu.make_async_copy(left_bufs[0].at[names], cols.at[slot], csem.at[slot]).wait()

        inner = cols[slot, 0:w, 0:lanes].astype(jnp.int32)
        valid = (inner >= 0) & (row < rb)
        step = jnp.full(inner.shape, info_ref[slots + STEPS + slot], jnp.int32)
        for _ in range(ratio - 1):
            beyond = inner >= rb
            step = jnp.where(beyond, step + 1, step)
            inner = jnp.where(beyond, inner - rb, inner)
        step = jnp.where(step >= n_row, step - n_row, step)
        code = step * rb + inner | tile_slot << 8 | slot * rb + row << 12 | row << 20
        valid = valid & (step < STEPS)
        coded[slot * w : (slot + 1) * w, :] = jnp.where(valid, jnp.where(used, code, -1), -1)
    places = jnp.full((w, lanes), 2 << 16, jnp.int32)
    for step in range(STEPS):
        pltpu.make_async_copy(right_bufs[0].at[names], cols.at[slots + step], csem.at[slots + step]).wait()
        col = cols[slots + step, 0:w, 0:lanes].astype(jnp.int32)
        place = jnp.where(col < 0, 2 << 16, (col >> 1) * 2 * BS | (col & 1) << 16)
        own_lanes = (row >= step * rb) & (row < (step + 1) * rb)
        places = jnp.where(own_lanes, pltpu.roll(place, step * rb, 1) if step else place, places)
    coded[slots * w : (slots + 1) * w, :] = places
    to_scalars = pltpu.make_async_copy(coded, scalars, csem.at[slots + STEPS])
    to_scalars.start()
    clear_blocks(ahead // 2, ahead)
    to_scalars.wait()

    part_rows = rb // PARTS

    def listed(row, place):
        for code in [scalars[line, row] for line in range(slots * w)]:
            codes[place] = code
            place = place + (code >= 0).astype(jnp.int32)
        ends[row] = (place + UNROLL - 1) // UNROLL
        clear(ahead * BS + row * beside, beside)
        return place

    listed_end = lax.fori_loop(0, rb, listed, jnp.int32(0))
    for u in range(UNROLL):
        codes[listed_end + u] = STEPS * rb

    for step in range(STEPS):
        pltpu.make_async_copy(right_bufs[0].at[tile], place_of(right, step), rsem.at[step]).wait()
    for slot in range(slots):
        @pl.when(info_ref[slot] >= 0)
        def _():
            pltpu.make_async_copy(left_bufs[0].at[tile], place_of(left, slot), lsem.at[slot]).wait()

    half = lax.broadcasted_iota(jnp.int32, (BS, 2 * BS), 1) // BS

    def block_at(index):
        return pl.ds(pl.multiple_of(index * BS, BS), BS)

    def product(code):
        slot = (code >> 8) & 15
        x = left[block_at((code >> 12) & 255), pl.ds(pl.multiple_of((slot >> 1) * 2 * BS, 2 * BS), 2 * BS)]
        both = jnp.where(half == (slot & 1), x, pltpu.roll(x, BS, 1))
        hi = both.astype(jnp.bfloat16).astype(jnp.float32)
        lhs = jnp.where(half == 0, hi, both - hi).astype(jnp.bfloat16)
        y = right[block_at(code & 255), :]
        hi = y.astype(jnp.bfloat16)
        lo = (y - hi.astype(jnp.float32)).astype(jnp.bfloat16)
        lhs = jnp.concatenate([lhs, lhs], axis=1)
        rhs = jnp.concatenate([hi, hi, lo, lo], axis=0)
        return jnp.dot(lhs, rhs, preferred_element_type=jnp.float32)

    def add(code, product):
        rows_at = block_at(code >> 20)
        for pair in range(w // 2):
            x = product[:, pair * 2 * BS : (pair + 1) * 2 * BS]
            turned = pltpu.roll(x, BS, 1)
            picked, at = [], []
            for side in range(2):
                place = scalars[slots * w + 2 * pair + side, code & 255]
                parity = place >> 16
                chosen = jnp.where(parity == side, x, turned)
                picked.append(jnp.where(half == parity, chosen, 0.0))
                at.append(place & 0xFFFF)
            picked[1] = jnp.where(at[0] == at[1], picked[0] + picked[1], picked[1])
            spots = [(rows_at, pl.ds(pl.multiple_of(base, 2 * BS), 2 * BS)) for base in at]
            sums = [acc[spot] + part for spot, part in zip(spots, picked)]
            for spot, total in zip(spots, sums):
                acc[spot] = total

    def out_copy(part):
        at = pl.ds(part * part_rows * BS, part_rows * BS)
        return pltpu.make_async_copy(acc.at[at], out_ref.at[at], osem.at[part])

    def products(group):
        for u in range(UNROLL):
            value[u] = product(codes[group * UNROLL + u])

    def sums(group):
        for u in range(UNROLL):
            add(codes[group * UNROLL + u], value[u])

    last = jnp.maximum(ends[rb - 1] - 1, 0)

    def leave(group):
        for part in range(PARTS):
            @pl.when(jnp.maximum(ends[(part + 1) * part_rows - 1] - 1, 0) == group)
            def _():
                out_copy(part).start()

    products(0)

    @pl.loop(0, last)
    def _(group):
        sums(group)
        products(group + 1)
        leave(group)

    sums(last)
    leave(last)
    for part in range(PARTS):
        out_copy(part).wait()


def local(p_cols, p_data):
    n_row, n_col = lax.axis_size("row"), lax.axis_size("col")
    ratio = n_row // n_col
    row_id, col_id = lax.axis_index("row"), lax.axis_index("col")
    rb, w = p_cols.shape
    rows, width = p_data.shape
    left_perms = left_plan(n_row, n_col, ratio)
    right_perms = right_plan(n_row, n_col, ratio)
    table, slots = device_table(left_perms, right_perms, n_row, n_col, ratio)
    info = jnp.asarray(table)[row_id, col_id]

    smem = pl.BlockSpec(memory_space=pltpu.SMEM)
    hbm = pl.BlockSpec(memory_space=pl.ANY)
    dma = pltpu.SemaphoreType.DMA
    own = pl.pallas_call(
        join_kernel,
        out_shape=jax.ShapeDtypeStruct((rows + EXTRA, width), jnp.float32),
        in_specs=[pl.BlockSpec(memory_space=pltpu.HBM)] * 2,
        out_specs=pl.BlockSpec(memory_space=pltpu.VMEM),
        scratch_shapes=[pltpu.VMEM((w, rb), jnp.int32), dma((2,))],
        compiler_params=pltpu.CompilerParams(vmem_limit_bytes=4 << 20),
        cost_estimate=pl.CostEstimate(flops=0, bytes_accessed=2 << 20, transcendentals=0),
    )(p_cols.T, p_data)

    def carry(perms):
        bufs = [own]
        for source, pairs in perms:
            flat = [(s[0] * n_col + s[1], d[0] * n_col + d[1]) for s, d in pairs]
            bufs.append(lax.ppermute(bufs[source], ("row", "col"), flat))
        return bufs

    left_bufs, right_bufs = carry(left_perms), carry(right_perms)
    out_shape = jax.ShapeDtypeStruct((rows, rb * ratio * BS), jnp.float32)
    bufs = right_bufs + left_bufs[1:]
    among = [sorted(set(table[:, :, i].ravel().tolist()) - {-1}) for i in range(slots + STEPS)]
    codings = -(-(slots + 1) * w // 8) * 8
    return pl.pallas_call(
        functools.partial(product_kernel, slots, n_row, ratio, rb, w, len(right_bufs), among),
        out_shape=out_shape,
        in_specs=[smem] + [hbm] * len(bufs),
        out_specs=hbm,
        scratch_shapes=[
            pltpu.VMEM((slots * rows, width), jnp.float32),
            pltpu.VMEM((STEPS * rows + BS, width), jnp.float32),
            pltpu.VMEM(out_shape.shape, jnp.float32),
            pltpu.VMEM((UNROLL, BS, width), jnp.float32),
            pltpu.VMEM((slots + STEPS, EXTRA, width), jnp.float32),
            pltpu.VMEM((codings, 128), jnp.int32),
            pltpu.SMEM((codings, 128), jnp.int32),
            pltpu.SMEM((slots * rb * w + UNROLL,), jnp.int32),
            pltpu.SMEM((rb,), jnp.int32),
            dma((slots,)),
            dma((STEPS,)),
            dma((PARTS,)),
            dma((slots + STEPS + 1,)),
        ],
        compiler_params=pltpu.CompilerParams(vmem_limit_bytes=18 << 20),
        cost_estimate=pl.CostEstimate(flops=10**9, bytes_accessed=20 << 20, transcendentals=0),
    )(info, *bufs)


def solution(mesh):
    in_specs = (P("row", "col"), P("row", "col"))
    return jax.shard_map(local, mesh=mesh, in_specs=in_specs, out_specs=P("row", "col"), check_vma=False)
```

```python
import functools

import jax
import jax.numpy as jnp
import numpy as np
from jax import lax
from jax.experimental import pallas as pl
from jax.experimental.pallas import tpu as pltpu
from jax.sharding import PartitionSpec as P

BS = 64
STEPS = 4
UNROLL = 12
EXTRA = 8
PARTS = 16


def left_offsets(row, ratio, n_col):
    seen = []
    for step in range(STEPS):
        offset = (row + step) // ratio % n_col
        if offset not in seen:
            seen.append(offset)
    return seen


def shift(rows, step, count):
    return [((r, c), (r, (c + step) % count)) for r in rows for c in range(count)]


def left_plan(n_row, n_col, ratio):
    offsets = [left_offsets(row, ratio, n_col) for row in range(n_row)]
    if (n_row, n_col, ratio) != (8, 4, 2):
        perms = []
        for slot in range(max(len(o) for o in offsets)):
            pairs = [
                ((row, (col + offsets[row][slot]) % n_col), (row, col))
                for row in range(n_row)
                for col in range(n_col)
                if slot < len(offsets[row]) and offsets[row][slot] != 0
            ]
            perms.append((0, pairs))
        return perms
    whole = [r for r in range(8) if {1, 2, 3} <= set(offsets[r])]
    once, twice = {-1: [], 1: []}, {-1: [], 1: []}
    for r in range(8):
        for offset, step in ((1, -1), (3, 1)):
            if offset in offsets[r] and r not in whole:
                once[step].append(r)
                if 2 in offsets[r]:
                    twice[step].append(r)
    plain = lambda step: [r for r in once[step] if r not in twice[step] and r != 7]
    early = shift(twice[-1] + [7], -1, 4) + shift(twice[1], 1, 4)
    early += [((3, c), (3, c - 1)) for c in (1, 2, 3)] + [((3, 0), (0, 0))]
    late = shift(plain(-1), -1, 4) + shift(plain(1) + [7], 1, 4)
    late += [((3, c), (3, c + 1)) for c in (0, 1, 2)] + [((3, 3), (1, 3))]
    again_early = shift(twice[-1], -1, 4) + shift(twice[1], 1, 4) + [((3, 1), (3, 0)), ((3, 2), (3, 1)), ((0, 0), (3, 3))]
    again_late = [((3, 1), (3, 2)), ((3, 2), (3, 3)), ((1, 3), (3, 0))]
    return [(0, late), (0, early), (1, again_late), (2, again_early)]


def right_plan(n_row, n_col, ratio):
    everyone = [(row, col) for row in range(n_row) for col in range(n_col)]
    if (n_row, n_col, ratio) != (8, 4, 2):
        return [
            (0, [(((r + ratio * c + step) % n_row, c), (r, c)) for r, c in everyone if (ratio * c + step) % n_row])
            for step in range(STEPS)
        ]
    first = [(((r + 2 * c) % 8, c), (r, c)) for r, c in everyone if c != 0]
    first += [((r ^ 1, 0), (r, 0)) for r in range(8)]
    second = [(((r + 2 * c + 2) % 8, c), (r, c)) for r, c in everyone if c != 3]
    second += [((r ^ 1, 3), (r, 3)) for r in range(8)]
    last = [(((r - 1 + 2 * c + 4) % 8, c), (r, c)) for r, c in everyone if r % 2 == 1]
    last += [((r + 1, c), (r, c)) for r, c in everyone if r % 2 == 0]
    swap = [((r ^ 1, c), (r, c)) for r, c in everyone]
    return [(0, first), (0, second), (0, last), (1, swap), (2, swap)]


def carry_out(perms, n_row, n_col):
    held = [{(r, c): (r, c) for r in range(n_row) for c in range(n_col)}]
    for source, pairs in perms:
        held.append({dst: held[source][src] for src, dst in pairs if src in held[source]})
    return held


def device_table(left_perms, right_perms, n_row, n_col, ratio):
    left_held = carry_out(left_perms, n_row, n_col)
    right_held = carry_out(right_perms, n_row, n_col)
    slots = (ratio - 1 + STEPS - 1) // ratio + 1
    table = np.full((n_row, n_col, 2 * slots + STEPS), -1, np.int32)

    def find(held, device, tile):
        return [i for i, h in enumerate(held) if h.get(device) == tile][0]

    for r in range(n_row):
        for c in range(n_col):
            for slot, offset in enumerate(left_offsets(r, ratio, n_col)):
                tile_col = (c + offset) % n_col
                table[r, c, slot] = find(left_held, (r, c), (r, tile_col))
                table[r, c, slots + STEPS + slot] = (tile_col * ratio - r - ratio * c) % n_row
            for step in range(STEPS):
                table[r, c, slots + step] = find(right_held, (r, c), ((r + ratio * c + step) % n_row, c))
    return table, slots


def fetch(choice, among, bufs, target, sem):
    for number in among:
        @pl.when(choice == number)
        def _():
            pltpu.make_async_copy(bufs[number], target, sem).start()


def join_kernel(cols_ref, data_ref, out_ref, cols, sem):
    rows = data_ref.shape[0]
    data_copy = pltpu.make_async_copy(data_ref, out_ref.at[pl.ds(0, rows)], sem.at[0])
    cols_copy = pltpu.make_async_copy(cols_ref, cols, sem.at[1])
    data_copy.start()
    cols_copy.start()
    out_ref[pl.ds(rows, EXTRA), :] = jnp.zeros((EXTRA, out_ref.shape[1]), jnp.float32)
    cols_copy.wait()
    out_ref[pl.ds(rows, cols.shape[0]), pl.ds(0, cols.shape[1])] = cols[...].astype(jnp.float32)
    data_copy.wait()


def bufs_rows(bufs):
    return bufs[0].shape[0] - EXTRA


def product_kernel(slots, n_row, ratio, rb, w, n_right, among, info_ref, *refs):
    out_ref, left, right, acc, value, cols, coded, scalars, codes, ends, lsem, rsem, osem, csem = refs[-14:]
    right_bufs, left_bufs = refs[:n_right], refs[:1] + refs[n_right:-14]
    rows, width = bufs_rows(right_bufs), left.shape[1]
    names, tile = pl.ds(rows, EXTRA), pl.ds(0, rows)
    place_of = lambda ref, index: ref.at[pl.ds(index * rows, rows)]
    for slot in range(slots):
        fetch(info_ref[slot], among[slot], [buf.at[names] for buf in left_bufs], cols.at[slot], csem.at[slot])
    for step in range(STEPS):
        at = slots + step
        fetch(info_ref[at], among[at], [buf.at[names] for buf in right_bufs], cols.at[at], csem.at[at])
    for step in range(STEPS):
        fetch(info_ref[slots + step], among[slots + step], [buf.at[tile] for buf in right_bufs], place_of(right, step), rsem.at[step])
    for slot in range(slots):
        fetch(info_ref[slot], among[slot], [buf.at[tile] for buf in left_bufs], place_of(left, slot), lsem.at[slot])

    def clear(first, rows_count):
        at = pl.ds(pl.multiple_of(first, 8), rows_count)
        acc[at, :] = jnp.zeros((rows_count, acc.shape[1]), jnp.float32)

    beside = BS // 64 * 24
    ahead = (BS - beside) * rb // BS

    def clear_blocks(first, last):
        @pl.loop(first, last)
        def _(block):
            clear(block * BS, BS)

    clear_blocks(0, ahead // 2)
    lanes = scalars.shape[1]
    row = lax.broadcasted_iota(jnp.int32, (w, lanes), 1)
    tile_slot = lax.broadcasted_iota(jnp.int32, (w, lanes), 0)
    for slot in range(slots):
        used = info_ref[slot] >= 0

        @pl.when(used)
        def _():
            pltpu.make_async_copy(left_bufs[0].at[names], cols.at[slot], csem.at[slot]).wait()

        inner = cols[slot, 0:w, 0:lanes].astype(jnp.int32)
        valid = (inner >= 0) & (row < rb)
        step = jnp.full(inner.shape, info_ref[slots + STEPS + slot], jnp.int32)
        for _ in range(ratio - 1):
            beyond = inner >= rb
            step = jnp.where(beyond, step + 1, step)
            inner = jnp.where(beyond, inner - rb, inner)
        step = jnp.where(step >= n_row, step - n_row, step)
        code = step * rb + inner | tile_slot << 8 | slot * rb + row << 12 | row << 20
        valid = valid & (step < STEPS)
        coded[slot * w : (slot + 1) * w, :] = jnp.where(valid, jnp.where(used, code, -1), -1)
    places = jnp.full((w, lanes), 2 << 16, jnp.int32)
    for step in range(STEPS):
        pltpu.make_async_copy(right_bufs[0].at[names], cols.at[slots + step], csem.at[slots + step]).wait()
        col = cols[slots + step, 0:w, 0:lanes].astype(jnp.int32)
        place = jnp.where(col < 0, 2 << 16, (col >> 1) * 2 * BS | (col & 1) << 16)
        own_lanes = (row >= step * rb) & (row < (step + 1) * rb)
        places = jnp.where(own_lanes, pltpu.roll(place, step * rb, 1) if step else place, places)
    coded[slots * w : (slots + 1) * w, :] = places
    to_scalars = pltpu.make_async_copy(coded, scalars, csem.at[slots + STEPS])
    to_scalars.start()
    clear_blocks(ahead // 2, ahead)
    to_scalars.wait()

    part_rows = rb // PARTS

    def listed(row, place):
        for code in [scalars[line, row] for line in range(slots * w)]:
            codes[place] = code
            place = place + (code >= 0).astype(jnp.int32)
        ends[row] = (place + UNROLL - 1) // UNROLL
        clear(ahead * BS + row * beside, beside)
        return place

    listed_end = lax.fori_loop(0, rb, listed, jnp.int32(0))
    for u in range(UNROLL):
        codes[listed_end + u] = STEPS * rb

    for step in range(STEPS):
        pltpu.make_async_copy(right_bufs[0].at[tile], place_of(right, step), rsem.at[step]).wait()
    for slot in range(slots):
        @pl.when(info_ref[slot] >= 0)
        def _():
            pltpu.make_async_copy(left_bufs[0].at[tile], place_of(left, slot), lsem.at[slot]).wait()

    half = lax.broadcasted_iota(jnp.int32, (BS, 2 * BS), 1) // BS

    def block_at(index):
        return pl.ds(pl.multiple_of(index * BS, BS), BS)

    def product(code):
        slot = (code >> 8) & 15
        x = left[block_at((code >> 12) & 255), pl.ds(pl.multiple_of((slot >> 1) * 2 * BS, 2 * BS), 2 * BS)]
        both = jnp.where(half == (slot & 1), x, pltpu.roll(x, BS, 1))
        hi = both.astype(jnp.bfloat16).astype(jnp.float32)
        lhs = jnp.where(half == 0, hi, both - hi).astype(jnp.bfloat16)
        y = right[block_at(code & 255), :]
        hi = y.astype(jnp.bfloat16)
        lo = (y - hi.astype(jnp.float32)).astype(jnp.bfloat16)
        lhs = jnp.concatenate([lhs, lhs], axis=1)
        rhs = jnp.concatenate([hi, hi, lo, lo], axis=0)
        return jnp.dot(lhs, rhs, preferred_element_type=jnp.float32)

    def add(code, product):
        rows_at = block_at(code >> 20)
        for pair in range(w // 2):
            x = product[:, pair * 2 * BS : (pair + 1) * 2 * BS]
            turned = pltpu.roll(x, BS, 1)
            picked, at = [], []
            for side in range(2):
                place = scalars[slots * w + 2 * pair + side, code & 255]
                parity = place >> 16
                chosen = jnp.where(parity == side, x, turned)
                picked.append(jnp.where(half == parity, chosen, 0.0))
                at.append(place & 0xFFFF)
            picked[1] = jnp.where(at[0] == at[1], picked[0] + picked[1], picked[1])
            spots = [(rows_at, pl.ds(pl.multiple_of(base, 2 * BS), 2 * BS)) for base in at]
            sums = [acc[spot] + part for spot, part in zip(spots, picked)]
            for spot, total in zip(spots, sums):
                acc[spot] = total

    def out_copy(part):
        at = pl.ds(part * part_rows * BS, part_rows * BS)
        return pltpu.make_async_copy(acc.at[at], out_ref.at[at], osem.at[part])

    def products(group):
        for u in range(UNROLL):
            value[u] = product(codes[group * UNROLL + u])

    def sums(group):
        for u in range(UNROLL):
            add(codes[group * UNROLL + u], value[u])

    last = jnp.maximum(ends[rb - 1] - 1, 0)

    def leave(group):
        for part in range(PARTS):
            @pl.when(jnp.maximum(ends[(part + 1) * part_rows - 1] - 1, 0) == group)
            def _():
                out_copy(part).start()

    products(0)

    @pl.loop(0, last)
    def _(group):
        sums(group)
        products(group + 1)
        leave(group)

    sums(last)
    leave(last)
    for part in range(PARTS):
        out_copy(part).wait()


def local(p_cols, p_data):
    n_row, n_col = lax.axis_size("row"), lax.axis_size("col")
    ratio = n_row // n_col
    row_id, col_id = lax.axis_index("row"), lax.axis_index("col")
    rb, w = p_cols.shape
    rows, width = p_data.shape
    left_perms = left_plan(n_row, n_col, ratio)
    right_perms = right_plan(n_row, n_col, ratio)
    table, slots = device_table(left_perms, right_perms, n_row, n_col, ratio)
    info = jnp.asarray(table)[row_id, col_id]

    smem = pl.BlockSpec(memory_space=pltpu.SMEM)
    hbm = pl.BlockSpec(memory_space=pl.ANY)
    dma = pltpu.SemaphoreType.DMA
    own = pl.pallas_call(
        join_kernel,
        out_shape=jax.ShapeDtypeStruct((rows + EXTRA, width), jnp.float32),
        in_specs=[pl.BlockSpec(memory_space=pltpu.HBM)] * 2,
        out_specs=pl.BlockSpec(memory_space=pltpu.VMEM),
        scratch_shapes=[pltpu.VMEM((w, rb), jnp.int32), dma((2,))],
        compiler_params=pltpu.CompilerParams(vmem_limit_bytes=4 << 20),
        cost_estimate=pl.CostEstimate(flops=0, bytes_accessed=2 << 20, transcendentals=0),
    )(p_cols.T, p_data)

    def carry(perms):
        bufs = [own]
        for source, pairs in perms:
            flat = [(s[0] * n_col + s[1], d[0] * n_col + d[1]) for s, d in pairs]
            bufs.append(lax.ppermute(bufs[source], ("row", "col"), flat))
        return bufs

    left_bufs, right_bufs = carry(left_perms), carry(right_perms)
    out_shape = jax.ShapeDtypeStruct((rows, rb * ratio * BS), jnp.float32)
    bufs = right_bufs + left_bufs[1:]
    among = [sorted(set(table[:, :, i].ravel().tolist()) - {-1}) for i in range(slots + STEPS)]
    codings = -(-(slots + 1) * w // 8) * 8
    return pl.pallas_call(
        functools.partial(product_kernel, slots, n_row, ratio, rb, w, len(right_bufs), among),
        out_shape=out_shape,
        in_specs=[smem] + [hbm] * len(bufs),
        out_specs=hbm,
        scratch_shapes=[
            pltpu.VMEM((slots * rows, width), jnp.float32),
            pltpu.VMEM((STEPS * rows + BS, width), jnp.float32),
            pltpu.VMEM(out_shape.shape, jnp.float32),
            pltpu.VMEM((UNROLL, BS, width), jnp.float32),
            pltpu.VMEM((slots + STEPS, EXTRA, width), jnp.float32),
            pltpu.VMEM((codings, 128), jnp.int32),
            pltpu.SMEM((codings, 128), jnp.int32),
            pltpu.SMEM((slots * rb * w + UNROLL,), jnp.int32),
            pltpu.SMEM((rb,), jnp.int32),
            dma((slots,)),
            dma((STEPS,)),
            dma((PARTS,)),
            dma((slots + STEPS + 1,)),
        ],
        compiler_params=pltpu.CompilerParams(vmem_limit_bytes=18 << 20),
        cost_estimate=pl.CostEstimate(flops=10**9, bytes_accessed=20 << 20, transcendentals=0),
    )(info, *bufs)


def solution(mesh):
    in_specs = (P("row", "col"), P("row", "col"))
    return jax.shard_map(local, mesh=mesh, in_specs=in_specs, out_specs=P("row", "col"), check_vma=False)
```

```python
import functools

import jax
import jax.numpy as jnp
import numpy as np
from jax import lax
from jax.experimental import pallas as pl
from jax.experimental.pallas import tpu as pltpu
from jax.sharding import PartitionSpec as P

BS = 64
STEPS = 4
UNROLL = 10
EXTRA = 8
PARTS = 16


def left_offsets(row, ratio, n_col):
    seen = []
    for step in range(STEPS):
        offset = (row + step) // ratio % n_col
        if offset not in seen:
            seen.append(offset)
    return seen


def shift(rows, step, count):
    return [((r, c), (r, (c + step) % count)) for r in rows for c in range(count)]


def left_plan(n_row, n_col, ratio):
    offsets = [left_offsets(row, ratio, n_col) for row in range(n_row)]
    if (n_row, n_col, ratio) != (8, 4, 2):
        perms = []
        for slot in range(max(len(o) for o in offsets)):
            pairs = [
                ((row, (col + offsets[row][slot]) % n_col), (row, col))
                for row in range(n_row)
                for col in range(n_col)
                if slot < len(offsets[row]) and offsets[row][slot] != 0
            ]
            perms.append((0, pairs))
        return perms
    whole = [r for r in range(8) if {1, 2, 3} <= set(offsets[r])]
    once, twice = {-1: [], 1: []}, {-1: [], 1: []}
    for r in range(8):
        for offset, step in ((1, -1), (3, 1)):
            if offset in offsets[r] and r not in whole:
                once[step].append(r)
                if 2 in offsets[r]:
                    twice[step].append(r)
    plain = lambda step: [r for r in once[step] if r not in twice[step] and r != 7]
    early = shift(twice[-1] + [7], -1, 4) + shift(twice[1], 1, 4)
    early += [((3, c), (3, c - 1)) for c in (1, 2, 3)] + [((3, 0), (0, 0))]
    late = shift(plain(-1), -1, 4) + shift(plain(1) + [7], 1, 4)
    late += [((3, c), (3, c + 1)) for c in (0, 1, 2)] + [((3, 3), (1, 3))]
    again_early = shift(twice[-1], -1, 4) + shift(twice[1], 1, 4) + [((3, 1), (3, 0)), ((3, 2), (3, 1)), ((0, 0), (3, 3))]
    again_late = [((3, 1), (3, 2)), ((3, 2), (3, 3)), ((1, 3), (3, 0))]
    return [(0, late), (0, early), (1, again_late), (2, again_early)]


def right_plan(n_row, n_col, ratio):
    everyone = [(row, col) for row in range(n_row) for col in range(n_col)]
    if (n_row, n_col, ratio) != (8, 4, 2):
        return [
            (0, [(((r + ratio * c + step) % n_row, c), (r, c)) for r, c in everyone if (ratio * c + step) % n_row])
            for step in range(STEPS)
        ]
    first = [(((r + 2 * c) % 8, c), (r, c)) for r, c in everyone if c != 0]
    first += [((r ^ 1, 0), (r, 0)) for r in range(8)]
    second = [(((r + 2 * c + 2) % 8, c), (r, c)) for r, c in everyone if c != 3]
    second += [((r ^ 1, 3), (r, 3)) for r in range(8)]
    last = [(((r - 1 + 2 * c + 4) % 8, c), (r, c)) for r, c in everyone if r % 2 == 1]
    last += [((r + 1, c), (r, c)) for r, c in everyone if r % 2 == 0]
    swap = [((r ^ 1, c), (r, c)) for r, c in everyone]
    return [(0, first), (0, second), (0, last), (1, swap), (2, swap)]


def carry_out(perms, n_row, n_col):
    held = [{(r, c): (r, c) for r in range(n_row) for c in range(n_col)}]
    for source, pairs in perms:
        held.append({dst: held[source][src] for src, dst in pairs if src in held[source]})
    return held


def device_table(left_perms, right_perms, n_row, n_col, ratio):
    left_held = carry_out(left_perms, n_row, n_col)
    right_held = carry_out(right_perms, n_row, n_col)
    slots = (ratio - 1 + STEPS - 1) // ratio + 1
    table = np.full((n_row, n_col, 2 * slots + STEPS), -1, np.int32)

    def find(held, device, tile):
        return [i for i, h in enumerate(held) if h.get(device) == tile][0]

    for r in range(n_row):
        for c in range(n_col):
            for slot, offset in enumerate(left_offsets(r, ratio, n_col)):
                tile_col = (c + offset) % n_col
                table[r, c, slot] = find(left_held, (r, c), (r, tile_col))
                table[r, c, slots + STEPS + slot] = (tile_col * ratio - r - ratio * c) % n_row
            for step in range(STEPS):
                table[r, c, slots + step] = find(right_held, (r, c), ((r + ratio * c + step) % n_row, c))
    return table, slots


def fetch(choice, among, bufs, target, sem):
    for number in among:
        @pl.when(choice == number)
        def _():
            pltpu.make_async_copy(bufs[number], target, sem).start()


def join_kernel(cols_ref, data_ref, out_ref, cols, sem):
    rows = data_ref.shape[0]
    data_copy = pltpu.make_async_copy(data_ref, out_ref.at[pl.ds(0, rows)], sem.at[0])
    cols_copy = pltpu.make_async_copy(cols_ref, cols, sem.at[1])
    data_copy.start()
    cols_copy.start()
    out_ref[pl.ds(rows, EXTRA), :] = jnp.zeros((EXTRA, out_ref.shape[1]), jnp.float32)
    cols_copy.wait()
    out_ref[pl.ds(rows, cols.shape[0]), pl.ds(0, cols.shape[1])] = cols[...].astype(jnp.float32)
    data_copy.wait()


def bufs_rows(bufs):
    return bufs[0].shape[0] - EXTRA


def product_kernel(slots, n_row, ratio, rb, w, n_right, among, info_ref, *refs):
    out_ref, left, right, acc, value, cols, coded, scalars, codes, ends, lsem, rsem, osem, csem = refs[-14:]
    right_bufs, left_bufs = refs[:n_right], refs[:1] + refs[n_right:-14]
    rows, width = bufs_rows(right_bufs), left.shape[1]
    names, tile = pl.ds(rows, EXTRA), pl.ds(0, rows)
    place_of = lambda ref, index: ref.at[pl.ds(index * rows, rows)]
    for slot in range(slots):
        fetch(info_ref[slot], among[slot], [buf.at[names] for buf in left_bufs], cols.at[slot], csem.at[slot])
    for step in range(STEPS):
        at = slots + step
        fetch(info_ref[at], among[at], [buf.at[names] for buf in right_bufs], cols.at[at], csem.at[at])
    for step in range(STEPS):
        fetch(info_ref[slots + step], among[slots + step], [buf.at[tile] for buf in right_bufs], place_of(right, step), rsem.at[step])
    for slot in range(slots):
        fetch(info_ref[slot], among[slot], [buf.at[tile] for buf in left_bufs], place_of(left, slot), lsem.at[slot])

    def clear(first, rows_count):
        at = pl.ds(pl.multiple_of(first, 8), rows_count)
        acc[at, :] = jnp.zeros((rows_count, acc.shape[1]), jnp.float32)

    beside = BS // 64 * 24
    ahead = (BS - beside) * rb // BS

    def clear_blocks(first, last):
        @pl.loop(first, last)
        def _(block):
            clear(block * BS, BS)

    clear_blocks(0, ahead // 2)
    lanes = scalars.shape[1]
    row = lax.broadcasted_iota(jnp.int32, (w, lanes), 1)
    tile_slot = lax.broadcasted_iota(jnp.int32, (w, lanes), 0)
    for slot in range(slots):
        used = info_ref[slot] >= 0

        @pl.when(used)
        def _():
            pltpu.make_async_copy(left_bufs[0].at[names], cols.at[slot], csem.at[slot]).wait()

        inner = cols[slot, 0:w, 0:lanes].astype(jnp.int32)
        valid = (inner >= 0) & (row < rb)
        step = jnp.full(inner.shape, info_ref[slots + STEPS + slot], jnp.int32)
        for _ in range(ratio - 1):
            beyond = inner >= rb
            step = jnp.where(beyond, step + 1, step)
            inner = jnp.where(beyond, inner - rb, inner)
        step = jnp.where(step >= n_row, step - n_row, step)
        code = step * rb + inner | tile_slot << 8 | slot * rb + row << 12 | row << 20
        valid = valid & (step < STEPS)
        coded[slot * w : (slot + 1) * w, :] = jnp.where(valid, jnp.where(used, code, -1), -1)
    places = jnp.full((w, lanes), 2 << 16, jnp.int32)
    for step in range(STEPS):
        pltpu.make_async_copy(right_bufs[0].at[names], cols.at[slots + step], csem.at[slots + step]).wait()
        col = cols[slots + step, 0:w, 0:lanes].astype(jnp.int32)
        place = jnp.where(col < 0, 2 << 16, (col >> 1) * 2 * BS | (col & 1) << 16)
        own_lanes = (row >= step * rb) & (row < (step + 1) * rb)
        places = jnp.where(own_lanes, pltpu.roll(place, step * rb, 1) if step else place, places)
    coded[slots * w : (slots + 1) * w, :] = places
    to_scalars = pltpu.make_async_copy(coded, scalars, csem.at[slots + STEPS])
    to_scalars.start()
    clear_blocks(ahead // 2, ahead)
    to_scalars.wait()

    part_rows = rb // PARTS

    def listed(row, place):
        for code in [scalars[line, row] for line in range(slots * w)]:
            codes[place] = code
            place = place + (code >= 0).astype(jnp.int32)
        ends[row] = (place + UNROLL - 1) // UNROLL
        clear(ahead * BS + row * beside, beside)
        return place

    listed_end = lax.fori_loop(0, rb, listed, jnp.int32(0))
    for u in range(UNROLL):
        codes[listed_end + u] = STEPS * rb

    for step in range(STEPS):
        pltpu.make_async_copy(right_bufs[0].at[tile], place_of(right, step), rsem.at[step]).wait()
    for slot in range(slots):
        @pl.when(info_ref[slot] >= 0)
        def _():
            pltpu.make_async_copy(left_bufs[0].at[tile], place_of(left, slot), lsem.at[slot]).wait()

    half = lax.broadcasted_iota(jnp.int32, (BS, 2 * BS), 1) // BS

    def block_at(index):
        return pl.ds(pl.multiple_of(index * BS, BS), BS)

    def product(code):
        slot = (code >> 8) & 15
        x = left[block_at((code >> 12) & 255), pl.ds(pl.multiple_of((slot >> 1) * 2 * BS, 2 * BS), 2 * BS)]
        both = jnp.where(half == (slot & 1), x, pltpu.roll(x, BS, 1))
        hi = both.astype(jnp.bfloat16).astype(jnp.float32)
        lhs = jnp.where(half == 0, hi, both - hi).astype(jnp.bfloat16)
        y = right[block_at(code & 255), :]
        hi = y.astype(jnp.bfloat16)
        lo = (y - hi.astype(jnp.float32)).astype(jnp.bfloat16)
        lhs = jnp.concatenate([lhs, lhs], axis=1)
        rhs = jnp.concatenate([hi, hi, lo, lo], axis=0)
        return jnp.dot(lhs, rhs, preferred_element_type=jnp.float32)

    def add(code, product):
        rows_at = block_at(code >> 20)
        for pair in range(w // 2):
            x = product[:, pair * 2 * BS : (pair + 1) * 2 * BS]
            turned = pltpu.roll(x, BS, 1)
            picked, at = [], []
            for side in range(2):
                place = scalars[slots * w + 2 * pair + side, code & 255]
                parity = place >> 16
                chosen = jnp.where(parity == side, x, turned)
                picked.append(jnp.where(half == parity, chosen, 0.0))
                at.append(place & 0xFFFF)
            picked[1] = jnp.where(at[0] == at[1], picked[0] + picked[1], picked[1])
            spots = [(rows_at, pl.ds(pl.multiple_of(base, 2 * BS), 2 * BS)) for base in at]
            sums = [acc[spot] + part for spot, part in zip(spots, picked)]
            for spot, total in zip(spots, sums):
                acc[spot] = total

    def out_copy(part):
        at = pl.ds(part * part_rows * BS, part_rows * BS)
        return pltpu.make_async_copy(acc.at[at], out_ref.at[at], osem.at[part])

    def products(group):
        for u in range(UNROLL):
            value[u] = product(codes[group * UNROLL + u])

    def sums(group):
        for u in range(UNROLL):
            add(codes[group * UNROLL + u], value[u])

    last = jnp.maximum(ends[rb - 1] - 1, 0)

    def leave(group):
        for part in range(PARTS):
            @pl.when(jnp.maximum(ends[(part + 1) * part_rows - 1] - 1, 0) == group)
            def _():
                out_copy(part).start()

    products(0)

    @pl.loop(0, last)
    def _(group):
        sums(group)
        products(group + 1)
        leave(group)

    sums(last)
    leave(last)
    for part in range(PARTS):
        out_copy(part).wait()


def local(p_cols, p_data):
    n_row, n_col = lax.axis_size("row"), lax.axis_size("col")
    ratio = n_row // n_col
    row_id, col_id = lax.axis_index("row"), lax.axis_index("col")
    rb, w = p_cols.shape
    rows, width = p_data.shape
    left_perms = left_plan(n_row, n_col, ratio)
    right_perms = right_plan(n_row, n_col, ratio)
    table, slots = device_table(left_perms, right_perms, n_row, n_col, ratio)
    info = jnp.asarray(table)[row_id, col_id]

    smem = pl.BlockSpec(memory_space=pltpu.SMEM)
    hbm = pl.BlockSpec(memory_space=pl.ANY)
    dma = pltpu.SemaphoreType.DMA
    own = pl.pallas_call(
        join_kernel,
        out_shape=jax.ShapeDtypeStruct((rows + EXTRA, width), jnp.float32),
        in_specs=[pl.BlockSpec(memory_space=pltpu.HBM)] * 2,
        out_specs=pl.BlockSpec(memory_space=pltpu.VMEM),
        scratch_shapes=[pltpu.VMEM((w, rb), jnp.int32), dma((2,))],
        compiler_params=pltpu.CompilerParams(vmem_limit_bytes=4 << 20),
        cost_estimate=pl.CostEstimate(flops=0, bytes_accessed=2 << 20, transcendentals=0),
    )(p_cols.T, p_data)

    def carry(perms):
        bufs = [own]
        for source, pairs in perms:
            flat = [(s[0] * n_col + s[1], d[0] * n_col + d[1]) for s, d in pairs]
            bufs.append(lax.ppermute(bufs[source], ("row", "col"), flat))
        return bufs

    left_bufs, right_bufs = carry(left_perms), carry(right_perms)
    out_shape = jax.ShapeDtypeStruct((rows, rb * ratio * BS), jnp.float32)
    bufs = right_bufs + left_bufs[1:]
    among = [sorted(set(table[:, :, i].ravel().tolist()) - {-1}) for i in range(slots + STEPS)]
    codings = -(-(slots + 1) * w // 8) * 8
    return pl.pallas_call(
        functools.partial(product_kernel, slots, n_row, ratio, rb, w, len(right_bufs), among),
        out_shape=out_shape,
        in_specs=[smem] + [hbm] * len(bufs),
        out_specs=hbm,
        scratch_shapes=[
            pltpu.VMEM((slots * rows, width), jnp.float32),
            pltpu.VMEM((STEPS * rows + BS, width), jnp.float32),
            pltpu.VMEM(out_shape.shape, jnp.float32),
            pltpu.VMEM((UNROLL, BS, width), jnp.float32),
            pltpu.VMEM((slots + STEPS, EXTRA, width), jnp.float32),
            pltpu.VMEM((codings, 128), jnp.int32),
            pltpu.SMEM((codings, 128), jnp.int32),
            pltpu.SMEM((slots * rb * w + UNROLL,), jnp.int32),
            pltpu.SMEM((rb,), jnp.int32),
            dma((slots,)),
            dma((STEPS,)),
            dma((PARTS,)),
            dma((slots + STEPS + 1,)),
        ],
        compiler_params=pltpu.CompilerParams(vmem_limit_bytes=18 << 20),
        cost_estimate=pl.CostEstimate(flops=10**9, bytes_accessed=20 << 20, transcendentals=0),
    )(info, *bufs)


def solution(mesh):
    in_specs = (P("row", "col"), P("row", "col"))
    return jax.shard_map(local, mesh=mesh, in_specs=in_specs, out_specs=P("row", "col"), check_vma=False)
```
